32 devices in a mesh: seq: 2 (over x), dp: 16 (over z, y, core).
Axes of the slice: x: 2, y: 2, z: 4, core: 2. Of those that a mesh axis runs over, the one named last changes fastest.
Arguments:
- hidden_in: bfloat16 [1024, 32, 1024], P('seq', 'dp'), may hold values from -6 to 6
- lengths: int32 [32], P('dp'), may hold values from 128 to 1024, as said below
- w_query: bfloat16 [1024, 1024], replicated, may hold values from -0.1875 to 0.1875
- w_key: bfloat16 [1024, 1024], replicated, may hold values from -0.1875 to 0.1875
- w_value: bfloat16 [1024, 1024], replicated, may hold values from -0.1875 to 0.1875
- w_output: bfloat16 [1024, 1024], replicated, may hold values from -0.75 to 0.75
- attn_gain: float32 [1024], replicated, may hold values from 0.1 to 1.9
- ffn_in: bfloat16 [1024, 4096], replicated, may hold values from -0.1875 to 0.1875
- ffn_out: bfloat16 [4096, 1024], replicated, may hold values from -0.09375 to 0.09375
- ffn_gain: float32 [1024], replicated, may hold values from 0.1 to 1.9
- adapter_down: bfloat16 [1024, 512], replicated, may hold values from -0.1875 to 0.1875
- adapter_down_bias: float32 [512], replicated, may hold values from -3 to 3
- adapter_up: bfloat16 [512, 1024], replicated, may hold values from -0.125 to 0.125
- adapter_up_bias: float32 [1024], replicated, may hold values from -0.9 to 0.9
- prefix_embed: float32 [30, 1024], replicated, may hold values from -6 to 6
- prefix_hidden_w: bfloat16 [1024, 512], replicated, may hold values from -0.1875 to 0.1875
- prefix_hidden_b: float32 [512], replicated, may hold values from -3 to 3
- prefix_out_w: bfloat16 [512, 2048], replicated, may hold values from -0.5 to 0.5
- prefix_out_b: float32 [2048], replicated, may hold values from -3 to 3
- out_grad: bfloat16 [1024, 32, 1024], P('seq', 'dp'), may hold values from -6 to 6
Outputs:
- layer_out: bfloat16 [1024, 32, 1024], P('seq', 'dp')
- hidden_grad: bfloat16 [1024, 32, 1024], P('seq', 'dp')
- adapter_down_grad: float32 [1024, 512], replicated
- adapter_down_bias_grad: float32 [512], replicated
- adapter_up_grad: float32 [512, 1024], replicated
- adapter_up_bias_grad: float32 [1024], replicated
- prefix_embed_grad: float32 [30, 1024], replicated
- prefix_hidden_w_grad: float32 [1024, 512], replicated
- prefix_hidden_b_grad: float32 [512], replicated
- prefix_out_w_grad: float32 [512, 2048], replicated
- prefix_out_b_grad: float32 [2048], replicated
The draws below stay inside these ranges and needn't reach their ends.
Inputs may be any that keep to these rules, and one draw needn't show every extreme that they name: `lengths`: in each aligned group of 2 sequences (those of one index of dp) one sequence, at a place drawn from the seed, has 1024 tokens; positions at or past a sequence's length are padding.
All inputs are finite; a program needn't handle non-finite values.
Results may differ from the reference program's by a relative error of at most 0.02.
Values may be sent and summed in bfloat16 or wider, within the bound.
No kernel may reach another device: no remote copies, remote signals or barrier semaphores. Data moves between devices by JAX's collectives and lax.ppermute only.
A program may use at most 384 MiB of HBM per device.

```python
import math
import jax
import jax.numpy as jnp
from jax import lax

D = 1024
HEADS = 16
FF = 4096
ADAPT = 512
PREFIX = 30
PHID = 512
LEN = 1024
SEQS = 2
BATCH = 32


def draw_lengths(key, part):
    key = jax.random.fold_in(key, 7)
    short_key, long_key, pick_key, full_key = jax.random.split(key, 4)
    shorter = jax.random.randint(short_key, (BATCH,), LEN // 8, LEN // 2)
    longer = jax.random.randint(long_key, (BATCH,), LEN // 2, LEN + 1)
    picker = jax.random.randint(pick_key, (BATCH,), 0, 3)
    chosen = jnp.where(picker == 0, longer, shorter)
    full_at = jax.random.randint(full_key, (BATCH // SEQS, 1), 0, SEQS)
    slots = lax.iota(jnp.int32, SEQS)[None, :]
    marked = (slots == full_at).reshape(BATCH)
    return jnp.where(marked, LEN, chosen).astype(jnp.int32)


def block_scale(rng, extent, shards, smallest, high):
    def one(dim, parts):
        draws = jax.random.uniform(jax.random.fold_in(jax.random.fold_in(rng, 6), dim), (parts,), jnp.float32, smallest / len(shards), high / len(shards))
        return jnp.repeat(jnp.exp(draws), extent[dim] // parts).reshape((-1,) + (1,) * (len(extent) - dim - 1))

    loudness = one(*shards[0])
    for cut in shards[1:]:
        loudness = loudness * one(*cut)
    return loudness


def scatter_about(own_key, dims, scale, bound, cuts=(), kind=jnp.bfloat16):
    values = jax.random.normal(own_key, dims, jnp.float32) * scale
    if len(cuts) > 0:
        values = block_scale(own_key, dims, cuts, -0.22, 0.18) * values
    return jnp.clip(values, min=-bound, max=bound).astype(kind)


def setup_inputs(seed: int = 0) -> dict:
    arg_keys = jax.random.split(jax.random.key(seed), 21)
    hidden_in = scatter_about(arg_keys[0], (LEN, BATCH, D), 1.0, 6.0, ((0, 2), (1, 16)))
    lengths = draw_lengths(jax.random.fold_in(arg_keys[20], 71), 0)
    w_query = scatter_about(arg_keys[2], (D, D), D ** -0.5, 0.1875)
    w_key = scatter_about(arg_keys[3], (D, D), D ** -0.5, 0.1875)
    w_value = scatter_about(arg_keys[4], (D, D), D ** -0.5, 0.1875)
    w_output = scatter_about(arg_keys[5], (D, D), (D // 16) ** -0.5, 0.75)
    attn_gain = jnp.clip(1.0 + 0.18 * jax.random.normal(arg_keys[6], (D,), jnp.float32), 0.1, 1.9)
    ffn_in = scatter_about(arg_keys[7], (D, FF), D ** -0.5, 0.1875)
    ffn_out = scatter_about(arg_keys[8], (FF, D), FF ** -0.5, 0.09375)
    ffn_gain = jnp.clip(1.0 + 0.18 * jax.random.normal(arg_keys[9], (D,), jnp.float32), 0.1, 1.9)
    adapter_down = scatter_about(arg_keys[10], (D, ADAPT), D ** -0.5, 0.1875)
    adapter_down_bias = scatter_about(arg_keys[11], (ADAPT,), 0.5, 3.0, (), jnp.float32)
    adapter_up = scatter_about(arg_keys[12], (ADAPT, D), (4 * ADAPT) ** -0.5, 0.125)
    adapter_up_bias = scatter_about(arg_keys[13], (D,), 0.15, 0.9, (), jnp.float32)
    prefix_embed = scatter_about(arg_keys[14], (PREFIX, D), 1.0, 6.0, (), jnp.float32)
    prefix_hidden_w = scatter_about(arg_keys[15], (D, PHID), D ** -0.5, 0.1875)
    prefix_hidden_b = scatter_about(arg_keys[16], (PHID,), 0.5, 3.0, (), jnp.float32)
    prefix_out_w = scatter_about(arg_keys[17], (PHID, 2 * D), (PHID // 4) ** -0.5, 0.5)
    prefix_out_b = scatter_about(arg_keys[18], (2 * D,), 0.5, 3.0, (), jnp.float32)
    out_grad = scatter_about(arg_keys[19], (LEN, BATCH, D), 1.0, 6.0, ((0, 2), (1, 16)))
    return dict(hidden_in=hidden_in, lengths=lengths, w_query=w_query, w_key=w_key, w_value=w_value, w_output=w_output, attn_gain=attn_gain, ffn_in=ffn_in, ffn_out=ffn_out, ffn_gain=ffn_gain, adapter_down=adapter_down, adapter_down_bias=adapter_down_bias, adapter_up=adapter_up, adapter_up_bias=adapter_up_bias, prefix_embed=prefix_embed, prefix_hidden_w=prefix_hidden_w, prefix_hidden_b=prefix_hidden_b, prefix_out_w=prefix_out_w, prefix_out_b=prefix_out_b, out_grad=out_grad)


@jax.custom_vjp
def low(v):
    return lax.optimization_barrier(v.astype(jnp.bfloat16)).astype(jnp.float32)

@jax.custom_vjp
def low_back(v):
    return v

def low_keep(v):
    return (low(v), None)

def low_pass(kept, grad):
    return (grad,)

def back_keep(v):
    return (v, None)

def back_low(kept, grad):
    return (low(grad),)
low.defvjp(low_keep, low_pass)
low_back.defvjp(back_keep, back_low)
HIGHEST_PRECISION = lax.Precision.HIGHEST

def matmul(left, right):
    return jnp.dot(left, right, precision=HIGHEST_PRECISION, preferred_element_type=jnp.float32)

def gelu_value(inputs):
    return 0.5 * inputs * (1.0 + lax.erf(inputs * 0.7071067811865476))

def layer_norm(values):
    row_mean = lax.optimization_barrier(jnp.mean(values, axis=-1, keepdims=True))
    centred = values - row_mean
    spread = lax.optimization_barrier(jnp.mean(centred * centred, axis=-1, keepdims=True))
    return centred * lax.rsqrt(spread + 1e-05)

def forward(hidden, trained, frozen, seq_lengths):
    adapter_down, adapter_down_bias, adapter_up, adapter_up_bias, prefix_embed, prefix_hidden_w, prefix_hidden_b, prefix_out_w, prefix_out_b = trained
    w_query, w_key, w_value, w_output, attn_gain, ffn_in, ffn_out, ffn_gain = frozen
    length, count, model_width = hidden.shape
    head_dim = model_width // HEADS
    places = jnp.arange(length, dtype=jnp.int32)
    key_valid = places[None, :] < seq_lengths[:, None]
    valid = jnp.transpose(key_valid).astype(hidden.dtype).reshape(length * count, 1)
    flat_rows = hidden.reshape(length * count, model_width)
    queries = low_back(low(matmul(flat_rows, w_query))).reshape(length, count, HEADS, head_dim)
    keys = low_back(low(matmul(flat_rows, w_key))).reshape(length, count, HEADS, head_dim)
    values = low_back(low(matmul(flat_rows, w_value))).reshape(length, count, HEADS, head_dim)
    prefix_act = jnp.tanh(matmul(prefix_embed, prefix_hidden_w) + prefix_hidden_b)
    prefix_pair = matmul(prefix_act, prefix_out_w) + prefix_out_b
    prefix_keys = low(prefix_pair[:, :model_width]).reshape(PREFIX, HEADS, head_dim)
    prefix_values = low(prefix_pair[:, model_width:]).reshape(PREFIX, HEADS, head_dim)
    inv_root = 1.0 / math.sqrt(head_dim)
    lead_scores = jnp.einsum('rshd,phd->rshp', queries, prefix_keys, precision=HIGHEST_PRECISION) * inv_root
    own_scores = jnp.einsum('rshd,tshd->rsht', queries, keys, precision=HIGHEST_PRECISION) * inv_root
    scores = low_back(jnp.concatenate([lead_scores, own_scores], axis=3))
    allowed = jnp.concatenate([jnp.ones((count, PREFIX), dtype=bool), key_valid], axis=1)
    scores = jnp.where(allowed[None, :, None, :], scores, -jnp.inf)
    shifted = scores - lax.optimization_barrier(jnp.max(scores, axis=3, keepdims=True))
    expanded = jnp.exp(shifted)
    weights = low(expanded / lax.optimization_barrier(jnp.sum(expanded, axis=3, keepdims=True)))
    mixture = jnp.einsum('rshp,phd->rshd', weights[..., :PREFIX], prefix_values, precision=HIGHEST_PRECISION)
    mixture = mixture + jnp.einsum('rsht,tshd->rshd', weights[..., PREFIX:], values, precision=HIGHEST_PRECISION)
    attn_mix = low_back(low(mixture.reshape(length * count, model_width)))
    attn_proj = low_back(matmul(attn_mix, w_output))
    norm_one = layer_norm(flat_rows + attn_proj) * attn_gain
    norm_low = low(norm_one)
    inner_pre = low_back(matmul(norm_low, ffn_in))
    ffn_sum = low_back(matmul(low(gelu_value(inner_pre)), ffn_out))
    squeeze = low_back(matmul(norm_low, adapter_down) + adapter_down_bias)
    adapter_sum = low_back(matmul(low(gelu_value(squeeze)), adapter_up) + adapter_up_bias)
    resid_two = norm_one + ffn_sum + 4.0 * adapter_sum
    result = layer_norm(resid_two) * ffn_gain * valid
    return result.reshape(length, count, model_width)

def reference(hidden_in, lengths, w_query, w_key, w_value, w_output, attn_gain, ffn_in, ffn_out, ffn_gain, adapter_down, adapter_down_bias, adapter_up, adapter_up_bias, prefix_embed, prefix_hidden_w, prefix_hidden_b, prefix_out_w, prefix_out_b, out_grad):
    group_size = 4
    group_count = BATCH // group_size
    frozen = tuple((array.astype(jnp.float32) for array in (w_query, w_key, w_value, w_output, attn_gain, ffn_in, ffn_out, ffn_gain)))
    trained = tuple((array.astype(jnp.float32) for array in (adapter_down, adapter_down_bias, adapter_up, adapter_up_bias, prefix_embed, prefix_hidden_w, prefix_hidden_b, prefix_out_w, prefix_out_b)))

    def split_groups(array):
        return jnp.moveaxis(array.reshape(LEN, group_count, group_size, array.shape[-1]), 1, 0)

    def visit(running, pieces):
        hidden, seq_lengths, upstream = pieces

        def apply(hidden_values, params):
            return forward(hidden_values, params, frozen, seq_lengths)
        result, pull = jax.vjp(apply, hidden.astype(jnp.float32), trained)
        hidden_grad, param_grads = pull(upstream.astype(jnp.float32))
        running = jax.tree.map(jnp.add, running, param_grads)
        return (running, (result.astype(jnp.bfloat16), hidden_grad.astype(jnp.bfloat16)))
    zeros = jax.tree.map(jnp.zeros_like, trained)
    totals, (results, grads) = lax.scan(visit, zeros, (split_groups(hidden_in), lengths.reshape(group_count, group_size), split_groups(out_grad)))

    def restore(array):
        return jnp.moveaxis(array, 0, 1).reshape(LEN, BATCH, array.shape[-1])
    return (restore(results), restore(grads), totals[0], totals[1], totals[2], totals[3], totals[4], totals[5], totals[6], totals[7], totals[8])
```

```python
import functools
import math

import jax
import jax.numpy as jnp
from jax import lax
from jax.experimental import pallas as pl
from jax.experimental.pallas import tpu as pltpu
from jax.sharding import PartitionSpec as P

HEADS = 16


HIGHEST_PRECISION = lax.Precision.HIGHEST


def shifted(value, axis, steps):
    count = lax.axis_size(axis)
    pairs = [(source, (source + steps) % count) for source in range(count)]
    return lax.ppermute(value, axis, pairs)


def mixed(left, right):
    return jnp.dot(left, right, preferred_element_type=jnp.float32)


def mixed_left(left, right):
    return lax.dot_general(
        left, right, (((0,), (0,)), ((), ())), preferred_element_type=jnp.float32
    )


def mixed_right(left, right):
    return lax.dot_general(
        left, right, (((1,), (1,)), ((), ())), preferred_element_type=jnp.float32
    )


def precise(left, right):
    return jnp.dot(left, right, precision=HIGHEST_PRECISION, preferred_element_type=jnp.float32)


def precise_left(left, right):
    return lax.dot_general(
        left,
        right,
        (((0,), (0,)), ((), ())),
        precision=HIGHEST_PRECISION,
        preferred_element_type=jnp.float32,
    )


def precise_right(left, right):
    return lax.dot_general(
        left,
        right,
        (((1,), (1,)), ((), ())),
        precision=HIGHEST_PRECISION,
        preferred_element_type=jnp.float32,
    )


def gelu_value(inputs):
    return 0.5 * inputs * (1.0 + lax.erf(inputs * 0.7071067811865476))


def gelu_slope(inputs):
    return (
        0.5 * (1.0 + lax.erf(inputs * 0.7071067811865476))
        + inputs * jnp.exp(-0.5 * inputs * inputs) * 0.3989422804014327
    )


def normalize(values):
    row_mean = jnp.mean(values, axis=-1, keepdims=True)
    centred = values - row_mean
    spread = jnp.mean(centred * centred, axis=-1, keepdims=True)
    inv_std = lax.rsqrt(spread + 1e-05)
    return (centred * inv_std, inv_std)


def norm_back(upstream, normed, inv_std):
    mean_grad = jnp.mean(upstream, axis=-1, keepdims=True)
    mean_proj = jnp.mean(upstream * normed, axis=-1, keepdims=True)
    return inv_std * (upstream - mean_grad - normed * mean_proj)


def key_allowed(offset, key_count, seq_lengths):
    places = offset + lax.iota(jnp.int32, key_count)
    return places[None, :] < seq_lengths[:, None]


def lead_state(queries4, prefix_keys4, prefix_values4):
    inv_root = 1.0 / math.sqrt(queries4.shape[3])
    scores = (
        jnp.einsum("rshd,phd->rshp", queries4, prefix_keys4, preferred_element_type=jnp.float32)
        * inv_root
    )
    running_max = jnp.max(scores, axis=3)
    weights = jnp.exp(scores - running_max[..., None])
    running_sum = jnp.sum(weights, axis=3)
    running_mix = jnp.einsum(
        "rshp,phd->rshd",
        weights.astype(jnp.bfloat16),
        prefix_values4,
        preferred_element_type=jnp.float32,
    )
    return (running_max, running_sum, running_mix)


def fold_block(carried, key_block, value_block, offset, queries4, seq_lengths):
    key_count, seqs_here = (key_block.shape[0], key_block.shape[1])
    head_count, head_dim = (queries4.shape[2], queries4.shape[3])
    inv_root = 1.0 / math.sqrt(head_dim)
    keys4 = key_block.reshape(key_count, seqs_here, head_count, head_dim)
    values4 = value_block.reshape(key_count, seqs_here, head_count, head_dim)
    running_max, running_sum, running_mix = carried
    scores = (
        jnp.einsum("rshd,tshd->rsht", queries4, keys4, preferred_element_type=jnp.float32)
        * inv_root
    )
    allowed = key_allowed(offset, key_count, seq_lengths)[None, :, None, :]
    scores = jnp.where(allowed, scores, -jnp.inf)
    new_max = jnp.maximum(running_max, jnp.max(scores, axis=3))
    weights = jnp.exp(scores - new_max[..., None])
    rescale = jnp.exp(running_max - new_max)
    running_sum = running_sum * rescale + jnp.sum(weights, axis=3)
    running_mix = running_mix * rescale[..., None] + jnp.einsum(
        "rsht,tshd->rshd", weights.astype(jnp.bfloat16), values4, preferred_element_type=jnp.float32
    )
    return (new_max, running_sum, running_mix)


def lead_back(queries4, upstream4, log_total, row_delta, prefix_keys4, prefix_values4):
    inv_root = 1.0 / math.sqrt(queries4.shape[3])
    scores = (
        jnp.einsum("rshd,phd->rshp", queries4, prefix_keys4, preferred_element_type=jnp.float32)
        * inv_root
    )
    weights = jnp.exp(scores - log_total[..., None])
    weight_grads = jnp.einsum(
        "rshd,phd->rshp", upstream4, prefix_values4, preferred_element_type=jnp.float32
    )
    score_grads = (weights * (weight_grads - row_delta[..., None])).astype(jnp.bfloat16)
    query_term = (
        jnp.einsum("rshp,phd->rshd", score_grads, prefix_keys4, preferred_element_type=jnp.float32)
        * inv_root
    )
    key_term = (
        jnp.einsum("rshp,rshd->phd", score_grads, queries4, preferred_element_type=jnp.float32)
        * inv_root
    )
    value_term = jnp.einsum(
        "rshp,rshd->phd",
        weights.astype(jnp.bfloat16),
        upstream4,
        preferred_element_type=jnp.float32,
    )
    return (query_term, key_term, value_term)


def block_back(
    queries4, upstream4, log_total, row_delta, key_block, value_block, offset, seq_lengths
):
    key_count, seqs_here, model_width = key_block.shape
    head_count, head_dim = (queries4.shape[2], queries4.shape[3])
    inv_root = 1.0 / math.sqrt(head_dim)
    keys4 = key_block.reshape(key_count, seqs_here, head_count, head_dim)
    values4 = value_block.reshape(key_count, seqs_here, head_count, head_dim)
    scores = (
        jnp.einsum("rshd,tshd->rsht", queries4, keys4, preferred_element_type=jnp.float32)
        * inv_root
    )
    allowed = key_allowed(offset, key_count, seq_lengths)[None, :, None, :]
    scores = jnp.where(allowed, scores, -jnp.inf)
    weights = jnp.exp(scores - log_total[..., None])
    weight_grads = jnp.einsum(
        "rshd,tshd->rsht", upstream4, values4, preferred_element_type=jnp.float32
    )
    score_grads = (weights * (weight_grads - row_delta[..., None])).astype(jnp.bfloat16)
    query_term = (
        jnp.einsum("rsht,tshd->rshd", score_grads, keys4, preferred_element_type=jnp.float32)
        * inv_root
    )
    key_term = (
        jnp.einsum("rsht,rshd->tshd", score_grads, queries4, preferred_element_type=jnp.float32)
        * inv_root
    )
    value_term = jnp.einsum(
        "rsht,rshd->tshd",
        weights.astype(jnp.bfloat16),
        upstream4,
        preferred_element_type=jnp.float32,
    )
    pair_term = jnp.stack(
        [
            key_term.reshape(key_count, seqs_here, model_width),
            value_term.reshape(key_count, seqs_here, model_width),
        ]
    )
    return (query_term, pair_term)


def prefix_back(pair_grad, prefix_act, prefix_embed, hidden_weight, out_weight):
    out_w_grad = precise_left(prefix_act, pair_grad)
    out_b_grad = jnp.sum(pair_grad, axis=0)
    act_grad = precise_right(pair_grad, out_weight) * (1.0 - prefix_act * prefix_act)
    hidden_w_grad = precise_left(prefix_embed, act_grad)
    hidden_b_grad = jnp.sum(act_grad, axis=0)
    embed_grad = precise_right(act_grad, hidden_weight)
    return (embed_grad, hidden_w_grad, hidden_b_grad, out_w_grad, out_b_grad)


def on_device(
    hidden_in,
    lengths,
    w_query,
    w_key,
    w_value,
    w_output,
    attn_gain,
    ffn_in,
    ffn_out,
    ffn_gain,
    adapter_down,
    adapter_down_bias,
    adapter_up,
    adapter_up_bias,
    prefix_embed,
    prefix_hidden_w,
    prefix_hidden_b,
    prefix_out_w,
    prefix_out_b,
    out_grad,
):
    rows_here, seqs_here, model_width = hidden_in.shape
    token_count = rows_here * seqs_here
    head_count = HEADS
    head_dim = model_width // head_count
    axis_count = lax.axis_size("seq")
    position = lax.axis_index("seq")
    tokens = hidden_in.reshape(token_count, model_width)
    projected = jnp.stack([mixed(tokens, w_query), mixed(tokens, w_key), mixed(tokens, w_value)])
    triple = projected.astype(jnp.bfloat16).reshape(3, rows_here, seqs_here, model_width)
    hidden_weight = prefix_hidden_w.astype(jnp.float32)
    out_weight = prefix_out_w.astype(jnp.float32)
    prefix_act = jnp.tanh(precise(prefix_embed, hidden_weight) + prefix_hidden_b)
    prefix_pair = precise(prefix_act, out_weight) + prefix_out_b
    prefix_keys4 = (
        prefix_pair[:, :model_width].astype(jnp.bfloat16).reshape(-1, head_count, head_dim)
    )
    prefix_values4 = (
        prefix_pair[:, model_width:].astype(jnp.bfloat16).reshape(-1, head_count, head_dim)
    )
    row_places = position * rows_here + lax.iota(jnp.int32, rows_here)
    valid = (row_places[:, None] < lengths[None, :]).astype(jnp.float32).reshape(token_count, 1)
    queries4 = triple[0].reshape(rows_here, seqs_here, head_count, head_dim)
    key_value = triple[1:]
    pieces = lax.all_gather(key_value, "seq", axis=1, tiled=True)
    carried = fold_block(
        lead_state(queries4, prefix_keys4, prefix_values4),
        pieces[0],
        pieces[1],
        jnp.int32(0),
        queries4,
        lengths,
    )
    mix_full = carried[2] / carried[1][..., None]
    log_total = carried[0] + jnp.log(carried[1])
    mix_low = mix_full.astype(jnp.bfloat16).reshape(token_count, model_width)
    attn_proj = mixed(mix_low, w_output)
    normed_one, inv_one = normalize(tokens.astype(jnp.float32) + attn_proj)
    norm_one = normed_one * attn_gain
    norm_low = norm_one.astype(jnp.bfloat16)
    inner_pre = mixed(norm_low, ffn_in)
    inner_act = gelu_value(inner_pre).astype(jnp.bfloat16)
    squeeze = mixed(norm_low, adapter_down) + adapter_down_bias
    squeeze_act = gelu_value(squeeze).astype(jnp.bfloat16)
    ffn_sum = mixed(inner_act, ffn_out)
    adapter_sum = mixed(squeeze_act, adapter_up) + adapter_up_bias
    normed_two, inv_two = normalize(norm_one + ffn_sum + 4.0 * adapter_sum)
    layer_out = (
        (normed_two * ffn_gain * valid)
        .astype(jnp.bfloat16)
        .reshape(rows_here, seqs_here, model_width)
    )
    upstream_top = out_grad.reshape(token_count, model_width).astype(jnp.float32) * valid
    grad_two = norm_back(upstream_top * ffn_gain, normed_two, inv_two)
    grad_ffn_low = grad_two.astype(jnp.bfloat16)
    grad_adapt_low = (4.0 * grad_two).astype(jnp.bfloat16)
    up_grad = mixed_left(squeeze_act, grad_adapt_low)
    up_bias_grad = jnp.sum(grad_adapt_low.astype(jnp.float32), axis=0)
    grad_squeeze_low = (mixed_right(grad_adapt_low, adapter_up) * gelu_slope(squeeze)).astype(
        jnp.bfloat16
    )
    down_grad = mixed_left(norm_low, grad_squeeze_low)
    down_bias_grad = jnp.sum(grad_squeeze_low.astype(jnp.float32), axis=0)
    grad_inner_low = (mixed_right(grad_ffn_low, ffn_out) * gelu_slope(inner_pre)).astype(
        jnp.bfloat16
    )
    grad_norm = (
        grad_two + mixed_right(grad_squeeze_low, adapter_down) + mixed_right(grad_inner_low, ffn_in)
    )
    grad_one = norm_back(grad_norm * attn_gain, normed_one, inv_one)
    grad_attn_low = grad_one.astype(jnp.bfloat16)
    grad_mix_low = mixed_right(grad_attn_low, w_output).astype(jnp.bfloat16)
    upstream4 = grad_mix_low.reshape(rows_here, seqs_here, head_count, head_dim)
    row_delta = jnp.sum(upstream4.astype(jnp.float32) * mix_full, axis=3)
    query_grad, prefix_key_grad, prefix_value_grad = lead_back(
        queries4, upstream4, log_total, row_delta, prefix_keys4, prefix_values4
    )

    def visit(step_index, carried):
        moving, grads_moving, query_total = carried
        source = (position - step_index) % axis_count
        query_term, pair_term = block_back(
            queries4,
            upstream4,
            log_total,
            row_delta,
            moving[0],
            moving[1],
            source * rows_here,
            lengths,
        )
        return (moving, grads_moving + pair_term, query_total + query_term)

    def travel(step_index, carried):
        moving, grads_moving, query_total = visit(step_index, carried)
        moving = shifted(moving, "seq", 1)
        grads_moving = shifted(grads_moving.astype(jnp.bfloat16), "seq", 1).astype(
            grads_moving.dtype
        )
        return (moving, grads_moving, query_total)

    initial = (
        key_value,
        jnp.zeros((2, rows_here, seqs_here, model_width), jnp.float32),
        query_grad,
    )
    carried = lax.fori_loop(0, axis_count - 1, travel, initial)
    carried = visit(axis_count - 1, carried)
    pair_grads = shifted(carried[1].astype(jnp.bfloat16), "seq", 1).astype(jnp.float32)
    triple_grad = jnp.concatenate(
        [carried[2].reshape(1, rows_here, seqs_here, model_width), pair_grads]
    ).astype(jnp.bfloat16)
    hidden_grad = grad_one + mixed_right(triple_grad[0].reshape(token_count, model_width), w_query)
    hidden_grad = hidden_grad + mixed_right(triple_grad[1].reshape(token_count, model_width), w_key)
    hidden_grad = hidden_grad + mixed_right(
        triple_grad[2].reshape(token_count, model_width), w_value
    )
    hidden_grad = hidden_grad.astype(jnp.bfloat16).reshape(rows_here, seqs_here, model_width)
    pair_grad = jnp.concatenate(
        [prefix_key_grad.reshape(-1, model_width), prefix_value_grad.reshape(-1, model_width)],
        axis=1,
    )
    prefix_grads = prefix_back(pair_grad, prefix_act, prefix_embed, hidden_weight, out_weight)
    summed = lax.psum(
        (
            down_grad,
            down_bias_grad,
            up_grad,
            up_bias_grad,
            prefix_grads[0],
            prefix_grads[1],
            prefix_grads[2],
            prefix_grads[3],
            prefix_grads[4],
        ),
        ("seq", "dp"),
    )
    adapter_totals = summed[:4]
    prefix_totals = summed[4:]
    return (
        layer_out,
        hidden_grad,
        adapter_totals[0],
        adapter_totals[1],
        adapter_totals[2],
        adapter_totals[3],
        prefix_totals[0],
        prefix_totals[1],
        prefix_totals[2],
        prefix_totals[3],
        prefix_totals[4],
    )


BF16 = jnp.bfloat16
F32 = jnp.float32
MIB = 1024 * 1024
GROUP = 4
HEAD_DIM = 64
LANES = GROUP * HEAD_DIM
PAD = 32
MASKED = -1e30
LOG2E = 1.4426950408889634
VMEM_LIMIT = 60 * MIB


def dot_nn(left, right):
    return lax.dot_general(left, right, (((1,), (0,)), ((), ())), preferred_element_type=F32)


def dot_nt(left, right):
    return lax.dot_general(left, right, (((1,), (1,)), ((), ())), preferred_element_type=F32)


def dot_tn(left, right):
    return lax.dot_general(left, right, (((0,), (0,)), ((), ())), preferred_element_type=F32)


def dot_tt(left, right):
    return lax.dot_general(left, right, (((0,), (1,)), ((), ())), preferred_element_type=F32)


def shape_of(shape, dtype):
    return jax.ShapeDtypeStruct(shape, dtype)


def params(limit=VMEM_LIMIT):
    return pltpu.CompilerParams(vmem_limit_bytes=limit)


def cost(macs, moved):
    return pl.CostEstimate(flops=int(2 * macs), bytes_accessed=int(moved), transcendentals=0)


SMEM_SPEC = pl.BlockSpec(memory_space=pltpu.SMEM)
ANY_SPEC = pl.BlockSpec(memory_space=pl.ANY)


def whole(shape):
    return pl.BlockSpec(shape, lambda *_: (0,) * len(shape))


def kept(shape):
    return pl.BlockSpec(shape, lambda *_: (0,) * len(shape), pipeline_mode=pl.Buffered(1))


def split_kernel(place_ref, both_ref, own_ref, other_ref):
    apart = jnp.swapaxes(both_ref[...], 0, 1)
    first = place_ref[0] == 0
    own_ref[...] = jnp.where(first, apart[0], apart[1])
    other_ref[...] = jnp.where(first, apart[1], apart[0])


def split(place, both):
    rows, _, width = both.shape
    step = rows // 4
    half = pl.BlockSpec((step, width), lambda i: (i, 0))
    return pl.pallas_call(
        split_kernel,
        grid=(4,),
        in_specs=[SMEM_SPEC, pl.BlockSpec((step, 2, width), lambda i: (i, 0, 0))],
        out_specs=[half, half],
        out_shape=[shape_of((rows, width), both.dtype)] * 2,
        cost_estimate=cost(0, 4 * rows * width * 2),
    )(place, both)


def merge_kernel(place_ref, own_ref, other_ref, both_ref):
    first = place_ref[0] == 0
    own, other = own_ref[...], other_ref[...]
    apart = jnp.stack([jnp.where(first, own, other), jnp.where(first, other, own)])
    both_ref[...] = jnp.swapaxes(apart, 0, 1)


def merge(place, own, other):
    rows, width = other.shape
    step = rows // 4
    half = pl.BlockSpec((step, width), lambda i: (i, 0))
    return pl.pallas_call(
        merge_kernel,
        grid=(4,),
        in_specs=[SMEM_SPEC, half, half],
        out_specs=pl.BlockSpec((step, 2, width), lambda i: (i, 0, 0)),
        out_shape=shape_of((rows, 2, width), other.dtype),
        cost_estimate=cost(0, 4 * rows * width * 2),
    )(place, own, other)


def parts_of(values, count):
    parts = []
    for _ in range(count):
        part = values.astype(BF16)
        parts.append(part)
        values = values - part.astype(F32)
    return parts


def exact_dot(values, weight, dot):
    rows = values.shape[0]
    product = dot(jnp.concatenate(parts_of(values, 3), axis=0), weight)
    return product[:rows] + product[rows : 2 * rows] + product[2 * rows :]


def prefix_kernel(embed_ref, hw_ref, hb_ref, ow_ref, ob_ref, act_ref, key_ref, value_ref):
    width = key_ref.shape[1]
    act = jnp.tanh(exact_dot(embed_ref[...], hw_ref[...], dot_nn) + hb_ref[...])
    act_ref[...] = act
    pair = exact_dot(act, ow_ref[...], dot_nn) + ob_ref[...]
    key_ref[...] = pair[:, :width].astype(BF16)
    value_ref[...] = pair[:, width:].astype(BF16)


def prefix_forward(embed, hidden_w, hidden_b, out_w, out_b):
    width, hidden = hidden_w.shape
    return pl.pallas_call(
        prefix_kernel,
        out_shape=[
            shape_of((PAD, hidden), F32),
            shape_of((PAD, width), BF16),
            shape_of((PAD, width), BF16),
        ],
        compiler_params=params(),
        cost_estimate=cost(3 * PAD * hidden * 3 * width * 4, 6 * hidden * width),
    )(embed, hidden_w, hidden_b[None], out_w, out_b[None])


def prefix_back_kernel(
    count, pair_ref, act_ref, embed_ref, hw_ref, ow_ref, eg_ref, hwg_ref, hbg_ref, owg_ref, obg_ref
):
    pair = pair_ref[...]
    rows = lax.broadcasted_iota(jnp.int32, pair.shape, 0)
    pair = jnp.where(rows < count, pair, 0.0)
    act = act_ref[...]
    obg_ref[...] = jnp.sum(pair, axis=0, keepdims=True)
    high, low = parts_of(pair, 2)
    back = dot_nt(jnp.concatenate([high, low], axis=0), ow_ref[...])
    act_grad = (back[:PAD] + back[PAD:]) * (1.0 - act * act)
    act_high, act_low = parts_of(act, 2)
    owg_ref[...] = dot_tn(
        jnp.concatenate([act_high, act_low, act_high], axis=0),
        jnp.concatenate([high, high, low], axis=0),
    )
    hbg_ref[...] = jnp.sum(act_grad, axis=0, keepdims=True)
    high, low = parts_of(act_grad, 2)
    embed_high, embed_low = parts_of(embed_ref[...], 2)
    hwg_ref[...] = dot_tn(
        jnp.concatenate([embed_high, embed_low, embed_high], axis=0),
        jnp.concatenate([high, high, low], axis=0),
    )
    back = dot_nt(jnp.concatenate([high, low], axis=0), hw_ref[...])
    eg_ref[...] = (back[:PAD] + back[PAD:])[:count]


def prefix_backward(count, pair, act, embed, hidden_w, out_w):
    width, hidden = hidden_w.shape
    return pl.pallas_call(
        functools.partial(prefix_back_kernel, count),
        out_shape=[
            shape_of((count, width), F32),
            shape_of((width, hidden), F32),
            shape_of((1, hidden), F32),
            shape_of((hidden, 2 * width), F32),
            shape_of((1, 2 * width), F32),
        ],
        compiler_params=params(),
        cost_estimate=cost(96 * hidden * width * 6, 20 * hidden * width),
    )(pair, act, embed, hidden_w, out_w)


def project_kernel(x_ref, wq_ref, wk_ref, wv_ref, *refs):
    q_ref, k_ref, kt_ref, v_ref, vt_ref = refs[-5:]
    x = x_ref[...]
    scale = LOG2E / math.sqrt(HEAD_DIM)
    q_ref[...] = (dot_nn(x, wq_ref[...]) * scale).astype(BF16)
    k = dot_nn(x, wk_ref[...]).astype(BF16)
    k_ref[...] = k
    kt_ref[...] = k.T
    v = dot_nn(x, wv_ref[...]).astype(BF16)
    v_ref[...] = v
    vt_ref[...] = v.T


def project(half, x, w_query, w_key, w_value, earlier):
    rows, width = x.shape
    step = 256
    weight = pl.BlockSpec((width, step), lambda j: (0, j))
    straight = pl.BlockSpec((rows, step), lambda j: (half, j))
    turned = pl.BlockSpec((step, rows), lambda j: (j, half))
    return pl.pallas_call(
        project_kernel,
        grid=(width // step,),
        in_specs=[whole((rows, width)), weight, weight, weight] + [ANY_SPEC] * len(earlier),
        out_specs=[straight, straight, turned, straight, turned],
        out_shape=[
            shape_of((2 * rows, width), BF16),
            shape_of((2 * rows, width), BF16),
            shape_of((width, 2 * rows), BF16),
            shape_of((2 * rows, width), BF16),
            shape_of((width, 2 * rows), BF16),
        ],
        input_output_aliases={4 + i: i for i in range(len(earlier))},
        compiler_params=params(),
        cost_estimate=cost(3 * rows * width * width, 2 * (6 * rows * width + 3 * width * width)),
    )(x, w_query, w_key, w_value, *earlier)


def head_lanes(head, rows, lanes):
    place = lax.broadcasted_iota(jnp.int32, (rows, lanes), 1)
    return (place // HEAD_DIM == head).astype(F32).astype(BF16)


def first_lane(values):
    lane = lax.broadcasted_iota(jnp.int32, (values.shape[0], 128), 1)
    return jnp.where(lane == 0, values, 0.0).astype(BF16)


def block_diagonal(rows):
    return jnp.concatenate(
        [rows * head_lanes(head, rows.shape[0], LANES) for head in range(GROUP)], axis=0
    )


def attend_kernel(count, half, scal_ref, q_ref, k_ref, vt_ref, *refs):
    keys = k_ref.shape[0]
    queries = q_ref.shape[0]
    if count:
        pk_ref, pv_ref = refs[:2]
        pt_ref, ot_ref, st_ref, pp_ref = refs[-4:]
    else:
        pt_ref, ot_ref, st_ref = refs[-3:]
    place = scal_ref[half] + lax.broadcasted_iota(jnp.int32, (keys, 128), 0)
    bias = first_lane(jnp.where(place < scal_ref[2], 0.0, MASKED))
    ones = first_lane(jnp.ones((queries, 128), F32))
    tail = jnp.ones((16, keys), BF16)
    masks = [head_lanes(head, queries, 128) for head in range(2)]
    if count:
        lead = dot_nt(block_diagonal(pk_ref[...]), q_ref[...])
        row = lax.broadcasted_iota(jnp.int32, lead.shape, 0)
        lead = jnp.where(row % PAD < count, lead, MASKED)
    mixes = []
    leads = []
    for head in range(GROUP):
        pair = slice((head // 2) * 128, (head // 2 + 1) * 128)
        rows = slice(head * HEAD_DIM, (head + 1) * HEAD_DIM)
        k_aug = jnp.concatenate([k_ref[:, pair], bias], axis=1)
        q_aug = jnp.concatenate([q_ref[:, pair] * masks[head % 2], ones], axis=1)
        scores = dot_nt(k_aug, q_aug)
        top = jnp.max(scores, axis=0, keepdims=True)
        if count:
            lead_scores = lead[head * PAD : (head + 1) * PAD]
            top = jnp.maximum(top, jnp.max(lead_scores, axis=0, keepdims=True))
        weights = jnp.exp2(scores - top).astype(BF16)
        pt_ref[head] = weights
        mix = dot_nn(jnp.concatenate([vt_ref[rows, :], tail], axis=0), weights)
        total = mix[HEAD_DIM : HEAD_DIM + 1]
        mixes.append(mix[:HEAD_DIM])
        if count:
            lead_weights = jnp.exp2(lead_scores - top).astype(BF16)
            total = total + jnp.sum(lead_weights.astype(F32), axis=0, keepdims=True)
            leads.append(lead_weights)
        st_ref[0, head : head + 1, :] = top
        st_ref[0, GROUP + head : GROUP + head + 1, :] = total
    mix = jnp.concatenate(mixes, axis=0)
    if count:
        lead_weights = jnp.concatenate(leads, axis=0)
        pp_ref[0] = lead_weights
        mix = mix + dot_tn(block_diagonal(pv_ref[...]), lead_weights)
    ot_ref[...] = mix


def attend(count, scal, key_half, query_first, query_blocks, q, k, vt, lead, earlier):
    tokens, width = q.shape
    rows = tokens // 2
    groups = width // LANES
    in_specs = [
        SMEM_SPEC,
        pl.BlockSpec((rows, LANES), lambda i, g: (i + query_first, g)),
        pl.BlockSpec((rows, LANES), lambda i, g: (key_half, g)),
        pl.BlockSpec((LANES, rows), lambda i, g: (g, key_half)),
    ]
    in_specs += [pl.BlockSpec((PAD, LANES), lambda i, g: (0, g))] * len(lead)
    out_specs = [
        pl.BlockSpec((GROUP, rows, rows), lambda i, g: (g, 0, i + query_first)),
        pl.BlockSpec((LANES, rows), lambda i, g: (g, i + query_first)),
        pl.BlockSpec((1, 2 * GROUP, rows), lambda i, g: (g, 0, i + query_first)),
    ]
    out_shape = [
        shape_of((groups * GROUP, rows, tokens), BF16),
        shape_of((width, tokens), F32),
        shape_of((groups, 2 * GROUP, tokens), F32),
    ]
    if count:
        out_specs.append(pl.BlockSpec((1, GROUP * PAD, rows), lambda i, g: (g, 0, i + query_first)))
        out_shape.append(shape_of((groups, GROUP * PAD, tokens), BF16))
    start = len(in_specs)
    macs = query_blocks * groups * GROUP * rows * rows * 256 * 2
    return pl.pallas_call(
        functools.partial(attend_kernel, count, key_half),
        grid=(query_blocks, groups),
        in_specs=in_specs + [ANY_SPEC] * len(earlier),
        out_specs=out_specs,
        out_shape=out_shape,
        input_output_aliases={start + i: i for i in range(len(earlier))},
        compiler_params=params(),
        cost_estimate=cost(macs, query_blocks * 24 * MIB),
    )(scal, q, k, vt, *lead, *earlier)


def lead_back_kernel(q_ref, up_ref, rst_ref, del_ref, pp_ref, pk_ref, pv_ref, kg_ref, vg_ref, dqt_ref):
    queries = q_ref.shape[0]
    ups = []
    deltas = []
    for head in range(GROUP):
        rows = slice(head * HEAD_DIM, (head + 1) * HEAD_DIM)
        share = rst_ref[0, head : head + 1, :]
        ups.append((up_ref[rows, :].astype(F32) * share).astype(BF16))
        delta = del_ref[0, head : head + 1, :] * share
        deltas.append(jnp.broadcast_to(delta, (PAD, queries)))
    up = jnp.concatenate(ups, axis=0)
    delta = jnp.concatenate(deltas, axis=0)
    weights = pp_ref[0]
    key_diagonal = block_diagonal(pk_ref[...])
    value_diagonal = block_diagonal(pv_ref[...])
    weight_grads = dot_nn(value_diagonal, up)
    score_grads = (weights.astype(F32) * (weight_grads - delta)).astype(BF16)
    dqt_ref[...] = dot_tn(key_diagonal, score_grads)
    key_grads = dot_nn(score_grads, q_ref[...]) * (1.0 / LOG2E)
    value_grads = dot_nt(weights, up)
    lane = lax.broadcasted_iota(jnp.int32, (PAD, LANES), 1) // HEAD_DIM
    key_total = jnp.zeros((PAD, LANES), F32)
    value_total = jnp.zeros((PAD, LANES), F32)
    for head in range(GROUP):
        rows = slice(head * PAD, (head + 1) * PAD)
        key_total = jnp.where(lane == head, key_grads[rows], key_total)
        value_total = jnp.where(lane == head, value_grads[rows], value_total)
    kg_ref[...] = key_total
    vg_ref[...] = value_total


def lead_backward(q, up, shares, deltas, lead_weights, prefix_keys, prefix_values):
    tokens, width = q.shape
    groups = width // LANES
    small = pl.BlockSpec((PAD, LANES), lambda g: (0, g))
    stats = pl.BlockSpec((1, 2 * GROUP, tokens), lambda g: (g, 0, 0))
    return pl.pallas_call(
        lead_back_kernel,
        grid=(groups,),
        in_specs=[
            pl.BlockSpec((tokens, LANES), lambda g: (0, g)),
            pl.BlockSpec((LANES, tokens), lambda g: (g, 0)),
            stats,
            stats,
            pl.BlockSpec((1, GROUP * PAD, tokens), lambda g: (g, 0, 0)),
            small,
            small,
        ],
        out_specs=[small, small, pl.BlockSpec((LANES, tokens), lambda g: (g, 0))],
        out_shape=[
            shape_of((PAD, width), F32),
            shape_of((PAD, width), F32),
            shape_of((width, tokens), F32),
        ],
        compiler_params=params(),
        cost_estimate=cost(groups * 4 * GROUP * PAD * tokens * LANES, 10 * MIB),
    )(q, up, shares, deltas, lead_weights, prefix_keys, prefix_values)


def attend_back_kernel(
    half,
    steps,
    partial,
    has_earlier,
    q_ref,
    kt_ref,
    v_ref,
    up_ref,
    rst_ref,
    del_ref,
    pt_ref,
    dqt_in_ref,
    *refs,
):
    if has_earlier:
        dk_in_ref, dv_in_ref = refs[:2]
        refs = refs[2:]
    dqt_ref, dk_ref, dv_ref = refs[:3]
    queries = q_ref.shape[0]
    lane = lax.broadcasted_iota(jnp.int32, (queries, 128), 1) // HEAD_DIM
    masks = [(lane == head).astype(F32).astype(BF16) for head in range(2)]
    zeros = jnp.zeros((HEAD_DIM, queries), BF16)
    key_grads = []
    value_grads = []
    for duo in range(GROUP // 2):
        pair = slice(duo * 128, (duo + 1) * 128)
        key_grad = None
        value_grad = None
        for side in range(2):
            head = 2 * duo + side
            rows = slice(head * HEAD_DIM, (head + 1) * HEAD_DIM)
            share = rst_ref[0, half * GROUP + head : half * GROUP + head + 1, :]
            up = (up_ref[rows, :].astype(F32) * share).astype(BF16)
            up = jnp.concatenate([up, zeros] if side == 0 else [zeros, up], axis=0)
            delta = del_ref[0, head : head + 1, :] * share
            weights = pt_ref[head]
            weight_grads = dot_nn(v_ref[:, pair], up)
            score_grads = (weights.astype(F32) * (weight_grads - delta)).astype(BF16)
            dqt = dqt_in_ref[rows, :] + dot_nn(kt_ref[rows, :], score_grads)
            if partial:
                dqt_ref[rows, :] = dqt
            else:
                dqt_ref[rows, :] = (dqt * (1.0 / math.sqrt(HEAD_DIM))).astype(BF16)
            key_term = dot_nn(score_grads, q_ref[:, pair] * masks[side])
            value_term = dot_nt(weights, up)
            key_grad = key_term if side == 0 else key_grad + key_term
            value_grad = value_term if side == 0 else value_grad + value_term
        key_grads.append(key_grad)
        value_grads.append(value_grad)
    key_grad = jnp.concatenate(key_grads, axis=1)
    value_grad = jnp.concatenate(value_grads, axis=1)
    if has_earlier:
        key_grad = key_grad + dk_in_ref[...]
        value_grad = value_grad + dv_in_ref[...]
    if dk_ref.dtype == F32:
        dk_ref[...] = key_grad
        dv_ref[...] = value_grad
    elif steps == 1:
        dk_ref[...] = (key_grad * (1.0 / LOG2E)).astype(BF16)
        dv_ref[...] = value_grad.astype(BF16)
    else:
        dk_sum_ref, dv_sum_ref = refs[3:]
        step = pl.program_id(1)

        @pl.when(step == 0)
        def _():
            dk_sum_ref[...] = key_grad
            dv_sum_ref[...] = value_grad

        @pl.when(step > 0)
        def _():
            dk_sum_ref[...] += key_grad
            dv_sum_ref[...] += value_grad

        @pl.when(step == steps - 1)
        def _():
            dk_ref[...] = (dk_sum_ref[...] * (1.0 / LOG2E)).astype(BF16)
            dv_ref[...] = dv_sum_ref[...].astype(BF16)


def attend_back(
    key_half, query_first, query_blocks, partial, grads_type, q, kt, v, up, shares, deltas, weights, dqt, earlier
):
    tokens, width = q.shape
    rows = tokens // 2
    groups = width // LANES
    query_rows = pl.BlockSpec((rows, LANES), lambda g, i: (i + query_first, g))
    query_columns = pl.BlockSpec((LANES, rows), lambda g, i: (g, i + query_first))
    stats = pl.BlockSpec((1, 2 * GROUP, rows), lambda g, i: (g, 0, i + query_first))
    finished = pl.BlockSpec((rows, LANES), lambda g, i: (0, g))
    out_columns = pl.BlockSpec((LANES, rows), lambda g, i: (g, i))
    macs = query_blocks * groups * GROUP * rows * rows * 256 * 4
    return pl.pallas_call(
        functools.partial(attend_back_kernel, key_half, query_blocks, partial, len(earlier) > 0),
        grid=(groups, query_blocks),
        in_specs=[
            query_rows,
            pl.BlockSpec((LANES, rows), lambda g, i: (g, key_half)),
            pl.BlockSpec((rows, LANES), lambda g, i: (key_half, g)),
            query_columns,
            stats,
            stats,
            pl.BlockSpec((GROUP, rows, rows), lambda g, i: (g, 0, i + query_first)),
            query_columns,
        ]
        + [finished] * len(earlier),
        out_specs=[out_columns, finished, finished],
        out_shape=[
            shape_of((width, query_blocks * rows), F32 if partial else BF16),
            shape_of((rows, width), grads_type),
            shape_of((rows, width), grads_type),
        ],
        scratch_shapes=[pltpu.VMEM((rows, LANES), F32)] * (2 if query_blocks > 1 else 0),
        compiler_params=params(),
        cost_estimate=cost(macs, query_blocks * 24 * MIB),
    )(q, kt, v, up, shares, deltas, weights, dqt, *earlier)


def normal_density_parts(values):
    decay = jnp.exp2(values * values * (-0.5 * LOG2E))
    spread = 1.0 + jnp.abs(values) * (0.3275911 * 0.7071067811865476)
    t = pl.reciprocal(spread, approx=True)
    t = t * (2.0 - spread * t)
    series = 0.5 * 1.061405429
    for term in (-1.453152027, 1.421413741, -0.284496736, 0.254829592):
        series = series * t + 0.5 * term
    below = series * t * decay
    return jnp.where(values < 0.0, below, 1.0 - below), decay


def gelu_pair(values):
    below, decay = normal_density_parts(values)
    return values * below, below + values * decay * 0.3989422804014327


def row_mean(values):
    return jnp.mean(values, axis=-1, keepdims=True)


def front_kernel(
    tiles,
    scal_ref,
    x_own_ref,
    x_other_ref,
    ot_own_ref,
    ot_other_ref,
    st_own_ref,
    st_other_ref,
    og_own_ref,
    og_other_ref,
    wo_ref,
    gain_one_ref,
    fin_ref,
    fout_ref,
    gain_two_ref,
    down_ref,
    down_bias_ref,
    up_ref,
    up_bias_ref,
    out_ref,
    rst_ref,
    mix_ref,
    slope_ref,
    grad_low_ref,
    norm_grad_ref,
    normed_ref,
    inv_ref,
    up_grad_ref,
    up_bias_grad_ref,
    down_grad_ref,
    down_bias_grad_ref,
    up_sum_ref,
    down_sum_ref,
):
    step = pl.program_id(0)
    tile = x_own_ref.shape[0]
    width = x_own_ref.shape[1]
    own = step < tiles // 2
    x = jnp.where(own, x_own_ref[...], x_other_ref[...]).astype(F32)

    top_own, top_other = st_own_ref[:, :GROUP, :], st_other_ref[:, :GROUP, :]
    top = jnp.maximum(top_own, top_other)
    share_own, share_other = jnp.exp2(top_own - top), jnp.exp2(top_other - top)
    inverse = 1.0 / (
        st_own_ref[:, GROUP:, :] * share_own + st_other_ref[:, GROUP:, :] * share_other
    )
    rst_ref[:, :GROUP, :] = share_own * inverse
    rst_ref[:, GROUP:, :] = share_other * inverse
    mixes = []
    for head in range(width // HEAD_DIM):
        rows = slice(head * HEAD_DIM, (head + 1) * HEAD_DIM)
        group, place = head // GROUP, head % GROUP
        mixes.append(
            (
                ot_own_ref[rows, :] * rst_ref[group, place : place + 1, :]
                + ot_other_ref[rows, :] * rst_ref[group, GROUP + place : GROUP + place + 1, :]
            ).astype(BF16)
        )
    mix = jnp.concatenate(mixes, axis=0)
    mix_ref[...] = mix
    resid_one = x + dot_tn(mix, wo_ref[...])
    centred = resid_one - row_mean(resid_one)
    inv_one = lax.rsqrt(row_mean(centred * centred) + 1e-05)
    normed = centred * inv_one
    normed_ref[...] = normed.astype(BF16)
    inv_ref[...] = inv_one
    norm_one = normed * gain_one_ref[...]
    norm_low = norm_one.astype(BF16)

    squeeze = dot_nn(norm_low, down_ref[...]) + down_bias_ref[...]
    squeeze_act, squeeze_slope = gelu_pair(squeeze)
    squeeze_act = squeeze_act.astype(BF16)
    resid_two = norm_one + 4.0 * (dot_nn(squeeze_act, up_ref[...]) + up_bias_ref[...])
    hidden = fin_ref.shape[1]
    chunk = 1024
    for first in range(0, hidden, chunk):
        columns = slice(first, first + chunk)
        act, slope = gelu_pair(dot_nn(norm_low, fin_ref[:, columns]))
        slope_ref[:, columns] = slope.astype(BF16)
        resid_two = resid_two + dot_nn(act.astype(BF16), fout_ref[columns, :])

    centred = resid_two - row_mean(resid_two)
    inv_two = lax.rsqrt(row_mean(centred * centred) + 1e-05)
    normed_two = centred * inv_two
    base = jnp.where(own, scal_ref[0], scal_ref[1] - (tiles // 2) * tile) + step * tile
    place = base + lax.broadcasted_iota(jnp.int32, (tile, 1), 0)
    valid = (place < scal_ref[2]).astype(F32)
    gain_two = gain_two_ref[...]
    out_ref[...] = (normed_two * gain_two * valid).astype(BF16)
    upstream = jnp.where(own, og_own_ref[...], og_other_ref[...]).astype(F32) * valid * gain_two
    grad_two = inv_two * (
        upstream - row_mean(upstream) - normed_two * row_mean(upstream * normed_two)
    )
    grad_low_ref[...] = grad_two.astype(BF16)
    grad_adapt = (4.0 * grad_two).astype(BF16)
    grad_squeeze = (dot_nt(grad_adapt, up_ref[...]) * squeeze_slope).astype(BF16)
    norm_grad_ref[...] = grad_two + dot_nt(grad_squeeze, down_ref[...])
    up_grad = dot_tn(squeeze_act, grad_adapt)
    down_grad = dot_tn(grad_squeeze, norm_low)
    up_bias_grad = jnp.sum(grad_adapt.astype(F32), axis=0, keepdims=True)
    down_bias_grad = jnp.sum(grad_squeeze.astype(F32), axis=0, keepdims=True)

    @pl.when(step == 0)
    def _():
        up_sum_ref[...] = up_grad
        down_sum_ref[...] = down_grad
        up_bias_grad_ref[...] = up_bias_grad
        down_bias_grad_ref[...] = down_bias_grad

    @pl.when(step > 0)
    def _():
        up_sum_ref[...] += up_grad
        down_sum_ref[...] += down_grad
        up_bias_grad_ref[...] += up_bias_grad
        down_bias_grad_ref[...] += down_bias_grad

    @pl.when(step == tiles - 1)
    def _():
        up_grad_ref[...] = up_sum_ref[...].astype(BF16)
        down_grad_ref[...] = down_sum_ref[...].astype(BF16)


def front(
    scal, x_own, x_other, ot_own, ot_other, st_own, st_other, og_own, og_other,
    w_output, attn_gain, ffn_in, ffn_out, ffn_gain, down, down_bias, up, up_bias,
):
    rows, width = x_own.shape
    tokens = 2 * rows
    hidden = ffn_in.shape[1]
    adapt = down.shape[1]
    groups = width // LANES
    tile = 256
    tiles = tokens // tile
    near = pl.BlockSpec((tile, width), lambda i: (jnp.minimum(i, tiles // 2 - 1), 0))
    far = pl.BlockSpec((tile, width), lambda i: (jnp.maximum(i - tiles // 2, 0), 0))
    row_block = pl.BlockSpec((tile, width), lambda i: (i, 0))
    column_block = pl.BlockSpec((width, tile), lambda i: (0, i))
    stats = pl.BlockSpec((groups, 2 * GROUP, tile), lambda i: (0, 0, i))
    return pl.pallas_call(
        functools.partial(front_kernel, tiles),
        grid=(tiles,),
        in_specs=[
            SMEM_SPEC, near, far, column_block, column_block, stats, stats, near, far,
            kept((width, width)), whole((1, width)), kept((width, hidden)), kept((hidden, width)),
            whole((1, width)), kept((width, adapt)), whole((1, adapt)), kept((adapt, width)),
            whole((1, width)),
        ],
        out_specs=[
            row_block, stats, column_block, pl.BlockSpec((tile, hidden), lambda i: (i, 0)),
            row_block, row_block, row_block, pl.BlockSpec((tile, 1), lambda i: (i, 0)),
            whole((adapt, width)), whole((1, width)), whole((adapt, width)), whole((1, adapt)),
        ],
        out_shape=[
            shape_of((tokens, width), BF16),
            shape_of((groups, 2 * GROUP, tokens), F32),
            shape_of((width, tokens), BF16),
            shape_of((tokens, hidden), BF16),
            shape_of((tokens, width), BF16),
            shape_of((tokens, width), F32),
            shape_of((tokens, width), BF16),
            shape_of((tokens, 1), F32),
            shape_of((adapt, width), BF16),
            shape_of((1, width), F32),
            shape_of((adapt, width), BF16),
            shape_of((1, adapt), F32),
        ],
        scratch_shapes=[pltpu.VMEM((adapt, width), F32)] * 2,
        compiler_params=params(),
        cost_estimate=cost(tokens * width * (width + 2 * hidden + 6 * adapt), 60 * MIB),
    )(
        scal, x_own, x_other, ot_own, ot_other, st_own, st_other, og_own, og_other,
        w_output, attn_gain[None], ffn_in, ffn_out, ffn_gain[None], down, down_bias[None], up,
        up_bias[None],
    )


def rear_kernel(
    grad_low_ref, norm_grad_ref, slope_ref, normed_ref, inv_ref, mix_ref, wo_ref, gain_ref, fin_ref,
    fout_ref, grad_one_ref, up_ref, del_ref,
):
    grad_low = grad_low_ref[...]
    grad_norm = norm_grad_ref[...]
    hidden = fin_ref.shape[1]
    chunk = 1024
    for first in range(0, hidden, chunk):
        columns = slice(first, first + chunk)
        inner = dot_nt(grad_low, fout_ref[columns, :]) * slope_ref[:, columns].astype(F32)
        grad_norm = grad_norm + dot_nt(inner.astype(BF16), fin_ref[:, columns])
    grad = grad_norm * gain_ref[...]
    normed = normed_ref[...].astype(F32)
    grad_one = inv_ref[...] * (grad - row_mean(grad) - normed * row_mean(grad * normed))
    grad_one_ref[...] = grad_one
    up = dot_nt(wo_ref[...], grad_one.astype(BF16)).astype(BF16)
    up_ref[...] = up
    product = up.astype(F32) * mix_ref[...].astype(F32)
    for head in range(product.shape[0] // HEAD_DIM):
        rows = slice(head * HEAD_DIM, (head + 1) * HEAD_DIM)
        group, place = head // GROUP, head % GROUP
        del_ref[group, place : place + 1, :] = jnp.sum(product[rows], axis=0, keepdims=True)
    del_ref[:, GROUP:, :] = jnp.zeros_like(del_ref[:, GROUP:, :])


def rear(grad_low, norm_grad, slope, normed, inv, mix, w_output, attn_gain, ffn_in, ffn_out):
    tokens, width = grad_low.shape
    hidden = ffn_in.shape[1]
    groups = width // LANES
    tile = 256
    row_block = pl.BlockSpec((tile, width), lambda i: (i, 0))
    column_block = pl.BlockSpec((width, tile), lambda i: (0, i))
    return pl.pallas_call(
        rear_kernel,
        grid=(tokens // tile,),
        in_specs=[
            row_block, row_block, pl.BlockSpec((tile, hidden), lambda i: (i, 0)), row_block,
            pl.BlockSpec((tile, 1), lambda i: (i, 0)), column_block, kept((width, width)),
            whole((1, width)), kept((width, hidden)), kept((hidden, width)),
        ],
        out_specs=[
            row_block, column_block, pl.BlockSpec((groups, 2 * GROUP, tile), lambda i: (0, 0, i)),
        ],
        out_shape=[
            shape_of((tokens, width), F32),
            shape_of((width, tokens), BF16),
            shape_of((groups, 2 * GROUP, tokens), F32),
        ],
        compiler_params=params(),
        cost_estimate=cost(tokens * width * (width + 2 * hidden), 50 * MIB),
    )(grad_low, norm_grad, slope, normed, inv, mix, w_output, attn_gain[None], ffn_in, ffn_out)


def input_grad_kernel(grad_ref, dqt_ref, dk_ref, dv_ref, wq_ref, wk_ref, wv_ref, out_ref):
    total = grad_ref[...] + dot_tt(dqt_ref[...], wq_ref[...])
    total = total + dot_nt(dk_ref[...], wk_ref[...])
    total = total + dot_nt(dv_ref[...], wv_ref[...])
    out_ref[...] = total.astype(BF16)


def input_grad(half, grad_one, dqt, dk, dv, w_query, w_key, w_value):
    rows, width = dk.shape
    step = 256
    weight = pl.BlockSpec((step, width), lambda j: (j, 0))
    return pl.pallas_call(
        input_grad_kernel,
        grid=(width // step,),
        in_specs=[
            pl.BlockSpec((rows, step), lambda j: (half, j)),
            whole((width, rows)),
            whole((rows, width)),
            whole((rows, width)),
            weight,
            weight,
            weight,
        ],
        out_specs=pl.BlockSpec((rows, step), lambda j: (0, j)),
        out_shape=shape_of((rows, width), BF16),
        compiler_params=params(),
        cost_estimate=cost(3 * rows * width * width, 14 * MIB),
    )(grad_one, dqt, dk, dv, w_query, w_key, w_value)


def stage_groups():
    seqs, width = lax.axis_size("seq"), lax.axis_size("dp")
    seq, spot = lax.axis_index("seq"), lax.axis_index("dp")
    square = 2 * seqs

    def pair_peer(device, offset):
        return device ^ offset

    def square_peer(device, offset):
        return ((device // width) ^ (offset // 2)) * width + ((device % width) ^ (2 * (offset % 2)))

    def line_peer(device, offset):
        return (device // width) * width + ((device % width) ^ (4 * offset))

    return (
        (2, spot % 2, pair_peer),
        (square, seq * 2 + (spot // 2) % 2, square_peer),
        (width // 4, spot // 4, line_peer),
    )


def swap(value, peer, offset):
    count = lax.axis_size("seq") * lax.axis_size("dp")
    pairs = [(device, peer(device, offset)) for device in range(count)]
    return lax.ppermute(value, ("seq", "dp"), pairs)


def sum_whole(value):
    for size, _, peer in stage_groups():
        low = value.astype(BF16)
        arrived = [swap(low, peer, offset) for offset in range(1, size)]
        for item in arrived:
            value = value + item.astype(F32)
    return value


def sum_scattered(value):
    stages = stage_groups()
    for size, place, peer in stages:
        blocks = value.reshape(size, value.shape[0] // size, value.shape[1])
        total = lax.dynamic_index_in_dim(blocks, place, 0, keepdims=False).astype(F32)
        for offset in range(1, size):
            block = lax.dynamic_index_in_dim(blocks, place ^ offset, 0, keepdims=False)
            total = total + swap(block, peer, offset).astype(F32)
        value = total.astype(BF16)
    for size, place, peer in reversed(stages):
        gathered = jnp.zeros((size,) + value.shape, BF16)
        gathered = lax.dynamic_update_index_in_dim(gathered, value, place, 0)
        for offset in range(1, size):
            gathered = lax.dynamic_update_index_in_dim(
                gathered, swap(value, peer, offset), place ^ offset, 0
            )
        value = gathered.reshape(size * value.shape[0], value.shape[1])
    return value


def on_pair(
    hidden_in,
    lengths,
    w_query,
    w_key,
    w_value,
    w_output,
    attn_gain,
    ffn_in,
    ffn_out,
    ffn_gain,
    adapter_down,
    adapter_down_bias,
    adapter_up,
    adapter_up_bias,
    prefix_embed,
    prefix_hidden_w,
    prefix_hidden_b,
    prefix_out_w,
    prefix_out_b,
    out_grad,
):
    rows, _, width = hidden_in.shape
    count = prefix_embed.shape[0]
    position = lax.axis_index("seq")
    place = position.reshape(1).astype(jnp.int32)
    length = lax.dynamic_index_in_dim(lengths, position, 0, keepdims=False)
    scal = jnp.stack([position * rows, (1 - position) * rows, length]).astype(jnp.int32)

    x_own, x_send = split(place, hidden_in)
    x_other = shifted(x_send, "seq", 1)
    og_own, og_send = split(place, out_grad)
    og_other = shifted(og_send, "seq", 1)

    embed = jnp.pad(prefix_embed, ((0, PAD - count), (0, 0)))
    prefix_act, prefix_keys, prefix_values = prefix_forward(
        embed, prefix_hidden_w, prefix_hidden_b, prefix_out_w, prefix_out_b
    )
    lead = (prefix_keys, prefix_values)
    triple = project(0, x_own, w_query, w_key, w_value, ())
    q, k, _, _, vt = triple
    near = attend(count, scal, 0, 0, 1, q, k, vt, lead, ())
    q, k, kt, v, vt = project(1, x_other, w_query, w_key, w_value, triple)
    pt_own, ot_own, st_own, lead_weights = attend(count, scal, 0, 1, 1, q, k, vt, lead, near)
    pt_other, ot_other, st_other = attend(0, scal, 1, 0, 2, q, k, vt, (), ())

    (
        layer_out, shares, mix, slope, grad_low, norm_grad, normed, inv_one,
        up_grad, up_bias_grad, down_grad, down_bias_grad,
    ) = front(
        scal, x_own, x_other, ot_own, ot_other, st_own, st_other, og_own, og_other,
        w_output, attn_gain, ffn_in, ffn_out, ffn_gain, adapter_down, adapter_down_bias,
        adapter_up, adapter_up_bias,
    )
    out_other = shifted(layer_out[rows:], "seq", 1)
    up_total = sum_scattered(up_grad)
    down_total = sum_scattered(down_grad)
    grad_one, upstream, deltas = rear(
        grad_low, norm_grad, slope, normed, inv_one, mix, w_output, attn_gain, ffn_in, ffn_out
    )
    key_rows, value_rows, dqt = lead_backward(
        q, upstream, shares, deltas, lead_weights, prefix_keys, prefix_values
    )
    extra = jnp.concatenate(
        [
            jnp.pad(up_bias_grad, ((0, 0), (0, width))),
            jnp.pad(down_bias_grad, ((0, 0), (0, 2 * width - down_bias_grad.shape[1]))),
        ]
    )
    pair = jnp.concatenate([key_rows[:count], value_rows[:count]], axis=1)
    pair = sum_whole(jnp.concatenate([pair, extra]))

    dqt, dk_other, dv_other = attend_back(
        1, 0, 2, True, BF16, q, kt, v, upstream, shares, deltas, pt_other, dqt, ()
    )
    dqt_other, dk_own, dv_own = attend_back(
        0, 1, 1, False, F32, q, kt, v, upstream, shares, deltas, pt_own, dqt, ()
    )
    grad_other = input_grad(1, grad_one, dqt_other, dk_other, dv_other, w_query, w_key, w_value)
    grad_back = shifted(grad_other, "seq", 1)
    dqt_own, dk_own, dv_own = attend_back(
        0, 0, 1, False, BF16, q, kt, v, upstream, shares, deltas, pt_own, dqt, (dk_own, dv_own)
    )
    grad_own = input_grad(0, grad_one, dqt_own, dk_own, dv_own, w_query, w_key, w_value)

    prefix_grads = prefix_backward(count, pair, prefix_act, embed, prefix_hidden_w, prefix_out_w)
    return (
        merge(place, layer_out, out_other),
        merge(place, grad_own, grad_back),
        down_total.T.astype(F32),
        pair[count + 1, : down_bias_grad.shape[1]],
        up_total.astype(F32),
        pair[count, :width],
        prefix_grads[0],
        prefix_grads[1],
        prefix_grads[2][0],
        prefix_grads[3],
        prefix_grads[4][0],
    )


def solution(mesh):
    in_specs = (
        P("seq", "dp", None),
        P("dp"),
        P(),
        P(),
        P(),
        P(),
        P(),
        P(),
        P(),
        P(),
        P(),
        P(),
        P(),
        P(),
        P(),
        P(),
        P(),
        P(),
        P(),
        P("seq", "dp", None),
    )
    out_specs = (
        P("seq", "dp", None),
        P("seq", "dp", None),
        P(),
        P(),
        P(),
        P(),
        P(),
        P(),
        P(),
        P(),
        P(),
    )
    pairs = mesh.shape["seq"] == 2 and mesh.shape["dp"] % 8 == 0

    def on_one(*arrays):
        step = on_pair if pairs and arrays[0].shape[1] == 2 else on_device
        return step(*arrays)

    return jax.shard_map(
        on_one, mesh=mesh, in_specs=in_specs, out_specs=out_specs, check_vma=False
    )
```

```python
import functools
import math

import jax
import jax.numpy as jnp
from jax import lax
from jax.experimental import pallas as pl
from jax.experimental.pallas import tpu as pltpu
from jax.sharding import PartitionSpec as P

HEADS = 16


HIGHEST_PRECISION = lax.Precision.HIGHEST


def shifted(value, axis, steps):
    count = lax.axis_size(axis)
    pairs = [(source, (source + steps) % count) for source in range(count)]
    return lax.ppermute(value, axis, pairs)


def mixed(left, right):
    return jnp.dot(left, right, preferred_element_type=jnp.float32)


def mixed_left(left, right):
    return lax.dot_general(
        left, right, (((0,), (0,)), ((), ())), preferred_element_type=jnp.float32
    )


def mixed_right(left, right):
    return lax.dot_general(
        left, right, (((1,), (1,)), ((), ())), preferred_element_type=jnp.float32
    )


def precise(left, right):
    return jnp.dot(left, right, precision=HIGHEST_PRECISION, preferred_element_type=jnp.float32)


def precise_left(left, right):
    return lax.dot_general(
        left,
        right,
        (((0,), (0,)), ((), ())),
        precision=HIGHEST_PRECISION,
        preferred_element_type=jnp.float32,
    )


def precise_right(left, right):
    return lax.dot_general(
        left,
        right,
        (((1,), (1,)), ((), ())),
        precision=HIGHEST_PRECISION,
        preferred_element_type=jnp.float32,
    )


def gelu_value(inputs):
    return 0.5 * inputs * (1.0 + lax.erf(inputs * 0.7071067811865476))


def gelu_slope(inputs):
    return (
        0.5 * (1.0 + lax.erf(inputs * 0.7071067811865476))
        + inputs * jnp.exp(-0.5 * inputs * inputs) * 0.3989422804014327
    )


def normalize(values):
    row_mean = jnp.mean(values, axis=-1, keepdims=True)
    centred = values - row_mean
    spread = jnp.mean(centred * centred, axis=-1, keepdims=True)
    inv_std = lax.rsqrt(spread + 1e-05)
    return (centred * inv_std, inv_std)


def norm_back(upstream, normed, inv_std):
    mean_grad = jnp.mean(upstream, axis=-1, keepdims=True)
    mean_proj = jnp.mean(upstream * normed, axis=-1, keepdims=True)
    return inv_std * (upstream - mean_grad - normed * mean_proj)


def key_allowed(offset, key_count, seq_lengths):
    places = offset + lax.iota(jnp.int32, key_count)
    return places[None, :] < seq_lengths[:, None]


def lead_state(queries4, prefix_keys4, prefix_values4):
    inv_root = 1.0 / math.sqrt(queries4.shape[3])
    scores = (
        jnp.einsum("rshd,phd->rshp", queries4, prefix_keys4, preferred_element_type=jnp.float32)
        * inv_root
    )
    running_max = jnp.max(scores, axis=3)
    weights = jnp.exp(scores - running_max[..., None])
    running_sum = jnp.sum(weights, axis=3)
    running_mix = jnp.einsum(
        "rshp,phd->rshd",
        weights.astype(jnp.bfloat16),
        prefix_values4,
        preferred_element_type=jnp.float32,
    )
    return (running_max, running_sum, running_mix)


def fold_block(carried, key_block, value_block, offset, queries4, seq_lengths):
    key_count, seqs_here = (key_block.shape[0], key_block.shape[1])
    head_count, head_dim = (queries4.shape[2], queries4.shape[3])
    inv_root = 1.0 / math.sqrt(head_dim)
    keys4 = key_block.reshape(key_count, seqs_here, head_count, head_dim)
    values4 = value_block.reshape(key_count, seqs_here, head_count, head_dim)
    running_max, running_sum, running_mix = carried
    scores = (
        jnp.einsum("rshd,tshd->rsht", queries4, keys4, preferred_element_type=jnp.float32)
        * inv_root
    )
    allowed = key_allowed(offset, key_count, seq_lengths)[None, :, None, :]
    scores = jnp.where(allowed, scores, -jnp.inf)
    new_max = jnp.maximum(running_max, jnp.max(scores, axis=3))
    weights = jnp.exp(scores - new_max[..., None])
    rescale = jnp.exp(running_max - new_max)
    running_sum = running_sum * rescale + jnp.sum(weights, axis=3)
    running_mix = running_mix * rescale[..., None] + jnp.einsum(
        "rsht,tshd->rshd", weights.astype(jnp.bfloat16), values4, preferred_element_type=jnp.float32
    )
    return (new_max, running_sum, running_mix)


def lead_back(queries4, upstream4, log_total, row_delta, prefix_keys4, prefix_values4):
    inv_root = 1.0 / math.sqrt(queries4.shape[3])
    scores = (
        jnp.einsum("rshd,phd->rshp", queries4, prefix_keys4, preferred_element_type=jnp.float32)
        * inv_root
    )
    weights = jnp.exp(scores - log_total[..., None])
    weight_grads = jnp.einsum(
        "rshd,phd->rshp", upstream4, prefix_values4, preferred_element_type=jnp.float32
    )
    score_grads = (weights * (weight_grads - row_delta[..., None])).astype(jnp.bfloat16)
    query_term = (
        jnp.einsum("rshp,phd->rshd", score_grads, prefix_keys4, preferred_element_type=jnp.float32)
        * inv_root
    )
    key_term = (
        jnp.einsum("rshp,rshd->phd", score_grads, queries4, preferred_element_type=jnp.float32)
        * inv_root
    )
    value_term = jnp.einsum(
        "rshp,rshd->phd",
        weights.astype(jnp.bfloat16),
        upstream4,
        preferred_element_type=jnp.float32,
    )
    return (query_term, key_term, value_term)


def block_back(
    queries4, upstream4, log_total, row_delta, key_block, value_block, offset, seq_lengths
):
    key_count, seqs_here, model_width = key_block.shape
    head_count, head_dim = (queries4.shape[2], queries4.shape[3])
    inv_root = 1.0 / math.sqrt(head_dim)
    keys4 = key_block.reshape(key_count, seqs_here, head_count, head_dim)
    values4 = value_block.reshape(key_count, seqs_here, head_count, head_dim)
    scores = (
        jnp.einsum("rshd,tshd->rsht", queries4, keys4, preferred_element_type=jnp.float32)
        * inv_root
    )
    allowed = key_allowed(offset, key_count, seq_lengths)[None, :, None, :]
    scores = jnp.where(allowed, scores, -jnp.inf)
    weights = jnp.exp(scores - log_total[..., None])
    weight_grads = jnp.einsum(
        "rshd,tshd->rsht", upstream4, values4, preferred_element_type=jnp.float32
    )
    score_grads = (weights * (weight_grads - row_delta[..., None])).astype(jnp.bfloat16)
    query_term = (
        jnp.einsum("rsht,tshd->rshd", score_grads, keys4, preferred_element_type=jnp.float32)
        * inv_root
    )
    key_term = (
        jnp.einsum("rsht,rshd->tshd", score_grads, queries4, preferred_element_type=jnp.float32)
        * inv_root
    )
    value_term = jnp.einsum(
        "rsht,rshd->tshd",
        weights.astype(jnp.bfloat16),
        upstream4,
        preferred_element_type=jnp.float32,
    )
    pair_term = jnp.stack(
        [
            key_term.reshape(key_count, seqs_here, model_width),
            value_term.reshape(key_count, seqs_here, model_width),
        ]
    )
    return (query_term, pair_term)


def prefix_back(pair_grad, prefix_act, prefix_embed, hidden_weight, out_weight):
    out_w_grad = precise_left(prefix_act, pair_grad)
    out_b_grad = jnp.sum(pair_grad, axis=0)
    act_grad = precise_right(pair_grad, out_weight) * (1.0 - prefix_act * prefix_act)
    hidden_w_grad = precise_left(prefix_embed, act_grad)
    hidden_b_grad = jnp.sum(act_grad, axis=0)
    embed_grad = precise_right(act_grad, hidden_weight)
    return (embed_grad, hidden_w_grad, hidden_b_grad, out_w_grad, out_b_grad)


def on_device(
    hidden_in,
    lengths,
    w_query,
    w_key,
    w_value,
    w_output,
    attn_gain,
    ffn_in,
    ffn_out,
    ffn_gain,
    adapter_down,
    adapter_down_bias,
    adapter_up,
    adapter_up_bias,
    prefix_embed,
    prefix_hidden_w,
    prefix_hidden_b,
    prefix_out_w,
    prefix_out_b,
    out_grad,
):
    rows_here, seqs_here, model_width = hidden_in.shape
    token_count = rows_here * seqs_here
    head_count = HEADS
    head_dim = model_width // head_count
    axis_count = lax.axis_size("seq")
    position = lax.axis_index("seq")
    tokens = hidden_in.reshape(token_count, model_width)
    projected = jnp.stack([mixed(tokens, w_query), mixed(tokens, w_key), mixed(tokens, w_value)])
    triple = projected.astype(jnp.bfloat16).reshape(3, rows_here, seqs_here, model_width)
    hidden_weight = prefix_hidden_w.astype(jnp.float32)
    out_weight = prefix_out_w.astype(jnp.float32)
    prefix_act = jnp.tanh(precise(prefix_embed, hidden_weight) + prefix_hidden_b)
    prefix_pair = precise(prefix_act, out_weight) + prefix_out_b
    prefix_keys4 = (
        prefix_pair[:, :model_width].astype(jnp.bfloat16).reshape(-1, head_count, head_dim)
    )
    prefix_values4 = (
        prefix_pair[:, model_width:].astype(jnp.bfloat16).reshape(-1, head_count, head_dim)
    )
    row_places = position * rows_here + lax.iota(jnp.int32, rows_here)
    valid = (row_places[:, None] < lengths[None, :]).astype(jnp.float32).reshape(token_count, 1)
    queries4 = triple[0].reshape(rows_here, seqs_here, head_count, head_dim)
    key_value = triple[1:]
    pieces = lax.all_gather(key_value, "seq", axis=1, tiled=True)
    carried = fold_block(
        lead_state(queries4, prefix_keys4, prefix_values4),
        pieces[0],
        pieces[1],
        jnp.int32(0),
        queries4,
        lengths,
    )
    mix_full = carried[2] / carried[1][..., None]
    log_total = carried[0] + jnp.log(carried[1])
    mix_low = mix_full.astype(jnp.bfloat16).reshape(token_count, model_width)
    attn_proj = mixed(mix_low, w_output)
    normed_one, inv_one = normalize(tokens.astype(jnp.float32) + attn_proj)
    norm_one = normed_one * attn_gain
    norm_low = norm_one.astype(jnp.bfloat16)
    inner_pre = mixed(norm_low, ffn_in)
    inner_act = gelu_value(inner_pre).astype(jnp.bfloat16)
    squeeze = mixed(norm_low, adapter_down) + adapter_down_bias
    squeeze_act = gelu_value(squeeze).astype(jnp.bfloat16)
    ffn_sum = mixed(inner_act, ffn_out)
    adapter_sum = mixed(squeeze_act, adapter_up) + adapter_up_bias
    normed_two, inv_two = normalize(norm_one + ffn_sum + 4.0 * adapter_sum)
    layer_out = (
        (normed_two * ffn_gain * valid)
        .astype(jnp.bfloat16)
        .reshape(rows_here, seqs_here, model_width)
    )
    upstream_top = out_grad.reshape(token_count, model_width).astype(jnp.float32) * valid
    grad_two = norm_back(upstream_top * ffn_gain, normed_two, inv_two)
    grad_ffn_low = grad_two.astype(jnp.bfloat16)
    grad_adapt_low = (4.0 * grad_two).astype(jnp.bfloat16)
    up_grad = mixed_left(squeeze_act, grad_adapt_low)
    up_bias_grad = jnp.sum(grad_adapt_low.astype(jnp.float32), axis=0)
    grad_squeeze_low = (mixed_right(grad_adapt_low, adapter_up) * gelu_slope(squeeze)).astype(
        jnp.bfloat16
    )
    down_grad = mixed_left(norm_low, grad_squeeze_low)
    down_bias_grad = jnp.sum(grad_squeeze_low.astype(jnp.float32), axis=0)
    grad_inner_low = (mixed_right(grad_ffn_low, ffn_out) * gelu_slope(inner_pre)).astype(
        jnp.bfloat16
    )
    grad_norm = (
        grad_two + mixed_right(grad_squeeze_low, adapter_down) + mixed_right(grad_inner_low, ffn_in)
    )
    grad_one = norm_back(grad_norm * attn_gain, normed_one, inv_one)
    grad_attn_low = grad_one.astype(jnp.bfloat16)
    grad_mix_low = mixed_right(grad_attn_low, w_output).astype(jnp.bfloat16)
    upstream4 = grad_mix_low.reshape(rows_here, seqs_here, head_count, head_dim)
    row_delta = jnp.sum(upstream4.astype(jnp.float32) * mix_full, axis=3)
    query_grad, prefix_key_grad, prefix_value_grad = lead_back(
        queries4, upstream4, log_total, row_delta, prefix_keys4, prefix_values4
    )

    def visit(step_index, carried):
        moving, grads_moving, query_total = carried
        source = (position - step_index) % axis_count
        query_term, pair_term = block_back(
            queries4,
            upstream4,
            log_total,
            row_delta,
            moving[0],
            moving[1],
            source * rows_here,
            lengths,
        )
        return (moving, grads_moving + pair_term, query_total + query_term)

    def travel(step_index, carried):
        moving, grads_moving, query_total = visit(step_index, carried)
        moving = shifted(moving, "seq", 1)
        grads_moving = shifted(grads_moving.astype(jnp.bfloat16), "seq", 1).astype(
            grads_moving.dtype
        )
        return (moving, grads_moving, query_total)

    initial = (
        key_value,
        jnp.zeros((2, rows_here, seqs_here, model_width), jnp.float32),
        query_grad,
    )
    carried = lax.fori_loop(0, axis_count - 1, travel, initial)
    carried = visit(axis_count - 1, carried)
    pair_grads = shifted(carried[1].astype(jnp.bfloat16), "seq", 1).astype(jnp.float32)
    triple_grad = jnp.concatenate(
        [carried[2].reshape(1, rows_here, seqs_here, model_width), pair_grads]
    ).astype(jnp.bfloat16)
    hidden_grad = grad_one + mixed_right(triple_grad[0].reshape(token_count, model_width), w_query)
    hidden_grad = hidden_grad + mixed_right(triple_grad[1].reshape(token_count, model_width), w_key)
    hidden_grad = hidden_grad + mixed_right(
        triple_grad[2].reshape(token_count, model_width), w_value
    )
    hidden_grad = hidden_grad.astype(jnp.bfloat16).reshape(rows_here, seqs_here, model_width)
    pair_grad = jnp.concatenate(
        [prefix_key_grad.reshape(-1, model_width), prefix_value_grad.reshape(-1, model_width)],
        axis=1,
    )
    prefix_grads = prefix_back(pair_grad, prefix_act, prefix_embed, hidden_weight, out_weight)
    summed = lax.psum(
        (
            down_grad,
            down_bias_grad,
            up_grad,
            up_bias_grad,
            prefix_grads[0],
            prefix_grads[1],
            prefix_grads[2],
            prefix_grads[3],
            prefix_grads[4],
        ),
        ("seq", "dp"),
    )
    adapter_totals = summed[:4]
    prefix_totals = summed[4:]
    return (
        layer_out,
        hidden_grad,
        adapter_totals[0],
        adapter_totals[1],
        adapter_totals[2],
        adapter_totals[3],
        prefix_totals[0],
        prefix_totals[1],
        prefix_totals[2],
        prefix_totals[3],
        prefix_totals[4],
    )


BF16 = jnp.bfloat16
F32 = jnp.float32
MIB = 1024 * 1024
GROUP = 4
HEAD_DIM = 64
LANES = GROUP * HEAD_DIM
PAD = 32
MASKED = -1e30
LOG2E = 1.4426950408889634
VMEM_LIMIT = 60 * MIB


def dot_nn(left, right):
    return lax.dot_general(left, right, (((1,), (0,)), ((), ())), preferred_element_type=F32)


def dot_nt(left, right):
    return lax.dot_general(left, right, (((1,), (1,)), ((), ())), preferred_element_type=F32)


def dot_tn(left, right):
    return lax.dot_general(left, right, (((0,), (0,)), ((), ())), preferred_element_type=F32)


def dot_tt(left, right):
    return lax.dot_general(left, right, (((0,), (1,)), ((), ())), preferred_element_type=F32)


def shape_of(shape, dtype):
    return jax.ShapeDtypeStruct(shape, dtype)


def params(limit=VMEM_LIMIT):
    return pltpu.CompilerParams(vmem_limit_bytes=limit)


def cost(macs, moved):
    return pl.CostEstimate(flops=int(2 * macs), bytes_accessed=int(moved), transcendentals=0)


SMEM_SPEC = pl.BlockSpec(memory_space=pltpu.SMEM)
ANY_SPEC = pl.BlockSpec(memory_space=pl.ANY)


def whole(shape):
    return pl.BlockSpec(shape, lambda *_: (0,) * len(shape))


def kept(shape):
    return pl.BlockSpec(shape, lambda *_: (0,) * len(shape), pipeline_mode=pl.Buffered(1))


def split_kernel(place_ref, both_ref, own_ref, other_ref):
    apart = jnp.swapaxes(both_ref[...], 0, 1)
    first = place_ref[0] == 0
    own_ref[...] = jnp.where(first, apart[0], apart[1])
    other_ref[...] = jnp.where(first, apart[1], apart[0])


def split(place, both):
    rows, _, width = both.shape
    step = rows // 4
    half = pl.BlockSpec((step, width), lambda i: (i, 0))
    return pl.pallas_call(
        split_kernel,
        grid=(4,),
        in_specs=[SMEM_SPEC, pl.BlockSpec((step, 2, width), lambda i: (i, 0, 0))],
        out_specs=[half, half],
        out_shape=[shape_of((rows, width), both.dtype)] * 2,
        cost_estimate=cost(0, 4 * rows * width * 2),
    )(place, both)


def merge_kernel(place_ref, own_ref, other_ref, both_ref):
    first = place_ref[0] == 0
    own, other = own_ref[...], other_ref[...]
    apart = jnp.stack([jnp.where(first, own, other), jnp.where(first, other, own)])
    both_ref[...] = jnp.swapaxes(apart, 0, 1)


def merge(place, own, other):
    rows, width = other.shape
    step = rows // 4
    half = pl.BlockSpec((step, width), lambda i: (i, 0))
    return pl.pallas_call(
        merge_kernel,
        grid=(4,),
        in_specs=[SMEM_SPEC, half, half],
        out_specs=pl.BlockSpec((step, 2, width), lambda i: (i, 0, 0)),
        out_shape=shape_of((rows, 2, width), other.dtype),
        cost_estimate=cost(0, 4 * rows * width * 2),
    )(place, own, other)


def parts_of(values, count):
    parts = []
    for _ in range(count):
        part = values.astype(BF16)
        parts.append(part)
        values = values - part.astype(F32)
    return parts


def exact_dot(values, weight, dot):
    rows = values.shape[0]
    product = dot(jnp.concatenate(parts_of(values, 3), axis=0), weight)
    return product[:rows] + product[rows : 2 * rows] + product[2 * rows :]


def prefix_kernel(embed_ref, hw_ref, hb_ref, ow_ref, ob_ref, act_ref, key_ref, value_ref):
    width = key_ref.shape[1]
    act = jnp.tanh(exact_dot(embed_ref[...], hw_ref[...], dot_nn) + hb_ref[...])
    act_ref[...] = act
    pair = exact_dot(act, ow_ref[...], dot_nn) + ob_ref[...]
    key_ref[...] = pair[:, :width].astype(BF16)
    value_ref[...] = pair[:, width:].astype(BF16)


def prefix_forward(embed, hidden_w, hidden_b, out_w, out_b):
    width, hidden = hidden_w.shape
    return pl.pallas_call(
        prefix_kernel,
        out_shape=[
            shape_of((PAD, hidden), F32),
            shape_of((PAD, width), BF16),
            shape_of((PAD, width), BF16),
        ],
        compiler_params=params(),
        cost_estimate=cost(3 * PAD * hidden * 3 * width * 4, 6 * hidden * width),
    )(embed, hidden_w, hidden_b[None], out_w, out_b[None])


def prefix_back_kernel(
    count, pair_ref, act_ref, embed_ref, hw_ref, ow_ref, eg_ref, hwg_ref, hbg_ref, owg_ref, obg_ref
):
    pair = pair_ref[...]
    rows = lax.broadcasted_iota(jnp.int32, pair.shape, 0)
    pair = jnp.where(rows < count, pair, 0.0)
    act = act_ref[...]
    obg_ref[...] = jnp.sum(pair, axis=0, keepdims=True)
    high, low = parts_of(pair, 2)
    back = dot_nt(jnp.concatenate([high, low], axis=0), ow_ref[...])
    act_grad = (back[:PAD] + back[PAD:]) * (1.0 - act * act)
    act_high, act_low = parts_of(act, 2)
    owg_ref[...] = dot_tn(
        jnp.concatenate([act_high, act_low, act_high], axis=0),
        jnp.concatenate([high, high, low], axis=0),
    )
    hbg_ref[...] = jnp.sum(act_grad, axis=0, keepdims=True)
    high, low = parts_of(act_grad, 2)
    embed_high, embed_low = parts_of(embed_ref[...], 2)
    hwg_ref[...] = dot_tn(
        jnp.concatenate([embed_high, embed_low, embed_high], axis=0),
        jnp.concatenate([high, high, low], axis=0),
    )
    back = dot_nt(jnp.concatenate([high, low], axis=0), hw_ref[...])
    eg_ref[...] = (back[:PAD] + back[PAD:])[:count]


def prefix_backward(count, pair, act, embed, hidden_w, out_w):
    width, hidden = hidden_w.shape
    return pl.pallas_call(
        functools.partial(prefix_back_kernel, count),
        out_shape=[
            shape_of((count, width), F32),
            shape_of((width, hidden), F32),
            shape_of((1, hidden), F32),
            shape_of((hidden, 2 * width), F32),
            shape_of((1, 2 * width), F32),
        ],
        compiler_params=params(),
        cost_estimate=cost(96 * hidden * width * 6, 20 * hidden * width),
    )(pair, act, embed, hidden_w, out_w)


def project_kernel(x_ref, wq_ref, wk_ref, wv_ref, *refs):
    q_ref, k_ref, kt_ref, v_ref, vt_ref = refs[-5:]
    x = x_ref[...]
    scale = LOG2E / math.sqrt(HEAD_DIM)
    q_ref[...] = (dot_nn(x, wq_ref[...]) * scale).astype(BF16)
    k = dot_nn(x, wk_ref[...]).astype(BF16)
    k_ref[...] = k
    kt_ref[...] = k.T
    v = dot_nn(x, wv_ref[...]).astype(BF16)
    v_ref[...] = v
    vt_ref[...] = v.T


def project(half, x, w_query, w_key, w_value, earlier):
    rows, width = x.shape
    step = 256
    weight = pl.BlockSpec((width, step), lambda j: (0, j))
    straight = pl.BlockSpec((rows, step), lambda j: (half, j))
    turned = pl.BlockSpec((step, rows), lambda j: (j, half))
    return pl.pallas_call(
        project_kernel,
        grid=(width // step,),
        in_specs=[whole((rows, width)), weight, weight, weight] + [ANY_SPEC] * len(earlier),
        out_specs=[straight, straight, turned, straight, turned],
        out_shape=[
            shape_of((2 * rows, width), BF16),
            shape_of((2 * rows, width), BF16),
            shape_of((width, 2 * rows), BF16),
            shape_of((2 * rows, width), BF16),
            shape_of((width, 2 * rows), BF16),
        ],
        input_output_aliases={4 + i: i for i in range(len(earlier))},
        compiler_params=params(),
        cost_estimate=cost(3 * rows * width * width, 2 * (6 * rows * width + 3 * width * width)),
    )(x, w_query, w_key, w_value, *earlier)


def head_lanes(head, rows, lanes):
    place = lax.broadcasted_iota(jnp.int32, (rows, lanes), 1)
    return (place // HEAD_DIM == head).astype(F32).astype(BF16)


def first_lane(values):
    lane = lax.broadcasted_iota(jnp.int32, (values.shape[0], 128), 1)
    return jnp.where(lane == 0, values, 0.0).astype(BF16)


def block_diagonal(rows):
    return jnp.concatenate(
        [rows * head_lanes(head, rows.shape[0], LANES) for head in range(GROUP)], axis=0
    )


def attend_kernel(count, half, scal_ref, q_ref, k_ref, vt_ref, *refs):
    keys = k_ref.shape[0]
    queries = q_ref.shape[0]
    if count:
        pk_ref, pv_ref = refs[:2]
        pt_ref, ot_ref, st_ref, pp_ref = refs[-4:]
    else:
        pt_ref, ot_ref, st_ref = refs[-3:]
    place = scal_ref[half] + lax.broadcasted_iota(jnp.int32, (keys, 128), 0)
    bias = first_lane(jnp.where(place < scal_ref[2], 0.0, MASKED))
    ones = first_lane(jnp.ones((queries, 128), F32))
    tail = jnp.ones((16, keys), BF16)
    masks = [head_lanes(head, queries, 128) for head in range(2)]
    if count:
        lead = dot_nt(block_diagonal(pk_ref[...]), q_ref[...])
        row = lax.broadcasted_iota(jnp.int32, lead.shape, 0)
        lead = jnp.where(row % PAD < count, lead, MASKED)
    mixes = []
    leads = []
    for head in range(GROUP):
        pair = slice((head // 2) * 128, (head // 2 + 1) * 128)
        rows = slice(head * HEAD_DIM, (head + 1) * HEAD_DIM)
        k_aug = jnp.concatenate([k_ref[:, pair], bias], axis=1)
        q_aug = jnp.concatenate([q_ref[:, pair] * masks[head % 2], ones], axis=1)
        scores = dot_nt(k_aug, q_aug)
        top = jnp.max(scores, axis=0, keepdims=True)
        if count:
            lead_scores = lead[head * PAD : (head + 1) * PAD]
            top = jnp.maximum(top, jnp.max(lead_scores, axis=0, keepdims=True))
        weights = jnp.exp2(scores - top).astype(BF16)
        pt_ref[head] = weights
        mix = dot_nn(jnp.concatenate([vt_ref[rows, :], tail], axis=0), weights)
        total = mix[HEAD_DIM : HEAD_DIM + 1]
        mixes.append(mix[:HEAD_DIM])
        if count:
            lead_weights = jnp.exp2(lead_scores - top).astype(BF16)
            total = total + jnp.sum(lead_weights.astype(F32), axis=0, keepdims=True)
            leads.append(lead_weights)
        st_ref[0, head : head + 1, :] = top
        st_ref[0, GROUP + head : GROUP + head + 1, :] = total
    mix = jnp.concatenate(mixes, axis=0)
    if count:
        lead_weights = jnp.concatenate(leads, axis=0)
        pp_ref[0] = lead_weights
        mix = mix + dot_tn(block_diagonal(pv_ref[...]), lead_weights)
    ot_ref[...] = mix


def attend(count, scal, key_half, query_first, query_blocks, q, k, vt, lead, earlier):
    tokens, width = q.shape
    rows = tokens // 2
    groups = width // LANES
    in_specs = [
        SMEM_SPEC,
        pl.BlockSpec((rows, LANES), lambda i, g: (i + query_first, g)),
        pl.BlockSpec((rows, LANES), lambda i, g: (key_half, g)),
        pl.BlockSpec((LANES, rows), lambda i, g: (g, key_half)),
    ]
    in_specs += [pl.BlockSpec((PAD, LANES), lambda i, g: (0, g))] * len(lead)
    out_specs = [
        pl.BlockSpec((GROUP, rows, rows), lambda i, g: (g, 0, i + query_first)),
        pl.BlockSpec((LANES, rows), lambda i, g: (g, i + query_first)),
        pl.BlockSpec((1, 2 * GROUP, rows), lambda i, g: (g, 0, i + query_first)),
    ]
    out_shape = [
        shape_of((groups * GROUP, rows, tokens), BF16),
        shape_of((width, tokens), F32),
        shape_of((groups, 2 * GROUP, tokens), F32),
    ]
    if count:
        out_specs.append(pl.BlockSpec((1, GROUP * PAD, rows), lambda i, g: (g, 0, i + query_first)))
        out_shape.append(shape_of((groups, GROUP * PAD, tokens), BF16))
    start = len(in_specs)
    macs = query_blocks * groups * GROUP * rows * rows * 256 * 2
    return pl.pallas_call(
        functools.partial(attend_kernel, count, key_half),
        grid=(query_blocks, groups),
        in_specs=in_specs + [ANY_SPEC] * len(earlier),
        out_specs=out_specs,
        out_shape=out_shape,
        input_output_aliases={start + i: i for i in range(len(earlier))},
        compiler_params=params(),
        cost_estimate=cost(macs, query_blocks * 24 * MIB),
    )(scal, q, k, vt, *lead, *earlier)


def lead_back_kernel(q_ref, up_ref, rst_ref, del_ref, pp_ref, pk_ref, pv_ref, kg_ref, vg_ref, dqt_ref):
    queries = q_ref.shape[0]
    ups = []
    deltas = []
    for head in range(GROUP):
        rows = slice(head * HEAD_DIM, (head + 1) * HEAD_DIM)
        share = rst_ref[0, head : head + 1, :]
        ups.append((up_ref[rows, :].astype(F32) * share).astype(BF16))
        delta = del_ref[0, head : head + 1, :] * share
        deltas.append(jnp.broadcast_to(delta, (PAD, queries)))
    up = jnp.concatenate(ups, axis=0)
    delta = jnp.concatenate(deltas, axis=0)
    weights = pp_ref[0]
    key_diagonal = block_diagonal(pk_ref[...])
    value_diagonal = block_diagonal(pv_ref[...])
    weight_grads = dot_nn(value_diagonal, up)
    score_grads = (weights.astype(F32) * (weight_grads - delta)).astype(BF16)
    dqt_ref[...] = dot_tn(key_diagonal, score_grads)
    key_grads = dot_nn(score_grads, q_ref[...]) * (1.0 / LOG2E)
    value_grads = dot_nt(weights, up)
    lane = lax.broadcasted_iota(jnp.int32, (PAD, LANES), 1) // HEAD_DIM
    key_total = jnp.zeros((PAD, LANES), F32)
    value_total = jnp.zeros((PAD, LANES), F32)
    for head in range(GROUP):
        rows = slice(head * PAD, (head + 1) * PAD)
        key_total = jnp.where(lane == head, key_grads[rows], key_total)
        value_total = jnp.where(lane == head, value_grads[rows], value_total)
    kg_ref[...] = key_total
    vg_ref[...] = value_total


def lead_backward(q, up, shares, deltas, lead_weights, prefix_keys, prefix_values):
    tokens, width = q.shape
    groups = width // LANES
    small = pl.BlockSpec((PAD, LANES), lambda g: (0, g))
    stats = pl.BlockSpec((1, 2 * GROUP, tokens), lambda g: (g, 0, 0))
    return pl.pallas_call(
        lead_back_kernel,
        grid=(groups,),
        in_specs=[
            pl.BlockSpec((tokens, LANES), lambda g: (0, g)),
            pl.BlockSpec((LANES, tokens), lambda g: (g, 0)),
            stats,
            stats,
            pl.BlockSpec((1, GROUP * PAD, tokens), lambda g: (g, 0, 0)),
            small,
            small,
        ],
        out_specs=[small, small, pl.BlockSpec((LANES, tokens), lambda g: (g, 0))],
        out_shape=[
            shape_of((PAD, width), F32),
            shape_of((PAD, width), F32),
            shape_of((width, tokens), F32),
        ],
        compiler_params=params(),
        cost_estimate=cost(groups * 4 * GROUP * PAD * tokens * LANES, 10 * MIB),
    )(q, up, shares, deltas, lead_weights, prefix_keys, prefix_values)


def attend_back_kernel(
    half,
    has_earlier,
    q_ref,
    kt_ref,
    v_ref,
    up_ref,
    rst_ref,
    del_ref,
    pt_ref,
    dqt_in_ref,
    *refs,
):
    dqt_ref, dk_ref, dv_ref = refs[-3:]
    queries = q_ref.shape[0]
    lane = lax.broadcasted_iota(jnp.int32, (queries, 128), 1) // HEAD_DIM
    masks = [(lane == head).astype(F32).astype(BF16) for head in range(2)]
    zeros = jnp.zeros((HEAD_DIM, queries), BF16)
    key_grads = []
    value_grads = []
    for duo in range(GROUP // 2):
        pair = slice(duo * 128, (duo + 1) * 128)
        key_grad = None
        value_grad = None
        for side in range(2):
            head = 2 * duo + side
            rows = slice(head * HEAD_DIM, (head + 1) * HEAD_DIM)
            share = rst_ref[0, half * GROUP + head : half * GROUP + head + 1, :]
            up = (up_ref[rows, :].astype(F32) * share).astype(BF16)
            up = jnp.concatenate([up, zeros] if side == 0 else [zeros, up], axis=0)
            delta = del_ref[0, head : head + 1, :] * share
            weights = pt_ref[head]
            weight_grads = dot_nn(v_ref[:, pair], up)
            score_grads = (weights.astype(F32) * (weight_grads - delta)).astype(BF16)
            dqt = dqt_in_ref[rows, :] + dot_nn(kt_ref[rows, :], score_grads)
            if dqt_ref.dtype == F32:
                dqt_ref[rows, :] = dqt
            else:
                dqt_ref[rows, :] = (dqt * (1.0 / math.sqrt(HEAD_DIM))).astype(BF16)
            key_term = dot_nn(score_grads, q_ref[:, pair] * masks[side])
            value_term = dot_nt(weights, up)
            key_grad = key_term if side == 0 else key_grad + key_term
            value_grad = value_term if side == 0 else value_grad + value_term
        key_grads.append(key_grad)
        value_grads.append(value_grad)
    key_grad = jnp.concatenate(key_grads, axis=1)
    value_grad = jnp.concatenate(value_grads, axis=1)
    if has_earlier:
        key_grad = key_grad + refs[0][...]
        value_grad = value_grad + refs[1][...]
    if dk_ref.dtype == F32:
        dk_ref[...] = key_grad
        dv_ref[...] = value_grad
    else:
        dk_ref[...] = (key_grad * (1.0 / LOG2E)).astype(BF16)
        dv_ref[...] = value_grad.astype(BF16)


def attend_back(
    key_half, query_half, last_keys, last_queries, q, kt, v, up, shares, deltas, weights, dqt, earlier
):
    tokens, width = q.shape
    rows = tokens // 2
    groups = width // LANES
    query_columns = pl.BlockSpec((LANES, rows), lambda g: (g, query_half))
    stats = pl.BlockSpec((1, 2 * GROUP, rows), lambda g: (g, 0, query_half))
    finished = pl.BlockSpec((rows, LANES), lambda g: (0, g))
    out_columns = pl.BlockSpec((LANES, rows), lambda g: (g, 0))
    sofar = query_columns if dqt.shape[1] == tokens else out_columns
    macs = groups * GROUP * rows * rows * 256 * 4
    grads_type = BF16 if last_queries else F32
    return pl.pallas_call(
        functools.partial(attend_back_kernel, key_half, len(earlier) > 0),
        grid=(groups,),
        in_specs=[
            pl.BlockSpec((rows, LANES), lambda g: (query_half, g)),
            pl.BlockSpec((LANES, rows), lambda g: (g, key_half)),
            pl.BlockSpec((rows, LANES), lambda g: (key_half, g)),
            query_columns,
            stats,
            stats,
            pl.BlockSpec((GROUP, rows, rows), lambda g: (g, 0, query_half)),
            sofar,
        ]
        + [finished] * len(earlier),
        out_specs=[out_columns, finished, finished],
        out_shape=[
            shape_of((width, rows), BF16 if last_keys else F32),
            shape_of((rows, width), grads_type),
            shape_of((rows, width), grads_type),
        ],
        compiler_params=params(),
        cost_estimate=cost(macs, 12 * MIB),
    )(q, kt, v, up, shares, deltas, weights, dqt, *earlier)


def normal_density_parts(values):
    decay = jnp.exp2(values * values * (-0.5 * LOG2E))
    spread = 1.0 + jnp.abs(values) * (0.3275911 * 0.7071067811865476)
    t = pl.reciprocal(spread, approx=True)
    t = t * (2.0 - spread * t)
    series = 0.5 * 1.061405429
    for term in (-1.453152027, 1.421413741, -0.284496736, 0.254829592):
        series = series * t + 0.5 * term
    below = series * t * decay
    return jnp.where(values < 0.0, below, 1.0 - below), decay


def gelu_pair(values):
    below, decay = normal_density_parts(values)
    return values * below, below + values * decay * 0.3989422804014327


def row_mean(values):
    return jnp.mean(values, axis=-1, keepdims=True)


def front_kernel(
    tiles,
    scal_ref,
    x_own_ref,
    x_other_ref,
    ot_own_ref,
    ot_other_ref,
    st_own_ref,
    st_other_ref,
    og_own_ref,
    og_other_ref,
    wo_ref,
    gain_one_ref,
    fin_ref,
    fout_ref,
    gain_two_ref,
    down_ref,
    down_bias_ref,
    up_ref,
    up_bias_ref,
    out_ref,
    rst_ref,
    mix_ref,
    slope_ref,
    grad_low_ref,
    norm_grad_ref,
    normed_ref,
    inv_ref,
    adapt_grad_ref,
    up_bias_grad_ref,
    down_bias_grad_ref,
    up_sum_ref,
    down_sum_ref,
):
    step = pl.program_id(0)
    tile = x_own_ref.shape[0]
    width = x_own_ref.shape[1]
    own = step < tiles // 2
    x = jnp.where(own, x_own_ref[...], x_other_ref[...]).astype(F32)

    top_own, top_other = st_own_ref[:, :GROUP, :], st_other_ref[:, :GROUP, :]
    top = jnp.maximum(top_own, top_other)
    share_own, share_other = jnp.exp2(top_own - top), jnp.exp2(top_other - top)
    inverse = 1.0 / (
        st_own_ref[:, GROUP:, :] * share_own + st_other_ref[:, GROUP:, :] * share_other
    )
    rst_ref[:, :GROUP, :] = share_own * inverse
    rst_ref[:, GROUP:, :] = share_other * inverse
    mixes = []
    for head in range(width // HEAD_DIM):
        rows = slice(head * HEAD_DIM, (head + 1) * HEAD_DIM)
        group, place = head // GROUP, head % GROUP
        mixes.append(
            (
                ot_own_ref[rows, :] * rst_ref[group, place : place + 1, :]
                + ot_other_ref[rows, :] * rst_ref[group, GROUP + place : GROUP + place + 1, :]
            ).astype(BF16)
        )
    mix = jnp.concatenate(mixes, axis=0)
    mix_ref[...] = mix
    resid_one = x + dot_tn(mix, wo_ref[...])
    centred = resid_one - row_mean(resid_one)
    inv_one = lax.rsqrt(row_mean(centred * centred) + 1e-05)
    normed = centred * inv_one
    normed_ref[...] = normed.astype(BF16)
    inv_ref[...] = inv_one
    norm_one = normed * gain_one_ref[...]
    norm_low = norm_one.astype(BF16)

    squeeze = dot_nn(norm_low, down_ref[...]) + down_bias_ref[...]
    squeeze_act, squeeze_slope = gelu_pair(squeeze)
    squeeze_act = squeeze_act.astype(BF16)
    resid_two = norm_one + 4.0 * (dot_nn(squeeze_act, up_ref[...]) + up_bias_ref[...])
    hidden = fin_ref.shape[1]
    chunk = 1024
    for first in range(0, hidden, chunk):
        columns = slice(first, first + chunk)
        act, slope = gelu_pair(dot_nn(norm_low, fin_ref[:, columns]))
        slope_ref[:, columns] = slope.astype(BF16)
        resid_two = resid_two + dot_nn(act.astype(BF16), fout_ref[columns, :])

    centred = resid_two - row_mean(resid_two)
    inv_two = lax.rsqrt(row_mean(centred * centred) + 1e-05)
    normed_two = centred * inv_two
    base = jnp.where(own, scal_ref[0], scal_ref[1] - (tiles // 2) * tile) + step * tile
    place = base + lax.broadcasted_iota(jnp.int32, (tile, 1), 0)
    valid = (place < scal_ref[2]).astype(F32)
    gain_two = gain_two_ref[...]
    out_ref[...] = (normed_two * gain_two * valid).astype(BF16)
    upstream = jnp.where(own, og_own_ref[...], og_other_ref[...]).astype(F32) * valid * gain_two
    grad_two = inv_two * (
        upstream - row_mean(upstream) - normed_two * row_mean(upstream * normed_two)
    )
    grad_low_ref[...] = grad_two.astype(BF16)
    grad_adapt = (4.0 * grad_two).astype(BF16)
    grad_squeeze = (dot_nt(grad_adapt, up_ref[...]) * squeeze_slope).astype(BF16)
    norm_grad_ref[...] = grad_two + dot_nt(grad_squeeze, down_ref[...])
    up_grad = dot_tn(squeeze_act, grad_adapt)
    down_grad = dot_tn(grad_squeeze, norm_low)
    up_bias_grad = jnp.sum(grad_adapt.astype(F32), axis=0, keepdims=True)
    down_bias_grad = jnp.sum(grad_squeeze.astype(F32), axis=0, keepdims=True)

    @pl.when(step == 0)
    def _():
        up_sum_ref[...] = up_grad
        down_sum_ref[...] = down_grad
        up_bias_grad_ref[...] = up_bias_grad
        down_bias_grad_ref[...] = down_bias_grad

    @pl.when(step > 0)
    def _():
        up_sum_ref[...] += up_grad
        down_sum_ref[...] += down_grad
        up_bias_grad_ref[...] += up_bias_grad
        down_bias_grad_ref[...] += down_bias_grad

    @pl.when(step == tiles - 1)
    def _():
        adapt = up_sum_ref.shape[0]
        adapt_grad_ref[:adapt, :] = up_sum_ref[...].astype(BF16)
        adapt_grad_ref[adapt:, :] = down_sum_ref[...].astype(BF16)


def front(
    scal, x_own, x_other, ot_own, ot_other, st_own, st_other, og_own, og_other,
    w_output, attn_gain, ffn_in, ffn_out, ffn_gain, down, down_bias, up, up_bias,
):
    rows, width = x_own.shape
    tokens = 2 * rows
    hidden = ffn_in.shape[1]
    adapt = down.shape[1]
    groups = width // LANES
    tile = 256
    tiles = tokens // tile
    near = pl.BlockSpec((tile, width), lambda i: (jnp.minimum(i, tiles // 2 - 1), 0))
    far = pl.BlockSpec((tile, width), lambda i: (jnp.maximum(i - tiles // 2, 0), 0))
    row_block = pl.BlockSpec((tile, width), lambda i: (i, 0))
    column_block = pl.BlockSpec((width, tile), lambda i: (0, i))
    stats = pl.BlockSpec((groups, 2 * GROUP, tile), lambda i: (0, 0, i))
    return pl.pallas_call(
        functools.partial(front_kernel, tiles),
        grid=(tiles,),
        in_specs=[
            SMEM_SPEC, near, far, column_block, column_block, stats, stats, near, far,
            kept((width, width)), whole((1, width)), kept((width, hidden)), kept((hidden, width)),
            whole((1, width)), kept((width, adapt)), whole((1, adapt)), kept((adapt, width)),
            whole((1, width)),
        ],
        out_specs=[
            row_block, stats, column_block, pl.BlockSpec((tile, hidden), lambda i: (i, 0)),
            row_block, row_block, row_block, pl.BlockSpec((tile, 1), lambda i: (i, 0)),
            whole((2 * adapt, width)), whole((1, width)), whole((1, adapt)),
        ],
        out_shape=[
            shape_of((tokens, width), BF16),
            shape_of((groups, 2 * GROUP, tokens), F32),
            shape_of((width, tokens), BF16),
            shape_of((tokens, hidden), BF16),
            shape_of((tokens, width), BF16),
            shape_of((tokens, width), F32),
            shape_of((tokens, width), BF16),
            shape_of((tokens, 1), F32),
            shape_of((2 * adapt, width), BF16),
            shape_of((1, width), F32),
            shape_of((1, adapt), F32),
        ],
        scratch_shapes=[pltpu.VMEM((adapt, width), F32)] * 2,
        compiler_params=params(),
        cost_estimate=cost(tokens * width * (width + 2 * hidden + 6 * adapt), 60 * MIB),
    )(
        scal, x_own, x_other, ot_own, ot_other, st_own, st_other, og_own, og_other,
        w_output, attn_gain[None], ffn_in, ffn_out, ffn_gain[None], down, down_bias[None], up,
        up_bias[None],
    )


def rear_kernel(
    grad_low_ref, norm_grad_ref, slope_ref, normed_ref, inv_ref, mix_ref, wo_ref, gain_ref, fin_ref,
    fout_ref, grad_one_ref, up_ref, del_ref,
):
    grad_low = grad_low_ref[...]
    grad_norm = norm_grad_ref[...]
    hidden = fin_ref.shape[1]
    chunk = 1024
    for first in range(0, hidden, chunk):
        columns = slice(first, first + chunk)
        inner = dot_nt(grad_low, fout_ref[columns, :]) * slope_ref[:, columns].astype(F32)
        grad_norm = grad_norm + dot_nt(inner.astype(BF16), fin_ref[:, columns])
    grad = grad_norm * gain_ref[...]
    normed = normed_ref[...].astype(F32)
    grad_one = inv_ref[...] * (grad - row_mean(grad) - normed * row_mean(grad * normed))
    grad_one_ref[...] = grad_one
    up = dot_nt(wo_ref[...], grad_one.astype(BF16)).astype(BF16)
    up_ref[...] = up
    product = up.astype(F32) * mix_ref[...].astype(F32)
    for head in range(product.shape[0] // HEAD_DIM):
        rows = slice(head * HEAD_DIM, (head + 1) * HEAD_DIM)
        group, place = head // GROUP, head % GROUP
        del_ref[group, place : place + 1, :] = jnp.sum(product[rows], axis=0, keepdims=True)
    del_ref[:, GROUP:, :] = jnp.zeros_like(del_ref[:, GROUP:, :])


def rear(grad_low, norm_grad, slope, normed, inv, mix, w_output, attn_gain, ffn_in, ffn_out):
    tokens, width = grad_low.shape
    hidden = ffn_in.shape[1]
    groups = width // LANES
    tile = 256
    row_block = pl.BlockSpec((tile, width), lambda i: (i, 0))
    column_block = pl.BlockSpec((width, tile), lambda i: (0, i))
    return pl.pallas_call(
        rear_kernel,
        grid=(tokens // tile,),
        in_specs=[
            row_block, row_block, pl.BlockSpec((tile, hidden), lambda i: (i, 0)), row_block,
            pl.BlockSpec((tile, 1), lambda i: (i, 0)), column_block, kept((width, width)),
            whole((1, width)), kept((width, hidden)), kept((hidden, width)),
        ],
        out_specs=[
            row_block, column_block, pl.BlockSpec((groups, 2 * GROUP, tile), lambda i: (0, 0, i)),
        ],
        out_shape=[
            shape_of((tokens, width), F32),
            shape_of((width, tokens), BF16),
            shape_of((groups, 2 * GROUP, tokens), F32),
        ],
        compiler_params=params(),
        cost_estimate=cost(tokens * width * (width + 2 * hidden), 50 * MIB),
    )(grad_low, norm_grad, slope, normed, inv, mix, w_output, attn_gain[None], ffn_in, ffn_out)


def input_grad_kernel(grad_ref, dqt_ref, dk_ref, dv_ref, wq_ref, wk_ref, wv_ref, out_ref):
    total = grad_ref[...] + dot_tt(dqt_ref[...], wq_ref[...])
    total = total + dot_nt(dk_ref[...], wk_ref[...])
    total = total + dot_nt(dv_ref[...], wv_ref[...])
    out_ref[...] = total.astype(BF16)


def input_grad(half, grad_one, dqt, dk, dv, w_query, w_key, w_value):
    rows, width = dk.shape
    step = 256
    weight = pl.BlockSpec((step, width), lambda j: (j, 0))
    return pl.pallas_call(
        input_grad_kernel,
        grid=(width // step,),
        in_specs=[
            pl.BlockSpec((rows, step), lambda j: (half, j)),
            whole((width, rows)),
            whole((rows, width)),
            whole((rows, width)),
            weight,
            weight,
            weight,
        ],
        out_specs=pl.BlockSpec((rows, step), lambda j: (0, j)),
        out_shape=shape_of((rows, width), BF16),
        compiler_params=params(),
        cost_estimate=cost(3 * rows * width * width, 14 * MIB),
    )(grad_one, dqt, dk, dv, w_query, w_key, w_value)


def swap(value, seq_bit, dp_bits):
    width = lax.axis_size("dp")
    count = lax.axis_size("seq") * width
    pairs = [
        (device, ((device // width) ^ seq_bit) * width + ((device % width) ^ dp_bits))
        for device in range(count)
    ]
    return lax.ppermute(value, ("seq", "dp"), pairs)


def gather_line(value):
    width = lax.axis_size("dp")
    groups = [[4 * line + place for line in range(width // 4)] for place in range(4)]
    return lax.all_gather(value, "dp", axis_index_groups=groups)


def total(values):
    return jnp.sum(values.astype(F32), axis=0)


def sum_core(value):
    core = lax.axis_index("dp") % 2
    halves = value.reshape(2, value.shape[0] // 2, value.shape[1])
    kept_half = lax.dynamic_index_in_dim(halves, core, 0, keepdims=False)
    sent_half = lax.dynamic_index_in_dim(halves, 1 - core, 0, keepdims=False)
    return kept_half, swap(sent_half, 0, 1)


def square_place():
    return 2 * ((lax.axis_index("dp") // 2) % 2) + lax.axis_index("seq")


def square_swaps(values):
    return [swap(values[offset - 1], offset % 2, 2 * (offset // 2)) for offset in range(1, 4)]


def sum_square(value):
    place = square_place()
    quarters = value.reshape(4, value.shape[0] // 4, value.shape[1])
    pick = [
        lax.dynamic_index_in_dim(quarters, place ^ offset, 0, keepdims=False) for offset in range(4)
    ]
    return pick[:1] + square_swaps(pick[1:])


def line_swaps(value):
    lines = lax.axis_size("dp") // 4
    return [swap(value, 0, 4 * offset) for offset in range(1, lines)]


def add(terms):
    value = terms[0].astype(F32)
    for term in terms[1:]:
        value = value + term.astype(F32)
    return value.astype(BF16)


def tie(*values):
    return lax.optimization_barrier(values)


def on_pair(
    hidden_in,
    lengths,
    w_query,
    w_key,
    w_value,
    w_output,
    attn_gain,
    ffn_in,
    ffn_out,
    ffn_gain,
    adapter_down,
    adapter_down_bias,
    adapter_up,
    adapter_up_bias,
    prefix_embed,
    prefix_hidden_w,
    prefix_hidden_b,
    prefix_out_w,
    prefix_out_b,
    out_grad,
):
    rows, _, width = hidden_in.shape
    count = prefix_embed.shape[0]
    position = lax.axis_index("seq")
    place = position.reshape(1).astype(jnp.int32)
    length = lax.dynamic_index_in_dim(lengths, position, 0, keepdims=False)
    scal = jnp.stack([position * rows, (1 - position) * rows, length]).astype(jnp.int32)

    x_own, x_send = split(place, hidden_in)
    x_other = shifted(x_send, "seq", 1)
    og_own, og_send = split(place, out_grad)
    og_other = shifted(og_send, "seq", 1)

    embed = jnp.pad(prefix_embed, ((0, PAD - count), (0, 0)))
    prefix_act, prefix_keys, prefix_values = prefix_forward(
        embed, prefix_hidden_w, prefix_hidden_b, prefix_out_w, prefix_out_b
    )
    lead = (prefix_keys, prefix_values)
    triple = project(0, x_own, w_query, w_key, w_value, ())
    q, k, _, _, vt = triple
    near = attend(count, scal, 0, 0, 1, q, k, vt, lead, ())
    q, k, kt, v, vt = project(1, x_other, w_query, w_key, w_value, triple)
    pt_own, ot_own, st_own, lead_weights = attend(count, scal, 0, 1, 1, q, k, vt, lead, near)
    pt_other, ot_other, st_other = attend(0, scal, 1, 0, 2, q, k, vt, (), ())

    (
        layer_out, shares, mix, slope, grad_low, norm_grad, normed, inv_one,
        adapt_grad, up_bias_grad, down_bias_grad,
    ) = front(
        scal, x_own, x_other, ot_own, ot_other, st_own, st_other, og_own, og_other,
        w_output, attn_gain, ffn_in, ffn_out, ffn_gain, adapter_down, adapter_down_bias,
        adapter_up, adapter_up_bias,
    )
    out_other = shifted(layer_out[rows:], "seq", 1)
    core_terms = sum_core(adapt_grad)
    grad_one, upstream, deltas = rear(
        grad_low, norm_grad, slope, normed, inv_one, mix, w_output, attn_gain, ffn_in, ffn_out
    )
    upstream, adapt_sum, out_other = tie(upstream, add(core_terms), out_other)
    square_terms = sum_square(adapt_sum)
    key_rows, value_rows, dqt = lead_backward(
        q, upstream, shares, deltas, lead_weights, prefix_keys, prefix_values
    )
    extra = jnp.concatenate(
        [
            jnp.pad(up_bias_grad, ((0, 0), (0, width))),
            jnp.pad(down_bias_grad, ((0, 0), (0, 2 * width - down_bias_grad.shape[1]))),
        ]
    )
    pair = jnp.concatenate([key_rows[:count], value_rows[:count]], axis=1)
    pair = jnp.concatenate([pair, extra]).astype(BF16)
    pair_core = swap(pair, 0, 1)

    back = (q, kt, v)
    part_own, dk_other, dv_other = attend_back(
        1, 0, False, False, *back, upstream, shares, deltas, pt_other, dqt, ()
    )
    dk_other, adapt_sum, pair = tie(dk_other, add(square_terms), add([pair, pair_core]))
    adapt_line = gather_line(adapt_sum)
    pair_square = square_swaps([pair] * 3)
    part_other, dk_other, dv_other = attend_back(
        1, 1, False, True, *back, upstream, shares, deltas, pt_other, dqt, (dk_other, dv_other)
    )
    part_other, pair = tie(part_other, add([pair] + pair_square))
    pair_line = line_swaps(pair)
    dqt_other, dk_own, dv_own = attend_back(
        0, 1, True, False, *back, upstream, shares, deltas, pt_own, part_other, ()
    )
    grad_other = input_grad(1, grad_one, dqt_other, dk_other, dv_other, w_query, w_key, w_value)
    grad_back = shifted(grad_other, "seq", 1)
    dk_own, adapt_sum = tie(dk_own, jnp.sum(adapt_line.astype(F32), axis=0).astype(BF16))
    adapt_square = square_swaps([adapt_sum] * 3)
    dqt_own, dk_own, dv_own = attend_back(
        0, 0, True, True, *back, upstream, shares, deltas, pt_own, part_own, (dk_own, dv_own)
    )
    adapt_half = jnp.stack([adapt_sum] + adapt_square)
    place_here = square_place()
    adapt_half = jnp.concatenate(
        [lax.dynamic_slice_in_dim(adapt_half, spot ^ place_here, 1, 0) for spot in range(4)]
    )
    dqt_own, adapt_half = tie(dqt_own, adapt_half)
    adapt_far = swap(adapt_half, 0, 1)
    grad_own = input_grad(0, grad_one, dqt_own, dk_own, dv_own, w_query, w_key, w_value)

    pair = pair.astype(F32) + sum(item.astype(F32) for item in pair_line)
    prefix_grads = prefix_backward(count, pair, prefix_act, embed, prefix_hidden_w, prefix_out_w)
    first = lax.axis_index("dp") % 2 == 0
    adapt_rows = adapt_grad.shape[0] // 2
    up_total = jnp.where(first, adapt_half, adapt_far).astype(F32).reshape(adapt_rows, width)
    down_total = jnp.where(first, adapt_far, adapt_half).astype(F32).reshape(adapt_rows, width)
    return (
        merge(place, layer_out, out_other),
        merge(place, grad_own, grad_back),
        down_total.T,
        pair[count + 1, : down_bias_grad.shape[1]],
        up_total,
        pair[count, :width],
        prefix_grads[0],
        prefix_grads[1],
        prefix_grads[2][0],
        prefix_grads[3],
        prefix_grads[4][0],
    )


def solution(mesh):
    in_specs = (
        P("seq", "dp", None),
        P("dp"),
        P(),
        P(),
        P(),
        P(),
        P(),
        P(),
        P(),
        P(),
        P(),
        P(),
        P(),
        P(),
        P(),
        P(),
        P(),
        P(),
        P(),
        P("seq", "dp", None),
    )
    out_specs = (
        P("seq", "dp", None),
        P("seq", "dp", None),
        P(),
        P(),
        P(),
        P(),
        P(),
        P(),
        P(),
        P(),
        P(),
    )
    pairs = mesh.shape["seq"] == 2 and mesh.shape["dp"] % 8 == 0

    def on_one(*arrays):
        step = on_pair if pairs and arrays[0].shape[1] == 2 else on_device
        return step(*arrays)

    return jax.shard_map(
        on_one, mesh=mesh, in_specs=in_specs, out_specs=out_specs, check_vma=False
    )
```

```python
import functools
import math

import jax
import jax.numpy as jnp
from jax import lax
from jax.experimental import pallas as pl
from jax.experimental.pallas import tpu as pltpu
from jax.sharding import PartitionSpec as P

HEADS = 16


HIGHEST_PRECISION = lax.Precision.HIGHEST


def shifted(value, axis, steps):
    count = lax.axis_size(axis)
    pairs = [(source, (source + steps) % count) for source in range(count)]
    return lax.ppermute(value, axis, pairs)


def mixed(left, right):
    return jnp.dot(left, right, preferred_element_type=jnp.float32)


def mixed_left(left, right):
    return lax.dot_general(
        left, right, (((0,), (0,)), ((), ())), preferred_element_type=jnp.float32
    )


def mixed_right(left, right):
    return lax.dot_general(
        left, right, (((1,), (1,)), ((), ())), preferred_element_type=jnp.float32
    )


def precise(left, right):
    return jnp.dot(left, right, precision=HIGHEST_PRECISION, preferred_element_type=jnp.float32)


def precise_left(left, right):
    return lax.dot_general(
        left,
        right,
        (((0,), (0,)), ((), ())),
        precision=HIGHEST_PRECISION,
        preferred_element_type=jnp.float32,
    )


def precise_right(left, right):
    return lax.dot_general(
        left,
        right,
        (((1,), (1,)), ((), ())),
        precision=HIGHEST_PRECISION,
        preferred_element_type=jnp.float32,
    )


def gelu_value(inputs):
    return 0.5 * inputs * (1.0 + lax.erf(inputs * 0.7071067811865476))


def gelu_slope(inputs):
    return (
        0.5 * (1.0 + lax.erf(inputs * 0.7071067811865476))
        + inputs * jnp.exp(-0.5 * inputs * inputs) * 0.3989422804014327
    )


def normalize(values):
    row_mean = jnp.mean(values, axis=-1, keepdims=True)
    centred = values - row_mean
    spread = jnp.mean(centred * centred, axis=-1, keepdims=True)
    inv_std = lax.rsqrt(spread + 1e-05)
    return (centred * inv_std, inv_std)


def norm_back(upstream, normed, inv_std):
    mean_grad = jnp.mean(upstream, axis=-1, keepdims=True)
    mean_proj = jnp.mean(upstream * normed, axis=-1, keepdims=True)
    return inv_std * (upstream - mean_grad - normed * mean_proj)


def key_allowed(offset, key_count, seq_lengths):
    places = offset + lax.iota(jnp.int32, key_count)
    return places[None, :] < seq_lengths[:, None]


def lead_state(queries4, prefix_keys4, prefix_values4):
    inv_root = 1.0 / math.sqrt(queries4.shape[3])
    scores = (
        jnp.einsum("rshd,phd->rshp", queries4, prefix_keys4, preferred_element_type=jnp.float32)
        * inv_root
    )
    running_max = jnp.max(scores, axis=3)
    weights = jnp.exp(scores - running_max[..., None])
    running_sum = jnp.sum(weights, axis=3)
    running_mix = jnp.einsum(
        "rshp,phd->rshd",
        weights.astype(jnp.bfloat16),
        prefix_values4,
        preferred_element_type=jnp.float32,
    )
    return (running_max, running_sum, running_mix)


def fold_block(carried, key_block, value_block, offset, queries4, seq_lengths):
    key_count, seqs_here = (key_block.shape[0], key_block.shape[1])
    head_count, head_dim = (queries4.shape[2], queries4.shape[3])
    inv_root = 1.0 / math.sqrt(head_dim)
    keys4 = key_block.reshape(key_count, seqs_here, head_count, head_dim)
    values4 = value_block.reshape(key_count, seqs_here, head_count, head_dim)
    running_max, running_sum, running_mix = carried
    scores = (
        jnp.einsum("rshd,tshd->rsht", queries4, keys4, preferred_element_type=jnp.float32)
        * inv_root
    )
    allowed = key_allowed(offset, key_count, seq_lengths)[None, :, None, :]
    scores = jnp.where(allowed, scores, -jnp.inf)
    new_max = jnp.maximum(running_max, jnp.max(scores, axis=3))
    weights = jnp.exp(scores - new_max[..., None])
    rescale = jnp.exp(running_max - new_max)
    running_sum = running_sum * rescale + jnp.sum(weights, axis=3)
    running_mix = running_mix * rescale[..., None] + jnp.einsum(
        "rsht,tshd->rshd", weights.astype(jnp.bfloat16), values4, preferred_element_type=jnp.float32
    )
    return (new_max, running_sum, running_mix)


def lead_back(queries4, upstream4, log_total, row_delta, prefix_keys4, prefix_values4):
    inv_root = 1.0 / math.sqrt(queries4.shape[3])
    scores = (
        jnp.einsum("rshd,phd->rshp", queries4, prefix_keys4, preferred_element_type=jnp.float32)
        * inv_root
    )
    weights = jnp.exp(scores - log_total[..., None])
    weight_grads = jnp.einsum(
        "rshd,phd->rshp", upstream4, prefix_values4, preferred_element_type=jnp.float32
    )
    score_grads = (weights * (weight_grads - row_delta[..., None])).astype(jnp.bfloat16)
    query_term = (
        jnp.einsum("rshp,phd->rshd", score_grads, prefix_keys4, preferred_element_type=jnp.float32)
        * inv_root
    )
    key_term = (
        jnp.einsum("rshp,rshd->phd", score_grads, queries4, preferred_element_type=jnp.float32)
        * inv_root
    )
    value_term = jnp.einsum(
        "rshp,rshd->phd",
        weights.astype(jnp.bfloat16),
        upstream4,
        preferred_element_type=jnp.float32,
    )
    return (query_term, key_term, value_term)


def block_back(
    queries4, upstream4, log_total, row_delta, key_block, value_block, offset, seq_lengths
):
    key_count, seqs_here, model_width = key_block.shape
    head_count, head_dim = (queries4.shape[2], queries4.shape[3])
    inv_root = 1.0 / math.sqrt(head_dim)
    keys4 = key_block.reshape(key_count, seqs_here, head_count, head_dim)
    values4 = value_block.reshape(key_count, seqs_here, head_count, head_dim)
    scores = (
        jnp.einsum("rshd,tshd->rsht", queries4, keys4, preferred_element_type=jnp.float32)
        * inv_root
    )
    allowed = key_allowed(offset, key_count, seq_lengths)[None, :, None, :]
    scores = jnp.where(allowed, scores, -jnp.inf)
    weights = jnp.exp(scores - log_total[..., None])
    weight_grads = jnp.einsum(
        "rshd,tshd->rsht", upstream4, values4, preferred_element_type=jnp.float32
    )
    score_grads = (weights * (weight_grads - row_delta[..., None])).astype(jnp.bfloat16)
    query_term = (
        jnp.einsum("rsht,tshd->rshd", score_grads, keys4, preferred_element_type=jnp.float32)
        * inv_root
    )
    key_term = (
        jnp.einsum("rsht,rshd->tshd", score_grads, queries4, preferred_element_type=jnp.float32)
        * inv_root
    )
    value_term = jnp.einsum(
        "rsht,rshd->tshd",
        weights.astype(jnp.bfloat16),
        upstream4,
        preferred_element_type=jnp.float32,
    )
    pair_term = jnp.stack(
        [
            key_term.reshape(key_count, seqs_here, model_width),
            value_term.reshape(key_count, seqs_here, model_width),
        ]
    )
    return (query_term, pair_term)


def prefix_back(pair_grad, prefix_act, prefix_embed, hidden_weight, out_weight):
    out_w_grad = precise_left(prefix_act, pair_grad)
    out_b_grad = jnp.sum(pair_grad, axis=0)
    act_grad = precise_right(pair_grad, out_weight) * (1.0 - prefix_act * prefix_act)
    hidden_w_grad = precise_left(prefix_embed, act_grad)
    hidden_b_grad = jnp.sum(act_grad, axis=0)
    embed_grad = precise_right(act_grad, hidden_weight)
    return (embed_grad, hidden_w_grad, hidden_b_grad, out_w_grad, out_b_grad)


def on_device(
    hidden_in,
    lengths,
    w_query,
    w_key,
    w_value,
    w_output,
    attn_gain,
    ffn_in,
    ffn_out,
    ffn_gain,
    adapter_down,
    adapter_down_bias,
    adapter_up,
    adapter_up_bias,
    prefix_embed,
    prefix_hidden_w,
    prefix_hidden_b,
    prefix_out_w,
    prefix_out_b,
    out_grad,
):
    rows_here, seqs_here, model_width = hidden_in.shape
    token_count = rows_here * seqs_here
    head_count = HEADS
    head_dim = model_width // head_count
    axis_count = lax.axis_size("seq")
    position = lax.axis_index("seq")
    tokens = hidden_in.reshape(token_count, model_width)
    projected = jnp.stack([mixed(tokens, w_query), mixed(tokens, w_key), mixed(tokens, w_value)])
    triple = projected.astype(jnp.bfloat16).reshape(3, rows_here, seqs_here, model_width)
    hidden_weight = prefix_hidden_w.astype(jnp.float32)
    out_weight = prefix_out_w.astype(jnp.float32)
    prefix_act = jnp.tanh(precise(prefix_embed, hidden_weight) + prefix_hidden_b)
    prefix_pair = precise(prefix_act, out_weight) + prefix_out_b
    prefix_keys4 = (
        prefix_pair[:, :model_width].astype(jnp.bfloat16).reshape(-1, head_count, head_dim)
    )
    prefix_values4 = (
        prefix_pair[:, model_width:].astype(jnp.bfloat16).reshape(-1, head_count, head_dim)
    )
    row_places = position * rows_here + lax.iota(jnp.int32, rows_here)
    valid = (row_places[:, None] < lengths[None, :]).astype(jnp.float32).reshape(token_count, 1)
    queries4 = triple[0].reshape(rows_here, seqs_here, head_count, head_dim)
    key_value = triple[1:]
    pieces = lax.all_gather(key_value, "seq", axis=1, tiled=True)
    carried = fold_block(
        lead_state(queries4, prefix_keys4, prefix_values4),
        pieces[0],
        pieces[1],
        jnp.int32(0),
        queries4,
        lengths,
    )
    mix_full = carried[2] / carried[1][..., None]
    log_total = carried[0] + jnp.log(carried[1])
    mix_low = mix_full.astype(jnp.bfloat16).reshape(token_count, model_width)
    attn_proj = mixed(mix_low, w_output)
    normed_one, inv_one = normalize(tokens.astype(jnp.float32) + attn_proj)
    norm_one = normed_one * attn_gain
    norm_low = norm_one.astype(jnp.bfloat16)
    inner_pre = mixed(norm_low, ffn_in)
    inner_act = gelu_value(inner_pre).astype(jnp.bfloat16)
    squeeze = mixed(norm_low, adapter_down) + adapter_down_bias
    squeeze_act = gelu_value(squeeze).astype(jnp.bfloat16)
    ffn_sum = mixed(inner_act, ffn_out)
    adapter_sum = mixed(squeeze_act, adapter_up) + adapter_up_bias
    normed_two, inv_two = normalize(norm_one + ffn_sum + 4.0 * adapter_sum)
    layer_out = (
        (normed_two * ffn_gain * valid)
        .astype(jnp.bfloat16)
        .reshape(rows_here, seqs_here, model_width)
    )
    upstream_top = out_grad.reshape(token_count, model_width).astype(jnp.float32) * valid
    grad_two = norm_back(upstream_top * ffn_gain, normed_two, inv_two)
    grad_ffn_low = grad_two.astype(jnp.bfloat16)
    grad_adapt_low = (4.0 * grad_two).astype(jnp.bfloat16)
    up_grad = mixed_left(squeeze_act, grad_adapt_low)
    up_bias_grad = jnp.sum(grad_adapt_low.astype(jnp.float32), axis=0)
    grad_squeeze_low = (mixed_right(grad_adapt_low, adapter_up) * gelu_slope(squeeze)).astype(
        jnp.bfloat16
    )
    down_grad = mixed_left(norm_low, grad_squeeze_low)
    down_bias_grad = jnp.sum(grad_squeeze_low.astype(jnp.float32), axis=0)
    grad_inner_low = (mixed_right(grad_ffn_low, ffn_out) * gelu_slope(inner_pre)).astype(
        jnp.bfloat16
    )
    grad_norm = (
        grad_two + mixed_right(grad_squeeze_low, adapter_down) + mixed_right(grad_inner_low, ffn_in)
    )
    grad_one = norm_back(grad_norm * attn_gain, normed_one, inv_one)
    grad_attn_low = grad_one.astype(jnp.bfloat16)
    grad_mix_low = mixed_right(grad_attn_low, w_output).astype(jnp.bfloat16)
    upstream4 = grad_mix_low.reshape(rows_here, seqs_here, head_count, head_dim)
    row_delta = jnp.sum(upstream4.astype(jnp.float32) * mix_full, axis=3)
    query_grad, prefix_key_grad, prefix_value_grad = lead_back(
        queries4, upstream4, log_total, row_delta, prefix_keys4, prefix_values4
    )

    def visit(step_index, carried):
        moving, grads_moving, query_total = carried
        source = (position - step_index) % axis_count
        query_term, pair_term = block_back(
            queries4,
            upstream4,
            log_total,
            row_delta,
            moving[0],
            moving[1],
            source * rows_here,
            lengths,
        )
        return (moving, grads_moving + pair_term, query_total + query_term)

    def travel(step_index, carried):
        moving, grads_moving, query_total = visit(step_index, carried)
        moving = shifted(moving, "seq", 1)
        grads_moving = shifted(grads_moving.astype(jnp.bfloat16), "seq", 1).astype(
            grads_moving.dtype
        )
        return (moving, grads_moving, query_total)

    initial = (
        key_value,
        jnp.zeros((2, rows_here, seqs_here, model_width), jnp.float32),
        query_grad,
    )
    carried = lax.fori_loop(0, axis_count - 1, travel, initial)
    carried = visit(axis_count - 1, carried)
    pair_grads = shifted(carried[1].astype(jnp.bfloat16), "seq", 1).astype(jnp.float32)
    triple_grad = jnp.concatenate(
        [carried[2].reshape(1, rows_here, seqs_here, model_width), pair_grads]
    ).astype(jnp.bfloat16)
    hidden_grad = grad_one + mixed_right(triple_grad[0].reshape(token_count, model_width), w_query)
    hidden_grad = hidden_grad + mixed_right(triple_grad[1].reshape(token_count, model_width), w_key)
    hidden_grad = hidden_grad + mixed_right(
        triple_grad[2].reshape(token_count, model_width), w_value
    )
    hidden_grad = hidden_grad.astype(jnp.bfloat16).reshape(rows_here, seqs_here, model_width)
    pair_grad = jnp.concatenate(
        [prefix_key_grad.reshape(-1, model_width), prefix_value_grad.reshape(-1, model_width)],
        axis=1,
    )
    prefix_grads = prefix_back(pair_grad, prefix_act, prefix_embed, hidden_weight, out_weight)
    summed = lax.psum(
        (
            down_grad,
            down_bias_grad,
            up_grad,
            up_bias_grad,
            prefix_grads[0],
            prefix_grads[1],
            prefix_grads[2],
            prefix_grads[3],
            prefix_grads[4],
        ),
        ("seq", "dp"),
    )
    adapter_totals = summed[:4]
    prefix_totals = summed[4:]
    return (
        layer_out,
        hidden_grad,
        adapter_totals[0],
        adapter_totals[1],
        adapter_totals[2],
        adapter_totals[3],
        prefix_totals[0],
        prefix_totals[1],
        prefix_totals[2],
        prefix_totals[3],
        prefix_totals[4],
    )


BF16 = jnp.bfloat16
F32 = jnp.float32
MIB = 1024 * 1024
GROUP = 4
HEAD_DIM = 64
LANES = GROUP * HEAD_DIM
PAD = 32
MASKED = -1e30
LOG2E = 1.4426950408889634
VMEM_LIMIT = 60 * MIB


def dot_nn(left, right):
    return lax.dot_general(left, right, (((1,), (0,)), ((), ())), preferred_element_type=F32)


def dot_nt(left, right):
    return lax.dot_general(left, right, (((1,), (1,)), ((), ())), preferred_element_type=F32)


def dot_tn(left, right):
    return lax.dot_general(left, right, (((0,), (0,)), ((), ())), preferred_element_type=F32)


def shape_of(shape, dtype):
    return jax.ShapeDtypeStruct(shape, dtype)


def params(limit=VMEM_LIMIT):
    return pltpu.CompilerParams(vmem_limit_bytes=limit)


def cost(macs, moved):
    return pl.CostEstimate(flops=int(2 * macs), bytes_accessed=int(moved), transcendentals=0)


SMEM_SPEC = pl.BlockSpec(memory_space=pltpu.SMEM)
ANY_SPEC = pl.BlockSpec(memory_space=pl.ANY)


def whole(shape):
    return pl.BlockSpec(shape, lambda *_: (0,) * len(shape))


def kept(shape):
    return pl.BlockSpec(shape, lambda *_: (0,) * len(shape), pipeline_mode=pl.Buffered(1))


def split_kernel(place_ref, both_ref, own_ref, other_ref):
    apart = jnp.swapaxes(both_ref[...], 0, 1)
    first = place_ref[0] == 0
    own_ref[...] = jnp.where(first, apart[0], apart[1])
    other_ref[...] = jnp.where(first, apart[1], apart[0])


def split(place, both):
    rows, _, width = both.shape
    step = rows // 4
    half = pl.BlockSpec((step, width), lambda i: (i, 0))
    return pl.pallas_call(
        split_kernel,
        grid=(4,),
        in_specs=[SMEM_SPEC, pl.BlockSpec((step, 2, width), lambda i: (i, 0, 0))],
        out_specs=[half, half],
        out_shape=[shape_of((rows, width), both.dtype)] * 2,
        cost_estimate=cost(0, 4 * rows * width * 2),
    )(place, both)


def merge_kernel(place_ref, own_ref, other_ref, both_ref):
    first = place_ref[0] == 0
    own, other = own_ref[...], other_ref[...]
    apart = jnp.stack([jnp.where(first, own, other), jnp.where(first, other, own)])
    both_ref[...] = jnp.swapaxes(apart, 0, 1)


def merge(place, own, other):
    rows, width = other.shape
    step = rows // 4
    half = pl.BlockSpec((step, width), lambda i: (i, 0))
    return pl.pallas_call(
        merge_kernel,
        grid=(4,),
        in_specs=[SMEM_SPEC, half, half],
        out_specs=pl.BlockSpec((step, 2, width), lambda i: (i, 0, 0)),
        out_shape=shape_of((rows, 2, width), other.dtype),
        cost_estimate=cost(0, 4 * rows * width * 2),
    )(place, own, other)


def parts_of(values, count):
    parts = []
    for _ in range(count):
        part = values.astype(BF16)
        parts.append(part)
        values = values - part.astype(F32)
    return parts


def exact_dot(values, weight, dot):
    rows = values.shape[0]
    product = dot(jnp.concatenate(parts_of(values, 3), axis=0), weight)
    return product[:rows] + product[rows : 2 * rows] + product[2 * rows :]


def prefix_kernel(embed_ref, hw_ref, hb_ref, ow_ref, ob_ref, act_ref, key_ref, value_ref):
    width = key_ref.shape[1]
    act = jnp.tanh(exact_dot(embed_ref[...], hw_ref[...], dot_nn) + hb_ref[...])
    act_ref[...] = act
    pair = exact_dot(act, ow_ref[...], dot_nn) + ob_ref[...]
    key_ref[...] = pair[:, :width].astype(BF16)
    value_ref[...] = pair[:, width:].astype(BF16)


def prefix_forward(embed, hidden_w, hidden_b, out_w, out_b):
    width, hidden = hidden_w.shape
    return pl.pallas_call(
        prefix_kernel,
        out_shape=[
            shape_of((PAD, hidden), F32),
            shape_of((PAD, width), BF16),
            shape_of((PAD, width), BF16),
        ],
        compiler_params=params(),
        cost_estimate=cost(3 * PAD * hidden * 3 * width * 4, 6 * hidden * width),
    )(embed, hidden_w, hidden_b[None], out_w, out_b[None])


def prefix_back_kernel(
    count, pair_ref, act_ref, embed_ref, hw_ref, ow_ref, eg_ref, hwg_ref, hbg_ref, owg_ref, obg_ref
):
    pair = pair_ref[...]
    rows = lax.broadcasted_iota(jnp.int32, pair.shape, 0)
    pair = jnp.where(rows < count, pair, 0.0)
    act = act_ref[...]
    obg_ref[...] = jnp.sum(pair, axis=0, keepdims=True)
    high, low = parts_of(pair, 2)
    back = dot_nt(jnp.concatenate([high, low], axis=0), ow_ref[...])
    act_grad = (back[:PAD] + back[PAD:]) * (1.0 - act * act)
    act_high, act_low = parts_of(act, 2)
    owg_ref[...] = dot_tn(
        jnp.concatenate([act_high, act_low, act_high], axis=0),
        jnp.concatenate([high, high, low], axis=0),
    )
    hbg_ref[...] = jnp.sum(act_grad, axis=0, keepdims=True)
    high, low = parts_of(act_grad, 2)
    embed_high, embed_low = parts_of(embed_ref[...], 2)
    hwg_ref[...] = dot_tn(
        jnp.concatenate([embed_high, embed_low, embed_high], axis=0),
        jnp.concatenate([high, high, low], axis=0),
    )
    back = dot_nt(jnp.concatenate([high, low], axis=0), hw_ref[...])
    eg_ref[...] = (back[:PAD] + back[PAD:])[:count]


def prefix_backward(count, pair, act, embed, hidden_w, out_w):
    width, hidden = hidden_w.shape
    return pl.pallas_call(
        functools.partial(prefix_back_kernel, count),
        out_shape=[
            shape_of((count, width), F32),
            shape_of((width, hidden), F32),
            shape_of((1, hidden), F32),
            shape_of((hidden, 2 * width), F32),
            shape_of((1, 2 * width), F32),
        ],
        compiler_params=params(),
        cost_estimate=cost(96 * hidden * width * 6, 20 * hidden * width),
    )(pair, act, embed, hidden_w, out_w)


def project_kernel(x_ref, wq_ref, wk_ref, wv_ref, *refs):
    q_ref, k_ref, v_ref = refs[-3:]
    x = x_ref[...]
    scale = LOG2E / math.sqrt(HEAD_DIM)
    q_ref[...] = (dot_nn(x, wq_ref[...]) * scale).astype(BF16)
    k_ref[...] = dot_nn(x, wk_ref[...]).astype(BF16)
    v_ref[...] = dot_nn(x, wv_ref[...]).astype(BF16)


def project(half, x, w_query, w_key, w_value, earlier):
    rows, width = x.shape
    step = 256
    weight = pl.BlockSpec((width, step), lambda j: (0, j))
    return pl.pallas_call(
        project_kernel,
        grid=(width // step,),
        in_specs=[whole((rows, width)), weight, weight, weight] + [ANY_SPEC] * len(earlier),
        out_specs=[pl.BlockSpec((rows, step), lambda j: (half, j))] * 3,
        out_shape=[shape_of((2 * rows, width), BF16)] * 3,
        input_output_aliases={4 + i: i for i in range(len(earlier))},
        compiler_params=params(),
        cost_estimate=cost(3 * rows * width * width, 2 * (4 * rows * width + 3 * width * width)),
    )(x, w_query, w_key, w_value, *earlier)


def head_lanes(head, rows, lanes):
    place = lax.broadcasted_iota(jnp.int32, (rows, lanes), 1)
    return (place // HEAD_DIM == head).astype(F32).astype(BF16)


def first_lane(values):
    lane = lax.broadcasted_iota(jnp.int32, (values.shape[0], 128), 1)
    return jnp.where(lane == 0, values, 0.0).astype(BF16)


def block_diagonal(rows):
    return jnp.concatenate(
        [rows * head_lanes(head, rows.shape[0], LANES) for head in range(GROUP)], axis=0
    )


def attend_kernel(count, half, scal_ref, q_ref, k_ref, v_ref, *refs):
    keys = k_ref.shape[0]
    queries = q_ref.shape[0]
    scores = refs[-2:]
    refs = refs[:-2]
    if count:
        pk_ref, pv_ref = refs[:2]
        pt_ref, ot_ref, st_ref, pp_ref = refs[-4:]
    else:
        pt_ref, ot_ref, st_ref = refs[-3:]
    place = scal_ref[half] + lax.broadcasted_iota(jnp.int32, (keys, 128), 0)
    bias = first_lane(jnp.where(place < scal_ref[2], 0.0, MASKED))
    ones = first_lane(jnp.ones((queries, 128), F32))
    tail = jnp.ones((16, keys), BF16)
    masks = [head_lanes(head, queries, 128) for head in range(2)]

    def score(head):
        pair = slice((head // 2) * 128, (head // 2 + 1) * 128)
        k_aug = jnp.concatenate([k_ref[:, pair], bias], axis=1)
        q_aug = jnp.concatenate([q_ref[:, pair] * masks[head % 2], ones], axis=1)
        scores[head % 2][...] = dot_nt(k_aug, q_aug)

    def weigh(head):
        own = scores[head % 2]
        top = jnp.max(own[...], axis=0, keepdims=True)
        if count:
            lead_scores = lead[head * PAD : (head + 1) * PAD]
            top = jnp.maximum(top, jnp.max(lead_scores, axis=0, keepdims=True))
        pt_ref[head] = jnp.exp2(own[...] - top).astype(BF16)
        st_ref[0, head : head + 1, :] = top
        if not count:
            return 0.0
        lead_weights = jnp.exp2(lead_scores - top).astype(BF16)
        pp_ref[0, head * PAD : (head + 1) * PAD, :] = lead_weights
        return jnp.sum(lead_weights.astype(F32), axis=0, keepdims=True)

    def mix(head, lead_total):
        rows = slice(head * HEAD_DIM, (head + 1) * HEAD_DIM)
        mixed_rows = dot_nn(jnp.concatenate([turned[rows], tail], axis=0), pt_ref[head])
        ot_ref[rows, :] = mixed_rows[:HEAD_DIM]
        total_row = mixed_rows[HEAD_DIM : HEAD_DIM + 1] + lead_total
        st_ref[0, GROUP + head : GROUP + head + 1, :] = total_row

    score(0)
    turned = v_ref[...].T
    if count:
        lead = dot_nt(block_diagonal(pk_ref[...]), q_ref[...])
        row = lax.broadcasted_iota(jnp.int32, lead.shape, 0)
        lead = jnp.where(row % PAD < count, lead, MASKED)
    lead_totals = []
    for head in range(GROUP):
        if head + 1 < GROUP:
            score(head + 1)
        lead_totals.append(weigh(head))
        if head:
            mix(head - 1, lead_totals[head - 1])
    mix(GROUP - 1, lead_totals[GROUP - 1])
    if count:
        ot_ref[...] += dot_tn(block_diagonal(pv_ref[...]), pp_ref[0])


def attend(count, scal, key_half, query_first, query_blocks, q, k, v, lead, earlier):
    tokens, width = q.shape
    rows = tokens // 2
    groups = width // LANES
    in_specs = [
        SMEM_SPEC,
        pl.BlockSpec((rows, LANES), lambda i, g: (i + query_first, g)),
        pl.BlockSpec((rows, LANES), lambda i, g: (key_half, g)),
        pl.BlockSpec((rows, LANES), lambda i, g: (key_half, g)),
    ]
    in_specs += [pl.BlockSpec((PAD, LANES), lambda i, g: (0, g))] * len(lead)
    out_specs = [
        pl.BlockSpec((GROUP, rows, rows), lambda i, g: (g, 0, i + query_first)),
        pl.BlockSpec((LANES, rows), lambda i, g: (g, i + query_first)),
        pl.BlockSpec((1, 2 * GROUP, rows), lambda i, g: (g, 0, i + query_first)),
    ]
    out_shape = [
        shape_of((groups * GROUP, rows, tokens), BF16),
        shape_of((width, tokens), F32),
        shape_of((groups, 2 * GROUP, tokens), F32),
    ]
    if count:
        out_specs.append(pl.BlockSpec((1, GROUP * PAD, rows), lambda i, g: (g, 0, i + query_first)))
        out_shape.append(shape_of((groups, GROUP * PAD, tokens), BF16))
    start = len(in_specs)
    macs = query_blocks * groups * GROUP * rows * rows * 256 * 2
    return pl.pallas_call(
        functools.partial(attend_kernel, count, key_half),
        grid=(query_blocks, groups),
        in_specs=in_specs + [ANY_SPEC] * len(earlier),
        out_specs=out_specs,
        out_shape=out_shape,
        input_output_aliases={start + i: i for i in range(len(earlier))},
        scratch_shapes=[pltpu.VMEM((rows, rows), F32)] * 2,
        compiler_params=params(),
        cost_estimate=cost(macs, query_blocks * 24 * MIB),
    )(scal, q, k, v, *lead, *earlier)


def lead_back_kernel(q_ref, up_ref, rst_ref, del_ref, pp_ref, pk_ref, pv_ref, kg_ref, vg_ref, dqt_ref):
    queries = q_ref.shape[0]
    ups = []
    deltas = []
    for head in range(GROUP):
        rows = slice(head * HEAD_DIM, (head + 1) * HEAD_DIM)
        share = rst_ref[0, head : head + 1, :]
        ups.append((up_ref[rows, :].astype(F32) * share).astype(BF16))
        delta = del_ref[0, head : head + 1, :] * share
        deltas.append(jnp.broadcast_to(delta, (PAD, queries)))
    up = jnp.concatenate(ups, axis=0)
    delta = jnp.concatenate(deltas, axis=0)
    weights = pp_ref[0]
    key_diagonal = block_diagonal(pk_ref[...])
    value_diagonal = block_diagonal(pv_ref[...])
    weight_grads = dot_nn(value_diagonal, up)
    score_grads = (weights.astype(F32) * (weight_grads - delta)).astype(BF16)
    dqt_ref[...] = dot_tn(key_diagonal, score_grads)
    key_grads = dot_nn(score_grads, q_ref[...]) * (1.0 / LOG2E)
    value_grads = dot_nt(weights, up)
    lane = lax.broadcasted_iota(jnp.int32, (PAD, LANES), 1) // HEAD_DIM
    key_total = jnp.zeros((PAD, LANES), F32)
    value_total = jnp.zeros((PAD, LANES), F32)
    for head in range(GROUP):
        rows = slice(head * PAD, (head + 1) * PAD)
        key_total = jnp.where(lane == head, key_grads[rows], key_total)
        value_total = jnp.where(lane == head, value_grads[rows], value_total)
    kg_ref[...] = key_total
    vg_ref[...] = value_total


def lead_backward(q, up, shares, deltas, lead_weights, prefix_keys, prefix_values):
    tokens, width = q.shape
    groups = width // LANES
    small = pl.BlockSpec((PAD, LANES), lambda g: (0, g))
    stats = pl.BlockSpec((1, 2 * GROUP, tokens), lambda g: (g, 0, 0))
    return pl.pallas_call(
        lead_back_kernel,
        grid=(groups,),
        in_specs=[
            pl.BlockSpec((tokens, LANES), lambda g: (0, g)),
            pl.BlockSpec((LANES, tokens), lambda g: (g, 0)),
            stats,
            stats,
            pl.BlockSpec((1, GROUP * PAD, tokens), lambda g: (g, 0, 0)),
            small,
            small,
        ],
        out_specs=[small, small, pl.BlockSpec((LANES, tokens), lambda g: (g, 0))],
        out_shape=[
            shape_of((PAD, width), F32),
            shape_of((PAD, width), F32),
            shape_of((width, tokens), F32),
        ],
        compiler_params=params(),
        cost_estimate=cost(groups * 4 * GROUP * PAD * tokens * LANES, 10 * MIB),
    )(q, up, shares, deltas, lead_weights, prefix_keys, prefix_values)


def attend_back_kernel(
    half,
    has_earlier,
    q_ref,
    k_ref,
    v_ref,
    up_ref,
    rst_ref,
    del_ref,
    pt_ref,
    dqt_in_ref,
    *refs,
):
    dq_ref, dk_ref, dv_ref = refs[-5:-2]
    weight_grads = refs[-2:]
    queries = q_ref.shape[0]
    lane = lax.broadcasted_iota(jnp.int32, (queries, 128), 1) // HEAD_DIM
    masks = [(lane == head).astype(F32).astype(BF16) for head in range(2)]
    zeros = jnp.zeros((HEAD_DIM, queries), BF16)
    turned = k_ref[...].T
    ups = {}
    grads = {}
    query_grads = []
    key_grads = []
    value_grads = []

    def pair_of(head):
        return slice((head // 2) * 128, (head // 2 + 1) * 128)

    def rows_of(head):
        return slice(head * HEAD_DIM, (head + 1) * HEAD_DIM)

    def share_of(head):
        return rst_ref[0, half * GROUP + head : half * GROUP + head + 1, :]

    def weight_grad(head):
        up = (up_ref[rows_of(head), :].astype(F32) * share_of(head)).astype(BF16)
        ups[head] = jnp.concatenate([up, zeros] if head % 2 == 0 else [zeros, up], axis=0)
        weight_grads[head % 2][...] = dot_nn(v_ref[:, pair_of(head)], ups[head])

    def score_grad(head):
        delta = del_ref[0, head : head + 1, :] * share_of(head)
        return (pt_ref[head].astype(F32) * (weight_grads[head % 2][...] - delta)).astype(BF16)

    def value_term(head):
        return dot_nt(pt_ref[head], ups[head])

    def key_term(head):
        return dot_nn(grads[head], q_ref[:, pair_of(head)] * masks[head % 2])

    def query_term(head):
        return dqt_in_ref[rows_of(head), :] + dot_nn(turned[rows_of(head)], grads[head])

    weight_grad(0)
    for head in range(GROUP):
        if head + 1 < GROUP:
            weight_grad(head + 1)
        grads[head] = score_grad(head)
        value = value_term(head)
        query_grads.append(query_term(head))
        key = key_term(head)
        if head % 2:
            key_grads[-1] = key_grads[-1] + key
            value_grads[-1] = value_grads[-1] + value
        else:
            key_grads.append(key)
            value_grads.append(value)
    query_grad = jnp.concatenate(query_grads, axis=0)
    key_grad = jnp.concatenate(key_grads, axis=1)
    value_grad = jnp.concatenate(value_grads, axis=1)
    if dq_ref.dtype == F32:
        dq_ref[...] = query_grad
    else:
        dq_ref[...] = (query_grad * (1.0 / math.sqrt(HEAD_DIM))).astype(BF16).T
    if has_earlier:
        key_grad = key_grad + refs[0][...]
        value_grad = value_grad + refs[1][...]
    if dk_ref.dtype == F32:
        dk_ref[...] = key_grad
        dv_ref[...] = value_grad
    else:
        dk_ref[...] = (key_grad * (1.0 / LOG2E)).astype(BF16)
        dv_ref[...] = value_grad.astype(BF16)


def attend_back(
    key_half, query_half, last_keys, last_queries, q, k, v, up, shares, deltas, weights, dqt, earlier
):
    tokens, width = q.shape
    rows = tokens // 2
    groups = width // LANES
    query_columns = pl.BlockSpec((LANES, rows), lambda g: (g, query_half))
    stats = pl.BlockSpec((1, 2 * GROUP, rows), lambda g: (g, 0, query_half))
    finished = pl.BlockSpec((rows, LANES), lambda g: (0, g))
    out_columns = pl.BlockSpec((LANES, rows), lambda g: (g, 0))
    sofar = query_columns if dqt.shape[1] == tokens else out_columns
    macs = groups * GROUP * rows * rows * 256 * 4
    grads_type = BF16 if last_queries else F32
    return pl.pallas_call(
        functools.partial(attend_back_kernel, key_half, len(earlier) > 0),
        grid=(groups,),
        in_specs=[
            pl.BlockSpec((rows, LANES), lambda g: (query_half, g)),
            pl.BlockSpec((rows, LANES), lambda g: (key_half, g)),
            pl.BlockSpec((rows, LANES), lambda g: (key_half, g)),
            query_columns,
            stats,
            stats,
            pl.BlockSpec((GROUP, rows, rows), lambda g: (g, 0, query_half)),
            sofar,
        ]
        + [finished] * len(earlier),
        out_specs=[finished if last_keys else out_columns, finished, finished],
        out_shape=[
            shape_of((rows, width), BF16) if last_keys else shape_of((width, rows), F32),
            shape_of((rows, width), grads_type),
            shape_of((rows, width), grads_type),
        ],
        scratch_shapes=[pltpu.VMEM((rows, rows), F32)] * 2,
        compiler_params=params(),
        cost_estimate=cost(macs, 12 * MIB),
    )(q, k, v, up, shares, deltas, weights, dqt, *earlier)


def gelu_pair(values):
    scaled = values * 0.7071067811865476
    below = 0.5 * lax.erf(scaled) + 0.5
    decay = jnp.exp2(scaled * scaled * (-LOG2E))
    return values * below, below + values * 0.3989422804014327 * decay


def row_mean(values):
    return jnp.mean(values, axis=-1, keepdims=True)


def weight_stream(pairs, sems, begin, ahead=99):
    copies = [
        pltpu.make_async_copy(source, target, sems.at[place])
        for place, (source, target) in enumerate(pairs)
    ]
    waited = [0]

    @pl.when(begin)
    def _():
        for copy in copies[:ahead]:
            copy.start()

    def arrive(count):
        first = waited[0]
        waited[0] += count

        @pl.when(begin)
        def _():
            for place in range(first, first + count):
                copies[place].wait()
                if place + ahead < len(copies):
                    copies[place + ahead].start()

    return arrive


def front_kernel(
    tiles,
    scal_ref,
    x_own_ref,
    x_other_ref,
    ot_own_ref,
    ot_other_ref,
    st_own_ref,
    st_other_ref,
    og_own_ref,
    og_other_ref,
    gain_one_ref,
    gain_two_ref,
    down_bias_ref,
    up_bias_ref,
    wo_hbm,
    fin_hbm,
    fout_hbm,
    down_hbm,
    up_hbm,
    out_own_ref,
    out_other_ref,
    rst_ref,
    mix_ref,
    slope_ref,
    grad_low_ref,
    norm_grad_ref,
    normed_ref,
    inv_ref,
    kept_ref,
    sent_ref,
    up_bias_grad_ref,
    down_bias_grad_ref,
    wo_ref,
    fin_ref,
    fout_ref,
    down_ref,
    up_ref,
    up_sum_ref,
    down_sum_ref,
    sems,
):
    step = pl.program_id(0)
    tile = x_own_ref.shape[0]
    width = x_own_ref.shape[1]
    hidden = fin_ref.shape[1]
    chunk = 1024
    chunks = [slice(first, first + chunk) for first in range(0, hidden, chunk)]
    pairs = [(wo_hbm, wo_ref), (down_hbm, down_ref), (fin_hbm.at[:, chunks[0]], fin_ref.at[:, chunks[0]]), (up_hbm, up_ref)]
    for place, columns in enumerate(chunks):
        for later in chunks[place + 1 : place + 2]:
            pairs.append((fin_hbm.at[:, later], fin_ref.at[:, later]))
        pairs.append((fout_hbm.at[columns], fout_ref.at[columns]))
    arrive = weight_stream(pairs, sems, step == 0)

    own = step < tiles // 2
    x = jnp.where(own, x_own_ref[...], x_other_ref[...]).astype(F32)
    top_own, top_other = st_own_ref[:, :GROUP, :], st_other_ref[:, :GROUP, :]
    top = jnp.maximum(top_own, top_other)
    share_own, share_other = jnp.exp2(top_own - top), jnp.exp2(top_other - top)
    inverse = 1.0 / (
        st_own_ref[:, GROUP:, :] * share_own + st_other_ref[:, GROUP:, :] * share_other
    )
    rst_ref[:, :GROUP, :] = share_own * inverse
    rst_ref[:, GROUP:, :] = share_other * inverse
    mixes = []
    for head in range(width // HEAD_DIM):
        rows = slice(head * HEAD_DIM, (head + 1) * HEAD_DIM)
        group, place = head // GROUP, head % GROUP
        mixes.append(
            (
                ot_own_ref[rows, :] * rst_ref[group, place : place + 1, :]
                + ot_other_ref[rows, :] * rst_ref[group, GROUP + place : GROUP + place + 1, :]
            ).astype(BF16)
        )
    mix = jnp.concatenate(mixes, axis=0)
    mix_ref[...] = mix
    arrive(1)
    resid_one = x + dot_tn(mix, wo_ref[...])
    centred = resid_one - row_mean(resid_one)
    inv_one = lax.rsqrt(row_mean(centred * centred) + 1e-05)
    normed = centred * inv_one
    normed_ref[...] = normed.astype(BF16)
    inv_ref[...] = inv_one
    norm_one = normed * gain_one_ref[...]
    norm_low = norm_one.astype(BF16)

    arrive(2)
    squeeze = dot_nn(norm_low, down_ref[...]) + down_bias_ref[...]
    inner = dot_nn(norm_low, fin_ref[:, chunks[0]])
    arrive(1)
    squeeze_act, squeeze_slope = gelu_pair(squeeze)
    squeeze_act = squeeze_act.astype(BF16)
    resid_two = norm_one + 4.0 * (dot_nn(squeeze_act, up_ref[...]) + up_bias_ref[...])
    for place, columns in enumerate(chunks):
        more = place + 1 < len(chunks)
        arrive(2 if more else 1)
        coming = dot_nn(norm_low, fin_ref[:, chunks[place + 1]]) if more else None
        act, slope = gelu_pair(inner)
        slope_ref[:, columns] = slope.astype(BF16)
        resid_two = resid_two + dot_nn(act.astype(BF16), fout_ref[columns, :])
        inner = coming

    centred = resid_two - row_mean(resid_two)
    inv_two = lax.rsqrt(row_mean(centred * centred) + 1e-05)
    normed_two = centred * inv_two
    base = jnp.where(own, scal_ref[0], scal_ref[1] - (tiles // 2) * tile) + step * tile
    place = base + lax.broadcasted_iota(jnp.int32, (tile, 1), 0)
    valid = (place < scal_ref[2]).astype(F32)
    gain_two = gain_two_ref[...]
    out = (normed_two * gain_two * valid).astype(BF16)
    upstream = jnp.where(own, og_own_ref[...], og_other_ref[...]).astype(F32) * valid * gain_two
    grad_two = inv_two * (
        upstream - row_mean(upstream) - normed_two * row_mean(upstream * normed_two)
    )
    grad_low_ref[...] = grad_two.astype(BF16)
    grad_adapt = (4.0 * grad_two).astype(BF16)
    grad_squeeze = (dot_nt(grad_adapt, up_ref[...]) * squeeze_slope).astype(BF16)
    norm_grad_ref[...] = grad_two + dot_nt(grad_squeeze, down_ref[...])
    up_grad = dot_tn(squeeze_act, grad_adapt)
    down_grad = dot_tn(grad_squeeze, norm_low)
    up_bias_grad = jnp.sum(grad_adapt.astype(F32), axis=0, keepdims=True)
    down_bias_grad = jnp.sum(grad_squeeze.astype(F32), axis=0, keepdims=True)

    @pl.when(own)
    def _():
        out_own_ref[...] = out

    @pl.when(jnp.logical_not(own))
    def _():
        out_other_ref[...] = out

    @pl.when(step == 0)
    def _():
        up_sum_ref[...] = up_grad
        down_sum_ref[...] = down_grad
        up_bias_grad_ref[...] = up_bias_grad
        down_bias_grad_ref[...] = down_bias_grad

    @pl.when(step > 0)
    def _():
        up_sum_ref[...] += up_grad
        down_sum_ref[...] += down_grad
        up_bias_grad_ref[...] += up_bias_grad
        down_bias_grad_ref[...] += down_bias_grad

    @pl.when(step == tiles - 1)
    def _():
        first = scal_ref[3] == 0
        up_total, down_total = up_sum_ref[...].astype(BF16), down_sum_ref[...].astype(BF16)
        kept_ref[...] = jnp.where(first, up_total, down_total)
        sent_ref[...] = jnp.where(first, down_total, up_total)


def front(
    scal, x_own, x_other, ot_own, ot_other, st_own, st_other, og_own, og_other,
    w_output, attn_gain, ffn_in, ffn_out, ffn_gain, down, down_bias, up, up_bias,
):
    rows, width = x_own.shape
    tokens = 2 * rows
    hidden = ffn_in.shape[1]
    adapt = down.shape[1]
    groups = width // LANES
    tile = 256
    tiles = tokens // tile
    near = pl.BlockSpec((tile, width), lambda i: (jnp.minimum(i, tiles // 2 - 1), 0))
    far = pl.BlockSpec((tile, width), lambda i: (jnp.maximum(i - tiles // 2, 0), 0))
    row_block = pl.BlockSpec((tile, width), lambda i: (i, 0))
    column_block = pl.BlockSpec((width, tile), lambda i: (0, i))
    stats = pl.BlockSpec((groups, 2 * GROUP, tile), lambda i: (0, 0, i))
    return pl.pallas_call(
        functools.partial(front_kernel, tiles),
        grid=(tiles,),
        in_specs=[
            SMEM_SPEC, near, far, column_block, column_block, stats, stats, near, far,
            whole((1, width)), whole((1, width)), whole((1, adapt)), whole((1, width)),
        ] + [ANY_SPEC] * 5,
        out_specs=[
            near, far, stats, column_block, pl.BlockSpec((tile, hidden), lambda i: (i, 0)),
            row_block, row_block, row_block, pl.BlockSpec((tile, 1), lambda i: (i, 0)),
            whole((adapt, width)), whole((adapt, width)), whole((1, width)), whole((1, adapt)),
        ],
        out_shape=[
            shape_of((rows, width), BF16),
            shape_of((rows, width), BF16),
            shape_of((groups, 2 * GROUP, tokens), F32),
            shape_of((width, tokens), BF16),
            shape_of((tokens, hidden), BF16),
            shape_of((tokens, width), BF16),
            shape_of((tokens, width), F32),
            shape_of((tokens, width), BF16),
            shape_of((tokens, 1), F32),
            shape_of((adapt, width), BF16),
            shape_of((adapt, width), BF16),
            shape_of((1, width), F32),
            shape_of((1, adapt), F32),
        ],
        scratch_shapes=[
            pltpu.VMEM((width, width), BF16),
            pltpu.VMEM((width, hidden), BF16),
            pltpu.VMEM((hidden, width), BF16),
            pltpu.VMEM((width, adapt), BF16),
            pltpu.VMEM((adapt, width), BF16),
            pltpu.VMEM((adapt, width), F32),
            pltpu.VMEM((adapt, width), F32),
            pltpu.SemaphoreType.DMA((3 + 2 * (hidden // 1024),)),
        ],
        compiler_params=params(),
        cost_estimate=cost(tokens * width * (width + 2 * hidden + 6 * adapt), 60 * MIB),
    )(
        scal, x_own, x_other, ot_own, ot_other, st_own, st_other, og_own, og_other,
        attn_gain[None], ffn_gain[None], down_bias[None], up_bias[None],
        w_output, ffn_in, ffn_out, down, up,
    )


def rear_kernel(
    grad_low_ref, norm_grad_ref, slope_ref, normed_ref, inv_ref, mix_ref, gain_ref, wo_hbm, fin_hbm,
    fout_hbm, grad_one_ref, up_ref, del_ref, wo_ref, fin_ref, fout_ref, sems,
):
    step = pl.program_id(0)
    hidden = fin_ref.shape[1]
    chunk = 1024
    chunks = [slice(first, first + chunk) for first in range(0, hidden, chunk)]
    pairs = []
    for columns in chunks:
        pairs.append((fout_hbm.at[columns], fout_ref.at[columns]))
        pairs.append((fin_hbm.at[:, columns], fin_ref.at[:, columns]))
    pairs.append((wo_hbm, wo_ref))
    arrive = weight_stream(pairs, sems, step == 0)

    grad_low = grad_low_ref[...]
    grad_norm = norm_grad_ref[...]
    arrive(1)
    inner = dot_nt(grad_low, fout_ref[chunks[0], :])
    for place, columns in enumerate(chunks):
        more = place + 1 < len(chunks)
        arrive(2 if more else 1)
        coming = dot_nt(grad_low, fout_ref[chunks[place + 1], :]) if more else None
        low = (inner * slope_ref[:, columns].astype(F32)).astype(BF16)
        grad_norm = grad_norm + dot_nt(low, fin_ref[:, columns])
        inner = coming
    grad = grad_norm * gain_ref[...]
    normed = normed_ref[...].astype(F32)
    grad_one = inv_ref[...] * (grad - row_mean(grad) - normed * row_mean(grad * normed))
    grad_one_ref[...] = grad_one
    arrive(1)
    up = dot_nt(wo_ref[...], grad_one.astype(BF16)).astype(BF16)
    up_ref[...] = up
    product = up.astype(F32) * mix_ref[...].astype(F32)
    for head in range(product.shape[0] // HEAD_DIM):
        rows = slice(head * HEAD_DIM, (head + 1) * HEAD_DIM)
        group, place = head // GROUP, head % GROUP
        del_ref[group, place : place + 1, :] = jnp.sum(product[rows], axis=0, keepdims=True)
    del_ref[:, GROUP:, :] = jnp.zeros_like(del_ref[:, GROUP:, :])


def rear(grad_low, norm_grad, slope, normed, inv, mix, w_output, attn_gain, ffn_in, ffn_out):
    tokens, width = grad_low.shape
    hidden = ffn_in.shape[1]
    groups = width // LANES
    tile = 256
    row_block = pl.BlockSpec((tile, width), lambda i: (i, 0))
    column_block = pl.BlockSpec((width, tile), lambda i: (0, i))
    return pl.pallas_call(
        rear_kernel,
        grid=(tokens // tile,),
        in_specs=[
            row_block, row_block, pl.BlockSpec((tile, hidden), lambda i: (i, 0)), row_block,
            pl.BlockSpec((tile, 1), lambda i: (i, 0)), column_block, whole((1, width)),
        ] + [ANY_SPEC] * 3,
        out_specs=[
            row_block, column_block, pl.BlockSpec((groups, 2 * GROUP, tile), lambda i: (0, 0, i)),
        ],
        out_shape=[
            shape_of((tokens, width), F32),
            shape_of((width, tokens), BF16),
            shape_of((groups, 2 * GROUP, tokens), F32),
        ],
        scratch_shapes=[
            pltpu.VMEM((width, width), BF16),
            pltpu.VMEM((width, hidden), BF16),
            pltpu.VMEM((hidden, width), BF16),
            pltpu.SemaphoreType.DMA((1 + 2 * (hidden // 1024),)),
        ],
        compiler_params=params(),
        cost_estimate=cost(tokens * width * (width + 2 * hidden), 50 * MIB),
    )(grad_low, norm_grad, slope, normed, inv, mix, attn_gain[None], w_output, ffn_in, ffn_out)


def input_grad_kernel(grad_ref, dq_ref, dk_ref, dv_ref, wq_ref, wk_ref, wv_ref, out_ref):
    total = grad_ref[...] + dot_nt(dq_ref[...], wq_ref[...])
    total = total + dot_nt(dk_ref[...], wk_ref[...])
    total = total + dot_nt(dv_ref[...], wv_ref[...])
    out_ref[...] = total.astype(BF16)


def input_grad(half, grad_one, dq, dk, dv, w_query, w_key, w_value):
    rows, width = dk.shape
    step = 256
    weight = pl.BlockSpec((step, width), lambda j: (j, 0))
    return pl.pallas_call(
        input_grad_kernel,
        grid=(width // step,),
        in_specs=[
            pl.BlockSpec((rows, step), lambda j: (half, j)),
            whole((rows, width)),
            whole((rows, width)),
            whole((rows, width)),
            weight,
            weight,
            weight,
        ],
        out_specs=pl.BlockSpec((rows, step), lambda j: (0, j)),
        out_shape=shape_of((rows, width), BF16),
        compiler_params=params(),
        cost_estimate=cost(3 * rows * width * width, 14 * MIB),
    )(grad_one, dq, dk, dv, w_query, w_key, w_value)


def swap(value, seq_bit, dp_bits):
    width = lax.axis_size("dp")
    count = lax.axis_size("seq") * width
    pairs = [
        (device, ((device // width) ^ seq_bit) * width + ((device % width) ^ dp_bits))
        for device in range(count)
    ]
    return lax.ppermute(value, ("seq", "dp"), pairs)


def gather_line(value):
    width = lax.axis_size("dp")
    groups = [[4 * line + place for line in range(width // 4)] for place in range(4)]
    return lax.all_gather(value, "dp", axis_index_groups=groups)


def total(values):
    return jnp.sum(values.astype(F32), axis=0)


def square_place():
    return 2 * ((lax.axis_index("dp") // 2) % 2) + lax.axis_index("seq")


def square_swaps(values):
    return [swap(values[offset - 1], offset % 2, 2 * (offset // 2)) for offset in range(1, 4)]


def sum_square(value):
    place = square_place()
    quarters = value.reshape(4, value.shape[0] // 4, value.shape[1])
    pick = [
        lax.dynamic_index_in_dim(quarters, place ^ offset, 0, keepdims=False) for offset in range(4)
    ]
    return pick[:1] + square_swaps(pick[1:])


def line_swaps(value):
    lines = lax.axis_size("dp") // 4
    return [swap(value, 0, 4 * offset) for offset in range(1, lines)]


def add(terms):
    value = terms[0].astype(F32)
    for term in terms[1:]:
        value = value + term.astype(F32)
    return value.astype(BF16)


def tie(*values):
    return lax.optimization_barrier(values)


def on_pair(
    hidden_in,
    lengths,
    w_query,
    w_key,
    w_value,
    w_output,
    attn_gain,
    ffn_in,
    ffn_out,
    ffn_gain,
    adapter_down,
    adapter_down_bias,
    adapter_up,
    adapter_up_bias,
    prefix_embed,
    prefix_hidden_w,
    prefix_hidden_b,
    prefix_out_w,
    prefix_out_b,
    out_grad,
):
    rows, _, width = hidden_in.shape
    count = prefix_embed.shape[0]
    position = lax.axis_index("seq")
    place = position.reshape(1).astype(jnp.int32)
    length = lax.dynamic_index_in_dim(lengths, position, 0, keepdims=False)
    core = lax.axis_index("dp") % 2
    scal = jnp.stack([position * rows, (1 - position) * rows, length, core]).astype(jnp.int32)

    x_own, x_send = split(place, hidden_in)
    x_other = shifted(x_send, "seq", 1)
    og_own, og_send = split(place, out_grad)
    og_other = shifted(og_send, "seq", 1)

    embed = jnp.pad(prefix_embed, ((0, PAD - count), (0, 0)))
    prefix_act, prefix_keys, prefix_values = prefix_forward(
        embed, prefix_hidden_w, prefix_hidden_b, prefix_out_w, prefix_out_b
    )
    lead = (prefix_keys, prefix_values)
    triple = project(0, x_own, w_query, w_key, w_value, ())
    near = attend(count, scal, 0, 0, 1, *triple, lead, ())
    q, k, v = project(1, x_other, w_query, w_key, w_value, triple)
    pt_own, ot_own, st_own, lead_weights = attend(count, scal, 0, 1, 1, q, k, v, lead, near)
    pt_other, ot_other, st_other = attend(0, scal, 1, 0, 2, q, k, v, (), ())

    (
        out_own, out_send, shares, mix, slope, grad_low, norm_grad, normed, inv_one,
        adapt_kept, adapt_sent, up_bias_grad, down_bias_grad,
    ) = front(
        scal, x_own, x_other, ot_own, ot_other, st_own, st_other, og_own, og_other,
        w_output, attn_gain, ffn_in, ffn_out, ffn_gain, adapter_down, adapter_down_bias,
        adapter_up, adapter_up_bias,
    )
    out_other = shifted(out_send, "seq", 1)
    core_terms = [adapt_kept, swap(adapt_sent, 0, 1)]
    grad_one, upstream, deltas = rear(
        grad_low, norm_grad, slope, normed, inv_one, mix, w_output, attn_gain, ffn_in, ffn_out
    )
    upstream, adapt_sum, out_other = tie(upstream, add(core_terms), out_other)
    square_terms = sum_square(adapt_sum)
    key_rows, value_rows, dqt = lead_backward(
        q, upstream, shares, deltas, lead_weights, prefix_keys, prefix_values
    )
    extra = jnp.concatenate(
        [
            jnp.pad(up_bias_grad, ((0, 0), (0, width))),
            jnp.pad(down_bias_grad, ((0, 0), (0, 2 * width - down_bias_grad.shape[1]))),
        ]
    )
    pair = jnp.concatenate([key_rows[:count], value_rows[:count]], axis=1)
    pair = jnp.concatenate([pair, extra]).astype(BF16)
    pair_core = swap(pair, 0, 1)

    back = (q, k, v)
    part_own, dk_other, dv_other = attend_back(
        1, 0, False, False, *back, upstream, shares, deltas, pt_other, dqt, ()
    )
    dk_other, adapt_sum, pair = tie(dk_other, add(square_terms), add([pair, pair_core]))
    adapt_line = gather_line(adapt_sum)
    pair_square = square_swaps([pair] * 3)
    part_other, dk_other, dv_other = attend_back(
        1, 1, False, True, *back, upstream, shares, deltas, pt_other, dqt, (dk_other, dv_other)
    )
    part_other, pair = tie(part_other, add([pair] + pair_square))
    pair_line = line_swaps(pair)
    dq_other, dk_own, dv_own = attend_back(
        0, 1, True, False, *back, upstream, shares, deltas, pt_own, part_other, ()
    )
    grad_other = input_grad(1, grad_one, dq_other, dk_other, dv_other, w_query, w_key, w_value)
    grad_back = shifted(grad_other, "seq", 1)
    adapt_sum = jnp.sum(adapt_line.astype(F32), axis=0).astype(BF16)
    dk_own, adapt_sum, *pair_line = tie(dk_own, adapt_sum, *pair_line)
    adapt_square = square_swaps([adapt_sum] * 3)
    dq_own, dk_own, dv_own = attend_back(
        0, 0, True, True, *back, upstream, shares, deltas, pt_own, part_own, (dk_own, dv_own)
    )
    grad_own = input_grad(0, grad_one, dq_own, dk_own, dv_own, w_query, w_key, w_value)
    pair = pair.astype(F32) + sum(item.astype(F32) for item in pair_line)
    prefix_grads = prefix_backward(count, pair, prefix_act, embed, prefix_hidden_w, prefix_out_w)
    layer_out = merge(place, out_own, out_other)
    grad_own, layer_out, out_w_grad, *adapt_square = tie(
        grad_own, layer_out, prefix_grads[3], *adapt_square
    )
    adapt_half = jnp.stack([adapt_sum] + adapt_square)
    place_here = square_place()
    adapt_half = jnp.concatenate(
        [lax.dynamic_slice_in_dim(adapt_half, spot ^ place_here, 1, 0) for spot in range(4)]
    )
    adapt_far = swap(adapt_half, 0, 1)
    first = lax.axis_index("dp") % 2 == 0
    adapt_rows = adapt_kept.shape[0]
    up_total = jnp.where(first, adapt_half, adapt_far).astype(F32).reshape(adapt_rows, width)
    down_total = jnp.where(first, adapt_far, adapt_half).astype(F32).reshape(adapt_rows, width)
    return (
        layer_out,
        merge(place, grad_own, grad_back),
        down_total.T,
        pair[count + 1, : down_bias_grad.shape[1]],
        up_total,
        pair[count, :width],
        prefix_grads[0],
        prefix_grads[1],
        prefix_grads[2][0],
        out_w_grad,
        prefix_grads[4][0],
    )


def solution(mesh):
    in_specs = (
        P("seq", "dp", None),
        P("dp"),
        P(),
        P(),
        P(),
        P(),
        P(),
        P(),
        P(),
        P(),
        P(),
        P(),
        P(),
        P(),
        P(),
        P(),
        P(),
        P(),
        P(),
        P("seq", "dp", None),
    )
    out_specs = (
        P("seq", "dp", None),
        P("seq", "dp", None),
        P(),
        P(),
        P(),
        P(),
        P(),
        P(),
        P(),
        P(),
        P(),
    )
    pairs = mesh.shape["seq"] == 2 and mesh.shape["dp"] % 8 == 0

    def on_one(*arrays):
        step = on_pair if pairs and arrays[0].shape[1] == 2 else on_device
        return step(*arrays)

    return jax.shard_map(
        on_one, mesh=mesh, in_specs=in_specs, out_specs=out_specs, check_vma=False
    )
```

```python
import functools
import math

import jax
import jax.numpy as jnp
from jax import lax
from jax.experimental import pallas as pl
from jax.experimental.pallas import tpu as pltpu
from jax.sharding import PartitionSpec as P

HEADS = 16


HIGHEST_PRECISION = lax.Precision.HIGHEST


def shifted(value, axis, steps):
    count = lax.axis_size(axis)
    pairs = [(source, (source + steps) % count) for source in range(count)]
    return lax.ppermute(value, axis, pairs)


def mixed(left, right):
    return jnp.dot(left, right, preferred_element_type=jnp.float32)


def mixed_left(left, right):
    return lax.dot_general(
        left, right, (((0,), (0,)), ((), ())), preferred_element_type=jnp.float32
    )


def mixed_right(left, right):
    return lax.dot_general(
        left, right, (((1,), (1,)), ((), ())), preferred_element_type=jnp.float32
    )


def precise(left, right):
    return jnp.dot(left, right, precision=HIGHEST_PRECISION, preferred_element_type=jnp.float32)


def precise_left(left, right):
    return lax.dot_general(
        left,
        right,
        (((0,), (0,)), ((), ())),
        precision=HIGHEST_PRECISION,
        preferred_element_type=jnp.float32,
    )


def precise_right(left, right):
    return lax.dot_general(
        left,
        right,
        (((1,), (1,)), ((), ())),
        precision=HIGHEST_PRECISION,
        preferred_element_type=jnp.float32,
    )


def gelu_value(inputs):
    return 0.5 * inputs * (1.0 + lax.erf(inputs * 0.7071067811865476))


def gelu_slope(inputs):
    return (
        0.5 * (1.0 + lax.erf(inputs * 0.7071067811865476))
        + inputs * jnp.exp(-0.5 * inputs * inputs) * 0.3989422804014327
    )


def normalize(values):
    row_mean = jnp.mean(values, axis=-1, keepdims=True)
    centred = values - row_mean
    spread = jnp.mean(centred * centred, axis=-1, keepdims=True)
    inv_std = lax.rsqrt(spread + 1e-05)
    return (centred * inv_std, inv_std)


def norm_back(upstream, normed, inv_std):
    mean_grad = jnp.mean(upstream, axis=-1, keepdims=True)
    mean_proj = jnp.mean(upstream * normed, axis=-1, keepdims=True)
    return inv_std * (upstream - mean_grad - normed * mean_proj)


def key_allowed(offset, key_count, seq_lengths):
    places = offset + lax.iota(jnp.int32, key_count)
    return places[None, :] < seq_lengths[:, None]


def lead_state(queries4, prefix_keys4, prefix_values4):
    inv_root = 1.0 / math.sqrt(queries4.shape[3])
    scores = (
        jnp.einsum("rshd,phd->rshp", queries4, prefix_keys4, preferred_element_type=jnp.float32)
        * inv_root
    )
    running_max = jnp.max(scores, axis=3)
    weights = jnp.exp(scores - running_max[..., None])
    running_sum = jnp.sum(weights, axis=3)
    running_mix = jnp.einsum(
        "rshp,phd->rshd",
        weights.astype(jnp.bfloat16),
        prefix_values4,
        preferred_element_type=jnp.float32,
    )
    return (running_max, running_sum, running_mix)


def fold_block(carried, key_block, value_block, offset, queries4, seq_lengths):
    key_count, seqs_here = (key_block.shape[0], key_block.shape[1])
    head_count, head_dim = (queries4.shape[2], queries4.shape[3])
    inv_root = 1.0 / math.sqrt(head_dim)
    keys4 = key_block.reshape(key_count, seqs_here, head_count, head_dim)
    values4 = value_block.reshape(key_count, seqs_here, head_count, head_dim)
    running_max, running_sum, running_mix = carried
    scores = (
        jnp.einsum("rshd,tshd->rsht", queries4, keys4, preferred_element_type=jnp.float32)
        * inv_root
    )
    allowed = key_allowed(offset, key_count, seq_lengths)[None, :, None, :]
    scores = jnp.where(allowed, scores, -jnp.inf)
    new_max = jnp.maximum(running_max, jnp.max(scores, axis=3))
    weights = jnp.exp(scores - new_max[..., None])
    rescale = jnp.exp(running_max - new_max)
    running_sum = running_sum * rescale + jnp.sum(weights, axis=3)
    running_mix = running_mix * rescale[..., None] + jnp.einsum(
        "rsht,tshd->rshd", weights.astype(jnp.bfloat16), values4, preferred_element_type=jnp.float32
    )
    return (new_max, running_sum, running_mix)


def lead_back(queries4, upstream4, log_total, row_delta, prefix_keys4, prefix_values4):
    inv_root = 1.0 / math.sqrt(queries4.shape[3])
    scores = (
        jnp.einsum("rshd,phd->rshp", queries4, prefix_keys4, preferred_element_type=jnp.float32)
        * inv_root
    )
    weights = jnp.exp(scores - log_total[..., None])
    weight_grads = jnp.einsum(
        "rshd,phd->rshp", upstream4, prefix_values4, preferred_element_type=jnp.float32
    )
    score_grads = (weights * (weight_grads - row_delta[..., None])).astype(jnp.bfloat16)
    query_term = (
        jnp.einsum("rshp,phd->rshd", score_grads, prefix_keys4, preferred_element_type=jnp.float32)
        * inv_root
    )
    key_term = (
        jnp.einsum("rshp,rshd->phd", score_grads, queries4, preferred_element_type=jnp.float32)
        * inv_root
    )
    value_term = jnp.einsum(
        "rshp,rshd->phd",
        weights.astype(jnp.bfloat16),
        upstream4,
        preferred_element_type=jnp.float32,
    )
    return (query_term, key_term, value_term)


def block_back(
    queries4, upstream4, log_total, row_delta, key_block, value_block, offset, seq_lengths
):
    key_count, seqs_here, model_width = key_block.shape
    head_count, head_dim = (queries4.shape[2], queries4.shape[3])
    inv_root = 1.0 / math.sqrt(head_dim)
    keys4 = key_block.reshape(key_count, seqs_here, head_count, head_dim)
    values4 = value_block.reshape(key_count, seqs_here, head_count, head_dim)
    scores = (
        jnp.einsum("rshd,tshd->rsht", queries4, keys4, preferred_element_type=jnp.float32)
        * inv_root
    )
    allowed = key_allowed(offset, key_count, seq_lengths)[None, :, None, :]
    scores = jnp.where(allowed, scores, -jnp.inf)
    weights = jnp.exp(scores - log_total[..., None])
    weight_grads = jnp.einsum(
        "rshd,tshd->rsht", upstream4, values4, preferred_element_type=jnp.float32
    )
    score_grads = (weights * (weight_grads - row_delta[..., None])).astype(jnp.bfloat16)
    query_term = (
        jnp.einsum("rsht,tshd->rshd", score_grads, keys4, preferred_element_type=jnp.float32)
        * inv_root
    )
    key_term = (
        jnp.einsum("rsht,rshd->tshd", score_grads, queries4, preferred_element_type=jnp.float32)
        * inv_root
    )
    value_term = jnp.einsum(
        "rsht,rshd->tshd",
        weights.astype(jnp.bfloat16),
        upstream4,
        preferred_element_type=jnp.float32,
    )
    pair_term = jnp.stack(
        [
            key_term.reshape(key_count, seqs_here, model_width),
            value_term.reshape(key_count, seqs_here, model_width),
        ]
    )
    return (query_term, pair_term)


def prefix_back(pair_grad, prefix_act, prefix_embed, hidden_weight, out_weight):
    out_w_grad = precise_left(prefix_act, pair_grad)
    out_b_grad = jnp.sum(pair_grad, axis=0)
    act_grad = precise_right(pair_grad, out_weight) * (1.0 - prefix_act * prefix_act)
    hidden_w_grad = precise_left(prefix_embed, act_grad)
    hidden_b_grad = jnp.sum(act_grad, axis=0)
    embed_grad = precise_right(act_grad, hidden_weight)
    return (embed_grad, hidden_w_grad, hidden_b_grad, out_w_grad, out_b_grad)


def on_device(
    hidden_in,
    lengths,
    w_query,
    w_key,
    w_value,
    w_output,
    attn_gain,
    ffn_in,
    ffn_out,
    ffn_gain,
    adapter_down,
    adapter_down_bias,
    adapter_up,
    adapter_up_bias,
    prefix_embed,
    prefix_hidden_w,
    prefix_hidden_b,
    prefix_out_w,
    prefix_out_b,
    out_grad,
):
    rows_here, seqs_here, model_width = hidden_in.shape
    token_count = rows_here * seqs_here
    head_count = HEADS
    head_dim = model_width // head_count
    axis_count = lax.axis_size("seq")
    position = lax.axis_index("seq")
    tokens = hidden_in.reshape(token_count, model_width)
    projected = jnp.stack([mixed(tokens, w_query), mixed(tokens, w_key), mixed(tokens, w_value)])
    triple = projected.astype(jnp.bfloat16).reshape(3, rows_here, seqs_here, model_width)
    hidden_weight = prefix_hidden_w.astype(jnp.float32)
    out_weight = prefix_out_w.astype(jnp.float32)
    prefix_act = jnp.tanh(precise(prefix_embed, hidden_weight) + prefix_hidden_b)
    prefix_pair = precise(prefix_act, out_weight) + prefix_out_b
    prefix_keys4 = (
        prefix_pair[:, :model_width].astype(jnp.bfloat16).reshape(-1, head_count, head_dim)
    )
    prefix_values4 = (
        prefix_pair[:, model_width:].astype(jnp.bfloat16).reshape(-1, head_count, head_dim)
    )
    row_places = position * rows_here + lax.iota(jnp.int32, rows_here)
    valid = (row_places[:, None] < lengths[None, :]).astype(jnp.float32).reshape(token_count, 1)
    queries4 = triple[0].reshape(rows_here, seqs_here, head_count, head_dim)
    key_value = triple[1:]
    pieces = lax.all_gather(key_value, "seq", axis=1, tiled=True)
    carried = fold_block(
        lead_state(queries4, prefix_keys4, prefix_values4),
        pieces[0],
        pieces[1],
        jnp.int32(0),
        queries4,
        lengths,
    )
    mix_full = carried[2] / carried[1][..., None]
    log_total = carried[0] + jnp.log(carried[1])
    mix_low = mix_full.astype(jnp.bfloat16).reshape(token_count, model_width)
    attn_proj = mixed(mix_low, w_output)
    normed_one, inv_one = normalize(tokens.astype(jnp.float32) + attn_proj)
    norm_one = normed_one * attn_gain
    norm_low = norm_one.astype(jnp.bfloat16)
    inner_pre = mixed(norm_low, ffn_in)
    inner_act = gelu_value(inner_pre).astype(jnp.bfloat16)
    squeeze = mixed(norm_low, adapter_down) + adapter_down_bias
    squeeze_act = gelu_value(squeeze).astype(jnp.bfloat16)
    ffn_sum = mixed(inner_act, ffn_out)
    adapter_sum = mixed(squeeze_act, adapter_up) + adapter_up_bias
    normed_two, inv_two = normalize(norm_one + ffn_sum + 4.0 * adapter_sum)
    layer_out = (
        (normed_two * ffn_gain * valid)
        .astype(jnp.bfloat16)
        .reshape(rows_here, seqs_here, model_width)
    )
    upstream_top = out_grad.reshape(token_count, model_width).astype(jnp.float32) * valid
    grad_two = norm_back(upstream_top * ffn_gain, normed_two, inv_two)
    grad_ffn_low = grad_two.astype(jnp.bfloat16)
    grad_adapt_low = (4.0 * grad_two).astype(jnp.bfloat16)
    up_grad = mixed_left(squeeze_act, grad_adapt_low)
    up_bias_grad = jnp.sum(grad_adapt_low.astype(jnp.float32), axis=0)
    grad_squeeze_low = (mixed_right(grad_adapt_low, adapter_up) * gelu_slope(squeeze)).astype(
        jnp.bfloat16
    )
    down_grad = mixed_left(norm_low, grad_squeeze_low)
    down_bias_grad = jnp.sum(grad_squeeze_low.astype(jnp.float32), axis=0)
    grad_inner_low = (mixed_right(grad_ffn_low, ffn_out) * gelu_slope(inner_pre)).astype(
        jnp.bfloat16
    )
    grad_norm = (
        grad_two + mixed_right(grad_squeeze_low, adapter_down) + mixed_right(grad_inner_low, ffn_in)
    )
    grad_one = norm_back(grad_norm * attn_gain, normed_one, inv_one)
    grad_attn_low = grad_one.astype(jnp.bfloat16)
    grad_mix_low = mixed_right(grad_attn_low, w_output).astype(jnp.bfloat16)
    upstream4 = grad_mix_low.reshape(rows_here, seqs_here, head_count, head_dim)
    row_delta = jnp.sum(upstream4.astype(jnp.float32) * mix_full, axis=3)
    query_grad, prefix_key_grad, prefix_value_grad = lead_back(
        queries4, upstream4, log_total, row_delta, prefix_keys4, prefix_values4
    )

    def visit(step_index, carried):
        moving, grads_moving, query_total = carried
        source = (position - step_index) % axis_count
        query_term, pair_term = block_back(
            queries4,
            upstream4,
            log_total,
            row_delta,
            moving[0],
            moving[1],
            source * rows_here,
            lengths,
        )
        return (moving, grads_moving + pair_term, query_total + query_term)

    def travel(step_index, carried):
        moving, grads_moving, query_total = visit(step_index, carried)
        moving = shifted(moving, "seq", 1)
        grads_moving = shifted(grads_moving.astype(jnp.bfloat16), "seq", 1).astype(
            grads_moving.dtype
        )
        return (moving, grads_moving, query_total)

    initial = (
        key_value,
        jnp.zeros((2, rows_here, seqs_here, model_width), jnp.float32),
        query_grad,
    )
    carried = lax.fori_loop(0, axis_count - 1, travel, initial)
    carried = visit(axis_count - 1, carried)
    pair_grads = shifted(carried[1].astype(jnp.bfloat16), "seq", 1).astype(jnp.float32)
    triple_grad = jnp.concatenate(
        [carried[2].reshape(1, rows_here, seqs_here, model_width), pair_grads]
    ).astype(jnp.bfloat16)
    hidden_grad = grad_one + mixed_right(triple_grad[0].reshape(token_count, model_width), w_query)
    hidden_grad = hidden_grad + mixed_right(triple_grad[1].reshape(token_count, model_width), w_key)
    hidden_grad = hidden_grad + mixed_right(
        triple_grad[2].reshape(token_count, model_width), w_value
    )
    hidden_grad = hidden_grad.astype(jnp.bfloat16).reshape(rows_here, seqs_here, model_width)
    pair_grad = jnp.concatenate(
        [prefix_key_grad.reshape(-1, model_width), prefix_value_grad.reshape(-1, model_width)],
        axis=1,
    )
    prefix_grads = prefix_back(pair_grad, prefix_act, prefix_embed, hidden_weight, out_weight)
    summed = lax.psum(
        (
            down_grad,
            down_bias_grad,
            up_grad,
            up_bias_grad,
            prefix_grads[0],
            prefix_grads[1],
            prefix_grads[2],
            prefix_grads[3],
            prefix_grads[4],
        ),
        ("seq", "dp"),
    )
    adapter_totals = summed[:4]
    prefix_totals = summed[4:]
    return (
        layer_out,
        hidden_grad,
        adapter_totals[0],
        adapter_totals[1],
        adapter_totals[2],
        adapter_totals[3],
        prefix_totals[0],
        prefix_totals[1],
        prefix_totals[2],
        prefix_totals[3],
        prefix_totals[4],
    )


BF16 = jnp.bfloat16
F32 = jnp.float32
MIB = 1024 * 1024
GROUP = 4
HEAD_DIM = 64
LANES = GROUP * HEAD_DIM
PAD = 32
MASKED = -1e30
LOG2E = 1.4426950408889634
VMEM_LIMIT = 60 * MIB


def dot_nn(left, right):
    return lax.dot_general(left, right, (((1,), (0,)), ((), ())), preferred_element_type=F32)


def dot_nt(left, right):
    return lax.dot_general(left, right, (((1,), (1,)), ((), ())), preferred_element_type=F32)


def dot_tn(left, right):
    return lax.dot_general(left, right, (((0,), (0,)), ((), ())), preferred_element_type=F32)


def shape_of(shape, dtype):
    return pltpu.HBM(shape, dtype)


def far(value):
    return pltpu.with_memory_space_constraint(value, pltpu.HBM)


def bring(value):
    return pltpu.with_memory_space_constraint(value, pltpu.VMEM)


def all_far(values):
    return [far(value) for value in values]


def params(limit=VMEM_LIMIT):
    return pltpu.CompilerParams(vmem_limit_bytes=limit)


def cost(macs, moved):
    return pl.CostEstimate(flops=int(2 * macs), bytes_accessed=int(moved), transcendentals=0)


SMEM_SPEC = pl.BlockSpec(memory_space=pltpu.SMEM)
ANY_SPEC = pl.BlockSpec(memory_space=pl.ANY)
CORE_SPEC = pl.BlockSpec(memory_space=pltpu.VMEM)


def whole(shape):
    return pl.BlockSpec(shape, lambda *_: (0,) * len(shape))


def kept(shape):
    return pl.BlockSpec(shape, lambda *_: (0,) * len(shape), pipeline_mode=pl.Buffered(1))


def split_kernel(place_ref, both_ref, own_ref, other_ref):
    apart = jnp.swapaxes(both_ref[...], 0, 1)
    first = place_ref[0] == 0
    own_ref[...] = jnp.where(first, apart[0], apart[1])
    other_ref[...] = jnp.where(first, apart[1], apart[0])


def split(place, both):
    rows, _, width = both.shape
    step = rows // 4
    half = pl.BlockSpec((step, width), lambda i: (i, 0))
    return pl.pallas_call(
        split_kernel,
        grid=(4,),
        in_specs=[SMEM_SPEC, pl.BlockSpec((step, 2, width), lambda i: (i, 0, 0))],
        out_specs=[half, half],
        out_shape=[shape_of((rows, width), both.dtype)] * 2,
        compiler_params=params(8 * MIB),
        cost_estimate=cost(0, 4 * rows * width * 2),
    )(place, far(both))


def merge_kernel(place_ref, own_ref, other_ref, both_ref):
    first = place_ref[0] == 0
    own, other = own_ref[...], other_ref[...]
    apart = jnp.stack([jnp.where(first, own, other), jnp.where(first, other, own)])
    both_ref[...] = jnp.swapaxes(apart, 0, 1)


def merge(place, own, other):
    rows, width = other.shape
    step = rows // 4
    half = pl.BlockSpec((step, width), lambda i: (i, 0))
    return pl.pallas_call(
        merge_kernel,
        grid=(4,),
        in_specs=[SMEM_SPEC, half, half],
        out_specs=pl.BlockSpec((step, 2, width), lambda i: (i, 0, 0)),
        out_shape=shape_of((rows, 2, width), other.dtype),
        compiler_params=params(8 * MIB),
        cost_estimate=cost(0, 4 * rows * width * 2),
    )(place, far(own), far(other))


def parts_of(values, count):
    parts = []
    for _ in range(count):
        part = values.astype(BF16)
        parts.append(part)
        values = values - part.astype(F32)
    return parts


def exact_dot(values, weight, dot):
    rows = values.shape[0]
    product = dot(jnp.concatenate(parts_of(values, 3), axis=0), weight)
    return product[:rows] + product[rows : 2 * rows] + product[2 * rows :]


def prefix_kernel(embed_ref, hw_ref, hb_ref, ow_ref, ob_ref, act_ref, key_ref, value_ref):
    width = key_ref.shape[1]
    act = jnp.tanh(exact_dot(embed_ref[...], hw_ref[...], dot_nn) + hb_ref[...])
    act_ref[...] = act
    pair = exact_dot(act, ow_ref[...], dot_nn) + ob_ref[...]
    key_ref[...] = pair[:, :width].astype(BF16)
    value_ref[...] = pair[:, width:].astype(BF16)


def prefix_forward(embed, hidden_w, hidden_b, out_w, out_b):
    width, hidden = hidden_w.shape
    return pl.pallas_call(
        prefix_kernel,
        out_shape=[
            shape_of((PAD, hidden), F32),
            shape_of((PAD, width), BF16),
            shape_of((PAD, width), BF16),
        ],
        compiler_params=params(16 * MIB),
        cost_estimate=cost(3 * PAD * hidden * 3 * width * 4, 6 * hidden * width),
    )(embed, hidden_w, hidden_b[None], out_w, out_b[None])


def prefix_back_kernel(
    count, terms, *refs
):
    pair_refs, refs = refs[:terms], refs[terms:]
    act_ref, embed_ref, hw_ref, ow_ref = refs[:4]
    eg_ref, hwg_ref, hbg_ref, owg_ref, obg_ref, ubg_ref, dbg_ref = refs[4:]
    total = pair_refs[0][...].astype(F32)
    for pair_ref in pair_refs[1:]:
        total = total + pair_ref[...].astype(F32)
    ubg_ref[...] = total[count : count + 1]
    dbg_ref[...] = total[count + 1 : count + 2, : dbg_ref.shape[1]]
    pair = jnp.concatenate([total[:PAD], total[PAD:]], axis=1)
    rows = lax.broadcasted_iota(jnp.int32, pair.shape, 0)
    pair = jnp.where(rows < count, pair, 0.0)
    act = act_ref[...]
    obg_ref[...] = jnp.sum(pair, axis=0, keepdims=True)
    high, low = parts_of(pair, 2)
    back = dot_nt(jnp.concatenate([high, low], axis=0), ow_ref[...])
    act_grad = (back[:PAD] + back[PAD:]) * (1.0 - act * act)
    act_high, act_low = parts_of(act, 2)
    owg_ref[...] = dot_tn(
        jnp.concatenate([act_high, act_low, act_high], axis=0),
        jnp.concatenate([high, high, low], axis=0),
    )
    hbg_ref[...] = jnp.sum(act_grad, axis=0, keepdims=True)
    high, low = parts_of(act_grad, 2)
    embed_high, embed_low = parts_of(embed_ref[...], 2)
    hwg_ref[...] = dot_tn(
        jnp.concatenate([embed_high, embed_low, embed_high], axis=0),
        jnp.concatenate([high, high, low], axis=0),
    )
    back = dot_nt(jnp.concatenate([high, low], axis=0), hw_ref[...])
    eg_ref[...] = (back[:PAD] + back[PAD:])[:count]


def prefix_backward(count, adapt, pairs, act, embed, hidden_w, out_w):
    width, hidden = hidden_w.shape
    return pl.pallas_call(
        functools.partial(prefix_back_kernel, count, len(pairs)),
        out_shape=[
            shape_of((count, width), F32),
            shape_of((width, hidden), F32),
            shape_of((1, hidden), F32),
            shape_of((hidden, 2 * width), F32),
            shape_of((1, 2 * width), F32),
            shape_of((1, width), F32),
            shape_of((1, adapt), F32),
        ],
        compiler_params=params(20 * MIB),
        cost_estimate=cost(96 * hidden * width * 6, 20 * hidden * width),
    )(*pairs, act, embed, hidden_w, out_w)


def project_kernel(x_ref, wq_ref, wk_ref, wv_ref, *refs):
    q_ref, k_ref, v_ref = refs[-3:]
    x = x_ref[...]
    scale = LOG2E / math.sqrt(HEAD_DIM)
    q_ref[...] = (dot_nn(x, wq_ref[...]) * scale).astype(BF16)
    k_ref[...] = dot_nn(x, wk_ref[...]).astype(BF16)
    v_ref[...] = dot_nn(x, wv_ref[...]).astype(BF16)


def project(half, x, w_query, w_key, w_value, earlier):
    rows, width = x.shape
    step = rows // 2
    return pl.pallas_call(
        project_kernel,
        grid=(2,),
        in_specs=[pl.BlockSpec((step, width), lambda i: (i, 0))]
        + [CORE_SPEC] * 3
        + [ANY_SPEC] * len(earlier),
        out_specs=[pl.BlockSpec((step, width), lambda i: (2 * half + i, 0))] * 3,
        out_shape=[shape_of((2 * rows, width), BF16)] * 3,
        input_output_aliases={4 + i: i for i in range(len(earlier))},
        compiler_params=params(14 * MIB),
        cost_estimate=cost(3 * rows * width * width, 2 * (4 * rows * width + 3 * width * width)),
    )(far(x), bring(w_query), bring(w_key), bring(w_value), *all_far(earlier))


def head_lanes(head, rows, lanes):
    place = lax.broadcasted_iota(jnp.int32, (rows, lanes), 1)
    return (place // HEAD_DIM == head).astype(F32).astype(BF16)


def first_lane(values):
    lane = lax.broadcasted_iota(jnp.int32, (values.shape[0], 128), 1)
    return jnp.where(lane == 0, values, 0.0).astype(BF16)


def block_diagonal(rows):
    return jnp.concatenate(
        [rows * head_lanes(head, rows.shape[0], LANES) for head in range(GROUP)], axis=0
    )


def attend_kernel(count, half, scal_ref, q_ref, k_ref, v_ref, *refs):
    keys = k_ref.shape[0]
    queries = q_ref.shape[0]
    scores = refs[-2:]
    refs = refs[:-2]
    if count:
        pk_ref, pv_ref = refs[:2]
        pt_ref, ot_ref, st_ref, pp_ref = refs[-4:]
    else:
        pt_ref, ot_ref, st_ref = refs[-3:]
    place = scal_ref[half] + lax.broadcasted_iota(jnp.int32, (keys, 128), 0)
    bias = first_lane(jnp.where(place < scal_ref[2], 0.0, MASKED))
    ones = first_lane(jnp.ones((queries, 128), F32))
    tail = jnp.ones((16, keys), BF16)
    masks = [head_lanes(head, queries, 128) for head in range(2)]

    def score(head):
        pair = slice((head // 2) * 128, (head // 2 + 1) * 128)
        k_aug = jnp.concatenate([k_ref[:, pair], bias], axis=1)
        q_aug = jnp.concatenate([q_ref[:, pair] * masks[head % 2], ones], axis=1)
        scores[head % 2][...] = dot_nt(k_aug, q_aug)

    def weigh(head):
        own = scores[head % 2]
        top = jnp.max(own[...], axis=0, keepdims=True)
        if count:
            lead_scores = lead[head * PAD : (head + 1) * PAD]
            top = jnp.maximum(top, jnp.max(lead_scores, axis=0, keepdims=True))
        pt_ref[head] = jnp.exp2(own[...] - top).astype(BF16)
        st_ref[0, head : head + 1, :] = top
        if not count:
            return 0.0
        lead_weights = jnp.exp2(lead_scores - top).astype(BF16)
        pp_ref[0, head * PAD : (head + 1) * PAD, :] = lead_weights
        return jnp.sum(lead_weights.astype(F32), axis=0, keepdims=True)

    def mix(head, lead_total):
        rows = slice(head * HEAD_DIM, (head + 1) * HEAD_DIM)
        mixed_rows = dot_nn(jnp.concatenate([turned[rows], tail], axis=0), pt_ref[head])
        mixed = mixed_rows[:HEAD_DIM]
        if count:
            own_lanes = pv_ref[...] * head_lanes(head, PAD, LANES)
            lead_weights = pp_ref[0, head * PAD : (head + 1) * PAD, :]
            mixed = mixed + dot_tn(own_lanes, lead_weights)[rows]
        ot_ref[rows, :] = mixed.astype(BF16)
        total_row = mixed_rows[HEAD_DIM : HEAD_DIM + 1] + lead_total
        st_ref[0, GROUP + head : GROUP + head + 1, :] = total_row

    score(0)
    turned = v_ref[...].T
    if count:
        lead = dot_nt(block_diagonal(pk_ref[...]), q_ref[...])
        row = lax.broadcasted_iota(jnp.int32, lead.shape, 0)
        lead = jnp.where(row % PAD < count, lead, MASKED)
    lead_totals = []
    for head in range(GROUP):
        if head + 1 < GROUP:
            score(head + 1)
        lead_totals.append(weigh(head))
        if head:
            mix(head - 1, lead_totals[head - 1])
    mix(GROUP - 1, lead_totals[GROUP - 1])


def attend(count, scal, key_half, query_first, query_blocks, q, k, v, lead, earlier):
    tokens, width = q.shape
    rows = tokens // 2
    groups = width // LANES
    in_specs = [
        SMEM_SPEC,
        pl.BlockSpec((rows, LANES), lambda i, g: (i + query_first, g)),
        pl.BlockSpec((rows, LANES), lambda i, g: (key_half, g)),
        pl.BlockSpec((rows, LANES), lambda i, g: (key_half, g)),
    ]
    in_specs += [pl.BlockSpec((PAD, LANES), lambda i, g: (0, g))] * len(lead)
    out_specs = [
        pl.BlockSpec((GROUP, rows, rows), lambda i, g: (g, 0, i + query_first)),
        pl.BlockSpec((LANES, rows), lambda i, g: (g, i + query_first)),
        pl.BlockSpec((1, 2 * GROUP, rows), lambda i, g: (g, 0, i + query_first)),
    ]
    out_shape = [
        shape_of((groups * GROUP, rows, tokens), BF16),
        shape_of((width, tokens), BF16),
        shape_of((groups, 2 * GROUP, tokens), F32),
    ]
    if count:
        out_specs.append(pl.BlockSpec((1, GROUP * PAD, rows), lambda i, g: (g, 0, i + query_first)))
        out_shape.append(shape_of((groups, GROUP * PAD, tokens), BF16))
    start = len(in_specs)
    macs = query_blocks * groups * GROUP * rows * rows * 256 * 2
    return pl.pallas_call(
        functools.partial(attend_kernel, count, key_half),
        grid=(query_blocks, groups),
        in_specs=in_specs + [ANY_SPEC] * len(earlier),
        out_specs=out_specs,
        out_shape=out_shape,
        input_output_aliases={start + i: i for i in range(len(earlier))},
        scratch_shapes=[pltpu.VMEM((rows, rows), F32)] * 2,
        compiler_params=params(16 * MIB),
        cost_estimate=cost(macs, query_blocks * 24 * MIB),
    )(scal, far(q), far(k), far(v), *lead, *all_far(earlier))


def lead_back_kernel(
    count, q_ref, up_ref, rst_ref, del_ref, pp_ref, pk_ref, pv_ref, bias_ref, pair_ref, dqt_ref
):
    queries = q_ref.shape[0]
    ups = []
    deltas = []
    for head in range(GROUP):
        rows = slice(head * HEAD_DIM, (head + 1) * HEAD_DIM)
        share = rst_ref[0, head : head + 1, :]
        ups.append((up_ref[rows, :].astype(F32) * share).astype(BF16))
        delta = del_ref[0, head : head + 1, :] * share
        deltas.append(jnp.broadcast_to(delta, (PAD, queries)))
    up = jnp.concatenate(ups, axis=0)
    delta = jnp.concatenate(deltas, axis=0)
    weights = pp_ref[0]
    key_diagonal = block_diagonal(pk_ref[...])
    value_diagonal = block_diagonal(pv_ref[...])
    weight_grads = dot_nn(value_diagonal, up)
    score_grads = (weights.astype(F32) * (weight_grads - delta)).astype(BF16)
    dqt_ref[...] = dot_tn(key_diagonal, score_grads).astype(BF16)
    key_grads = dot_nn(score_grads, q_ref[...]) * (1.0 / LOG2E)
    value_grads = dot_nt(weights, up)
    lane = lax.broadcasted_iota(jnp.int32, (PAD, LANES), 1) // HEAD_DIM
    key_total = jnp.zeros((PAD, LANES), F32)
    value_total = jnp.zeros((PAD, LANES), F32)
    for head in range(GROUP):
        rows = slice(head * PAD, (head + 1) * PAD)
        key_total = jnp.where(lane == head, key_grads[rows], key_total)
        value_total = jnp.where(lane == head, value_grads[rows], value_total)
    row = lax.broadcasted_iota(jnp.int32, (PAD, LANES), 0)
    key_total = jnp.where(row == count, bias_ref[0:1, :], key_total)
    key_total = jnp.where(row == count + 1, bias_ref[1:2, :], key_total)
    pair_ref[:PAD, :] = key_total.astype(BF16)
    pair_ref[PAD:, :] = value_total.astype(BF16)


def lead_backward(count, q, up, shares, deltas, lead_weights, prefix_keys, prefix_values, biases):
    tokens, width = q.shape
    groups = width // LANES
    small = pl.BlockSpec((PAD, LANES), lambda g: (0, g))
    stats = pl.BlockSpec((1, 2 * GROUP, tokens), lambda g: (g, 0, 0))
    return pl.pallas_call(
        functools.partial(lead_back_kernel, count),
        grid=(groups,),
        in_specs=[
            pl.BlockSpec((tokens, LANES), lambda g: (0, g)),
            pl.BlockSpec((LANES, tokens), lambda g: (g, 0)),
            stats,
            stats,
            pl.BlockSpec((1, GROUP * PAD, tokens), lambda g: (g, 0, 0)),
            small,
            small,
            pl.BlockSpec((8, LANES), lambda g: (0, g)),
        ],
        out_specs=[
            pl.BlockSpec((2 * PAD, LANES), lambda g: (0, g)),
            pl.BlockSpec((LANES, tokens), lambda g: (g, 0)),
        ],
        out_shape=[
            jax.ShapeDtypeStruct((2 * PAD, width), BF16),
            shape_of((width, tokens), BF16),
        ],
        compiler_params=params(14 * MIB),
        cost_estimate=cost(groups * 4 * GROUP * PAD * tokens * LANES, 10 * MIB),
    )(*all_far((q, up, shares, deltas, lead_weights)), prefix_keys, prefix_values, biases)


def attend_back_kernel(
    half,
    last_keys,
    last_queries,
    has_earlier,
    q_ref,
    k_ref,
    v_ref,
    up_ref,
    rst_ref,
    del_ref,
    pt_ref,
    dqt_in_ref,
    *refs,
):
    dq_ref, dk_ref, dv_ref = refs[-5:-2]
    weight_grads = refs[-2:]
    queries = q_ref.shape[0]
    lane = lax.broadcasted_iota(jnp.int32, (queries, 128), 1) // HEAD_DIM
    masks = [(lane == head).astype(F32).astype(BF16) for head in range(2)]
    zeros = jnp.zeros((HEAD_DIM, queries), BF16)
    turned = k_ref[...].T
    ups = {}
    grads = {}
    query_grads = []
    key_grads = []
    value_grads = []

    def pair_of(head):
        return slice((head // 2) * 128, (head // 2 + 1) * 128)

    def rows_of(head):
        return slice(head * HEAD_DIM, (head + 1) * HEAD_DIM)

    def share_of(head):
        return rst_ref[0, half * GROUP + head : half * GROUP + head + 1, :]

    def weight_grad(head):
        up = (up_ref[rows_of(head), :].astype(F32) * share_of(head)).astype(BF16)
        ups[head] = jnp.concatenate([up, zeros] if head % 2 == 0 else [zeros, up], axis=0)
        weight_grads[head % 2][...] = dot_nn(v_ref[:, pair_of(head)], ups[head])

    def score_grad(head):
        delta = del_ref[0, head : head + 1, :] * share_of(head)
        return (pt_ref[head].astype(F32) * (weight_grads[head % 2][...] - delta)).astype(BF16)

    def value_term(head):
        return dot_nt(pt_ref[head], ups[head])

    def key_term(head):
        return dot_nn(grads[head], q_ref[:, pair_of(head)] * masks[head % 2])

    def query_term(head):
        return dqt_in_ref[rows_of(head), :].astype(F32) + dot_nn(turned[rows_of(head)], grads[head])

    weight_grad(0)
    for head in range(GROUP):
        if head + 1 < GROUP:
            weight_grad(head + 1)
        grads[head] = score_grad(head)
        value = value_term(head)
        query_grads.append(query_term(head))
        key = key_term(head)
        if head % 2:
            key_grads[-1] = key_grads[-1] + key
            value_grads[-1] = value_grads[-1] + value
        else:
            key_grads.append(key)
            value_grads.append(value)
    query_grad = jnp.concatenate(query_grads, axis=0)
    key_grad = jnp.concatenate(key_grads, axis=1)
    value_grad = jnp.concatenate(value_grads, axis=1)
    if not last_keys:
        dq_ref[...] = query_grad.astype(BF16)
    else:
        dq_ref[...] = (query_grad * (1.0 / math.sqrt(HEAD_DIM))).astype(BF16).T
    if has_earlier:
        key_grad = key_grad + refs[0][...].astype(F32)
        value_grad = value_grad + refs[1][...].astype(F32)
    if last_queries:
        key_grad = key_grad * (1.0 / LOG2E)
    dk_ref[...] = key_grad.astype(BF16)
    dv_ref[...] = value_grad.astype(BF16)


def attend_back(
    key_half, query_half, last_keys, last_queries, q, k, v, up, shares, deltas, weights, dqt, earlier
):
    tokens, width = q.shape
    rows = tokens // 2
    groups = width // LANES
    query_columns = pl.BlockSpec((LANES, rows), lambda g: (g, query_half))
    stats = pl.BlockSpec((1, 2 * GROUP, rows), lambda g: (g, 0, query_half))
    finished = pl.BlockSpec((rows, LANES), lambda g: (0, g))
    out_columns = pl.BlockSpec((LANES, rows), lambda g: (g, 0))
    sofar = query_columns if dqt.shape[1] == tokens else out_columns
    macs = groups * GROUP * rows * rows * 256 * 4
    return pl.pallas_call(
        functools.partial(
            attend_back_kernel, key_half, last_keys, last_queries, len(earlier) > 0
        ),
        grid=(groups,),
        in_specs=[
            pl.BlockSpec((rows, LANES), lambda g: (query_half, g)),
            pl.BlockSpec((rows, LANES), lambda g: (key_half, g)),
            pl.BlockSpec((rows, LANES), lambda g: (key_half, g)),
            query_columns,
            stats,
            stats,
            pl.BlockSpec((GROUP, rows, rows), lambda g: (g, 0, query_half)),
            sofar,
        ]
        + [finished] * len(earlier),
        out_specs=[finished if last_keys else out_columns, finished, finished],
        out_shape=[
            shape_of((rows, width) if last_keys else (width, rows), BF16),
            shape_of((rows, width), BF16),
            shape_of((rows, width), BF16),
        ],
        scratch_shapes=[pltpu.VMEM((rows, rows), F32)] * 2,
        compiler_params=params(18 * MIB),
        cost_estimate=cost(macs, 12 * MIB),
    )(*all_far((q, k, v, up, shares, deltas, weights, dqt, *earlier)))


def gelu_pair(values):
    scaled = values * 0.7071067811865476
    below = 0.5 * lax.erf(scaled) + 0.5
    decay = jnp.exp2(scaled * scaled * (-LOG2E))
    return values * below, below + values * 0.3989422804014327 * decay


def row_mean(values):
    return jnp.mean(values, axis=-1, keepdims=True)


def front_kernel(
    tiles,
    scal_ref,
    x_own_ref,
    x_other_ref,
    ot_own_ref,
    ot_other_ref,
    st_own_ref,
    st_other_ref,
    og_own_ref,
    og_other_ref,
    gain_one_ref,
    gain_two_ref,
    down_bias_ref,
    up_bias_ref,
    wo_ref,
    fin_ref,
    fout_ref,
    down_ref,
    up_ref,
    out_own_ref,
    out_other_ref,
    rst_ref,
    mix_ref,
    slope_ref,
    grad_low_ref,
    norm_grad_ref,
    normed_ref,
    inv_ref,
    kept_ref,
    sent_ref,
    bias_grad_ref,
    act_ref,
    squeeze_ref,
    low_ref,
):
    step = pl.program_id(0)
    tile = x_own_ref.shape[0]
    width = x_own_ref.shape[1]
    hidden = fin_ref.shape[1]
    chunk = 512
    chunks = [slice(first, first + chunk) for first in range(0, hidden, chunk)]
    own = step < tiles // 2
    x = jnp.where(own, x_own_ref[...], x_other_ref[...]).astype(F32)
    top_own, top_other = st_own_ref[:, :GROUP, :], st_other_ref[:, :GROUP, :]
    top = jnp.maximum(top_own, top_other)
    share_own, share_other = jnp.exp2(top_own - top), jnp.exp2(top_other - top)
    inverse = 1.0 / (
        st_own_ref[:, GROUP:, :] * share_own + st_other_ref[:, GROUP:, :] * share_other
    )
    rst_ref[:, :GROUP, :] = share_own * inverse
    rst_ref[:, GROUP:, :] = share_other * inverse
    mixes = []
    for head in range(width // HEAD_DIM):
        rows = slice(head * HEAD_DIM, (head + 1) * HEAD_DIM)
        group, place = head // GROUP, head % GROUP
        mixes.append(
            (
                ot_own_ref[rows, :].astype(F32) * rst_ref[group, place : place + 1, :]
                + ot_other_ref[rows, :].astype(F32) * rst_ref[group, GROUP + place : GROUP + place + 1, :]
            ).astype(BF16)
        )
    mix = jnp.concatenate(mixes, axis=0)
    mix_ref[...] = mix
    resid_one = x + dot_tn(mix, wo_ref[...])
    centred = resid_one - row_mean(resid_one)
    inv_one = lax.rsqrt(row_mean(centred * centred) + 1e-05)
    normed = centred * inv_one
    normed_ref[...] = normed.astype(BF16)
    inv_ref[...] = inv_one
    norm_one = normed * gain_one_ref[...]
    norm_low = norm_one.astype(BF16)

    squeeze = dot_nn(norm_low, down_ref[...]) + down_bias_ref[...]
    inner = dot_nn(norm_low, fin_ref[:, chunks[0]])
    squeeze_act, squeeze_slope = gelu_pair(squeeze)
    squeeze_act = squeeze_act.astype(BF16)
    resid_two = norm_one + 4.0 * (dot_nn(squeeze_act, up_ref[...]) + up_bias_ref[...])
    for place, columns in enumerate(chunks):
        more = place + 1 < len(chunks)
        coming = dot_nn(norm_low, fin_ref[:, chunks[place + 1]]) if more else None
        act, slope = gelu_pair(inner)
        slope_ref[:, columns] = slope.astype(BF16)
        resid_two = resid_two + dot_nn(act.astype(BF16), fout_ref[columns, :])
        inner = coming

    centred = resid_two - row_mean(resid_two)
    inv_two = lax.rsqrt(row_mean(centred * centred) + 1e-05)
    normed_two = centred * inv_two
    base = jnp.where(own, scal_ref[0], scal_ref[1] - (tiles // 2) * tile) + step * tile
    place = base + lax.broadcasted_iota(jnp.int32, (tile, 1), 0)
    valid = (place < scal_ref[2]).astype(F32)
    gain_two = gain_two_ref[...]
    out = (normed_two * gain_two * valid).astype(BF16)
    upstream = jnp.where(own, og_own_ref[...], og_other_ref[...]).astype(F32) * valid * gain_two
    grad_two = inv_two * (
        upstream - row_mean(upstream) - normed_two * row_mean(upstream * normed_two)
    )
    grad_low = grad_two.astype(BF16)
    grad_adapt = 4.0 * grad_low
    grad_squeeze = (dot_nt(grad_adapt, up_ref[...]) * squeeze_slope).astype(BF16)
    norm_grad_ref[...] = (grad_two + dot_nt(grad_squeeze, down_ref[...])).astype(BF16)
    here = pl.ds(pl.multiple_of(step * tile, tile), tile)
    grad_low_ref[here, :] = grad_low
    act_ref[here, :] = squeeze_act
    squeeze_ref[here, :] = grad_squeeze
    low_ref[here, :] = norm_low
    up_bias_grad = jnp.sum(grad_adapt.astype(F32), axis=0, keepdims=True)
    down_bias_grad = jnp.sum(grad_squeeze.astype(F32), axis=0, keepdims=True)
    adapt = down_bias_grad.shape[1]

    @pl.when(own)
    def _():
        out_own_ref[...] = out

    @pl.when(jnp.logical_not(own))
    def _():
        out_other_ref[...] = out

    @pl.when(step == 0)
    def _():
        bias_grad_ref[...] = jnp.zeros_like(bias_grad_ref)
        bias_grad_ref[0:1, :] = up_bias_grad
        bias_grad_ref[1:2, :adapt] = down_bias_grad

    @pl.when(step > 0)
    def _():
        bias_grad_ref[0:1, :] += up_bias_grad
        bias_grad_ref[1:2, :adapt] += down_bias_grad

    @pl.when(step == tiles - 1)
    def _():
        first = scal_ref[3] == 0
        up_total = (4.0 * dot_tn(act_ref[...], grad_low_ref[...])).astype(BF16)
        down_total = dot_tn(squeeze_ref[...], low_ref[...]).astype(BF16)
        kept_ref[...] = jnp.where(first, up_total, down_total)
        sent_ref[...] = jnp.where(first, down_total, up_total)


def front(
    scal, x_own, x_other, ot_own, ot_other, st_own, st_other, og_own, og_other,
    w_output, attn_gain, ffn_in, ffn_out, ffn_gain, down, down_bias, up, up_bias,
):
    rows, width = x_own.shape
    tokens = 2 * rows
    hidden = ffn_in.shape[1]
    adapt = down.shape[1]
    groups = width // LANES
    tile = 256
    tiles = tokens // tile
    near = pl.BlockSpec((tile, width), lambda i: (jnp.minimum(i, tiles // 2 - 1), 0))
    far = pl.BlockSpec((tile, width), lambda i: (jnp.maximum(i - tiles // 2, 0), 0))
    row_block = pl.BlockSpec((tile, width), lambda i: (i, 0))
    column_block = pl.BlockSpec((width, tile), lambda i: (0, i))
    stats = pl.BlockSpec((groups, 2 * GROUP, tile), lambda i: (0, 0, i))
    return pl.pallas_call(
        functools.partial(front_kernel, tiles),
        grid=(tiles,),
        in_specs=[
            SMEM_SPEC, near, far, column_block, column_block, stats, stats, near, far,
            whole((1, width)), whole((1, width)), whole((1, adapt)), whole((1, width)),
        ] + [CORE_SPEC] * 5,
        out_specs=[
            near, far, stats, column_block, pl.BlockSpec((tile, hidden), lambda i: (i, 0)),
            kept((tokens, width)), row_block, row_block, pl.BlockSpec((tile, 1), lambda i: (i, 0)),
            kept((adapt, width)), kept((adapt, width)), whole((8, width)),
        ],
        out_shape=[
            shape_of((rows, width), BF16),
            shape_of((rows, width), BF16),
            shape_of((groups, 2 * GROUP, tokens), F32),
            shape_of((width, tokens), BF16),
            shape_of((tokens, hidden), BF16),
            shape_of((tokens, width), BF16),
            shape_of((tokens, width), BF16),
            shape_of((tokens, width), BF16),
            shape_of((tokens, 1), F32),
            shape_of((adapt, width), BF16),
            shape_of((adapt, width), BF16),
            shape_of((8, width), F32),
        ],
        scratch_shapes=[
            pltpu.VMEM((tokens, adapt), BF16),
            pltpu.VMEM((tokens, adapt), BF16),
            pltpu.VMEM((tokens, width), BF16),
        ],
        compiler_params=params(32 * MIB),
        cost_estimate=cost(tokens * width * (width + 2 * hidden + 6 * adapt), 60 * MIB),
    )(
        scal,
        *all_far((x_own, x_other, ot_own, ot_other, st_own, st_other, og_own, og_other)),
        attn_gain[None], ffn_gain[None], down_bias[None], up_bias[None],
        *[bring(item) for item in (w_output, ffn_in, ffn_out, down, up)],
    )


def rear_kernel(
    grad_low_ref, norm_grad_ref, slope_ref, normed_ref, inv_ref, mix_ref, gain_ref, wo_ref, fin_ref,
    fout_ref, grad_one_ref, up_ref, del_ref,
):
    hidden = fin_ref.shape[1]
    chunk = 1024
    chunks = [slice(first, first + chunk) for first in range(0, hidden, chunk)]
    grad_low = grad_low_ref[...]
    grad_norm = norm_grad_ref[...].astype(F32)
    inner = dot_nt(grad_low, fout_ref[chunks[0], :])
    for place, columns in enumerate(chunks):
        more = place + 1 < len(chunks)
        coming = dot_nt(grad_low, fout_ref[chunks[place + 1], :]) if more else None
        low = (inner * slope_ref[:, columns].astype(F32)).astype(BF16)
        grad_norm = grad_norm + dot_nt(low, fin_ref[:, columns])
        inner = coming
    grad = grad_norm * gain_ref[...]
    normed = normed_ref[...].astype(F32)
    grad_one = inv_ref[...] * (grad - row_mean(grad) - normed * row_mean(grad * normed))
    grad_low_one = grad_one.astype(BF16)
    grad_one_ref[...] = grad_low_one
    up = dot_nt(wo_ref[...], grad_low_one).astype(BF16)
    up_ref[...] = up
    product = up.astype(F32) * mix_ref[...].astype(F32)
    for head in range(product.shape[0] // HEAD_DIM):
        rows = slice(head * HEAD_DIM, (head + 1) * HEAD_DIM)
        group, place = head // GROUP, head % GROUP
        del_ref[group, place : place + 1, :] = jnp.sum(product[rows], axis=0, keepdims=True)
    del_ref[:, GROUP:, :] = jnp.zeros_like(del_ref[:, GROUP:, :])


def rear(grad_low, norm_grad, slope, normed, inv, mix, w_output, attn_gain, ffn_in, ffn_out):
    tokens, width = grad_low.shape
    hidden = ffn_in.shape[1]
    groups = width // LANES
    tile = 256
    row_block = pl.BlockSpec((tile, width), lambda i: (i, 0))
    column_block = pl.BlockSpec((width, tile), lambda i: (0, i))
    return pl.pallas_call(
        rear_kernel,
        grid=(tokens // tile,),
        in_specs=[
            row_block, row_block, pl.BlockSpec((tile, hidden), lambda i: (i, 0)), row_block,
            pl.BlockSpec((tile, 1), lambda i: (i, 0)), column_block, whole((1, width)),
        ] + [CORE_SPEC] * 3,
        out_specs=[
            row_block, column_block, pl.BlockSpec((groups, 2 * GROUP, tile), lambda i: (0, 0, i)),
        ],
        out_shape=[
            shape_of((tokens, width), BF16),
            shape_of((width, tokens), BF16),
            shape_of((groups, 2 * GROUP, tokens), F32),
        ],
        compiler_params=params(22 * MIB),
        cost_estimate=cost(tokens * width * (width + 2 * hidden), 50 * MIB),
    )(*all_far((grad_low, norm_grad, slope, normed, inv, mix)), attn_gain[None], bring(w_output), bring(ffn_in), bring(ffn_out))


def input_grad_kernel(merged, *refs):
    place_ref, grad_ref, dq_ref, dk_ref, dv_ref, wq_ref, wk_ref, wv_ref = refs[:8]
    total = grad_ref[...].astype(F32) + dot_nt(dq_ref[...], wq_ref[...])
    total = total + dot_nt(dk_ref[...], wk_ref[...])
    total = total + dot_nt(dv_ref[...], wv_ref[...])
    total = total.astype(BF16)
    if merged:
        merge_kernel(place_ref, total, *refs[8:])
    else:
        refs[8][...] = total


def input_grad(place, half, grad_one, dq, dk, dv, w_query, w_key, w_value, arrived):
    rows, width = dk.shape
    step = rows // 2
    block = pl.BlockSpec((step, width), lambda i: (i, 0))
    return pl.pallas_call(
        functools.partial(input_grad_kernel, len(arrived)),
        grid=(2,),
        in_specs=[SMEM_SPEC, pl.BlockSpec((step, width), lambda i: (2 * half + i, 0))]
        + [block] * 3
        + [CORE_SPEC] * 3
        + [block] * len(arrived),
        out_specs=pl.BlockSpec((step, 2, width), lambda i: (i, 0, 0)) if arrived else block,
        out_shape=shape_of((rows, 2, width) if arrived else (rows, width), BF16),
        compiler_params=params(16 * MIB),
        cost_estimate=cost(3 * rows * width * width, 14 * MIB),
    )(
        place,
        *all_far((grad_one, dq, dk, dv)),
        bring(w_query),
        bring(w_key),
        bring(w_value),
        *all_far(arrived),
    )


def swap(value, seq_bit, dp_bits):
    width = lax.axis_size("dp")
    count = lax.axis_size("seq") * width
    pairs = [
        (device, ((device // width) ^ seq_bit) * width + ((device % width) ^ dp_bits))
        for device in range(count)
    ]
    return lax.ppermute(value, ("seq", "dp"), pairs)


def gather_line(value):
    width = lax.axis_size("dp")
    groups = [[4 * line + place for line in range(width // 4)] for place in range(4)]
    return lax.all_gather(value, "dp", axis_index_groups=groups)


def total(values):
    return jnp.sum(values.astype(F32), axis=0)


def square_place():
    return 2 * ((lax.axis_index("dp") // 2) % 2) + lax.axis_index("seq")


def square_swaps(values):
    return [swap(values[offset - 1], offset % 2, 2 * (offset // 2)) for offset in range(1, 4)]


def sum_square(value):
    place = square_place()
    quarters = value.reshape(4, value.shape[0] // 4, value.shape[1])
    pick = [
        lax.dynamic_index_in_dim(quarters, place ^ offset, 0, keepdims=False) for offset in range(4)
    ]
    return pick[:1] + square_swaps(pick[1:])


def line_swaps(value):
    lines = lax.axis_size("dp") // 4
    return [swap(value, 0, 4 * offset) for offset in range(1, lines)]


def add(terms):
    value = terms[0].astype(F32)
    for term in terms[1:]:
        value = value + term.astype(F32)
    return value.astype(BF16)


def tie(*values):
    return lax.optimization_barrier(values)


def spread_kernel(scal_ref, half_ref, far_ref, up_ref, down_ref):
    first = scal_ref[3] == 0
    half, other = half_ref[...].astype(F32), far_ref[...].astype(F32)
    up_ref[...] = jnp.where(first, half, other)
    down_ref[...] = jnp.where(first, other, half).T


def spread(scal, half, other):
    adapt, width = half.shape
    step = adapt // 2
    block = pl.BlockSpec((step, width), lambda i: (i, 0))
    return pl.pallas_call(
        spread_kernel,
        grid=(2,),
        in_specs=[SMEM_SPEC, block, block],
        out_specs=[block, pl.BlockSpec((width, step), lambda i: (0, i))],
        out_shape=[shape_of((adapt, width), F32), shape_of((width, adapt), F32)],
        compiler_params=params(16 * MIB),
        cost_estimate=cost(0, 12 * adapt * width),
    )(scal, half, other)


def on_pair(
    hidden_in,
    lengths,
    w_query,
    w_key,
    w_value,
    w_output,
    attn_gain,
    ffn_in,
    ffn_out,
    ffn_gain,
    adapter_down,
    adapter_down_bias,
    adapter_up,
    adapter_up_bias,
    prefix_embed,
    prefix_hidden_w,
    prefix_hidden_b,
    prefix_out_w,
    prefix_out_b,
    out_grad,
):
    rows, _, width = hidden_in.shape
    count = prefix_embed.shape[0]
    position = lax.axis_index("seq")
    place = position.reshape(1).astype(jnp.int32)
    length = lax.dynamic_index_in_dim(lengths, position, 0, keepdims=False)
    core = lax.axis_index("dp") % 2
    scal = jnp.stack([position * rows, (1 - position) * rows, length, core]).astype(jnp.int32)

    x_own, x_send = split(place, hidden_in)
    x_other = shifted(x_send, "seq", 1)
    og_own, og_send = split(place, out_grad)
    og_other = shifted(og_send, "seq", 1)

    embed = jnp.pad(prefix_embed, ((0, PAD - count), (0, 0)))
    prefix_act, prefix_keys, prefix_values = prefix_forward(
        embed, prefix_hidden_w, prefix_hidden_b, prefix_out_w, prefix_out_b
    )
    lead = (prefix_keys, prefix_values)
    triple = project(0, x_own, w_query, w_key, w_value, ())
    near = attend(count, scal, 0, 0, 1, *triple, lead, ())
    q, k, v = project(1, x_other, w_query, w_key, w_value, triple)
    pt_own, ot_own, st_own, lead_weights = attend(count, scal, 0, 1, 1, q, k, v, lead, near)
    pt_other, ot_other, st_other = attend(0, scal, 1, 0, 2, q, k, v, (), ())

    (
        out_own, out_send, shares, mix, slope, grad_low, norm_grad, normed, inv_one,
        adapt_kept, adapt_sent, bias_grads,
    ) = front(
        scal, x_own, x_other, ot_own, ot_other, st_own, st_other, og_own, og_other,
        w_output, attn_gain, ffn_in, ffn_out, ffn_gain, adapter_down, adapter_down_bias,
        adapter_up, adapter_up_bias,
    )
    out_other = shifted(out_send, "seq", 1)
    core_terms = [adapt_kept, swap(adapt_sent, 0, 1)]
    grad_one, upstream, deltas = rear(
        grad_low, norm_grad, slope, normed, inv_one, mix, w_output, attn_gain, ffn_in, ffn_out
    )
    upstream, out_other, adapt_sum = tie(upstream, out_other, add(core_terms))
    square_terms = sum_square(adapt_sum)
    pair, dqt = lead_backward(
        count, q, upstream, shares, deltas, lead_weights, prefix_keys, prefix_values, bias_grads
    )
    pair_core = swap(pair, 0, 1)

    back = (q, k, v)
    part_own, dk_other, dv_other = attend_back(
        1, 0, False, False, *back, upstream, shares, deltas, pt_other, dqt, ()
    )
    dk_other, pair, adapt_sum = tie(dk_other, add([pair, pair_core]), add(square_terms))
    adapt_line = gather_line(adapt_sum)
    pair_square = square_swaps([pair] * 3)
    part_other, dk_other, dv_other = attend_back(
        1, 1, False, True, *back, upstream, shares, deltas, pt_other, dqt, (dk_other, dv_other)
    )
    part_other, pair = tie(part_other, add([pair] + pair_square))
    pair_line = line_swaps(pair)
    dq_other, dk_own, dv_own = attend_back(
        0, 1, True, False, *back, upstream, shares, deltas, pt_own, part_other, ()
    )
    triple_weights = (w_query, w_key, w_value)
    grad_other = input_grad(place, 1, grad_one, dq_other, dk_other, dv_other, *triple_weights, ())
    grad_back = shifted(grad_other, "seq", 1)
    adapt_sum = jnp.sum(adapt_line.astype(F32), axis=0).astype(BF16)
    dk_own, adapt_sum, *pair_line = tie(dk_own, adapt_sum, *pair_line)
    adapt_square = square_swaps([adapt_sum] * 3)
    dq_own, dk_own, dv_own = attend_back(
        0, 0, True, True, *back, upstream, shares, deltas, pt_own, part_own, (dk_own, dv_own)
    )
    dq_own, pair, out_other = tie(dq_own, pair, out_other)
    prefix_grads = prefix_backward(
        count,
        adapter_down_bias.shape[0],
        [pair, *pair_line],
        prefix_act,
        embed,
        prefix_hidden_w,
        prefix_out_w,
    )
    layer_out = merge(place, out_own, out_other)
    dq_own, layer_out, out_w_grad, *adapt_square = tie(
        dq_own, layer_out, prefix_grads[3], *adapt_square
    )
    adapt_half = jnp.stack([adapt_sum] + adapt_square)
    place_here = square_place()
    adapt_half = jnp.concatenate(
        [lax.dynamic_slice_in_dim(adapt_half, spot ^ place_here, 1, 0) for spot in range(4)]
    ).reshape(adapt_kept.shape)
    adapt_far = swap(adapt_half, 0, 1)
    input_total = input_grad(
        place, 0, grad_one, dq_own, dk_own, dv_own, *triple_weights, (grad_back,)
    )
    up_total, down_total = spread(scal, adapt_half, adapt_far)
    return (
        layer_out,
        input_total,
        down_total,
        prefix_grads[6][0],
        up_total,
        prefix_grads[5][0],
        prefix_grads[0],
        prefix_grads[1],
        prefix_grads[2][0],
        out_w_grad,
        prefix_grads[4][0],
    )


def solution(mesh):
    in_specs = (
        P("seq", "dp", None),
        P("dp"),
        P(),
        P(),
        P(),
        P(),
        P(),
        P(),
        P(),
        P(),
        P(),
        P(),
        P(),
        P(),
        P(),
        P(),
        P(),
        P(),
        P(),
        P("seq", "dp", None),
    )
    out_specs = (
        P("seq", "dp", None),
        P("seq", "dp", None),
        P(),
        P(),
        P(),
        P(),
        P(),
        P(),
        P(),
        P(),
        P(),
    )
    pairs = mesh.shape["seq"] == 2 and mesh.shape["dp"] % 8 == 0

    def on_one(*arrays):
        step = on_pair if pairs and arrays[0].shape[1] == 2 else on_device
        return step(*arrays)

    return jax.shard_map(
        on_one, mesh=mesh, in_specs=in_specs, out_specs=out_specs, check_vma=False
    )
```

```python
import functools
import math

import jax
import jax.numpy as jnp
from jax import lax
from jax.experimental import pallas as pl
from jax.experimental.pallas import tpu as pltpu
from jax.sharding import PartitionSpec as P

HEADS = 16


HIGHEST_PRECISION = lax.Precision.HIGHEST


def shifted(value, axis, steps):
    count = lax.axis_size(axis)
    pairs = [(source, (source + steps) % count) for source in range(count)]
    return lax.ppermute(value, axis, pairs)


def mixed(left, right):
    return jnp.dot(left, right, preferred_element_type=jnp.float32)


def mixed_left(left, right):
    return lax.dot_general(
        left, right, (((0,), (0,)), ((), ())), preferred_element_type=jnp.float32
    )


def mixed_right(left, right):
    return lax.dot_general(
        left, right, (((1,), (1,)), ((), ())), preferred_element_type=jnp.float32
    )


def precise(left, right):
    return jnp.dot(left, right, precision=HIGHEST_PRECISION, preferred_element_type=jnp.float32)


def precise_left(left, right):
    return lax.dot_general(
        left,
        right,
        (((0,), (0,)), ((), ())),
        precision=HIGHEST_PRECISION,
        preferred_element_type=jnp.float32,
    )


def precise_right(left, right):
    return lax.dot_general(
        left,
        right,
        (((1,), (1,)), ((), ())),
        precision=HIGHEST_PRECISION,
        preferred_element_type=jnp.float32,
    )


def gelu_value(inputs):
    return 0.5 * inputs * (1.0 + lax.erf(inputs * 0.7071067811865476))


def gelu_slope(inputs):
    return (
        0.5 * (1.0 + lax.erf(inputs * 0.7071067811865476))
        + inputs * jnp.exp(-0.5 * inputs * inputs) * 0.3989422804014327
    )


def normalize(values):
    row_mean = jnp.mean(values, axis=-1, keepdims=True)
    centred = values - row_mean
    spread = jnp.mean(centred * centred, axis=-1, keepdims=True)
    inv_std = lax.rsqrt(spread + 1e-05)
    return (centred * inv_std, inv_std)


def norm_back(upstream, normed, inv_std):
    mean_grad = jnp.mean(upstream, axis=-1, keepdims=True)
    mean_proj = jnp.mean(upstream * normed, axis=-1, keepdims=True)
    return inv_std * (upstream - mean_grad - normed * mean_proj)


def key_allowed(offset, key_count, seq_lengths):
    places = offset + lax.iota(jnp.int32, key_count)
    return places[None, :] < seq_lengths[:, None]


def lead_state(queries4, prefix_keys4, prefix_values4):
    inv_root = 1.0 / math.sqrt(queries4.shape[3])
    scores = (
        jnp.einsum("rshd,phd->rshp", queries4, prefix_keys4, preferred_element_type=jnp.float32)
        * inv_root
    )
    running_max = jnp.max(scores, axis=3)
    weights = jnp.exp(scores - running_max[..., None])
    running_sum = jnp.sum(weights, axis=3)
    running_mix = jnp.einsum(
        "rshp,phd->rshd",
        weights.astype(jnp.bfloat16),
        prefix_values4,
        preferred_element_type=jnp.float32,
    )
    return (running_max, running_sum, running_mix)


def fold_block(carried, key_block, value_block, offset, queries4, seq_lengths):
    key_count, seqs_here = (key_block.shape[0], key_block.shape[1])
    head_count, head_dim = (queries4.shape[2], queries4.shape[3])
    inv_root = 1.0 / math.sqrt(head_dim)
    keys4 = key_block.reshape(key_count, seqs_here, head_count, head_dim)
    values4 = value_block.reshape(key_count, seqs_here, head_count, head_dim)
    running_max, running_sum, running_mix = carried
    scores = (
        jnp.einsum("rshd,tshd->rsht", queries4, keys4, preferred_element_type=jnp.float32)
        * inv_root
    )
    allowed = key_allowed(offset, key_count, seq_lengths)[None, :, None, :]
    scores = jnp.where(allowed, scores, -jnp.inf)
    new_max = jnp.maximum(running_max, jnp.max(scores, axis=3))
    weights = jnp.exp(scores - new_max[..., None])
    rescale = jnp.exp(running_max - new_max)
    running_sum = running_sum * rescale + jnp.sum(weights, axis=3)
    running_mix = running_mix * rescale[..., None] + jnp.einsum(
        "rsht,tshd->rshd", weights.astype(jnp.bfloat16), values4, preferred_element_type=jnp.float32
    )
    return (new_max, running_sum, running_mix)


def lead_back(queries4, upstream4, log_total, row_delta, prefix_keys4, prefix_values4):
    inv_root = 1.0 / math.sqrt(queries4.shape[3])
    scores = (
        jnp.einsum("rshd,phd->rshp", queries4, prefix_keys4, preferred_element_type=jnp.float32)
        * inv_root
    )
    weights = jnp.exp(scores - log_total[..., None])
    weight_grads = jnp.einsum(
        "rshd,phd->rshp", upstream4, prefix_values4, preferred_element_type=jnp.float32
    )
    score_grads = (weights * (weight_grads - row_delta[..., None])).astype(jnp.bfloat16)
    query_term = (
        jnp.einsum("rshp,phd->rshd", score_grads, prefix_keys4, preferred_element_type=jnp.float32)
        * inv_root
    )
    key_term = (
        jnp.einsum("rshp,rshd->phd", score_grads, queries4, preferred_element_type=jnp.float32)
        * inv_root
    )
    value_term = jnp.einsum(
        "rshp,rshd->phd",
        weights.astype(jnp.bfloat16),
        upstream4,
        preferred_element_type=jnp.float32,
    )
    return (query_term, key_term, value_term)


def block_back(
    queries4, upstream4, log_total, row_delta, key_block, value_block, offset, seq_lengths
):
    key_count, seqs_here, model_width = key_block.shape
    head_count, head_dim = (queries4.shape[2], queries4.shape[3])
    inv_root = 1.0 / math.sqrt(head_dim)
    keys4 = key_block.reshape(key_count, seqs_here, head_count, head_dim)
    values4 = value_block.reshape(key_count, seqs_here, head_count, head_dim)
    scores = (
        jnp.einsum("rshd,tshd->rsht", queries4, keys4, preferred_element_type=jnp.float32)
        * inv_root
    )
    allowed = key_allowed(offset, key_count, seq_lengths)[None, :, None, :]
    scores = jnp.where(allowed, scores, -jnp.inf)
    weights = jnp.exp(scores - log_total[..., None])
    weight_grads = jnp.einsum(
        "rshd,tshd->rsht", upstream4, values4, preferred_element_type=jnp.float32
    )
    score_grads = (weights * (weight_grads - row_delta[..., None])).astype(jnp.bfloat16)
    query_term = (
        jnp.einsum("rsht,tshd->rshd", score_grads, keys4, preferred_element_type=jnp.float32)
        * inv_root
    )
    key_term = (
        jnp.einsum("rsht,rshd->tshd", score_grads, queries4, preferred_element_type=jnp.float32)
        * inv_root
    )
    value_term = jnp.einsum(
        "rsht,rshd->tshd",
        weights.astype(jnp.bfloat16),
        upstream4,
        preferred_element_type=jnp.float32,
    )
    pair_term = jnp.stack(
        [
            key_term.reshape(key_count, seqs_here, model_width),
            value_term.reshape(key_count, seqs_here, model_width),
        ]
    )
    return (query_term, pair_term)


def prefix_back(pair_grad, prefix_act, prefix_embed, hidden_weight, out_weight):
    out_w_grad = precise_left(prefix_act, pair_grad)
    out_b_grad = jnp.sum(pair_grad, axis=0)
    act_grad = precise_right(pair_grad, out_weight) * (1.0 - prefix_act * prefix_act)
    hidden_w_grad = precise_left(prefix_embed, act_grad)
    hidden_b_grad = jnp.sum(act_grad, axis=0)
    embed_grad = precise_right(act_grad, hidden_weight)
    return (embed_grad, hidden_w_grad, hidden_b_grad, out_w_grad, out_b_grad)


def on_device(
    hidden_in,
    lengths,
    w_query,
    w_key,
    w_value,
    w_output,
    attn_gain,
    ffn_in,
    ffn_out,
    ffn_gain,
    adapter_down,
    adapter_down_bias,
    adapter_up,
    adapter_up_bias,
    prefix_embed,
    prefix_hidden_w,
    prefix_hidden_b,
    prefix_out_w,
    prefix_out_b,
    out_grad,
):
    rows_here, seqs_here, model_width = hidden_in.shape
    token_count = rows_here * seqs_here
    head_count = HEADS
    head_dim = model_width // head_count
    axis_count = lax.axis_size("seq")
    position = lax.axis_index("seq")
    tokens = hidden_in.reshape(token_count, model_width)
    projected = jnp.stack([mixed(tokens, w_query), mixed(tokens, w_key), mixed(tokens, w_value)])
    triple = projected.astype(jnp.bfloat16).reshape(3, rows_here, seqs_here, model_width)
    hidden_weight = prefix_hidden_w.astype(jnp.float32)
    out_weight = prefix_out_w.astype(jnp.float32)
    prefix_act = jnp.tanh(precise(prefix_embed, hidden_weight) + prefix_hidden_b)
    prefix_pair = precise(prefix_act, out_weight) + prefix_out_b
    prefix_keys4 = (
        prefix_pair[:, :model_width].astype(jnp.bfloat16).reshape(-1, head_count, head_dim)
    )
    prefix_values4 = (
        prefix_pair[:, model_width:].astype(jnp.bfloat16).reshape(-1, head_count, head_dim)
    )
    row_places = position * rows_here + lax.iota(jnp.int32, rows_here)
    valid = (row_places[:, None] < lengths[None, :]).astype(jnp.float32).reshape(token_count, 1)
    queries4 = triple[0].reshape(rows_here, seqs_here, head_count, head_dim)
    key_value = triple[1:]
    pieces = lax.all_gather(key_value, "seq", axis=1, tiled=True)
    carried = fold_block(
        lead_state(queries4, prefix_keys4, prefix_values4),
        pieces[0],
        pieces[1],
        jnp.int32(0),
        queries4,
        lengths,
    )
    mix_full = carried[2] / carried[1][..., None]
    log_total = carried[0] + jnp.log(carried[1])
    mix_low = mix_full.astype(jnp.bfloat16).reshape(token_count, model_width)
    attn_proj = mixed(mix_low, w_output)
    normed_one, inv_one = normalize(tokens.astype(jnp.float32) + attn_proj)
    norm_one = normed_one * attn_gain
    norm_low = norm_one.astype(jnp.bfloat16)
    inner_pre = mixed(norm_low, ffn_in)
    inner_act = gelu_value(inner_pre).astype(jnp.bfloat16)
    squeeze = mixed(norm_low, adapter_down) + adapter_down_bias
    squeeze_act = gelu_value(squeeze).astype(jnp.bfloat16)
    ffn_sum = mixed(inner_act, ffn_out)
    adapter_sum = mixed(squeeze_act, adapter_up) + adapter_up_bias
    normed_two, inv_two = normalize(norm_one + ffn_sum + 4.0 * adapter_sum)
    layer_out = (
        (normed_two * ffn_gain * valid)
        .astype(jnp.bfloat16)
        .reshape(rows_here, seqs_here, model_width)
    )
    upstream_top = out_grad.reshape(token_count, model_width).astype(jnp.float32) * valid
    grad_two = norm_back(upstream_top * ffn_gain, normed_two, inv_two)
    grad_ffn_low = grad_two.astype(jnp.bfloat16)
    grad_adapt_low = (4.0 * grad_two).astype(jnp.bfloat16)
    up_grad = mixed_left(squeeze_act, grad_adapt_low)
    up_bias_grad = jnp.sum(grad_adapt_low.astype(jnp.float32), axis=0)
    grad_squeeze_low = (mixed_right(grad_adapt_low, adapter_up) * gelu_slope(squeeze)).astype(
        jnp.bfloat16
    )
    down_grad = mixed_left(norm_low, grad_squeeze_low)
    down_bias_grad = jnp.sum(grad_squeeze_low.astype(jnp.float32), axis=0)
    grad_inner_low = (mixed_right(grad_ffn_low, ffn_out) * gelu_slope(inner_pre)).astype(
        jnp.bfloat16
    )
    grad_norm = (
        grad_two + mixed_right(grad_squeeze_low, adapter_down) + mixed_right(grad_inner_low, ffn_in)
    )
    grad_one = norm_back(grad_norm * attn_gain, normed_one, inv_one)
    grad_attn_low = grad_one.astype(jnp.bfloat16)
    grad_mix_low = mixed_right(grad_attn_low, w_output).astype(jnp.bfloat16)
    upstream4 = grad_mix_low.reshape(rows_here, seqs_here, head_count, head_dim)
    row_delta = jnp.sum(upstream4.astype(jnp.float32) * mix_full, axis=3)
    query_grad, prefix_key_grad, prefix_value_grad = lead_back(
        queries4, upstream4, log_total, row_delta, prefix_keys4, prefix_values4
    )

    def visit(step_index, carried):
        moving, grads_moving, query_total = carried
        source = (position - step_index) % axis_count
        query_term, pair_term = block_back(
            queries4,
            upstream4,
            log_total,
            row_delta,
            moving[0],
            moving[1],
            source * rows_here,
            lengths,
        )
        return (moving, grads_moving + pair_term, query_total + query_term)

    def travel(step_index, carried):
        moving, grads_moving, query_total = visit(step_index, carried)
        moving = shifted(moving, "seq", 1)
        grads_moving = shifted(grads_moving.astype(jnp.bfloat16), "seq", 1).astype(
            grads_moving.dtype
        )
        return (moving, grads_moving, query_total)

    initial = (
        key_value,
        jnp.zeros((2, rows_here, seqs_here, model_width), jnp.float32),
        query_grad,
    )
    carried = lax.fori_loop(0, axis_count - 1, travel, initial)
    carried = visit(axis_count - 1, carried)
    pair_grads = shifted(carried[1].astype(jnp.bfloat16), "seq", 1).astype(jnp.float32)
    triple_grad = jnp.concatenate(
        [carried[2].reshape(1, rows_here, seqs_here, model_width), pair_grads]
    ).astype(jnp.bfloat16)
    hidden_grad = grad_one + mixed_right(triple_grad[0].reshape(token_count, model_width), w_query)
    hidden_grad = hidden_grad + mixed_right(triple_grad[1].reshape(token_count, model_width), w_key)
    hidden_grad = hidden_grad + mixed_right(
        triple_grad[2].reshape(token_count, model_width), w_value
    )
    hidden_grad = hidden_grad.astype(jnp.bfloat16).reshape(rows_here, seqs_here, model_width)
    pair_grad = jnp.concatenate(
        [prefix_key_grad.reshape(-1, model_width), prefix_value_grad.reshape(-1, model_width)],
        axis=1,
    )
    prefix_grads = prefix_back(pair_grad, prefix_act, prefix_embed, hidden_weight, out_weight)
    summed = lax.psum(
        (
            down_grad,
            down_bias_grad,
            up_grad,
            up_bias_grad,
            prefix_grads[0],
            prefix_grads[1],
            prefix_grads[2],
            prefix_grads[3],
            prefix_grads[4],
        ),
        ("seq", "dp"),
    )
    adapter_totals = summed[:4]
    prefix_totals = summed[4:]
    return (
        layer_out,
        hidden_grad,
        adapter_totals[0],
        adapter_totals[1],
        adapter_totals[2],
        adapter_totals[3],
        prefix_totals[0],
        prefix_totals[1],
        prefix_totals[2],
        prefix_totals[3],
        prefix_totals[4],
    )


BF16 = jnp.bfloat16
F32 = jnp.float32
MIB = 1024 * 1024
GROUP = 4
HEAD_DIM = 64
LANES = GROUP * HEAD_DIM
PAD = 32
MASKED = -1e30
LOG2E = 1.4426950408889634
VMEM_LIMIT = 60 * MIB


def dot_nn(left, right):
    return lax.dot_general(left, right, (((1,), (0,)), ((), ())), preferred_element_type=F32)


def dot_nt(left, right):
    return lax.dot_general(left, right, (((1,), (1,)), ((), ())), preferred_element_type=F32)


def dot_tn(left, right):
    return lax.dot_general(left, right, (((0,), (0,)), ((), ())), preferred_element_type=F32)


def shape_of(shape, dtype):
    return pltpu.HBM(shape, dtype)


def far(value):
    return pltpu.with_memory_space_constraint(value, pltpu.HBM)


def bring(value):
    return pltpu.with_memory_space_constraint(value, pltpu.VMEM)


def all_far(values):
    return [far(value) for value in values]


def params(limit=VMEM_LIMIT):
    return pltpu.CompilerParams(vmem_limit_bytes=limit)


def cost(macs, moved):
    return pl.CostEstimate(flops=int(2 * macs), bytes_accessed=int(moved), transcendentals=0)


SMEM_SPEC = pl.BlockSpec(memory_space=pltpu.SMEM)
ANY_SPEC = pl.BlockSpec(memory_space=pl.ANY)
CORE_SPEC = pl.BlockSpec(memory_space=pltpu.VMEM)


def whole(shape):
    return pl.BlockSpec(shape, lambda *_: (0,) * len(shape))


def kept(shape):
    return pl.BlockSpec(shape, lambda *_: (0,) * len(shape), pipeline_mode=pl.Buffered(1))


def split_kernel(place_ref, both_ref, own_ref, other_ref):
    apart = jnp.swapaxes(both_ref[...], 0, 1)
    first = place_ref[0] == 0
    own_ref[...] = jnp.where(first, apart[0], apart[1])
    other_ref[...] = jnp.where(first, apart[1], apart[0])


def split(place, both):
    rows, _, width = both.shape
    step = rows // 4
    half = pl.BlockSpec((step, width), lambda i: (i, 0))
    return pl.pallas_call(
        split_kernel,
        grid=(4,),
        in_specs=[SMEM_SPEC, pl.BlockSpec((step, 2, width), lambda i: (i, 0, 0))],
        out_specs=[half, half],
        out_shape=[shape_of((rows, width), both.dtype)] * 2,
        compiler_params=params(8 * MIB),
        cost_estimate=cost(0, 4 * rows * width * 2),
    )(place, far(both))


def merge_kernel(place_ref, own_ref, other_ref, both_ref):
    first = place_ref[0] == 0
    own, other = own_ref[...], other_ref[...]
    apart = jnp.stack([jnp.where(first, own, other), jnp.where(first, other, own)])
    both_ref[...] = jnp.swapaxes(apart, 0, 1)


def parts_of(values, count):
    parts = []
    for _ in range(count):
        part = values.astype(BF16)
        parts.append(part)
        values = values - part.astype(F32)
    return parts


def exact_dot(values, weight, dot):
    rows = values.shape[0]
    product = dot(jnp.concatenate(parts_of(values, 3), axis=0), weight)
    return product[:rows] + product[rows : 2 * rows] + product[2 * rows :]


def prefix_kernel(embed_ref, hw_ref, hb_ref, ow_ref, ob_ref, act_ref, key_ref, value_ref):
    width = key_ref.shape[1]
    act = jnp.tanh(exact_dot(embed_ref[...], hw_ref[...], dot_nn) + hb_ref[...])
    act_ref[...] = act
    pair = exact_dot(act, ow_ref[...], dot_nn) + ob_ref[...]
    key_ref[...] = pair[:, :width].astype(BF16)
    value_ref[...] = pair[:, width:].astype(BF16)


def prefix_forward(embed, hidden_w, hidden_b, out_w, out_b):
    width, hidden = hidden_w.shape
    return pl.pallas_call(
        prefix_kernel,
        out_shape=[
            shape_of((PAD, hidden), F32),
            shape_of((PAD, width), BF16),
            shape_of((PAD, width), BF16),
        ],
        compiler_params=params(16 * MIB),
        cost_estimate=cost(3 * PAD * hidden * 3 * width * 4, 6 * hidden * width),
    )(embed, hidden_w, hidden_b[None], out_w, out_b[None])


def prefix_back_kernel(
    count, pairs_ref, act_ref, embed_ref, hw_ref, ow_ref, place_ref, own_ref, other_ref,
    both_ref, eg_ref, hwg_ref, hbg_ref, owg_ref, obg_ref, ubg_ref, dbg_ref,
):
    merge_kernel(place_ref, own_ref[...], other_ref, both_ref)
    total = pairs_ref[0]
    for line in range(1, pairs_ref.shape[0]):
        total = total + pairs_ref[line]
    ubg_ref[...] = total[count : count + 1]
    dbg_ref[...] = total[count + 1 : count + 2, : dbg_ref.shape[1]]
    pair = jnp.concatenate([total[:PAD], total[PAD:]], axis=1)
    rows = lax.broadcasted_iota(jnp.int32, pair.shape, 0)
    pair = jnp.where(rows < count, pair, 0.0)
    act = act_ref[...]
    obg_ref[...] = jnp.sum(pair, axis=0, keepdims=True)
    high, low = parts_of(pair, 2)
    back = dot_nt(jnp.concatenate([high, low], axis=0), ow_ref[...])
    act_grad = (back[:PAD] + back[PAD:]) * (1.0 - act * act)
    act_high, act_low = parts_of(act, 2)
    owg_ref[...] = dot_tn(
        jnp.concatenate([act_high, act_low, act_high], axis=0),
        jnp.concatenate([high, high, low], axis=0),
    )
    hbg_ref[...] = jnp.sum(act_grad, axis=0, keepdims=True)
    high, low = parts_of(act_grad, 2)
    embed_high, embed_low = parts_of(embed_ref[...], 2)
    hwg_ref[...] = dot_tn(
        jnp.concatenate([embed_high, embed_low, embed_high], axis=0),
        jnp.concatenate([high, high, low], axis=0),
    )
    back = dot_nt(jnp.concatenate([high, low], axis=0), hw_ref[...])
    eg_ref[...] = (back[:PAD] + back[PAD:])[:count]


def prefix_backward(count, adapt, pairs, act, embed, hidden_w, out_w, place, own, other):
    width, hidden = hidden_w.shape
    core = [CORE_SPEC] * 5
    return pl.pallas_call(
        functools.partial(prefix_back_kernel, count),
        in_specs=core + [SMEM_SPEC, CORE_SPEC, CORE_SPEC],
        out_shape=[
            shape_of((own.shape[0], 2, width), BF16),
            shape_of((count, width), F32),
            shape_of((width, hidden), F32),
            shape_of((1, hidden), F32),
            shape_of((hidden, 2 * width), F32),
            shape_of((1, 2 * width), F32),
            shape_of((1, width), F32),
            shape_of((1, adapt), F32),
        ],
        compiler_params=params(24 * MIB),
        cost_estimate=cost(96 * hidden * width * 6, 20 * hidden * width),
    )(pairs, act, embed, hidden_w, out_w, place, far(own), far(other))


def project_kernel(x_ref, wq_ref, wk_ref, wv_ref, *refs):
    q_ref, k_ref, v_ref = refs[-3:]
    x = x_ref[...]
    scale = LOG2E / math.sqrt(HEAD_DIM)
    q_ref[...] = (dot_nn(x, wq_ref[...]) * scale).astype(BF16)
    k_ref[...] = dot_nn(x, wk_ref[...]).astype(BF16)
    v_ref[...] = dot_nn(x, wv_ref[...]).astype(BF16)


def project(half, x, w_query, w_key, w_value, earlier):
    rows, width = x.shape
    step = rows // 2
    return pl.pallas_call(
        project_kernel,
        grid=(2,),
        in_specs=[pl.BlockSpec((step, width), lambda i: (i, 0))]
        + [CORE_SPEC] * 3
        + [ANY_SPEC] * len(earlier),
        out_specs=[pl.BlockSpec((step, width), lambda i: (2 * half + i, 0))] * 3,
        out_shape=[shape_of((2 * rows, width), BF16)] * 3,
        input_output_aliases={4 + i: i for i in range(len(earlier))},
        compiler_params=params(14 * MIB),
        cost_estimate=cost(3 * rows * width * width, 2 * (4 * rows * width + 3 * width * width)),
    )(far(x), bring(w_query), bring(w_key), bring(w_value), *all_far(earlier))


def head_lanes(head, rows, lanes):
    place = lax.broadcasted_iota(jnp.int32, (rows, lanes), 1)
    return (place // HEAD_DIM == head).astype(F32).astype(BF16)


def first_lane(values):
    lane = lax.broadcasted_iota(jnp.int32, (values.shape[0], 128), 1)
    return jnp.where(lane == 0, values, 0.0).astype(BF16)


def block_diagonal(rows):
    return jnp.concatenate(
        [rows * head_lanes(head, rows.shape[0], LANES) for head in range(GROUP)], axis=0
    )


def attend_kernel(
    prefixed, first, scal_ref, q_ref, k_ref, v_ref, pk_ref, pv_ref, *refs
):
    pt_ref, ot_ref, st_ref, pp_ref, *scores = refs[-6:]
    keys = k_ref.shape[0]
    queries = q_ref.shape[0]
    half = (pl.program_id(0) + first) // 2

    def quadrant(count):
        place = scal_ref[half] + lax.broadcasted_iota(jnp.int32, (keys, 128), 0)
        bias = first_lane(jnp.where(place < scal_ref[2], 0.0, MASKED))
        ones = first_lane(jnp.ones((queries, 128), F32))
        tail = jnp.ones((16, keys), BF16)
        masks = [head_lanes(head, queries, 128) for head in range(2)]

        def score(head):
            pair = slice((head // 2) * 128, (head // 2 + 1) * 128)
            k_aug = jnp.concatenate([k_ref[:, pair], bias], axis=1)
            q_aug = jnp.concatenate([q_ref[:, pair] * masks[head % 2], ones], axis=1)
            scores[head % 2][...] = dot_nt(k_aug, q_aug)

        def weigh(head):
            own = scores[head % 2]
            top = jnp.max(own[...], axis=0, keepdims=True)
            if count:
                lead_scores = lead[head * PAD : (head + 1) * PAD]
                top = jnp.maximum(top, jnp.max(lead_scores, axis=0, keepdims=True))
            pt_ref[head] = jnp.exp2(own[...] - top).astype(BF16)
            st_ref[0, head : head + 1, :] = top
            if not count:
                return 0.0
            lead_weights = jnp.exp2(lead_scores - top).astype(BF16)
            pp_ref[0, head * PAD : (head + 1) * PAD, :] = lead_weights
            return jnp.sum(lead_weights.astype(F32), axis=0, keepdims=True)

        def mix(head, lead_total):
            rows = slice(head * HEAD_DIM, (head + 1) * HEAD_DIM)
            mixed_rows = dot_nn(jnp.concatenate([turned[rows], tail], axis=0), pt_ref[head])
            mixed = mixed_rows[:HEAD_DIM]
            if count:
                lead_weights = pp_ref[0, head * PAD : (head + 1) * PAD, :]
                mixed = mixed + dot_nn(lead_turned[rows], lead_weights)
            ot_ref[rows, :] = mixed.astype(BF16)
            total_row = mixed_rows[HEAD_DIM : HEAD_DIM + 1] + lead_total
            st_ref[0, GROUP + head : GROUP + head + 1, :] = total_row

        score(0)
        turned = v_ref[...].T
        if count:
            lead_turned = pv_ref[...].T
            lead = dot_nt(block_diagonal(pk_ref[...]), q_ref[...])
            row = lax.broadcasted_iota(jnp.int32, lead.shape, 0)
            lead = jnp.where(row % PAD < count, lead, MASKED)
        lead_totals = []
        for head in range(GROUP):
            if head + 1 < GROUP:
                score(head + 1)
            lead_totals.append(weigh(head))
            if head:
                mix(head - 1, lead_totals[head - 1])
        mix(GROUP - 1, lead_totals[GROUP - 1])

    @pl.when(half == 0)
    def _():
        quadrant(prefixed)

    @pl.when(half == 1)
    def _():
        quadrant(0)


def attend(count, scal, first, quadrants, q, k, v, lead, earlier):
    tokens, width = q.shape
    rows = tokens // 2
    groups = width // LANES
    last = groups - 1

    def lead_place(i, g):
        quadrant = i + first
        return (jnp.where(quadrant < 2, g, last), 0, jnp.minimum(quadrant, 1))

    keys = pl.BlockSpec((rows, LANES), lambda i, g: ((i + first) // 2, g))
    in_specs = [
        SMEM_SPEC,
        pl.BlockSpec((rows, LANES), lambda i, g: ((i + first) % 2, g)),
        keys,
        keys,
    ]
    in_specs += [pl.BlockSpec((PAD, LANES), lambda i, g: (0, g))] * 2
    out_specs = [
        pl.BlockSpec(
            (None, GROUP, rows, rows), lambda i, g: ((i + first) // 2, g, 0, (i + first) % 2)
        ),
        pl.BlockSpec((None, LANES, rows), lambda i, g: ((i + first) // 2, g, (i + first) % 2)),
        pl.BlockSpec(
            (None, 1, 2 * GROUP, rows), lambda i, g: ((i + first) // 2, g, 0, (i + first) % 2)
        ),
        pl.BlockSpec((1, GROUP * PAD, rows), lead_place),
    ]
    out_shape = [
        shape_of((2, groups * GROUP, rows, tokens), BF16),
        shape_of((2, width, tokens), BF16),
        shape_of((2, groups, 2 * GROUP, tokens), F32),
        shape_of((groups, GROUP * PAD, tokens), BF16),
    ]
    macs = quadrants * groups * GROUP * rows * rows * 256 * 2
    return pl.pallas_call(
        functools.partial(attend_kernel, count, first),
        grid=(quadrants, groups),
        in_specs=in_specs + [ANY_SPEC] * len(earlier),
        out_specs=out_specs,
        out_shape=out_shape,
        input_output_aliases={6 + i: i for i in range(len(earlier))},
        scratch_shapes=[pltpu.VMEM((rows, rows), F32)] * 2,
        compiler_params=params(16 * MIB),
        cost_estimate=cost(macs, quadrants * 14 * MIB),
    )(scal, far(q), far(k), far(v), *lead, *all_far(earlier))


def lead_back_kernel(
    count, q_ref, up_ref, rst_ref, del_ref, pp_ref, pk_ref, pv_ref, bias_ref, pair_ref, dqt_ref
):
    queries = q_ref.shape[0]
    ups = []
    deltas = []
    for head in range(GROUP):
        rows = slice(head * HEAD_DIM, (head + 1) * HEAD_DIM)
        share = rst_ref[0, head : head + 1, :]
        ups.append((up_ref[rows, :].astype(F32) * share).astype(BF16))
        delta = del_ref[0, head : head + 1, :] * share
        deltas.append(jnp.broadcast_to(delta, (PAD, queries)))
    up = jnp.concatenate(ups, axis=0)
    delta = jnp.concatenate(deltas, axis=0)
    weights = pp_ref[0]
    key_diagonal = block_diagonal(pk_ref[...])
    value_diagonal = block_diagonal(pv_ref[...])
    weight_grads = dot_nn(value_diagonal, up)
    score_grads = (weights.astype(F32) * (weight_grads - delta)).astype(BF16)
    dqt_ref[...] = dot_tn(key_diagonal, score_grads).astype(BF16)
    key_grads = dot_nn(score_grads, q_ref[...]) * (1.0 / LOG2E)
    value_grads = dot_nt(weights, up)
    lane = lax.broadcasted_iota(jnp.int32, (PAD, LANES), 1) // HEAD_DIM
    key_total = jnp.zeros((PAD, LANES), F32)
    value_total = jnp.zeros((PAD, LANES), F32)
    for head in range(GROUP):
        rows = slice(head * PAD, (head + 1) * PAD)
        key_total = jnp.where(lane == head, key_grads[rows], key_total)
        value_total = jnp.where(lane == head, value_grads[rows], value_total)
    row = lax.broadcasted_iota(jnp.int32, (PAD, LANES), 0)
    key_total = jnp.where(row == count, bias_ref[0:1, :], key_total)
    key_total = jnp.where(row == count + 1, bias_ref[1:2, :], key_total)
    pair_ref[:PAD, :] = key_total.astype(BF16)
    pair_ref[PAD:, :] = value_total.astype(BF16)


def lead_backward(count, q, up, shares, deltas, lead_weights, prefix_keys, prefix_values, biases):
    tokens, width = q.shape
    groups = width // LANES
    small = pl.BlockSpec((PAD, LANES), lambda g: (0, g))
    stats = pl.BlockSpec((1, 2 * GROUP, tokens), lambda g: (g, 0, 0))
    return pl.pallas_call(
        functools.partial(lead_back_kernel, count),
        grid=(groups,),
        in_specs=[
            pl.BlockSpec((tokens, LANES), lambda g: (0, g)),
            pl.BlockSpec((LANES, tokens), lambda g: (g, 0)),
            stats,
            stats,
            pl.BlockSpec((1, GROUP * PAD, tokens), lambda g: (g, 0, 0)),
            small,
            small,
            pl.BlockSpec((8, LANES), lambda g: (0, g)),
        ],
        out_specs=[
            pl.BlockSpec((2 * PAD, LANES), lambda g: (0, g)),
            pl.BlockSpec((LANES, tokens), lambda g: (g, 0)),
        ],
        out_shape=[
            jax.ShapeDtypeStruct((2 * PAD, width), BF16),
            shape_of((width, tokens), BF16),
        ],
        compiler_params=params(14 * MIB),
        cost_estimate=cost(groups * 4 * GROUP * PAD * tokens * LANES, 10 * MIB),
    )(*all_far((q, up, shares, deltas, lead_weights)), prefix_keys, prefix_values, biases)


def attend_back_kernel(
    half,
    last_keys,
    last_queries,
    has_earlier,
    q_ref,
    k_ref,
    v_ref,
    up_ref,
    rst_ref,
    del_ref,
    pt_ref,
    dqt_in_ref,
    *refs,
):
    dq_ref, dk_ref, dv_ref = refs[-5:-2]
    weight_grads = refs[-2:]
    queries = q_ref.shape[0]
    lane = lax.broadcasted_iota(jnp.int32, (queries, 128), 1) // HEAD_DIM
    masks = [(lane == head).astype(F32).astype(BF16) for head in range(2)]
    zeros = jnp.zeros((HEAD_DIM, queries), BF16)
    turned = k_ref[...].T
    ups = {}
    grads = {}
    query_grads = []
    key_grads = []
    value_grads = []

    def pair_of(head):
        return slice((head // 2) * 128, (head // 2 + 1) * 128)

    def rows_of(head):
        return slice(head * HEAD_DIM, (head + 1) * HEAD_DIM)

    def share_of(head):
        return rst_ref[0, half * GROUP + head : half * GROUP + head + 1, :]

    def weight_grad(head):
        up = (up_ref[rows_of(head), :].astype(F32) * share_of(head)).astype(BF16)
        ups[head] = jnp.concatenate([up, zeros] if head % 2 == 0 else [zeros, up], axis=0)
        weight_grads[head % 2][...] = dot_nn(v_ref[:, pair_of(head)], ups[head])

    def score_grad(head):
        delta = del_ref[0, head : head + 1, :] * share_of(head)
        return (pt_ref[head].astype(F32) * (weight_grads[head % 2][...] - delta)).astype(BF16)

    def value_term(head):
        return dot_nt(pt_ref[head], ups[head])

    def key_term(head):
        return dot_nn(grads[head], q_ref[:, pair_of(head)] * masks[head % 2])

    def query_term(head):
        return dqt_in_ref[rows_of(head), :].astype(F32) + dot_nn(turned[rows_of(head)], grads[head])

    weight_grad(0)
    for head in range(GROUP):
        if head + 1 < GROUP:
            weight_grad(head + 1)
        grads[head] = score_grad(head)
        value = value_term(head)
        query_grads.append(query_term(head))
        key = key_term(head)
        if head % 2:
            key_grads[-1] = key_grads[-1] + key
            value_grads[-1] = value_grads[-1] + value
        else:
            key_grads.append(key)
            value_grads.append(value)
    query_grad = jnp.concatenate(query_grads, axis=0)
    key_grad = jnp.concatenate(key_grads, axis=1)
    value_grad = jnp.concatenate(value_grads, axis=1)
    if not last_keys:
        dq_ref[...] = query_grad.astype(BF16)
    else:
        dq_ref[...] = (query_grad * (1.0 / math.sqrt(HEAD_DIM))).astype(BF16).T
    if has_earlier:
        key_grad = key_grad + refs[0][...].astype(F32)
        value_grad = value_grad + refs[1][...].astype(F32)
    if last_queries:
        key_grad = key_grad * (1.0 / LOG2E)
    dk_ref[...] = key_grad.astype(BF16)
    dv_ref[...] = value_grad.astype(BF16)


def attend_back(
    key_half, query_half, last_keys, last_queries, q, k, v, up, shares, deltas, weights, dqt, earlier
):
    tokens, width = q.shape
    rows = tokens // 2
    groups = width // LANES
    query_columns = pl.BlockSpec((LANES, rows), lambda g: (g, query_half))
    stats = pl.BlockSpec((1, 2 * GROUP, rows), lambda g: (g, 0, query_half))
    finished = pl.BlockSpec((rows, LANES), lambda g: (0, g))
    out_columns = pl.BlockSpec((LANES, rows), lambda g: (g, 0))
    sofar = query_columns if dqt.shape[1] == tokens else out_columns
    macs = groups * GROUP * rows * rows * 256 * 4
    return pl.pallas_call(
        functools.partial(
            attend_back_kernel, key_half, last_keys, last_queries, len(earlier) > 0
        ),
        grid=(groups,),
        in_specs=[
            pl.BlockSpec((rows, LANES), lambda g: (query_half, g)),
            pl.BlockSpec((rows, LANES), lambda g: (key_half, g)),
            pl.BlockSpec((rows, LANES), lambda g: (key_half, g)),
            query_columns,
            stats,
            stats,
            pl.BlockSpec((None, GROUP, rows, rows), lambda g: (key_half, g, 0, query_half)),
            sofar,
        ]
        + [finished] * len(earlier),
        out_specs=[finished if last_keys else out_columns, finished, finished],
        out_shape=[
            shape_of((rows, width) if last_keys else (width, rows), BF16),
            shape_of((rows, width), BF16),
            shape_of((rows, width), BF16),
        ],
        scratch_shapes=[pltpu.VMEM((rows, rows), F32)] * 2,
        compiler_params=params(18 * MIB),
        cost_estimate=cost(macs, 12 * MIB),
    )(*all_far((q, k, v, up, shares, deltas, weights, dqt, *earlier)))


def gelu_pair(values):
    scaled = values * 0.7071067811865476
    below = 0.5 * lax.erf(scaled) + 0.5
    decay = jnp.exp2(scaled * scaled * (-LOG2E))
    return values * below, below + values * 0.3989422804014327 * decay


def row_mean(values):
    return jnp.mean(values, axis=-1, keepdims=True)


def front_kernel(
    tiles,
    scal_ref,
    x_own_ref,
    x_other_ref,
    ot_own_ref,
    ot_other_ref,
    st_own_ref,
    st_other_ref,
    og_own_ref,
    og_other_ref,
    gain_one_ref,
    gain_two_ref,
    down_bias_ref,
    up_bias_ref,
    wo_ref,
    fin_ref,
    fout_ref,
    down_ref,
    up_ref,
    out_own_ref,
    out_other_ref,
    rst_ref,
    mix_ref,
    slope_ref,
    grad_low_ref,
    norm_grad_ref,
    normed_ref,
    inv_ref,
    kept_ref,
    sent_ref,
    bias_grad_ref,
    act_ref,
    squeeze_ref,
    low_ref,
):
    step = pl.program_id(0)
    tile = x_own_ref.shape[0]
    width = x_own_ref.shape[1]
    hidden = fin_ref.shape[1]
    chunk = 512
    chunks = [slice(first, first + chunk) for first in range(0, hidden, chunk)]
    own = step < tiles // 2
    x = jnp.where(own, x_own_ref[...], x_other_ref[...]).astype(F32)
    top_own, top_other = st_own_ref[:, :GROUP, :], st_other_ref[:, :GROUP, :]
    top = jnp.maximum(top_own, top_other)
    share_own, share_other = jnp.exp2(top_own - top), jnp.exp2(top_other - top)
    inverse = 1.0 / (
        st_own_ref[:, GROUP:, :] * share_own + st_other_ref[:, GROUP:, :] * share_other
    )
    rst_ref[:, :GROUP, :] = share_own * inverse
    rst_ref[:, GROUP:, :] = share_other * inverse
    mixes = []
    for head in range(width // HEAD_DIM):
        rows = slice(head * HEAD_DIM, (head + 1) * HEAD_DIM)
        group, place = head // GROUP, head % GROUP
        mixes.append(
            (
                ot_own_ref[rows, :].astype(F32) * rst_ref[group, place : place + 1, :]
                + ot_other_ref[rows, :].astype(F32) * rst_ref[group, GROUP + place : GROUP + place + 1, :]
            ).astype(BF16)
        )
    mix = jnp.concatenate(mixes, axis=0)
    mix_ref[...] = mix
    resid_one = x + dot_tn(mix, wo_ref[...])
    centred = resid_one - row_mean(resid_one)
    inv_one = lax.rsqrt(row_mean(centred * centred) + 1e-05)
    normed = centred * inv_one
    normed_ref[...] = normed.astype(BF16)
    inv_ref[...] = inv_one
    norm_one = normed * gain_one_ref[...]
    norm_low = norm_one.astype(BF16)

    squeeze = dot_nn(norm_low, down_ref[...]) + down_bias_ref[...]
    inner = dot_nn(norm_low, fin_ref[:, chunks[0]])
    squeeze_act, squeeze_slope = gelu_pair(squeeze)
    squeeze_act = squeeze_act.astype(BF16)
    resid_two = norm_one + 4.0 * (dot_nn(squeeze_act, up_ref[...]) + up_bias_ref[...])
    for place, columns in enumerate(chunks):
        more = place + 1 < len(chunks)
        coming = dot_nn(norm_low, fin_ref[:, chunks[place + 1]]) if more else None
        act, slope = gelu_pair(inner)
        slope_ref[:, columns] = slope.astype(BF16)
        resid_two = resid_two + dot_nn(act.astype(BF16), fout_ref[columns, :])
        inner = coming

    centred = resid_two - row_mean(resid_two)
    inv_two = lax.rsqrt(row_mean(centred * centred) + 1e-05)
    normed_two = centred * inv_two
    base = jnp.where(own, scal_ref[0], scal_ref[1] - (tiles // 2) * tile) + step * tile
    place = base + lax.broadcasted_iota(jnp.int32, (tile, 1), 0)
    valid = (place < scal_ref[2]).astype(F32)
    gain_two = gain_two_ref[...]
    out = (normed_two * gain_two * valid).astype(BF16)
    upstream = jnp.where(own, og_own_ref[...], og_other_ref[...]).astype(F32) * valid * gain_two
    grad_two = inv_two * (
        upstream - row_mean(upstream) - normed_two * row_mean(upstream * normed_two)
    )
    grad_low = grad_two.astype(BF16)
    grad_adapt = 4.0 * grad_low
    grad_squeeze = (dot_nt(grad_adapt, up_ref[...]) * squeeze_slope).astype(BF16)
    norm_grad_ref[...] = (grad_two + dot_nt(grad_squeeze, down_ref[...])).astype(BF16)
    here = pl.ds(pl.multiple_of(step * tile, tile), tile)
    grad_low_ref[here, :] = grad_low
    act_ref[here, :] = squeeze_act
    squeeze_ref[here, :] = grad_squeeze
    low_ref[here, :] = norm_low
    up_bias_grad = jnp.sum(grad_adapt.astype(F32), axis=0, keepdims=True)
    down_bias_grad = jnp.sum(grad_squeeze.astype(F32), axis=0, keepdims=True)
    adapt = down_bias_grad.shape[1]

    @pl.when(own)
    def _():
        out_own_ref[...] = out

    @pl.when(jnp.logical_not(own))
    def _():
        out_other_ref[...] = out

    @pl.when(step == 0)
    def _():
        bias_grad_ref[...] = jnp.zeros_like(bias_grad_ref)
        bias_grad_ref[0:1, :] = up_bias_grad
        bias_grad_ref[1:2, :adapt] = down_bias_grad

    @pl.when(step > 0)
    def _():
        bias_grad_ref[0:1, :] += up_bias_grad
        bias_grad_ref[1:2, :adapt] += down_bias_grad

    @pl.when(step == tiles - 1)
    def _():
        first = scal_ref[3] == 0
        up_total = (4.0 * dot_tn(act_ref[...], grad_low_ref[...])).astype(BF16)
        down_total = dot_tn(squeeze_ref[...], low_ref[...]).astype(BF16)
        kept_ref[...] = jnp.where(first, up_total, down_total)
        sent_ref[...] = jnp.where(first, down_total, up_total)


def front(
    scal, x_own, x_other, mix_parts, tops_sums, og_own, og_other, w_output, attn_gain, ffn_in,
    ffn_out, ffn_gain, down, down_bias, up, up_bias,
):
    rows, width = x_own.shape
    tokens = 2 * rows
    hidden = ffn_in.shape[1]
    adapt = down.shape[1]
    groups = width // LANES
    tile = 256
    tiles = tokens // tile
    near = pl.BlockSpec((tile, width), lambda i: (jnp.minimum(i, tiles // 2 - 1), 0))
    far = pl.BlockSpec((tile, width), lambda i: (jnp.maximum(i - tiles // 2, 0), 0))
    row_block = pl.BlockSpec((tile, width), lambda i: (i, 0))
    column_block = pl.BlockSpec((width, tile), lambda i: (0, i))
    stats = pl.BlockSpec((groups, 2 * GROUP, tile), lambda i: (0, 0, i))
    mixes = [pl.BlockSpec((None, width, tile), lambda i, half=half: (half, 0, i)) for half in range(2)]
    tops = [
        pl.BlockSpec((None, groups, 2 * GROUP, tile), lambda i, half=half: (half, 0, 0, i))
        for half in range(2)
    ]
    return pl.pallas_call(
        functools.partial(front_kernel, tiles),
        grid=(tiles,),
        in_specs=[
            SMEM_SPEC, near, far, *mixes, *tops, near, far,
            whole((1, width)), whole((1, width)), whole((1, adapt)), whole((1, width)),
        ] + [CORE_SPEC] * 5,
        out_specs=[
            near, far, stats, column_block, pl.BlockSpec((tile, hidden), lambda i: (i, 0)),
            kept((tokens, width)), row_block, row_block, pl.BlockSpec((tile, 1), lambda i: (i, 0)),
            kept((adapt, width)), kept((adapt, width)), whole((8, width)),
        ],
        out_shape=[
            shape_of((rows, width), BF16),
            shape_of((rows, width), BF16),
            shape_of((groups, 2 * GROUP, tokens), F32),
            shape_of((width, tokens), BF16),
            shape_of((tokens, hidden), BF16),
            shape_of((tokens, width), BF16),
            shape_of((tokens, width), BF16),
            shape_of((tokens, width), BF16),
            shape_of((tokens, 1), F32),
            shape_of((adapt, width), BF16),
            shape_of((adapt, width), BF16),
            shape_of((8, width), F32),
        ],
        scratch_shapes=[
            pltpu.VMEM((tokens, adapt), BF16),
            pltpu.VMEM((tokens, adapt), BF16),
            pltpu.VMEM((tokens, width), BF16),
        ],
        compiler_params=params(32 * MIB),
        cost_estimate=cost(tokens * width * (width + 2 * hidden + 6 * adapt), 60 * MIB),
    )(
        scal,
        *all_far((x_own, x_other, mix_parts, mix_parts, tops_sums, tops_sums, og_own, og_other)),
        attn_gain[None], ffn_gain[None], down_bias[None], up_bias[None],
        *[bring(item) for item in (w_output, ffn_in, ffn_out, down, up)],
    )


def rear_kernel(
    grad_low_ref, norm_grad_ref, slope_ref, normed_ref, inv_ref, mix_ref, gain_ref, wo_ref, fin_ref,
    fout_ref, grad_one_ref, up_ref, del_ref,
):
    hidden = fin_ref.shape[1]
    chunk = 1024
    chunks = [slice(first, first + chunk) for first in range(0, hidden, chunk)]
    grad_low = grad_low_ref[...]
    grad_norm = norm_grad_ref[...].astype(F32)
    inner = dot_nt(grad_low, fout_ref[chunks[0], :])
    for place, columns in enumerate(chunks):
        more = place + 1 < len(chunks)
        coming = dot_nt(grad_low, fout_ref[chunks[place + 1], :]) if more else None
        low = (inner * slope_ref[:, columns].astype(F32)).astype(BF16)
        grad_norm = grad_norm + dot_nt(low, fin_ref[:, columns])
        inner = coming
    grad = grad_norm * gain_ref[...]
    normed = normed_ref[...].astype(F32)
    grad_one = inv_ref[...] * (grad - row_mean(grad) - normed * row_mean(grad * normed))
    grad_low_one = grad_one.astype(BF16)
    grad_one_ref[...] = grad_low_one
    up = dot_nt(wo_ref[...], grad_low_one).astype(BF16)
    up_ref[...] = up
    product = up.astype(F32) * mix_ref[...].astype(F32)
    for head in range(product.shape[0] // HEAD_DIM):
        rows = slice(head * HEAD_DIM, (head + 1) * HEAD_DIM)
        group, place = head // GROUP, head % GROUP
        del_ref[group, place : place + 1, :] = jnp.sum(product[rows], axis=0, keepdims=True)
    del_ref[:, GROUP:, :] = jnp.zeros_like(del_ref[:, GROUP:, :])


def rear(grad_low, norm_grad, slope, normed, inv, mix, w_output, attn_gain, ffn_in, ffn_out):
    tokens, width = grad_low.shape
    hidden = ffn_in.shape[1]
    groups = width // LANES
    tile = 256
    row_block = pl.BlockSpec((tile, width), lambda i: (i, 0))
    column_block = pl.BlockSpec((width, tile), lambda i: (0, i))
    return pl.pallas_call(
        rear_kernel,
        grid=(tokens // tile,),
        in_specs=[
            row_block, row_block, pl.BlockSpec((tile, hidden), lambda i: (i, 0)), row_block,
            pl.BlockSpec((tile, 1), lambda i: (i, 0)), column_block, whole((1, width)),
        ] + [CORE_SPEC] * 3,
        out_specs=[
            row_block, column_block, pl.BlockSpec((groups, 2 * GROUP, tile), lambda i: (0, 0, i)),
        ],
        out_shape=[
            shape_of((tokens, width), BF16),
            shape_of((width, tokens), BF16),
            shape_of((groups, 2 * GROUP, tokens), F32),
        ],
        compiler_params=params(22 * MIB),
        cost_estimate=cost(tokens * width * (width + 2 * hidden), 50 * MIB),
    )(*all_far((grad_low, norm_grad, slope, normed, inv, mix)), attn_gain[None], bring(w_output), bring(ffn_in), bring(ffn_out))


def input_grad_kernel(merged, *refs):
    place_ref, grad_ref, dq_ref, dk_ref, dv_ref, wq_ref, wk_ref, wv_ref = refs[:8]
    total = grad_ref[...].astype(F32) + dot_nt(dq_ref[...], wq_ref[...])
    total = total + dot_nt(dk_ref[...], wk_ref[...])
    total = total + dot_nt(dv_ref[...], wv_ref[...])
    total = total.astype(BF16)
    if merged:
        merge_kernel(place_ref, total, *refs[8:])
    else:
        refs[8][...] = total


def input_grad(place, half, grad_one, dq, dk, dv, w_query, w_key, w_value, arrived):
    rows, width = dk.shape
    step = rows // 2
    block = pl.BlockSpec((step, width), lambda i: (i, 0))
    return pl.pallas_call(
        functools.partial(input_grad_kernel, len(arrived)),
        grid=(2,),
        in_specs=[SMEM_SPEC, pl.BlockSpec((step, width), lambda i: (2 * half + i, 0))]
        + [block] * 3
        + [CORE_SPEC] * 3
        + [block] * len(arrived),
        out_specs=pl.BlockSpec((step, 2, width), lambda i: (i, 0, 0)) if arrived else block,
        out_shape=shape_of((rows, 2, width) if arrived else (rows, width), BF16),
        compiler_params=params(16 * MIB),
        cost_estimate=cost(3 * rows * width * width, 14 * MIB),
    )(
        place,
        *all_far((grad_one, dq, dk, dv)),
        bring(w_query),
        bring(w_key),
        bring(w_value),
        *all_far(arrived),
    )


def swap(value, seq_bit, dp_bits):
    width = lax.axis_size("dp")
    count = lax.axis_size("seq") * width
    pairs = [
        (device, ((device // width) ^ seq_bit) * width + ((device % width) ^ dp_bits))
        for device in range(count)
    ]
    return lax.ppermute(value, ("seq", "dp"), pairs)


def gather_line(value):
    width = lax.axis_size("dp")
    groups = [[4 * line + place for line in range(width // 4)] for place in range(4)]
    return lax.all_gather(value, "dp", axis_index_groups=groups)


def total(values):
    return jnp.sum(values.astype(F32), axis=0)


def square_place():
    return 2 * ((lax.axis_index("dp") // 2) % 2) + lax.axis_index("seq")


def square_swaps(values):
    return [swap(values[offset - 1], offset % 2, 2 * (offset // 2)) for offset in range(1, 4)]


def sum_square(value):
    place = square_place()
    quarters = value.reshape(4, value.shape[0] // 4, value.shape[1])
    pick = [
        lax.dynamic_index_in_dim(quarters, place ^ offset, 0, keepdims=False) for offset in range(4)
    ]
    return pick[:1] + square_swaps(pick[1:])


def add(terms):
    value = terms[0].astype(F32)
    for term in terms[1:]:
        value = value + term.astype(F32)
    return value.astype(BF16)


def tie(*values):
    return lax.optimization_barrier(values)


def spread_kernel(scal_ref, half_ref, far_ref, up_ref, down_ref):
    first = scal_ref[3] == 0
    half, other = half_ref[...].astype(F32), far_ref[...].astype(F32)
    up_ref[...] = jnp.where(first, half, other)
    down_ref[...] = jnp.where(first, other, half).T


def spread(scal, half, other):
    adapt, width = half.shape
    step = adapt // 2
    block = pl.BlockSpec((step, width), lambda i: (i, 0))
    return pl.pallas_call(
        spread_kernel,
        grid=(2,),
        in_specs=[SMEM_SPEC, block, block],
        out_specs=[block, pl.BlockSpec((width, step), lambda i: (0, i))],
        out_shape=[shape_of((adapt, width), F32), shape_of((width, adapt), F32)],
        compiler_params=params(16 * MIB),
        cost_estimate=cost(0, 12 * adapt * width),
    )(scal, half, other)


def on_pair(
    hidden_in,
    lengths,
    w_query,
    w_key,
    w_value,
    w_output,
    attn_gain,
    ffn_in,
    ffn_out,
    ffn_gain,
    adapter_down,
    adapter_down_bias,
    adapter_up,
    adapter_up_bias,
    prefix_embed,
    prefix_hidden_w,
    prefix_hidden_b,
    prefix_out_w,
    prefix_out_b,
    out_grad,
):
    rows, _, width = hidden_in.shape
    count = prefix_embed.shape[0]
    position = lax.axis_index("seq")
    place = position.reshape(1).astype(jnp.int32)
    length = lax.dynamic_index_in_dim(lengths, position, 0, keepdims=False)
    core = lax.axis_index("dp") % 2
    scal = jnp.stack([position * rows, (1 - position) * rows, length, core]).astype(jnp.int32)

    x_own, x_send = split(place, hidden_in)
    x_other = shifted(x_send, "seq", 1)
    og_own, og_send = split(place, out_grad)
    og_other = shifted(og_send, "seq", 1)

    embed = jnp.pad(prefix_embed, ((0, PAD - count), (0, 0)))
    prefix_act, prefix_keys, prefix_values = prefix_forward(
        embed, prefix_hidden_w, prefix_hidden_b, prefix_out_w, prefix_out_b
    )
    lead = (prefix_keys, prefix_values)
    triple = project(0, x_own, w_query, w_key, w_value, ())
    begun = attend(count, scal, 0, 1, *triple, lead, ())
    q, k, v = project(1, x_other, w_query, w_key, w_value, triple)
    weights, mix_parts, tops_sums, lead_weights = attend(count, scal, 1, 3, q, k, v, lead, begun)

    (
        out_own, out_send, shares, mix, slope, grad_low, norm_grad, normed, inv_one,
        adapt_kept, adapt_sent, bias_grads,
    ) = front(
        scal, x_own, x_other, mix_parts, tops_sums, og_own, og_other,
        w_output, attn_gain, ffn_in, ffn_out, ffn_gain, adapter_down, adapter_down_bias,
        adapter_up, adapter_up_bias,
    )
    out_other = shifted(out_send, "seq", 1)
    core_terms = [adapt_kept, swap(adapt_sent, 0, 1)]
    grad_one, upstream, deltas = rear(
        grad_low, norm_grad, slope, normed, inv_one, mix, w_output, attn_gain, ffn_in, ffn_out
    )
    upstream, out_other, adapt_sum = tie(upstream, out_other, add(core_terms))
    square_terms = sum_square(adapt_sum)
    pair, dqt = lead_backward(
        count, q, upstream, shares, deltas, lead_weights, prefix_keys, prefix_values, bias_grads
    )
    pair_core = swap(pair, 0, 1)

    back = (q, k, v)
    part_own, dk_other, dv_other = attend_back(
        1, 0, False, False, *back, upstream, shares, deltas, weights, dqt, ()
    )
    dk_other, pair, adapt_sum = tie(dk_other, add([pair, pair_core]), add(square_terms))
    adapt_line = gather_line(adapt_sum)
    pair_square = square_swaps([pair] * 3)
    part_other, dk_other, dv_other = attend_back(
        1, 1, False, True, *back, upstream, shares, deltas, weights, dqt, (dk_other, dv_other)
    )
    pair_sum = pair.astype(F32) + sum(item.astype(F32) for item in pair_square)
    part_other, pair_sum = tie(part_other, pair_sum)
    dq_other, dk_own, dv_own = attend_back(
        0, 1, True, False, *back, upstream, shares, deltas, weights, part_other, ()
    )
    adapt_sum = jnp.sum(adapt_line.astype(F32), axis=0).astype(BF16)
    dq_other, adapt_sum, pair_sum = tie(dq_other, adapt_sum, pair_sum)
    pair_line = gather_line(pair_sum)
    adapt_x, adapt_y = swap(adapt_sum, 1, 0), swap(adapt_sum, 0, 2)
    triple_weights = (w_query, w_key, w_value)
    grad_other = input_grad(place, 1, grad_one, dq_other, dk_other, dv_other, *triple_weights, ())
    grad_other, dk_own, adapt_x = tie(grad_other, dk_own, adapt_x)
    grad_back = shifted(grad_other, "seq", 1)
    adapt_xy = swap(adapt_x, 0, 2)
    dq_own, dk_own, dv_own = attend_back(
        0, 0, True, True, *back, upstream, shares, deltas, weights, part_own, (dk_own, dv_own)
    )
    dq_own, pair_line, out_other, adapt_y, adapt_xy = tie(
        dq_own, pair_line, out_other, adapt_y, adapt_xy
    )
    adapt_half = jnp.stack([adapt_sum, adapt_x, adapt_y, adapt_xy])
    place_here = square_place()
    adapt_half = jnp.concatenate(
        [lax.dynamic_slice_in_dim(adapt_half, spot ^ place_here, 1, 0) for spot in range(4)]
    ).reshape(adapt_kept.shape)
    adapt_far = swap(adapt_half, 0, 1)
    layer_out, *prefix_grads = prefix_backward(
        count,
        adapter_down_bias.shape[0],
        pair_line,
        prefix_act,
        embed,
        prefix_hidden_w,
        prefix_out_w,
        place,
        out_own,
        out_other,
    )
    layer_out, grad_back, dq_own = tie(layer_out, grad_back, dq_own)
    out_w_grad = prefix_grads[3]
    input_total = input_grad(
        place, 0, grad_one, dq_own, dk_own, dv_own, *triple_weights, (grad_back,)
    )
    up_total, down_total = spread(scal, adapt_half, adapt_far)
    return (
        layer_out,
        input_total,
        down_total,
        prefix_grads[6][0],
        up_total,
        prefix_grads[5][0],
        prefix_grads[0],
        prefix_grads[1],
        prefix_grads[2][0],
        out_w_grad,
        prefix_grads[4][0],
    )


def solution(mesh):
    in_specs = (
        P("seq", "dp", None),
        P("dp"),
        P(),
        P(),
        P(),
        P(),
        P(),
        P(),
        P(),
        P(),
        P(),
        P(),
        P(),
        P(),
        P(),
        P(),
        P(),
        P(),
        P(),
        P("seq", "dp", None),
    )
    out_specs = (
        P("seq", "dp", None),
        P("seq", "dp", None),
        P(),
        P(),
        P(),
        P(),
        P(),
        P(),
        P(),
        P(),
        P(),
    )
    pairs = mesh.shape["seq"] == 2 and mesh.shape["dp"] % 8 == 0

    def on_one(*arrays):
        step = on_pair if pairs and arrays[0].shape[1] == 2 else on_device
        return step(*arrays)

    return jax.shard_map(
        on_one, mesh=mesh, in_specs=in_specs, out_specs=out_specs, check_vma=False
    )
```

```python
import functools
import math

import jax
import jax.numpy as jnp
from jax import lax
from jax.experimental import pallas as pl
from jax.experimental.pallas import tpu as pltpu
from jax.sharding import PartitionSpec as P

HEADS = 16


HIGHEST_PRECISION = lax.Precision.HIGHEST


def shifted(value, axis, steps):
    count = lax.axis_size(axis)
    pairs = [(source, (source + steps) % count) for source in range(count)]
    return lax.ppermute(value, axis, pairs)


def mixed(left, right):
    return jnp.dot(left, right, preferred_element_type=jnp.float32)


def mixed_left(left, right):
    return lax.dot_general(
        left, right, (((0,), (0,)), ((), ())), preferred_element_type=jnp.float32
    )


def mixed_right(left, right):
    return lax.dot_general(
        left, right, (((1,), (1,)), ((), ())), preferred_element_type=jnp.float32
    )


def precise(left, right):
    return jnp.dot(left, right, precision=HIGHEST_PRECISION, preferred_element_type=jnp.float32)


def precise_left(left, right):
    return lax.dot_general(
        left,
        right,
        (((0,), (0,)), ((), ())),
        precision=HIGHEST_PRECISION,
        preferred_element_type=jnp.float32,
    )


def precise_right(left, right):
    return lax.dot_general(
        left,
        right,
        (((1,), (1,)), ((), ())),
        precision=HIGHEST_PRECISION,
        preferred_element_type=jnp.float32,
    )


def gelu_value(inputs):
    return 0.5 * inputs * (1.0 + lax.erf(inputs * 0.7071067811865476))


def gelu_slope(inputs):
    return (
        0.5 * (1.0 + lax.erf(inputs * 0.7071067811865476))
        + inputs * jnp.exp(-0.5 * inputs * inputs) * 0.3989422804014327
    )


def normalize(values):
    row_mean = jnp.mean(values, axis=-1, keepdims=True)
    centred = values - row_mean
    spread = jnp.mean(centred * centred, axis=-1, keepdims=True)
    inv_std = lax.rsqrt(spread + 1e-05)
    return (centred * inv_std, inv_std)


def norm_back(upstream, normed, inv_std):
    mean_grad = jnp.mean(upstream, axis=-1, keepdims=True)
    mean_proj = jnp.mean(upstream * normed, axis=-1, keepdims=True)
    return inv_std * (upstream - mean_grad - normed * mean_proj)


def key_allowed(offset, key_count, seq_lengths):
    places = offset + lax.iota(jnp.int32, key_count)
    return places[None, :] < seq_lengths[:, None]


def lead_state(queries4, prefix_keys4, prefix_values4):
    inv_root = 1.0 / math.sqrt(queries4.shape[3])
    scores = (
        jnp.einsum("rshd,phd->rshp", queries4, prefix_keys4, preferred_element_type=jnp.float32)
        * inv_root
    )
    running_max = jnp.max(scores, axis=3)
    weights = jnp.exp(scores - running_max[..., None])
    running_sum = jnp.sum(weights, axis=3)
    running_mix = jnp.einsum(
        "rshp,phd->rshd",
        weights.astype(jnp.bfloat16),
        prefix_values4,
        preferred_element_type=jnp.float32,
    )
    return (running_max, running_sum, running_mix)


def fold_block(carried, key_block, value_block, offset, queries4, seq_lengths):
    key_count, seqs_here = (key_block.shape[0], key_block.shape[1])
    head_count, head_dim = (queries4.shape[2], queries4.shape[3])
    inv_root = 1.0 / math.sqrt(head_dim)
    keys4 = key_block.reshape(key_count, seqs_here, head_count, head_dim)
    values4 = value_block.reshape(key_count, seqs_here, head_count, head_dim)
    running_max, running_sum, running_mix = carried
    scores = (
        jnp.einsum("rshd,tshd->rsht", queries4, keys4, preferred_element_type=jnp.float32)
        * inv_root
    )
    allowed = key_allowed(offset, key_count, seq_lengths)[None, :, None, :]
    scores = jnp.where(allowed, scores, -jnp.inf)
    new_max = jnp.maximum(running_max, jnp.max(scores, axis=3))
    weights = jnp.exp(scores - new_max[..., None])
    rescale = jnp.exp(running_max - new_max)
    running_sum = running_sum * rescale + jnp.sum(weights, axis=3)
    running_mix = running_mix * rescale[..., None] + jnp.einsum(
        "rsht,tshd->rshd", weights.astype(jnp.bfloat16), values4, preferred_element_type=jnp.float32
    )
    return (new_max, running_sum, running_mix)


def lead_back(queries4, upstream4, log_total, row_delta, prefix_keys4, prefix_values4):
    inv_root = 1.0 / math.sqrt(queries4.shape[3])
    scores = (
        jnp.einsum("rshd,phd->rshp", queries4, prefix_keys4, preferred_element_type=jnp.float32)
        * inv_root
    )
    weights = jnp.exp(scores - log_total[..., None])
    weight_grads = jnp.einsum(
        "rshd,phd->rshp", upstream4, prefix_values4, preferred_element_type=jnp.float32
    )
    score_grads = (weights * (weight_grads - row_delta[..., None])).astype(jnp.bfloat16)
    query_term = (
        jnp.einsum("rshp,phd->rshd", score_grads, prefix_keys4, preferred_element_type=jnp.float32)
        * inv_root
    )
    key_term = (
        jnp.einsum("rshp,rshd->phd", score_grads, queries4, preferred_element_type=jnp.float32)
        * inv_root
    )
    value_term = jnp.einsum(
        "rshp,rshd->phd",
        weights.astype(jnp.bfloat16),
        upstream4,
        preferred_element_type=jnp.float32,
    )
    return (query_term, key_term, value_term)


def block_back(
    queries4, upstream4, log_total, row_delta, key_block, value_block, offset, seq_lengths
):
    key_count, seqs_here, model_width = key_block.shape
    head_count, head_dim = (queries4.shape[2], queries4.shape[3])
    inv_root = 1.0 / math.sqrt(head_dim)
    keys4 = key_block.reshape(key_count, seqs_here, head_count, head_dim)
    values4 = value_block.reshape(key_count, seqs_here, head_count, head_dim)
    scores = (
        jnp.einsum("rshd,tshd->rsht", queries4, keys4, preferred_element_type=jnp.float32)
        * inv_root
    )
    allowed = key_allowed(offset, key_count, seq_lengths)[None, :, None, :]
    scores = jnp.where(allowed, scores, -jnp.inf)
    weights = jnp.exp(scores - log_total[..., None])
    weight_grads = jnp.einsum(
        "rshd,tshd->rsht", upstream4, values4, preferred_element_type=jnp.float32
    )
    score_grads = (weights * (weight_grads - row_delta[..., None])).astype(jnp.bfloat16)
    query_term = (
        jnp.einsum("rsht,tshd->rshd", score_grads, keys4, preferred_element_type=jnp.float32)
        * inv_root
    )
    key_term = (
        jnp.einsum("rsht,rshd->tshd", score_grads, queries4, preferred_element_type=jnp.float32)
        * inv_root
    )
    value_term = jnp.einsum(
        "rsht,rshd->tshd",
        weights.astype(jnp.bfloat16),
        upstream4,
        preferred_element_type=jnp.float32,
    )
    pair_term = jnp.stack(
        [
            key_term.reshape(key_count, seqs_here, model_width),
            value_term.reshape(key_count, seqs_here, model_width),
        ]
    )
    return (query_term, pair_term)


def prefix_back(pair_grad, prefix_act, prefix_embed, hidden_weight, out_weight):
    out_w_grad = precise_left(prefix_act, pair_grad)
    out_b_grad = jnp.sum(pair_grad, axis=0)
    act_grad = precise_right(pair_grad, out_weight) * (1.0 - prefix_act * prefix_act)
    hidden_w_grad = precise_left(prefix_embed, act_grad)
    hidden_b_grad = jnp.sum(act_grad, axis=0)
    embed_grad = precise_right(act_grad, hidden_weight)
    return (embed_grad, hidden_w_grad, hidden_b_grad, out_w_grad, out_b_grad)


def on_device(
    hidden_in,
    lengths,
    w_query,
    w_key,
    w_value,
    w_output,
    attn_gain,
    ffn_in,
    ffn_out,
    ffn_gain,
    adapter_down,
    adapter_down_bias,
    adapter_up,
    adapter_up_bias,
    prefix_embed,
    prefix_hidden_w,
    prefix_hidden_b,
    prefix_out_w,
    prefix_out_b,
    out_grad,
):
    rows_here, seqs_here, model_width = hidden_in.shape
    token_count = rows_here * seqs_here
    head_count = HEADS
    head_dim = model_width // head_count
    axis_count = lax.axis_size("seq")
    position = lax.axis_index("seq")
    tokens = hidden_in.reshape(token_count, model_width)
    projected = jnp.stack([mixed(tokens, w_query), mixed(tokens, w_key), mixed(tokens, w_value)])
    triple = projected.astype(jnp.bfloat16).reshape(3, rows_here, seqs_here, model_width)
    hidden_weight = prefix_hidden_w.astype(jnp.float32)
    out_weight = prefix_out_w.astype(jnp.float32)
    prefix_act = jnp.tanh(precise(prefix_embed, hidden_weight) + prefix_hidden_b)
    prefix_pair = precise(prefix_act, out_weight) + prefix_out_b
    prefix_keys4 = (
        prefix_pair[:, :model_width].astype(jnp.bfloat16).reshape(-1, head_count, head_dim)
    )
    prefix_values4 = (
        prefix_pair[:, model_width:].astype(jnp.bfloat16).reshape(-1, head_count, head_dim)
    )
    row_places = position * rows_here + lax.iota(jnp.int32, rows_here)
    valid = (row_places[:, None] < lengths[None, :]).astype(jnp.float32).reshape(token_count, 1)
    queries4 = triple[0].reshape(rows_here, seqs_here, head_count, head_dim)
    key_value = triple[1:]
    pieces = lax.all_gather(key_value, "seq", axis=1, tiled=True)
    carried = fold_block(
        lead_state(queries4, prefix_keys4, prefix_values4),
        pieces[0],
        pieces[1],
        jnp.int32(0),
        queries4,
        lengths,
    )
    mix_full = carried[2] / carried[1][..., None]
    log_total = carried[0] + jnp.log(carried[1])
    mix_low = mix_full.astype(jnp.bfloat16).reshape(token_count, model_width)
    attn_proj = mixed(mix_low, w_output)
    normed_one, inv_one = normalize(tokens.astype(jnp.float32) + attn_proj)
    norm_one = normed_one * attn_gain
    norm_low = norm_one.astype(jnp.bfloat16)
    inner_pre = mixed(norm_low, ffn_in)
    inner_act = gelu_value(inner_pre).astype(jnp.bfloat16)
    squeeze = mixed(norm_low, adapter_down) + adapter_down_bias
    squeeze_act = gelu_value(squeeze).astype(jnp.bfloat16)
    ffn_sum = mixed(inner_act, ffn_out)
    adapter_sum = mixed(squeeze_act, adapter_up) + adapter_up_bias
    normed_two, inv_two = normalize(norm_one + ffn_sum + 4.0 * adapter_sum)
    layer_out = (
        (normed_two * ffn_gain * valid)
        .astype(jnp.bfloat16)
        .reshape(rows_here, seqs_here, model_width)
    )
    upstream_top = out_grad.reshape(token_count, model_width).astype(jnp.float32) * valid
    grad_two = norm_back(upstream_top * ffn_gain, normed_two, inv_two)
    grad_ffn_low = grad_two.astype(jnp.bfloat16)
    grad_adapt_low = (4.0 * grad_two).astype(jnp.bfloat16)
    up_grad = mixed_left(squeeze_act, grad_adapt_low)
    up_bias_grad = jnp.sum(grad_adapt_low.astype(jnp.float32), axis=0)
    grad_squeeze_low = (mixed_right(grad_adapt_low, adapter_up) * gelu_slope(squeeze)).astype(
        jnp.bfloat16
    )
    down_grad = mixed_left(norm_low, grad_squeeze_low)
    down_bias_grad = jnp.sum(grad_squeeze_low.astype(jnp.float32), axis=0)
    grad_inner_low = (mixed_right(grad_ffn_low, ffn_out) * gelu_slope(inner_pre)).astype(
        jnp.bfloat16
    )
    grad_norm = (
        grad_two + mixed_right(grad_squeeze_low, adapter_down) + mixed_right(grad_inner_low, ffn_in)
    )
    grad_one = norm_back(grad_norm * attn_gain, normed_one, inv_one)
    grad_attn_low = grad_one.astype(jnp.bfloat16)
    grad_mix_low = mixed_right(grad_attn_low, w_output).astype(jnp.bfloat16)
    upstream4 = grad_mix_low.reshape(rows_here, seqs_here, head_count, head_dim)
    row_delta = jnp.sum(upstream4.astype(jnp.float32) * mix_full, axis=3)
    query_grad, prefix_key_grad, prefix_value_grad = lead_back(
        queries4, upstream4, log_total, row_delta, prefix_keys4, prefix_values4
    )

    def visit(step_index, carried):
        moving, grads_moving, query_total = carried
        source = (position - step_index) % axis_count
        query_term, pair_term = block_back(
            queries4,
            upstream4,
            log_total,
            row_delta,
            moving[0],
            moving[1],
            source * rows_here,
            lengths,
        )
        return (moving, grads_moving + pair_term, query_total + query_term)

    def travel(step_index, carried):
        moving, grads_moving, query_total = visit(step_index, carried)
        moving = shifted(moving, "seq", 1)
        grads_moving = shifted(grads_moving.astype(jnp.bfloat16), "seq", 1).astype(
            grads_moving.dtype
        )
        return (moving, grads_moving, query_total)

    initial = (
        key_value,
        jnp.zeros((2, rows_here, seqs_here, model_width), jnp.float32),
        query_grad,
    )
    carried = lax.fori_loop(0, axis_count - 1, travel, initial)
    carried = visit(axis_count - 1, carried)
    pair_grads = shifted(carried[1].astype(jnp.bfloat16), "seq", 1).astype(jnp.float32)
    triple_grad = jnp.concatenate(
        [carried[2].reshape(1, rows_here, seqs_here, model_width), pair_grads]
    ).astype(jnp.bfloat16)
    hidden_grad = grad_one + mixed_right(triple_grad[0].reshape(token_count, model_width), w_query)
    hidden_grad = hidden_grad + mixed_right(triple_grad[1].reshape(token_count, model_width), w_key)
    hidden_grad = hidden_grad + mixed_right(
        triple_grad[2].reshape(token_count, model_width), w_value
    )
    hidden_grad = hidden_grad.astype(jnp.bfloat16).reshape(rows_here, seqs_here, model_width)
    pair_grad = jnp.concatenate(
        [prefix_key_grad.reshape(-1, model_width), prefix_value_grad.reshape(-1, model_width)],
        axis=1,
    )
    prefix_grads = prefix_back(pair_grad, prefix_act, prefix_embed, hidden_weight, out_weight)
    summed = lax.psum(
        (
            down_grad,
            down_bias_grad,
            up_grad,
            up_bias_grad,
            prefix_grads[0],
            prefix_grads[1],
            prefix_grads[2],
            prefix_grads[3],
            prefix_grads[4],
        ),
        ("seq", "dp"),
    )
    adapter_totals = summed[:4]
    prefix_totals = summed[4:]
    return (
        layer_out,
        hidden_grad,
        adapter_totals[0],
        adapter_totals[1],
        adapter_totals[2],
        adapter_totals[3],
        prefix_totals[0],
        prefix_totals[1],
        prefix_totals[2],
        prefix_totals[3],
        prefix_totals[4],
    )


BF16 = jnp.bfloat16
F32 = jnp.float32
MIB = 1024 * 1024
GROUP = 4
HEAD_DIM = 64
LANES = GROUP * HEAD_DIM
PAD = 32
MASKED = -1e30
LOG2E = 1.4426950408889634
VMEM_LIMIT = 60 * MIB


def dot_nn(left, right):
    return lax.dot_general(left, right, (((1,), (0,)), ((), ())), preferred_element_type=F32)


def dot_nt(left, right):
    return lax.dot_general(left, right, (((1,), (1,)), ((), ())), preferred_element_type=F32)


def dot_tn(left, right):
    return lax.dot_general(left, right, (((0,), (0,)), ((), ())), preferred_element_type=F32)


def shape_of(shape, dtype):
    return pltpu.HBM(shape, dtype)


def far(value):
    return pltpu.with_memory_space_constraint(value, pltpu.HBM)


def bring(value):
    return pltpu.with_memory_space_constraint(value, pltpu.VMEM)


def all_far(values):
    return [far(value) for value in values]


def params(limit=VMEM_LIMIT):
    return pltpu.CompilerParams(vmem_limit_bytes=limit)


def cost(macs, moved):
    return pl.CostEstimate(flops=int(2 * macs), bytes_accessed=int(moved), transcendentals=0)


SMEM_SPEC = pl.BlockSpec(memory_space=pltpu.SMEM)
ANY_SPEC = pl.BlockSpec(memory_space=pl.ANY)
CORE_SPEC = pl.BlockSpec(memory_space=pltpu.VMEM)


def whole(shape):
    return pl.BlockSpec(shape, lambda *_: (0,) * len(shape))


def kept(shape):
    return pl.BlockSpec(shape, lambda *_: (0,) * len(shape), pipeline_mode=pl.Buffered(1))


def split_kernel(place_ref, both_ref, own_ref, other_ref):
    apart = jnp.swapaxes(both_ref[...], 0, 1)
    first = place_ref[0] == 0
    own_ref[...] = jnp.where(first, apart[0], apart[1])
    other_ref[...] = jnp.where(first, apart[1], apart[0])


def split(place, both):
    rows, _, width = both.shape
    step = rows // 4
    half = pl.BlockSpec((step, width), lambda i: (i, 0))
    return pl.pallas_call(
        split_kernel,
        grid=(4,),
        in_specs=[SMEM_SPEC, pl.BlockSpec((step, 2, width), lambda i: (i, 0, 0))],
        out_specs=[half, half],
        out_shape=[shape_of((rows, width), both.dtype)] * 2,
        compiler_params=params(8 * MIB),
        cost_estimate=cost(0, 4 * rows * width * 2),
    )(place, far(both))


def merge_kernel(place_ref, own_ref, other_ref, both_ref):
    first = place_ref[0] == 0
    own, other = own_ref[...], other_ref[...]
    apart = jnp.stack([jnp.where(first, own, other), jnp.where(first, other, own)])
    both_ref[...] = jnp.swapaxes(apart, 0, 1)


def parts_of(values, count):
    parts = []
    for _ in range(count):
        part = values.astype(BF16)
        parts.append(part)
        values = values - part.astype(F32)
    return parts


def exact_dot(values, weight, dot):
    rows = values.shape[0]
    product = dot(jnp.concatenate(parts_of(values, 3), axis=0), weight)
    return product[:rows] + product[rows : 2 * rows] + product[2 * rows :]


def prefix_kernel(embed_ref, hw_ref, hb_ref, ow_ref, ob_ref, act_ref, key_ref, value_ref):
    width = key_ref.shape[1]
    act = jnp.tanh(exact_dot(embed_ref[...], hw_ref[...], dot_nn) + hb_ref[...])
    act_ref[...] = act
    pair = exact_dot(act, ow_ref[...], dot_nn) + ob_ref[...]
    key_ref[...] = pair[:, :width].astype(BF16)
    value_ref[...] = pair[:, width:].astype(BF16)


def prefix_forward(embed, hidden_w, hidden_b, out_w, out_b):
    width, hidden = hidden_w.shape
    return pl.pallas_call(
        prefix_kernel,
        out_shape=[
            shape_of((PAD, hidden), F32),
            shape_of((PAD, width), BF16),
            shape_of((PAD, width), BF16),
        ],
        compiler_params=params(16 * MIB),
        cost_estimate=cost(3 * PAD * hidden * 3 * width * 4, 6 * hidden * width),
    )(embed, far(hidden_w), hidden_b[None], far(out_w), out_b[None])


def prefix_back_kernel(
    count, pairs_ref, act_ref, embed_ref, hw_ref, ow_ref, place_ref, own_ref, other_ref,
    both_ref, eg_ref, hwg_ref, hbg_ref, owg_ref, obg_ref, ubg_ref, dbg_ref,
):
    merge_kernel(place_ref, own_ref[...], other_ref, both_ref)
    total = pairs_ref[0]
    for line in range(1, pairs_ref.shape[0]):
        total = total + pairs_ref[line]
    ubg_ref[...] = total[count : count + 1]
    dbg_ref[...] = total[count + 1 : count + 2, : dbg_ref.shape[1]]
    pair = jnp.concatenate([total[:PAD], total[PAD:]], axis=1)
    rows = lax.broadcasted_iota(jnp.int32, pair.shape, 0)
    pair = jnp.where(rows < count, pair, 0.0)
    act = act_ref[...]
    obg_ref[...] = jnp.sum(pair, axis=0, keepdims=True)
    high, low = parts_of(pair, 2)
    back = dot_nt(jnp.concatenate([high, low], axis=0), ow_ref[...])
    act_grad = (back[:PAD] + back[PAD:]) * (1.0 - act * act)
    act_high, act_low = parts_of(act, 2)
    owg_ref[...] = dot_tn(
        jnp.concatenate([act_high, act_low, act_high], axis=0),
        jnp.concatenate([high, high, low], axis=0),
    )
    hbg_ref[...] = jnp.sum(act_grad, axis=0, keepdims=True)
    high, low = parts_of(act_grad, 2)
    embed_high, embed_low = parts_of(embed_ref[...], 2)
    hwg_ref[...] = dot_tn(
        jnp.concatenate([embed_high, embed_low, embed_high], axis=0),
        jnp.concatenate([high, high, low], axis=0),
    )
    back = dot_nt(jnp.concatenate([high, low], axis=0), hw_ref[...])
    eg_ref[...] = (back[:PAD] + back[PAD:])[:count]


def prefix_backward(count, adapt, pairs, act, embed, hidden_w, out_w, place, own, other):
    width, hidden = hidden_w.shape
    core = [CORE_SPEC] * 5
    return pl.pallas_call(
        functools.partial(prefix_back_kernel, count),
        in_specs=core + [SMEM_SPEC, CORE_SPEC, CORE_SPEC],
        out_shape=[
            shape_of((own.shape[0], 2, width), BF16),
            shape_of((count, width), F32),
            shape_of((width, hidden), F32),
            shape_of((1, hidden), F32),
            shape_of((hidden, 2 * width), F32),
            shape_of((1, 2 * width), F32),
            shape_of((1, width), F32),
            shape_of((1, adapt), F32),
        ],
        compiler_params=params(24 * MIB),
        cost_estimate=cost(96 * hidden * width * 6, 20 * hidden * width),
    )(pairs, act, embed, far(hidden_w), far(out_w), place, far(own), far(other))


def project_kernel(apart, x_ref, wq_ref, wk_ref, wv_ref, *refs):
    x = x_ref[...]
    if apart:
        place_ref, both_ref, q_ref, k_ref, v_ref, own_ref, other_ref = refs
        split_kernel(place_ref, both_ref, own_ref, other_ref)
    else:
        q_ref, k_ref, v_ref = refs[-3:]
    scale = LOG2E / math.sqrt(HEAD_DIM)
    q_ref[...] = (dot_nn(x, wq_ref[...]) * scale).astype(BF16)
    k_ref[...] = dot_nn(x, wk_ref[...]).astype(BF16)
    v_ref[...] = dot_nn(x, wv_ref[...]).astype(BF16)


def project(half, x, w_query, w_key, w_value, earlier, place=None, both=None):
    rows, width = x.shape
    step = rows // 2
    apart = both is not None
    block = pl.BlockSpec((step, width), lambda i: (i, 0))
    out_specs = [pl.BlockSpec((step, width), lambda i: (2 * half + i, 0))] * 3
    out_shape = [shape_of((2 * rows, width), BF16)] * 3
    more_specs, more = [ANY_SPEC] * len(earlier), all_far(earlier)
    if apart:
        more_specs = [SMEM_SPEC, pl.BlockSpec((step, 2, width), lambda i: (i, 0, 0))]
        more = [place, far(both)]
        out_specs = out_specs + [block] * 2
        out_shape = out_shape + [shape_of((rows, width), BF16)] * 2
    return pl.pallas_call(
        functools.partial(project_kernel, apart),
        grid=(2,),
        in_specs=[block] + [CORE_SPEC] * 3 + more_specs,
        out_specs=out_specs,
        out_shape=out_shape,
        input_output_aliases={4 + i: i for i in range(len(earlier))},
        compiler_params=params(20 * MIB),
        cost_estimate=cost(3 * rows * width * width, 2 * (4 * rows * width + 3 * width * width)),
    )(x, bring(w_query), bring(w_key), bring(w_value), *more)


def head_lanes(head, rows, lanes):
    place = lax.broadcasted_iota(jnp.int32, (rows, lanes), 1)
    return (place // HEAD_DIM == head).astype(F32).astype(BF16)


def first_lane(values):
    lane = lax.broadcasted_iota(jnp.int32, (values.shape[0], 128), 1)
    return jnp.where(lane == 0, values, 0.0).astype(BF16)


def block_diagonal(rows):
    return jnp.concatenate(
        [rows * head_lanes(head, rows.shape[0], LANES) for head in range(GROUP)], axis=0
    )


def attend_kernel(
    prefixed, first, scal_ref, q_ref, k_ref, v_ref, pk_ref, pv_ref, *refs
):
    pt_ref, ot_ref, st_ref, pp_ref, *scores = refs[-6:]
    keys = k_ref.shape[0]
    queries = q_ref.shape[0]
    half = (pl.program_id(0) + first) // 2

    def quadrant(count):
        place = scal_ref[half] + lax.broadcasted_iota(jnp.int32, (keys, 128), 0)
        bias = first_lane(jnp.where(place < scal_ref[2], 0.0, MASKED))
        ones = first_lane(jnp.ones((queries, 128), F32))
        tail = jnp.ones((16, keys), BF16)
        masks = [head_lanes(head, queries, 128) for head in range(2)]

        def score(head):
            pair = slice((head // 2) * 128, (head // 2 + 1) * 128)
            k_aug = jnp.concatenate([k_ref[:, pair], bias], axis=1)
            q_aug = jnp.concatenate([q_ref[:, pair] * masks[head % 2], ones], axis=1)
            scores[head % 2][...] = dot_nt(k_aug, q_aug)

        def weigh(head):
            own = scores[head % 2]
            top = jnp.max(own[...], axis=0, keepdims=True)
            if count:
                lead_scores = lead[head * PAD : (head + 1) * PAD]
                top = jnp.maximum(top, jnp.max(lead_scores, axis=0, keepdims=True))
            pt_ref[head] = jnp.exp2(own[...] - top).astype(BF16)
            st_ref[0, head : head + 1, :] = top
            if not count:
                return 0.0
            lead_weights = jnp.exp2(lead_scores - top).astype(BF16)
            pp_ref[0, head * PAD : (head + 1) * PAD, :] = lead_weights
            return jnp.sum(lead_weights.astype(F32), axis=0, keepdims=True)

        def mix(head, lead_total):
            rows = slice(head * HEAD_DIM, (head + 1) * HEAD_DIM)
            mixed_rows = dot_nn(jnp.concatenate([turned[rows], tail], axis=0), pt_ref[head])
            mixed = mixed_rows[:HEAD_DIM]
            if count:
                lead_weights = pp_ref[0, head * PAD : (head + 1) * PAD, :]
                mixed = mixed + dot_nn(lead_turned[rows], lead_weights)
            ot_ref[rows, :] = mixed.astype(BF16)
            total_row = mixed_rows[HEAD_DIM : HEAD_DIM + 1] + lead_total
            st_ref[0, GROUP + head : GROUP + head + 1, :] = total_row

        score(0)
        turned = v_ref[...].T
        if count:
            lead_turned = pv_ref[...].T
            lead = dot_nt(block_diagonal(pk_ref[...]), q_ref[...])
            row = lax.broadcasted_iota(jnp.int32, lead.shape, 0)
            lead = jnp.where(row % PAD < count, lead, MASKED)
        lead_totals = []
        for head in range(GROUP):
            if head + 1 < GROUP:
                score(head + 1)
            lead_totals.append(weigh(head))
            if head:
                mix(head - 1, lead_totals[head - 1])
        mix(GROUP - 1, lead_totals[GROUP - 1])

    @pl.when(half == 0)
    def _():
        quadrant(prefixed)

    @pl.when(half == 1)
    def _():
        quadrant(0)


def attend(count, scal, first, quadrants, q, k, v, lead, earlier):
    tokens, width = q.shape
    rows = tokens // 2
    groups = width // LANES
    last = groups - 1

    def lead_place(i, g):
        quadrant = i + first
        return (jnp.where(quadrant < 2, g, last), 0, jnp.minimum(quadrant, 1))

    keys = pl.BlockSpec((rows, LANES), lambda i, g: ((i + first) // 2, g))
    in_specs = [
        SMEM_SPEC,
        pl.BlockSpec((rows, LANES), lambda i, g: ((i + first) % 2, g)),
        keys,
        keys,
    ]
    in_specs += [pl.BlockSpec((PAD, LANES), lambda i, g: (0, g))] * 2
    out_specs = [
        pl.BlockSpec(
            (None, GROUP, rows, rows), lambda i, g: ((i + first) // 2, g, 0, (i + first) % 2)
        ),
        pl.BlockSpec((None, LANES, rows), lambda i, g: ((i + first) // 2, g, (i + first) % 2)),
        pl.BlockSpec(
            (None, 1, 2 * GROUP, rows), lambda i, g: ((i + first) // 2, g, 0, (i + first) % 2)
        ),
        pl.BlockSpec((1, GROUP * PAD, rows), lead_place),
    ]
    out_shape = [
        shape_of((2, groups * GROUP, rows, tokens), BF16),
        shape_of((2, width, tokens), BF16),
        shape_of((2, groups, 2 * GROUP, tokens), F32),
        shape_of((groups, GROUP * PAD, tokens), BF16),
    ]
    macs = quadrants * groups * GROUP * rows * rows * 256 * 2
    return pl.pallas_call(
        functools.partial(attend_kernel, count, first),
        grid=(quadrants, groups),
        in_specs=in_specs + [ANY_SPEC] * len(earlier),
        out_specs=out_specs,
        out_shape=out_shape,
        input_output_aliases={6 + i: i for i in range(len(earlier))},
        scratch_shapes=[pltpu.VMEM((rows, rows), F32)] * 2,
        compiler_params=params(16 * MIB),
        cost_estimate=cost(macs, quadrants * 14 * MIB),
    )(scal, *all_far((q, k, v, *lead, *earlier)))


def lead_back_kernel(
    count, q_ref, up_ref, rst_ref, del_ref, pp_ref, pk_ref, pv_ref, bias_ref, pair_ref, dqt_ref
):
    queries = q_ref.shape[0]
    ups = []
    deltas = []
    for head in range(GROUP):
        rows = slice(head * HEAD_DIM, (head + 1) * HEAD_DIM)
        share = rst_ref[0, head : head + 1, :]
        ups.append((up_ref[rows, :].astype(F32) * share).astype(BF16))
        delta = del_ref[0, head : head + 1, :] * share
        deltas.append(jnp.broadcast_to(delta, (PAD, queries)))
    up = jnp.concatenate(ups, axis=0)
    delta = jnp.concatenate(deltas, axis=0)
    weights = pp_ref[0]
    key_diagonal = block_diagonal(pk_ref[...])
    value_diagonal = block_diagonal(pv_ref[...])
    weight_grads = dot_nn(value_diagonal, up)
    score_grads = (weights.astype(F32) * (weight_grads - delta)).astype(BF16)
    dqt_ref[...] = dot_tn(key_diagonal, score_grads).astype(BF16)
    key_grads = dot_nn(score_grads, q_ref[...]) * (1.0 / LOG2E)
    value_grads = dot_nt(weights, up)
    lane = lax.broadcasted_iota(jnp.int32, (PAD, LANES), 1) // HEAD_DIM
    key_total = jnp.zeros((PAD, LANES), F32)
    value_total = jnp.zeros((PAD, LANES), F32)
    for head in range(GROUP):
        rows = slice(head * PAD, (head + 1) * PAD)
        key_total = jnp.where(lane == head, key_grads[rows], key_total)
        value_total = jnp.where(lane == head, value_grads[rows], value_total)
    row = lax.broadcasted_iota(jnp.int32, (PAD, LANES), 0)
    key_total = jnp.where(row == count, bias_ref[0:1, :], key_total)
    key_total = jnp.where(row == count + 1, bias_ref[1:2, :], key_total)
    pair_ref[:PAD, :] = key_total.astype(BF16)
    pair_ref[PAD:, :] = value_total.astype(BF16)


def lead_backward(count, q, up, shares, deltas, lead_weights, prefix_keys, prefix_values, biases):
    tokens, width = q.shape
    groups = width // LANES
    small = pl.BlockSpec((PAD, LANES), lambda g: (0, g))
    stats = pl.BlockSpec((1, 2 * GROUP, tokens), lambda g: (g, 0, 0))
    return pl.pallas_call(
        functools.partial(lead_back_kernel, count),
        grid=(groups,),
        in_specs=[
            pl.BlockSpec((tokens, LANES), lambda g: (0, g)),
            pl.BlockSpec((LANES, tokens), lambda g: (g, 0)),
            stats,
            stats,
            pl.BlockSpec((1, GROUP * PAD, tokens), lambda g: (g, 0, 0)),
            small,
            small,
            pl.BlockSpec((8, LANES), lambda g: (0, g)),
        ],
        out_specs=[
            pl.BlockSpec((2 * PAD, LANES), lambda g: (0, g)),
            pl.BlockSpec((LANES, tokens), lambda g: (g, 0)),
        ],
        out_shape=[
            jax.ShapeDtypeStruct((2 * PAD, width), BF16),
            shape_of((width, tokens), BF16),
        ],
        compiler_params=params(14 * MIB),
        cost_estimate=cost(groups * 4 * GROUP * PAD * tokens * LANES, 10 * MIB),
    )(*all_far((q, up, shares, deltas, lead_weights)), prefix_keys, prefix_values, biases)


def attend_back_kernel(
    half,
    last_keys,
    last_queries,
    has_earlier,
    q_ref,
    k_ref,
    v_ref,
    up_ref,
    rst_ref,
    del_ref,
    pt_ref,
    dqt_in_ref,
    *refs,
):
    dq_ref, dk_ref, dv_ref = refs[-5:-2]
    weight_grads = refs[-2:]
    queries = q_ref.shape[0]
    lane = lax.broadcasted_iota(jnp.int32, (queries, 128), 1) // HEAD_DIM
    masks = [(lane == head).astype(F32).astype(BF16) for head in range(2)]
    zeros = jnp.zeros((HEAD_DIM, queries), BF16)
    turned = k_ref[...].T
    ups = {}
    grads = {}
    query_grads = []
    key_grads = []
    value_grads = []

    def pair_of(head):
        return slice((head // 2) * 128, (head // 2 + 1) * 128)

    def rows_of(head):
        return slice(head * HEAD_DIM, (head + 1) * HEAD_DIM)

    def share_of(head):
        return rst_ref[0, half * GROUP + head : half * GROUP + head + 1, :]

    def weight_grad(head):
        up = (up_ref[rows_of(head), :].astype(F32) * share_of(head)).astype(BF16)
        ups[head] = jnp.concatenate([up, zeros] if head % 2 == 0 else [zeros, up], axis=0)
        weight_grads[head % 2][...] = dot_nn(v_ref[:, pair_of(head)], ups[head])

    def score_grad(head):
        delta = del_ref[0, head : head + 1, :] * share_of(head)
        return (pt_ref[head].astype(F32) * (weight_grads[head % 2][...] - delta)).astype(BF16)

    def value_term(head):
        return dot_nt(pt_ref[head], ups[head])

    def key_term(head):
        return dot_nn(grads[head], q_ref[:, pair_of(head)] * masks[head % 2])

    def query_term(head):
        return dqt_in_ref[rows_of(head), :].astype(F32) + dot_nn(turned[rows_of(head)], grads[head])

    weight_grad(0)
    for head in range(GROUP):
        if head + 1 < GROUP:
            weight_grad(head + 1)
        grads[head] = score_grad(head)
        value = value_term(head)
        query_grads.append(query_term(head))
        key = key_term(head)
        if head % 2:
            key_grads[-1] = key_grads[-1] + key
            value_grads[-1] = value_grads[-1] + value
        else:
            key_grads.append(key)
            value_grads.append(value)
    query_grad = jnp.concatenate(query_grads, axis=0)
    key_grad = jnp.concatenate(key_grads, axis=1)
    value_grad = jnp.concatenate(value_grads, axis=1)
    if not last_keys:
        dq_ref[...] = query_grad.astype(BF16)
    else:
        dq_ref[...] = (query_grad * (1.0 / math.sqrt(HEAD_DIM))).astype(BF16).T
    if has_earlier:
        key_grad = key_grad + refs[0][...].astype(F32)
        value_grad = value_grad + refs[1][...].astype(F32)
    if last_queries:
        key_grad = key_grad * (1.0 / LOG2E)
    dk_ref[...] = key_grad.astype(BF16)
    dv_ref[...] = value_grad.astype(BF16)


def attend_back(
    key_half, query_half, last_keys, last_queries, q, k, v, up, shares, deltas, weights, dqt, earlier
):
    tokens, width = q.shape
    rows = tokens // 2
    groups = width // LANES
    query_columns = pl.BlockSpec((LANES, rows), lambda g: (g, query_half))
    stats = pl.BlockSpec((1, 2 * GROUP, rows), lambda g: (g, 0, query_half))
    finished = pl.BlockSpec((rows, LANES), lambda g: (0, g))
    out_columns = pl.BlockSpec((LANES, rows), lambda g: (g, 0))
    sofar = query_columns if dqt.shape[1] == tokens else out_columns
    macs = groups * GROUP * rows * rows * 256 * 4
    return pl.pallas_call(
        functools.partial(
            attend_back_kernel, key_half, last_keys, last_queries, len(earlier) > 0
        ),
        grid=(groups,),
        in_specs=[
            pl.BlockSpec((rows, LANES), lambda g: (query_half, g)),
            pl.BlockSpec((rows, LANES), lambda g: (key_half, g)),
            pl.BlockSpec((rows, LANES), lambda g: (key_half, g)),
            query_columns,
            stats,
            stats,
            pl.BlockSpec((None, GROUP, rows, rows), lambda g: (key_half, g, 0, query_half)),
            sofar,
        ]
        + [finished] * len(earlier),
        out_specs=[finished if last_keys else out_columns, finished, finished],
        out_shape=[
            shape_of((rows, width) if last_keys else (width, rows), BF16),
            shape_of((rows, width), BF16),
            shape_of((rows, width), BF16),
        ],
        scratch_shapes=[pltpu.VMEM((rows, rows), F32)] * 2,
        compiler_params=params(18 * MIB),
        cost_estimate=cost(macs, 12 * MIB),
    )(*all_far((q, k, v, up, shares, deltas, weights, dqt, *earlier)))


def gelu_pair(values):
    scaled = values * 0.7071067811865476
    below = 0.5 * lax.erf(scaled) + 0.5
    decay = jnp.exp2(scaled * scaled * (-LOG2E))
    return values * below, below + values * 0.3989422804014327 * decay


def row_mean(values):
    return jnp.mean(values, axis=-1, keepdims=True)


def front_kernel(
    tiles,
    scal_ref,
    x_own_ref,
    x_other_ref,
    ot_own_ref,
    ot_other_ref,
    st_own_ref,
    st_other_ref,
    og_own_ref,
    og_other_ref,
    gain_one_ref,
    gain_two_ref,
    down_bias_ref,
    up_bias_ref,
    wo_ref,
    fin_ref,
    fout_ref,
    down_ref,
    up_ref,
    out_own_ref,
    out_other_ref,
    rst_ref,
    mix_ref,
    slope_ref,
    grad_low_ref,
    norm_grad_ref,
    normed_ref,
    inv_ref,
    kept_ref,
    sent_ref,
    bias_grad_ref,
    act_ref,
    squeeze_ref,
    low_ref,
):
    step = pl.program_id(0)
    tile = x_own_ref.shape[0]
    width = x_own_ref.shape[1]
    hidden = fin_ref.shape[1]
    chunk = 512
    chunks = [slice(first, first + chunk) for first in range(0, hidden, chunk)]
    own = step < tiles // 2
    x = jnp.where(own, x_own_ref[...], x_other_ref[...]).astype(F32)
    top_own, top_other = st_own_ref[:, :GROUP, :], st_other_ref[:, :GROUP, :]
    top = jnp.maximum(top_own, top_other)
    share_own, share_other = jnp.exp2(top_own - top), jnp.exp2(top_other - top)
    inverse = 1.0 / (
        st_own_ref[:, GROUP:, :] * share_own + st_other_ref[:, GROUP:, :] * share_other
    )
    rst_ref[:, :GROUP, :] = share_own * inverse
    rst_ref[:, GROUP:, :] = share_other * inverse
    mixes = []
    for head in range(width // HEAD_DIM):
        rows = slice(head * HEAD_DIM, (head + 1) * HEAD_DIM)
        group, place = head // GROUP, head % GROUP
        mixes.append(
            (
                ot_own_ref[rows, :].astype(F32) * rst_ref[group, place : place + 1, :]
                + ot_other_ref[rows, :].astype(F32) * rst_ref[group, GROUP + place : GROUP + place + 1, :]
            ).astype(BF16)
        )
    mix = jnp.concatenate(mixes, axis=0)
    mix_ref[...] = mix
    resid_one = x + dot_tn(mix, wo_ref[...])
    centred = resid_one - row_mean(resid_one)
    inv_one = lax.rsqrt(row_mean(centred * centred) + 1e-05)
    normed = centred * inv_one
    normed_ref[...] = normed.astype(BF16)
    inv_ref[...] = inv_one
    norm_one = normed * gain_one_ref[...]
    norm_low = norm_one.astype(BF16)

    squeeze = dot_nn(norm_low, down_ref[...]) + down_bias_ref[...]
    inner = dot_nn(norm_low, fin_ref[:, chunks[0]])
    squeeze_act, squeeze_slope = gelu_pair(squeeze)
    squeeze_act = squeeze_act.astype(BF16)
    resid_two = norm_one + 4.0 * (dot_nn(squeeze_act, up_ref[...]) + up_bias_ref[...])
    for place, columns in enumerate(chunks):
        more = place + 1 < len(chunks)
        coming = dot_nn(norm_low, fin_ref[:, chunks[place + 1]]) if more else None
        act, slope = gelu_pair(inner)
        slope_ref[:, columns] = slope.astype(BF16)
        resid_two = resid_two + dot_nn(act.astype(BF16), fout_ref[columns, :])
        inner = coming

    centred = resid_two - row_mean(resid_two)
    inv_two = lax.rsqrt(row_mean(centred * centred) + 1e-05)
    normed_two = centred * inv_two
    base = jnp.where(own, scal_ref[0], scal_ref[1] - (tiles // 2) * tile) + step * tile
    place = base + lax.broadcasted_iota(jnp.int32, (tile, 1), 0)
    valid = (place < scal_ref[2]).astype(F32)
    gain_two = gain_two_ref[...]
    out = (normed_two * gain_two * valid).astype(BF16)
    upstream = jnp.where(own, og_own_ref[...], og_other_ref[...]).astype(F32) * valid * gain_two
    grad_two = inv_two * (
        upstream - row_mean(upstream) - normed_two * row_mean(upstream * normed_two)
    )
    grad_low = grad_two.astype(BF16)
    grad_adapt = 4.0 * grad_low
    grad_squeeze = (dot_nt(grad_adapt, up_ref[...]) * squeeze_slope).astype(BF16)
    norm_grad_ref[...] = (grad_two + dot_nt(grad_squeeze, down_ref[...])).astype(BF16)
    here = pl.ds(pl.multiple_of(step * tile, tile), tile)
    grad_low_ref[here, :] = grad_low
    act_ref[here, :] = squeeze_act
    squeeze_ref[here, :] = grad_squeeze
    low_ref[here, :] = norm_low
    up_bias_grad = jnp.sum(grad_adapt.astype(F32), axis=0, keepdims=True)
    down_bias_grad = jnp.sum(grad_squeeze.astype(F32), axis=0, keepdims=True)
    adapt = down_bias_grad.shape[1]

    @pl.when(own)
    def _():
        out_own_ref[...] = out

    @pl.when(jnp.logical_not(own))
    def _():
        out_other_ref[...] = out

    @pl.when(step == 0)
    def _():
        bias_grad_ref[...] = jnp.zeros_like(bias_grad_ref)
        bias_grad_ref[0:1, :] = up_bias_grad
        bias_grad_ref[1:2, :adapt] = down_bias_grad

    @pl.when(step > 0)
    def _():
        bias_grad_ref[0:1, :] += up_bias_grad
        bias_grad_ref[1:2, :adapt] += down_bias_grad

    @pl.when(step == tiles - 1)
    def _():
        first = scal_ref[3] == 0
        up_total = (4.0 * dot_tn(act_ref[...], grad_low_ref[...])).astype(BF16)
        down_total = dot_tn(squeeze_ref[...], low_ref[...]).astype(BF16)
        kept_ref[...] = jnp.where(first, up_total, down_total)
        sent_ref[...] = jnp.where(first, down_total, up_total)


def front(
    scal, x_own, x_other, mix_parts, tops_sums, og_own, og_other, w_output, attn_gain, ffn_in,
    ffn_out, ffn_gain, down, down_bias, up, up_bias,
):
    rows, width = x_own.shape
    tokens = 2 * rows
    hidden = ffn_in.shape[1]
    adapt = down.shape[1]
    groups = width // LANES
    tile = 256
    tiles = tokens // tile
    near = pl.BlockSpec((tile, width), lambda i: (jnp.minimum(i, tiles // 2 - 1), 0))
    far = pl.BlockSpec((tile, width), lambda i: (jnp.maximum(i - tiles // 2, 0), 0))
    row_block = pl.BlockSpec((tile, width), lambda i: (i, 0))
    column_block = pl.BlockSpec((width, tile), lambda i: (0, i))
    stats = pl.BlockSpec((groups, 2 * GROUP, tile), lambda i: (0, 0, i))
    mixes = [pl.BlockSpec((None, width, tile), lambda i, half=half: (half, 0, i)) for half in range(2)]
    tops = [
        pl.BlockSpec((None, groups, 2 * GROUP, tile), lambda i, half=half: (half, 0, 0, i))
        for half in range(2)
    ]
    return pl.pallas_call(
        functools.partial(front_kernel, tiles),
        grid=(tiles,),
        in_specs=[
            SMEM_SPEC, near, far, *mixes, *tops, near, far,
            whole((1, width)), whole((1, width)), whole((1, adapt)), whole((1, width)),
        ] + [CORE_SPEC] * 5,
        out_specs=[
            near, far, stats, column_block, pl.BlockSpec((tile, hidden), lambda i: (i, 0)),
            kept((tokens, width)), row_block, row_block, pl.BlockSpec((tile, 1), lambda i: (i, 0)),
            kept((adapt, width)), kept((adapt, width)), whole((8, width)),
        ],
        out_shape=[
            shape_of((rows, width), BF16),
            shape_of((rows, width), BF16),
            shape_of((groups, 2 * GROUP, tokens), F32),
            shape_of((width, tokens), BF16),
            shape_of((tokens, hidden), BF16),
            shape_of((tokens, width), BF16),
            shape_of((tokens, width), BF16),
            shape_of((tokens, width), BF16),
            shape_of((tokens, 1), F32),
            shape_of((adapt, width), BF16),
            shape_of((adapt, width), BF16),
            shape_of((8, width), F32),
        ],
        scratch_shapes=[
            pltpu.VMEM((tokens, adapt), BF16),
            pltpu.VMEM((tokens, adapt), BF16),
            pltpu.VMEM((tokens, width), BF16),
        ],
        compiler_params=params(32 * MIB),
        cost_estimate=cost(tokens * width * (width + 2 * hidden + 6 * adapt), 60 * MIB),
    )(
        scal,
        *all_far((x_own, x_other, mix_parts, mix_parts, tops_sums, tops_sums, og_own, og_other)),
        attn_gain[None], ffn_gain[None], down_bias[None], up_bias[None],
        *[bring(item) for item in (w_output, ffn_in, ffn_out, down, up)],
    )


def rear_kernel(
    grad_low_ref, norm_grad_ref, slope_ref, normed_ref, inv_ref, mix_ref, gain_ref, wo_ref, fin_ref,
    fout_ref, grad_one_ref, up_ref, del_ref,
):
    hidden = fin_ref.shape[1]
    chunk = 1024
    chunks = [slice(first, first + chunk) for first in range(0, hidden, chunk)]
    grad_low = grad_low_ref[...]
    grad_norm = norm_grad_ref[...].astype(F32)
    inner = dot_nt(grad_low, fout_ref[chunks[0], :])
    for place, columns in enumerate(chunks):
        more = place + 1 < len(chunks)
        coming = dot_nt(grad_low, fout_ref[chunks[place + 1], :]) if more else None
        low = (inner * slope_ref[:, columns].astype(F32)).astype(BF16)
        grad_norm = grad_norm + dot_nt(low, fin_ref[:, columns])
        inner = coming
    grad = grad_norm * gain_ref[...]
    normed = normed_ref[...].astype(F32)
    grad_one = inv_ref[...] * (grad - row_mean(grad) - normed * row_mean(grad * normed))
    grad_low_one = grad_one.astype(BF16)
    grad_one_ref[...] = grad_low_one
    up = dot_nt(wo_ref[...], grad_low_one).astype(BF16)
    up_ref[...] = up
    product = up.astype(F32) * mix_ref[...].astype(F32)
    for head in range(product.shape[0] // HEAD_DIM):
        rows = slice(head * HEAD_DIM, (head + 1) * HEAD_DIM)
        group, place = head // GROUP, head % GROUP
        del_ref[group, place : place + 1, :] = jnp.sum(product[rows], axis=0, keepdims=True)
    del_ref[:, GROUP:, :] = jnp.zeros_like(del_ref[:, GROUP:, :])


def rear(grad_low, norm_grad, slope, normed, inv, mix, w_output, attn_gain, ffn_in, ffn_out):
    tokens, width = grad_low.shape
    hidden = ffn_in.shape[1]
    groups = width // LANES
    tile = 256
    row_block = pl.BlockSpec((tile, width), lambda i: (i, 0))
    column_block = pl.BlockSpec((width, tile), lambda i: (0, i))
    return pl.pallas_call(
        rear_kernel,
        grid=(tokens // tile,),
        in_specs=[
            row_block, row_block, pl.BlockSpec((tile, hidden), lambda i: (i, 0)), row_block,
            pl.BlockSpec((tile, 1), lambda i: (i, 0)), column_block, whole((1, width)),
        ] + [CORE_SPEC] * 3,
        out_specs=[
            row_block, column_block, pl.BlockSpec((groups, 2 * GROUP, tile), lambda i: (0, 0, i)),
        ],
        out_shape=[
            shape_of((tokens, width), BF16),
            shape_of((width, tokens), BF16),
            shape_of((groups, 2 * GROUP, tokens), F32),
        ],
        compiler_params=params(22 * MIB),
        cost_estimate=cost(tokens * width * (width + 2 * hidden), 50 * MIB),
    )(*all_far((grad_low, norm_grad, slope, normed, inv, mix)), attn_gain[None], bring(w_output), bring(ffn_in), bring(ffn_out))


def input_grad_kernel(last, place_ref, grad_ref, dq_ref, dk_ref, dv_ref, wq_ref, wk_ref, wv_ref, *refs):
    total = grad_ref[...].astype(F32) + dot_nt(dq_ref[...], wq_ref[...])
    total = total + dot_nt(dk_ref[...], wk_ref[...])
    total = total + dot_nt(dv_ref[...], wv_ref[...])
    total = total.astype(BF16)
    if not last:
        refs[0][...] = total
        return
    arrived_ref, half_ref, far_ref, both_ref, up_ref, down_ref = refs
    merge_kernel(place_ref, total, arrived_ref, both_ref)
    first = place_ref[1] == 0
    half, other = half_ref[...].astype(F32), far_ref[...].astype(F32)
    up_ref[...] = jnp.where(first, half, other)
    down_ref[...] = jnp.where(first, other, half).T


def input_grad(place, half, grad_one, dq, dk, dv, weights, last):
    rows, width = dk.shape
    step = rows // 2
    block = pl.BlockSpec((step, width), lambda i: (i, 0))
    out_specs, out_shape = block, shape_of((rows, width), BF16)
    if last:
        out_specs = [
            pl.BlockSpec((step, 2, width), lambda i: (i, 0, 0)),
            block,
            pl.BlockSpec((width, step), lambda i: (0, i)),
        ]
        out_shape = [
            shape_of((rows, 2, width), BF16),
            shape_of((rows, width), F32),
            shape_of((width, rows), F32),
        ]
    return pl.pallas_call(
        functools.partial(input_grad_kernel, bool(last)),
        grid=(2,),
        in_specs=[SMEM_SPEC, pl.BlockSpec((step, width), lambda i: (2 * half + i, 0))]
        + [block] * 3
        + [CORE_SPEC] * 3
        + [block] * len(last),
        out_specs=out_specs,
        out_shape=out_shape,
        compiler_params=params(26 * MIB),
        cost_estimate=cost(3 * rows * width * width, 14 * MIB),
    )(place, *all_far((grad_one, dq, dk, dv)), *[bring(item) for item in weights], *last)


def swap(value, seq_bit, dp_bits):
    width = lax.axis_size("dp")
    count = lax.axis_size("seq") * width
    pairs = [
        (device, ((device // width) ^ seq_bit) * width + ((device % width) ^ dp_bits))
        for device in range(count)
    ]
    return lax.ppermute(value, ("seq", "dp"), pairs)


def gather_line(value):
    width = lax.axis_size("dp")
    groups = [[4 * line + place for line in range(width // 4)] for place in range(4)]
    return lax.all_gather(value, "dp", axis_index_groups=groups)


def total(values):
    return jnp.sum(values.astype(F32), axis=0)


def square_place():
    return 2 * ((lax.axis_index("dp") // 2) % 2) + lax.axis_index("seq")


def square_swaps(values):
    return [swap(values[offset - 1], offset % 2, 2 * (offset // 2)) for offset in range(1, 4)]


def sum_square(value):
    place = square_place()
    quarters = value.reshape(4, value.shape[0] // 4, value.shape[1])
    pick = [
        lax.dynamic_index_in_dim(quarters, place ^ offset, 0, keepdims=False) for offset in range(4)
    ]
    return pick[:1] + square_swaps(pick[1:])


def add(terms):
    value = terms[0].astype(F32)
    for term in terms[1:]:
        value = value + term.astype(F32)
    return value.astype(BF16)


def tie(*values):
    return lax.optimization_barrier(values)


def on_pair(
    hidden_in,
    lengths,
    w_query,
    w_key,
    w_value,
    w_output,
    attn_gain,
    ffn_in,
    ffn_out,
    ffn_gain,
    adapter_down,
    adapter_down_bias,
    adapter_up,
    adapter_up_bias,
    prefix_embed,
    prefix_hidden_w,
    prefix_hidden_b,
    prefix_out_w,
    prefix_out_b,
    out_grad,
):
    rows, _, width = hidden_in.shape
    count = prefix_embed.shape[0]
    position = lax.axis_index("seq")
    core = lax.axis_index("dp") % 2
    place = jnp.stack([position, core]).astype(jnp.int32)
    length = jnp.where(position == 0, lengths[0], lengths[1])
    scal = jnp.stack([position * rows, (1 - position) * rows, length, core]).astype(jnp.int32)

    x_own, x_send = split(place, hidden_in)
    x_other = shifted(x_send, "seq", 1)

    embed = jnp.pad(prefix_embed, ((0, PAD - count), (0, 0)))
    prefix_act, prefix_keys, prefix_values = prefix_forward(
        embed, prefix_hidden_w, prefix_hidden_b, prefix_out_w, prefix_out_b
    )
    x_own, prefix_keys = tie(x_own, prefix_keys)
    lead = (prefix_keys, prefix_values)
    *triple, og_own, og_send = project(0, x_own, w_query, w_key, w_value, (), place, out_grad)
    og_other = shifted(og_send, "seq", 1)
    begun = attend(count, scal, 0, 1, *triple, lead, ())
    q, k, v = project(1, x_other, w_query, w_key, w_value, triple)
    weights, mix_parts, tops_sums, lead_weights = attend(count, scal, 1, 3, q, k, v, lead, begun)

    (
        out_own, out_send, shares, mix, slope, grad_low, norm_grad, normed, inv_one,
        adapt_kept, adapt_sent, bias_grads,
    ) = front(
        scal, x_own, x_other, mix_parts, tops_sums, og_own, og_other,
        w_output, attn_gain, ffn_in, ffn_out, ffn_gain, adapter_down, adapter_down_bias,
        adapter_up, adapter_up_bias,
    )
    out_other = shifted(out_send, "seq", 1)
    core_terms = [adapt_kept, swap(adapt_sent, 0, 1)]
    grad_one, upstream, deltas = rear(
        grad_low, norm_grad, slope, normed, inv_one, mix, w_output, attn_gain, ffn_in, ffn_out
    )
    upstream, out_other, adapt_sum = tie(upstream, out_other, add(core_terms))
    square_terms = sum_square(adapt_sum)
    pair, dqt = lead_backward(
        count, q, upstream, shares, deltas, lead_weights, prefix_keys, prefix_values, bias_grads
    )
    pair_core = swap(pair, 0, 1)

    back = (q, k, v)
    part_own, dk_other, dv_other = attend_back(
        1, 0, False, False, *back, upstream, shares, deltas, weights, dqt, ()
    )
    dk_other, pair, adapt_sum = tie(dk_other, add([pair, pair_core]), add(square_terms))
    adapt_line = gather_line(adapt_sum)
    pair_square = square_swaps([pair] * 3)
    part_other, dk_other, dv_other = attend_back(
        1, 1, False, True, *back, upstream, shares, deltas, weights, dqt, (dk_other, dv_other)
    )
    pair_sum = pair.astype(F32) + sum(item.astype(F32) for item in pair_square)
    part_other, pair_sum = tie(part_other, pair_sum)
    dq_other, dk_own, dv_own = attend_back(
        0, 1, True, False, *back, upstream, shares, deltas, weights, part_other, ()
    )
    adapt_sum = jnp.sum(adapt_line.astype(F32), axis=0).astype(BF16)
    dq_other, adapt_sum, pair_sum = tie(dq_other, adapt_sum, pair_sum)
    pair_line = gather_line(pair_sum)
    adapt_x, adapt_y = swap(adapt_sum, 1, 0), swap(adapt_sum, 0, 2)
    triple_weights = (w_query, w_key, w_value)
    grad_other = input_grad(place, 1, grad_one, dq_other, dk_other, dv_other, triple_weights, ())
    grad_other, dk_own, adapt_x = tie(grad_other, dk_own, adapt_x)
    grad_back = shifted(grad_other, "seq", 1)
    adapt_xy = swap(adapt_x, 0, 2)
    dq_own, dk_own, dv_own = attend_back(
        0, 0, True, True, *back, upstream, shares, deltas, weights, part_own, (dk_own, dv_own)
    )
    dq_own, pair_line, out_other, adapt_y, adapt_xy = tie(
        dq_own, pair_line, out_other, adapt_y, adapt_xy
    )
    adapt_half = jnp.stack([adapt_sum, adapt_x, adapt_y, adapt_xy])
    place_here = square_place()
    adapt_half = jnp.concatenate(
        [lax.dynamic_slice_in_dim(adapt_half, spot ^ place_here, 1, 0) for spot in range(4)]
    ).reshape(adapt_kept.shape)
    adapt_far = swap(adapt_half, 0, 1)
    layer_out, *prefix_grads = prefix_backward(
        count,
        adapter_down_bias.shape[0],
        pair_line,
        prefix_act,
        embed,
        prefix_hidden_w,
        prefix_out_w,
        place,
        out_own,
        out_other,
    )
    layer_out, grad_back, dq_own = tie(layer_out, grad_back, dq_own)
    out_w_grad = prefix_grads[3]
    input_total, up_total, down_total = input_grad(
        place, 0, grad_one, dq_own, dk_own, dv_own, triple_weights, (grad_back, adapt_half, adapt_far)
    )
    return (
        layer_out,
        input_total,
        down_total,
        prefix_grads[6][0],
        up_total,
        prefix_grads[5][0],
        prefix_grads[0],
        prefix_grads[1],
        prefix_grads[2][0],
        out_w_grad,
        prefix_grads[4][0],
    )


def solution(mesh):
    in_specs = (
        P("seq", "dp", None),
        P("dp"),
        P(),
        P(),
        P(),
        P(),
        P(),
        P(),
        P(),
        P(),
        P(),
        P(),
        P(),
        P(),
        P(),
        P(),
        P(),
        P(),
        P(),
        P("seq", "dp", None),
    )
    out_specs = (
        P("seq", "dp", None),
        P("seq", "dp", None),
        P(),
        P(),
        P(),
        P(),
        P(),
        P(),
        P(),
        P(),
        P(),
    )
    pairs = mesh.shape["seq"] == 2 and mesh.shape["dp"] % 8 == 0

    def on_one(*arrays):
        step = on_pair if pairs and arrays[0].shape[1] == 2 else on_device
        return step(*arrays)

    return jax.shard_map(
        on_one, mesh=mesh, in_specs=in_specs, out_specs=out_specs, check_vma=False
    )
```

```python
import functools
import math

import jax
import jax.numpy as jnp
from jax import lax
from jax.experimental import pallas as pl
from jax.experimental.pallas import tpu as pltpu
from jax.sharding import PartitionSpec as P

HEADS = 16


HIGHEST_PRECISION = lax.Precision.HIGHEST


def shifted(value, axis, steps):
    count = lax.axis_size(axis)
    pairs = [(source, (source + steps) % count) for source in range(count)]
    return lax.ppermute(value, axis, pairs)


def mixed(left, right):
    return jnp.dot(left, right, preferred_element_type=jnp.float32)


def mixed_left(left, right):
    return lax.dot_general(
        left, right, (((0,), (0,)), ((), ())), preferred_element_type=jnp.float32
    )


def mixed_right(left, right):
    return lax.dot_general(
        left, right, (((1,), (1,)), ((), ())), preferred_element_type=jnp.float32
    )


def precise(left, right):
    return jnp.dot(left, right, precision=HIGHEST_PRECISION, preferred_element_type=jnp.float32)


def precise_left(left, right):
    return lax.dot_general(
        left,
        right,
        (((0,), (0,)), ((), ())),
        precision=HIGHEST_PRECISION,
        preferred_element_type=jnp.float32,
    )


def precise_right(left, right):
    return lax.dot_general(
        left,
        right,
        (((1,), (1,)), ((), ())),
        precision=HIGHEST_PRECISION,
        preferred_element_type=jnp.float32,
    )


def gelu_value(inputs):
    return 0.5 * inputs * (1.0 + lax.erf(inputs * 0.7071067811865476))


def gelu_slope(inputs):
    return (
        0.5 * (1.0 + lax.erf(inputs * 0.7071067811865476))
        + inputs * jnp.exp(-0.5 * inputs * inputs) * 0.3989422804014327
    )


def normalize(values):
    row_mean = jnp.mean(values, axis=-1, keepdims=True)
    centred = values - row_mean
    spread = jnp.mean(centred * centred, axis=-1, keepdims=True)
    inv_std = lax.rsqrt(spread + 1e-05)
    return (centred * inv_std, inv_std)


def norm_back(upstream, normed, inv_std):
    mean_grad = jnp.mean(upstream, axis=-1, keepdims=True)
    mean_proj = jnp.mean(upstream * normed, axis=-1, keepdims=True)
    return inv_std * (upstream - mean_grad - normed * mean_proj)


def key_allowed(offset, key_count, seq_lengths):
    places = offset + lax.iota(jnp.int32, key_count)
    return places[None, :] < seq_lengths[:, None]


def lead_state(queries4, prefix_keys4, prefix_values4):
    inv_root = 1.0 / math.sqrt(queries4.shape[3])
    scores = (
        jnp.einsum("rshd,phd->rshp", queries4, prefix_keys4, preferred_element_type=jnp.float32)
        * inv_root
    )
    running_max = jnp.max(scores, axis=3)
    weights = jnp.exp(scores - running_max[..., None])
    running_sum = jnp.sum(weights, axis=3)
    running_mix = jnp.einsum(
        "rshp,phd->rshd",
        weights.astype(jnp.bfloat16),
        prefix_values4,
        preferred_element_type=jnp.float32,
    )
    return (running_max, running_sum, running_mix)


def fold_block(carried, key_block, value_block, offset, queries4, seq_lengths):
    key_count, seqs_here = (key_block.shape[0], key_block.shape[1])
    head_count, head_dim = (queries4.shape[2], queries4.shape[3])
    inv_root = 1.0 / math.sqrt(head_dim)
    keys4 = key_block.reshape(key_count, seqs_here, head_count, head_dim)
    values4 = value_block.reshape(key_count, seqs_here, head_count, head_dim)
    running_max, running_sum, running_mix = carried
    scores = (
        jnp.einsum("rshd,tshd->rsht", queries4, keys4, preferred_element_type=jnp.float32)
        * inv_root
    )
    allowed = key_allowed(offset, key_count, seq_lengths)[None, :, None, :]
    scores = jnp.where(allowed, scores, -jnp.inf)
    new_max = jnp.maximum(running_max, jnp.max(scores, axis=3))
    weights = jnp.exp(scores - new_max[..., None])
    rescale = jnp.exp(running_max - new_max)
    running_sum = running_sum * rescale + jnp.sum(weights, axis=3)
    running_mix = running_mix * rescale[..., None] + jnp.einsum(
        "rsht,tshd->rshd", weights.astype(jnp.bfloat16), values4, preferred_element_type=jnp.float32
    )
    return (new_max, running_sum, running_mix)


def lead_back(queries4, upstream4, log_total, row_delta, prefix_keys4, prefix_values4):
    inv_root = 1.0 / math.sqrt(queries4.shape[3])
    scores = (
        jnp.einsum("rshd,phd->rshp", queries4, prefix_keys4, preferred_element_type=jnp.float32)
        * inv_root
    )
    weights = jnp.exp(scores - log_total[..., None])
    weight_grads = jnp.einsum(
        "rshd,phd->rshp", upstream4, prefix_values4, preferred_element_type=jnp.float32
    )
    score_grads = (weights * (weight_grads - row_delta[..., None])).astype(jnp.bfloat16)
    query_term = (
        jnp.einsum("rshp,phd->rshd", score_grads, prefix_keys4, preferred_element_type=jnp.float32)
        * inv_root
    )
    key_term = (
        jnp.einsum("rshp,rshd->phd", score_grads, queries4, preferred_element_type=jnp.float32)
        * inv_root
    )
    value_term = jnp.einsum(
        "rshp,rshd->phd",
        weights.astype(jnp.bfloat16),
        upstream4,
        preferred_element_type=jnp.float32,
    )
    return (query_term, key_term, value_term)


def block_back(
    queries4, upstream4, log_total, row_delta, key_block, value_block, offset, seq_lengths
):
    key_count, seqs_here, model_width = key_block.shape
    head_count, head_dim = (queries4.shape[2], queries4.shape[3])
    inv_root = 1.0 / math.sqrt(head_dim)
    keys4 = key_block.reshape(key_count, seqs_here, head_count, head_dim)
    values4 = value_block.reshape(key_count, seqs_here, head_count, head_dim)
    scores = (
        jnp.einsum("rshd,tshd->rsht", queries4, keys4, preferred_element_type=jnp.float32)
        * inv_root
    )
    allowed = key_allowed(offset, key_count, seq_lengths)[None, :, None, :]
    scores = jnp.where(allowed, scores, -jnp.inf)
    weights = jnp.exp(scores - log_total[..., None])
    weight_grads = jnp.einsum(
        "rshd,tshd->rsht", upstream4, values4, preferred_element_type=jnp.float32
    )
    score_grads = (weights * (weight_grads - row_delta[..., None])).astype(jnp.bfloat16)
    query_term = (
        jnp.einsum("rsht,tshd->rshd", score_grads, keys4, preferred_element_type=jnp.float32)
        * inv_root
    )
    key_term = (
        jnp.einsum("rsht,rshd->tshd", score_grads, queries4, preferred_element_type=jnp.float32)
        * inv_root
    )
    value_term = jnp.einsum(
        "rsht,rshd->tshd",
        weights.astype(jnp.bfloat16),
        upstream4,
        preferred_element_type=jnp.float32,
    )
    pair_term = jnp.stack(
        [
            key_term.reshape(key_count, seqs_here, model_width),
            value_term.reshape(key_count, seqs_here, model_width),
        ]
    )
    return (query_term, pair_term)


def prefix_back(pair_grad, prefix_act, prefix_embed, hidden_weight, out_weight):
    out_w_grad = precise_left(prefix_act, pair_grad)
    out_b_grad = jnp.sum(pair_grad, axis=0)
    act_grad = precise_right(pair_grad, out_weight) * (1.0 - prefix_act * prefix_act)
    hidden_w_grad = precise_left(prefix_embed, act_grad)
    hidden_b_grad = jnp.sum(act_grad, axis=0)
    embed_grad = precise_right(act_grad, hidden_weight)
    return (embed_grad, hidden_w_grad, hidden_b_grad, out_w_grad, out_b_grad)


def on_device(
    hidden_in,
    lengths,
    w_query,
    w_key,
    w_value,
    w_output,
    attn_gain,
    ffn_in,
    ffn_out,
    ffn_gain,
    adapter_down,
    adapter_down_bias,
    adapter_up,
    adapter_up_bias,
    prefix_embed,
    prefix_hidden_w,
    prefix_hidden_b,
    prefix_out_w,
    prefix_out_b,
    out_grad,
):
    rows_here, seqs_here, model_width = hidden_in.shape
    token_count = rows_here * seqs_here
    head_count = HEADS
    head_dim = model_width // head_count
    axis_count = lax.axis_size("seq")
    position = lax.axis_index("seq")
    tokens = hidden_in.reshape(token_count, model_width)
    projected = jnp.stack([mixed(tokens, w_query), mixed(tokens, w_key), mixed(tokens, w_value)])
    triple = projected.astype(jnp.bfloat16).reshape(3, rows_here, seqs_here, model_width)
    hidden_weight = prefix_hidden_w.astype(jnp.float32)
    out_weight = prefix_out_w.astype(jnp.float32)
    prefix_act = jnp.tanh(precise(prefix_embed, hidden_weight) + prefix_hidden_b)
    prefix_pair = precise(prefix_act, out_weight) + prefix_out_b
    prefix_keys4 = (
        prefix_pair[:, :model_width].astype(jnp.bfloat16).reshape(-1, head_count, head_dim)
    )
    prefix_values4 = (
        prefix_pair[:, model_width:].astype(jnp.bfloat16).reshape(-1, head_count, head_dim)
    )
    row_places = position * rows_here + lax.iota(jnp.int32, rows_here)
    valid = (row_places[:, None] < lengths[None, :]).astype(jnp.float32).reshape(token_count, 1)
    queries4 = triple[0].reshape(rows_here, seqs_here, head_count, head_dim)
    key_value = triple[1:]
    pieces = lax.all_gather(key_value, "seq", axis=1, tiled=True)
    carried = fold_block(
        lead_state(queries4, prefix_keys4, prefix_values4),
        pieces[0],
        pieces[1],
        jnp.int32(0),
        queries4,
        lengths,
    )
    mix_full = carried[2] / carried[1][..., None]
    log_total = carried[0] + jnp.log(carried[1])
    mix_low = mix_full.astype(jnp.bfloat16).reshape(token_count, model_width)
    attn_proj = mixed(mix_low, w_output)
    normed_one, inv_one = normalize(tokens.astype(jnp.float32) + attn_proj)
    norm_one = normed_one * attn_gain
    norm_low = norm_one.astype(jnp.bfloat16)
    inner_pre = mixed(norm_low, ffn_in)
    inner_act = gelu_value(inner_pre).astype(jnp.bfloat16)
    squeeze = mixed(norm_low, adapter_down) + adapter_down_bias
    squeeze_act = gelu_value(squeeze).astype(jnp.bfloat16)
    ffn_sum = mixed(inner_act, ffn_out)
    adapter_sum = mixed(squeeze_act, adapter_up) + adapter_up_bias
    normed_two, inv_two = normalize(norm_one + ffn_sum + 4.0 * adapter_sum)
    layer_out = (
        (normed_two * ffn_gain * valid)
        .astype(jnp.bfloat16)
        .reshape(rows_here, seqs_here, model_width)
    )
    upstream_top = out_grad.reshape(token_count, model_width).astype(jnp.float32) * valid
    grad_two = norm_back(upstream_top * ffn_gain, normed_two, inv_two)
    grad_ffn_low = grad_two.astype(jnp.bfloat16)
    grad_adapt_low = (4.0 * grad_two).astype(jnp.bfloat16)
    up_grad = mixed_left(squeeze_act, grad_adapt_low)
    up_bias_grad = jnp.sum(grad_adapt_low.astype(jnp.float32), axis=0)
    grad_squeeze_low = (mixed_right(grad_adapt_low, adapter_up) * gelu_slope(squeeze)).astype(
        jnp.bfloat16
    )
    down_grad = mixed_left(norm_low, grad_squeeze_low)
    down_bias_grad = jnp.sum(grad_squeeze_low.astype(jnp.float32), axis=0)
    grad_inner_low = (mixed_right(grad_ffn_low, ffn_out) * gelu_slope(inner_pre)).astype(
        jnp.bfloat16
    )
    grad_norm = (
        grad_two + mixed_right(grad_squeeze_low, adapter_down) + mixed_right(grad_inner_low, ffn_in)
    )
    grad_one = norm_back(grad_norm * attn_gain, normed_one, inv_one)
    grad_attn_low = grad_one.astype(jnp.bfloat16)
    grad_mix_low = mixed_right(grad_attn_low, w_output).astype(jnp.bfloat16)
    upstream4 = grad_mix_low.reshape(rows_here, seqs_here, head_count, head_dim)
    row_delta = jnp.sum(upstream4.astype(jnp.float32) * mix_full, axis=3)
    query_grad, prefix_key_grad, prefix_value_grad = lead_back(
        queries4, upstream4, log_total, row_delta, prefix_keys4, prefix_values4
    )

    def visit(step_index, carried):
        moving, grads_moving, query_total = carried
        source = (position - step_index) % axis_count
        query_term, pair_term = block_back(
            queries4,
            upstream4,
            log_total,
            row_delta,
            moving[0],
            moving[1],
            source * rows_here,
            lengths,
        )
        return (moving, grads_moving + pair_term, query_total + query_term)

    def travel(step_index, carried):
        moving, grads_moving, query_total = visit(step_index, carried)
        moving = shifted(moving, "seq", 1)
        grads_moving = shifted(grads_moving.astype(jnp.bfloat16), "seq", 1).astype(
            grads_moving.dtype
        )
        return (moving, grads_moving, query_total)

    initial = (
        key_value,
        jnp.zeros((2, rows_here, seqs_here, model_width), jnp.float32),
        query_grad,
    )
    carried = lax.fori_loop(0, axis_count - 1, travel, initial)
    carried = visit(axis_count - 1, carried)
    pair_grads = shifted(carried[1].astype(jnp.bfloat16), "seq", 1).astype(jnp.float32)
    triple_grad = jnp.concatenate(
        [carried[2].reshape(1, rows_here, seqs_here, model_width), pair_grads]
    ).astype(jnp.bfloat16)
    hidden_grad = grad_one + mixed_right(triple_grad[0].reshape(token_count, model_width), w_query)
    hidden_grad = hidden_grad + mixed_right(triple_grad[1].reshape(token_count, model_width), w_key)
    hidden_grad = hidden_grad + mixed_right(
        triple_grad[2].reshape(token_count, model_width), w_value
    )
    hidden_grad = hidden_grad.astype(jnp.bfloat16).reshape(rows_here, seqs_here, model_width)
    pair_grad = jnp.concatenate(
        [prefix_key_grad.reshape(-1, model_width), prefix_value_grad.reshape(-1, model_width)],
        axis=1,
    )
    prefix_grads = prefix_back(pair_grad, prefix_act, prefix_embed, hidden_weight, out_weight)
    summed = lax.psum(
        (
            down_grad,
            down_bias_grad,
            up_grad,
            up_bias_grad,
            prefix_grads[0],
            prefix_grads[1],
            prefix_grads[2],
            prefix_grads[3],
            prefix_grads[4],
        ),
        ("seq", "dp"),
    )
    adapter_totals = summed[:4]
    prefix_totals = summed[4:]
    return (
        layer_out,
        hidden_grad,
        adapter_totals[0],
        adapter_totals[1],
        adapter_totals[2],
        adapter_totals[3],
        prefix_totals[0],
        prefix_totals[1],
        prefix_totals[2],
        prefix_totals[3],
        prefix_totals[4],
    )


BF16 = jnp.bfloat16
F32 = jnp.float32
MIB = 1024 * 1024
GROUP = 4
HEAD_DIM = 64
LANES = GROUP * HEAD_DIM
PAD = 32
MASKED = -1e30
LOG2E = 1.4426950408889634
VMEM_LIMIT = 60 * MIB


def dot_nn(left, right):
    return lax.dot_general(left, right, (((1,), (0,)), ((), ())), preferred_element_type=F32)


def dot_nt(left, right):
    return lax.dot_general(left, right, (((1,), (1,)), ((), ())), preferred_element_type=F32)


def dot_tn(left, right):
    return lax.dot_general(left, right, (((0,), (0,)), ((), ())), preferred_element_type=F32)


def shape_of(shape, dtype):
    return pltpu.HBM(shape, dtype)


def far(value):
    return pltpu.with_memory_space_constraint(value, pltpu.HBM)


def bring(value):
    return pltpu.with_memory_space_constraint(value, pltpu.VMEM)


def all_far(values):
    return [far(value) for value in values]


def params(limit=VMEM_LIMIT):
    return pltpu.CompilerParams(vmem_limit_bytes=limit)


def cost(macs, moved):
    return pl.CostEstimate(flops=int(2 * macs), bytes_accessed=int(moved), transcendentals=0)


SMEM_SPEC = pl.BlockSpec(memory_space=pltpu.SMEM)
ANY_SPEC = pl.BlockSpec(memory_space=pl.ANY)
CORE_SPEC = pl.BlockSpec(memory_space=pltpu.VMEM)


def whole(shape):
    return pl.BlockSpec(shape, lambda *_: (0,) * len(shape))


def kept(shape):
    return pl.BlockSpec(shape, lambda *_: (0,) * len(shape), pipeline_mode=pl.Buffered(1))


def split_kernel(place_ref, both_ref, own_ref, other_ref):
    apart = jnp.swapaxes(both_ref[...], 0, 1)
    first = place_ref[0] == 0
    own_ref[...] = jnp.where(first, apart[0], apart[1])
    other_ref[...] = jnp.where(first, apart[1], apart[0])


def split(place, both):
    rows, _, width = both.shape
    step = rows // 2
    half = pl.BlockSpec((step, width), lambda i: (i, 0))
    return pl.pallas_call(
        split_kernel,
        grid=(2,),
        in_specs=[SMEM_SPEC, pl.BlockSpec((step, 2, width), lambda i: (i, 0, 0))],
        out_specs=[half, half],
        out_shape=[shape_of((rows, width), both.dtype)] * 2,
        compiler_params=params(16 * MIB),
        cost_estimate=cost(0, 4 * rows * width * 2),
    )(place, far(both))


def merge_kernel(place_ref, own_ref, other_ref, both_ref):
    first = place_ref[0] == 0
    own, other = own_ref[...], other_ref[...]
    apart = jnp.stack([jnp.where(first, own, other), jnp.where(first, other, own)])
    both_ref[...] = jnp.swapaxes(apart, 0, 1)


def place_of(half, place_ref, rows):
    return jnp.where(half == 0, place_ref[0], 1 - place_ref[0]) * rows


def length_of(place_ref, lengths_ref):
    return jnp.where(place_ref[0] == 0, lengths_ref[0], lengths_ref[1])


def parts_of(values, count):
    parts = []
    for _ in range(count):
        part = values.astype(BF16)
        parts.append(part)
        values = values - part.astype(F32)
    return parts


def exact_dot(values, weight, dot):
    rows = values.shape[0]
    product = dot(jnp.concatenate(parts_of(values, 3), axis=0), weight)
    return product[:rows] + product[rows : 2 * rows] + product[2 * rows :]


def prefix_kernel(embed_ref, hw_ref, hb_ref, ow_ref, ob_ref, act_ref, key_ref, value_ref):
    width = key_ref.shape[1]
    act = jnp.tanh(exact_dot(embed_ref[...], hw_ref[...], dot_nn) + hb_ref[...])
    act_ref[...] = act
    pair = exact_dot(act, ow_ref[...], dot_nn) + ob_ref[...]
    key_ref[...] = pair[:, :width].astype(BF16)
    value_ref[...] = pair[:, width:].astype(BF16)


def prefix_forward(embed, hidden_w, hidden_b, out_w, out_b):
    width, hidden = hidden_w.shape
    return pl.pallas_call(
        prefix_kernel,
        out_shape=[
            shape_of((PAD, hidden), F32),
            shape_of((PAD, width), BF16),
            shape_of((PAD, width), BF16),
        ],
        compiler_params=params(16 * MIB),
        cost_estimate=cost(3 * PAD * hidden * 3 * width * 4, 6 * hidden * width),
    )(embed, far(hidden_w), hidden_b[None], far(out_w), out_b[None])


def prefix_back_kernel(
    count, pairs_ref, act_ref, embed_ref, hw_ref, ow_ref, place_ref, own_ref, other_ref,
    both_ref, eg_ref, hwg_ref, hbg_ref, owg_ref, obg_ref, ubg_ref, dbg_ref,
):
    merge_kernel(place_ref, own_ref[...], other_ref, both_ref)
    total = pairs_ref[0]
    for line in range(1, pairs_ref.shape[0]):
        total = total + pairs_ref[line]
    ubg_ref[...] = total[count : count + 1]
    dbg_ref[...] = total[count + 1 : count + 2, : dbg_ref.shape[1]]
    pair = jnp.concatenate([total[:PAD], total[PAD:]], axis=1)
    rows = lax.broadcasted_iota(jnp.int32, pair.shape, 0)
    pair = jnp.where(rows < count, pair, 0.0)
    act = act_ref[...]
    obg_ref[...] = jnp.sum(pair, axis=0, keepdims=True)
    high, low = parts_of(pair, 2)
    back = dot_nt(jnp.concatenate([high, low], axis=0), ow_ref[...])
    act_grad = (back[:PAD] + back[PAD:]) * (1.0 - act * act)
    act_high, act_low = parts_of(act, 2)
    owg_ref[...] = dot_tn(
        jnp.concatenate([act_high, act_low, act_high], axis=0),
        jnp.concatenate([high, high, low], axis=0),
    )
    hbg_ref[...] = jnp.sum(act_grad, axis=0, keepdims=True)
    high, low = parts_of(act_grad, 2)
    embed_high, embed_low = parts_of(embed_ref[...], 2)
    hwg_ref[...] = dot_tn(
        jnp.concatenate([embed_high, embed_low, embed_high], axis=0),
        jnp.concatenate([high, high, low], axis=0),
    )
    back = dot_nt(jnp.concatenate([high, low], axis=0), hw_ref[...])
    eg_ref[...] = (back[:PAD] + back[PAD:])[:count]


def prefix_backward(count, adapt, pairs, act, embed, hidden_w, out_w, place, own, other):
    width, hidden = hidden_w.shape
    core = [CORE_SPEC] * 5
    return pl.pallas_call(
        functools.partial(prefix_back_kernel, count),
        in_specs=core + [SMEM_SPEC, CORE_SPEC, CORE_SPEC],
        out_shape=[
            shape_of((own.shape[0], 2, width), BF16),
            shape_of((count, width), F32),
            shape_of((width, hidden), F32),
            shape_of((1, hidden), F32),
            shape_of((hidden, 2 * width), F32),
            shape_of((1, 2 * width), F32),
            shape_of((1, width), F32),
            shape_of((1, adapt), F32),
        ],
        compiler_params=params(24 * MIB),
        cost_estimate=cost(96 * hidden * width * 6, 20 * hidden * width),
    )(far(pairs), act, embed, far(hidden_w), far(out_w), place, far(own), far(other))


def project_kernel(apart, x_ref, wq_ref, wk_ref, wv_ref, *refs):
    x = x_ref[...]
    if apart:
        place_ref, both_ref, q_ref, k_ref, v_ref, own_ref, other_ref = refs
        split_kernel(place_ref, both_ref, own_ref, other_ref)
    else:
        q_ref, k_ref, v_ref = refs[-3:]
    scale = LOG2E / math.sqrt(HEAD_DIM)
    q_ref[...] = (dot_nn(x, wq_ref[...]) * scale).astype(BF16)
    k_ref[...] = dot_nn(x, wk_ref[...]).astype(BF16)
    v_ref[...] = dot_nn(x, wv_ref[...]).astype(BF16)


def project(half, x, w_query, w_key, w_value, earlier, place=None, both=None):
    rows, width = x.shape
    step = rows // 2
    apart = both is not None
    block = pl.BlockSpec((step, width), lambda i: (i, 0))
    out_specs = [pl.BlockSpec((step, width), lambda i: (2 * half + i, 0))] * 3
    out_shape = [shape_of((2 * rows, width), BF16)] * 3
    more_specs, more = [ANY_SPEC] * len(earlier), all_far(earlier)
    if apart:
        more_specs = [SMEM_SPEC, pl.BlockSpec((step, 2, width), lambda i: (i, 0, 0))]
        more = [place, far(both)]
        out_specs = out_specs + [block] * 2
        out_shape = out_shape + [shape_of((rows, width), BF16)] * 2
    return pl.pallas_call(
        functools.partial(project_kernel, apart),
        grid=(2,),
        in_specs=[block] + [CORE_SPEC] * 3 + more_specs,
        out_specs=out_specs,
        out_shape=out_shape,
        input_output_aliases={4 + i: i for i in range(len(earlier))},
        compiler_params=params(20 * MIB),
        cost_estimate=cost(3 * rows * width * width, 2 * (4 * rows * width + 3 * width * width)),
    )(far(x) if apart else x, bring(w_query), bring(w_key), bring(w_value), *more)


def head_lanes(head, rows, lanes):
    place = lax.broadcasted_iota(jnp.int32, (rows, lanes), 1)
    return (place // HEAD_DIM == head).astype(F32).astype(BF16)


def first_lane(values):
    lane = lax.broadcasted_iota(jnp.int32, (values.shape[0], 128), 1)
    return jnp.where(lane == 0, values, 0.0).astype(BF16)


def block_diagonal(rows):
    return jnp.concatenate(
        [rows * head_lanes(head, rows.shape[0], LANES) for head in range(GROUP)], axis=0
    )


def attend_kernel(
    prefixed, first, place_ref, lengths_ref, q_ref, k_ref, v_ref, pk_ref, pv_ref, *refs
):
    pt_ref, ot_ref, st_ref, pp_ref, *scores = refs[-6:]
    keys = k_ref.shape[0]
    queries = q_ref.shape[0]
    half = (pl.program_id(0) + first) // 2

    def quadrant(count):
        place = place_of(half, place_ref, keys) + lax.broadcasted_iota(jnp.int32, (keys, 128), 0)
        bias = first_lane(jnp.where(place < length_of(place_ref, lengths_ref), 0.0, MASKED))
        ones = first_lane(jnp.ones((queries, 128), F32))
        tail = jnp.ones((16, keys), BF16)
        masks = [head_lanes(head, queries, 128) for head in range(2)]

        def score(head):
            pair = slice((head // 2) * 128, (head // 2 + 1) * 128)
            k_aug = jnp.concatenate([k_ref[:, pair], bias], axis=1)
            q_aug = jnp.concatenate([q_ref[:, pair] * masks[head % 2], ones], axis=1)
            scores[head % 2][...] = dot_nt(k_aug, q_aug)

        def weigh(head):
            own = scores[head % 2]
            top = jnp.max(own[...], axis=0, keepdims=True)
            if count:
                lead_scores = lead[head * PAD : (head + 1) * PAD]
                top = jnp.maximum(top, jnp.max(lead_scores, axis=0, keepdims=True))
            pt_ref[head] = jnp.exp2(own[...] - top).astype(BF16)
            st_ref[0, head : head + 1, :] = top
            if not count:
                return 0.0
            lead_weights = jnp.exp2(lead_scores - top).astype(BF16)
            pp_ref[0, head * PAD : (head + 1) * PAD, :] = lead_weights
            return jnp.sum(lead_weights.astype(F32), axis=0, keepdims=True)

        def mix(head, lead_total):
            rows = slice(head * HEAD_DIM, (head + 1) * HEAD_DIM)
            mixed_rows = dot_nn(jnp.concatenate([turned[rows], tail], axis=0), pt_ref[head])
            mixed = mixed_rows[:HEAD_DIM]
            if count:
                lead_weights = pp_ref[0, head * PAD : (head + 1) * PAD, :]
                mixed = mixed + dot_nn(lead_turned[rows], lead_weights)
            ot_ref[rows, :] = mixed.astype(BF16)
            total_row = mixed_rows[HEAD_DIM : HEAD_DIM + 1] + lead_total
            st_ref[0, GROUP + head : GROUP + head + 1, :] = total_row

        score(0)
        turned = v_ref[...].T
        if count:
            lead_turned = pv_ref[...].T
            lead = dot_nt(block_diagonal(pk_ref[...]), q_ref[...])
            row = lax.broadcasted_iota(jnp.int32, lead.shape, 0)
            lead = jnp.where(row % PAD < count, lead, MASKED)
        lead_totals = []
        for head in range(GROUP):
            if head + 1 < GROUP:
                score(head + 1)
            lead_totals.append(weigh(head))
            if head:
                mix(head - 1, lead_totals[head - 1])
        mix(GROUP - 1, lead_totals[GROUP - 1])

    @pl.when(half == 0)
    def _():
        quadrant(prefixed)

    @pl.when(half == 1)
    def _():
        quadrant(0)


def attend(count, place, lengths, first, quadrants, q, k, v, lead, earlier):
    tokens, width = q.shape
    rows = tokens // 2
    groups = width // LANES
    last = groups - 1

    def lead_place(i, g):
        quadrant = i + first
        return (jnp.where(quadrant < 2, g, last), 0, jnp.minimum(quadrant, 1))

    keys = pl.BlockSpec((rows, LANES), lambda i, g: ((i + first) // 2, g))
    in_specs = [
        SMEM_SPEC,
        SMEM_SPEC,
        pl.BlockSpec((rows, LANES), lambda i, g: ((i + first) % 2, g)),
        keys,
        keys,
    ]
    in_specs += [pl.BlockSpec((PAD, LANES), lambda i, g: (0, g))] * 2
    out_specs = [
        pl.BlockSpec(
            (None, GROUP, rows, rows), lambda i, g: ((i + first) // 2, g, 0, (i + first) % 2)
        ),
        pl.BlockSpec((None, LANES, rows), lambda i, g: ((i + first) // 2, g, (i + first) % 2)),
        pl.BlockSpec(
            (None, 1, 2 * GROUP, rows), lambda i, g: ((i + first) // 2, g, 0, (i + first) % 2)
        ),
        pl.BlockSpec((1, GROUP * PAD, rows), lead_place),
    ]
    out_shape = [
        shape_of((2, groups * GROUP, rows, tokens), BF16),
        shape_of((2, width, tokens), BF16),
        shape_of((2, groups, 2 * GROUP, tokens), F32),
        shape_of((groups, GROUP * PAD, tokens), BF16),
    ]
    macs = quadrants * groups * GROUP * rows * rows * 256 * 2
    return pl.pallas_call(
        functools.partial(attend_kernel, count, first),
        grid=(quadrants, groups),
        in_specs=in_specs + [ANY_SPEC] * len(earlier),
        out_specs=out_specs,
        out_shape=out_shape,
        input_output_aliases={7 + i: i for i in range(len(earlier))},
        scratch_shapes=[pltpu.VMEM((rows, rows), F32)] * 2,
        compiler_params=params(16 * MIB),
        cost_estimate=cost(macs, quadrants * 14 * MIB),
    )(place, lengths, *all_far((q, k, v, *lead, *earlier)))


def lead_back_kernel(
    count, q_ref, up_ref, rst_ref, del_ref, pp_ref, pk_ref, pv_ref, bias_ref, pair_ref, dqt_ref
):
    queries = q_ref.shape[0]
    ups = []
    deltas = []
    for head in range(GROUP):
        rows = slice(head * HEAD_DIM, (head + 1) * HEAD_DIM)
        share = rst_ref[0, head : head + 1, :]
        ups.append((up_ref[rows, :].astype(F32) * share).astype(BF16))
        delta = del_ref[0, head : head + 1, :] * share
        deltas.append(jnp.broadcast_to(delta, (PAD, queries)))
    up = jnp.concatenate(ups, axis=0)
    delta = jnp.concatenate(deltas, axis=0)
    weights = pp_ref[0]
    key_diagonal = block_diagonal(pk_ref[...])
    value_diagonal = block_diagonal(pv_ref[...])
    weight_grads = dot_nn(value_diagonal, up)
    score_grads = (weights.astype(F32) * (weight_grads - delta)).astype(BF16)
    dqt_ref[...] = dot_tn(key_diagonal, score_grads).astype(BF16)
    key_grads = dot_nn(score_grads, q_ref[...]) * (1.0 / LOG2E)
    value_grads = dot_nt(weights, up)
    lane = lax.broadcasted_iota(jnp.int32, (PAD, LANES), 1) // HEAD_DIM
    key_total = jnp.zeros((PAD, LANES), F32)
    value_total = jnp.zeros((PAD, LANES), F32)
    for head in range(GROUP):
        rows = slice(head * PAD, (head + 1) * PAD)
        key_total = jnp.where(lane == head, key_grads[rows], key_total)
        value_total = jnp.where(lane == head, value_grads[rows], value_total)
    row = lax.broadcasted_iota(jnp.int32, (PAD, LANES), 0)
    key_total = jnp.where(row == count, bias_ref[0:1, :], key_total)
    key_total = jnp.where(row == count + 1, bias_ref[1:2, :], key_total)
    pair_ref[:PAD, :] = key_total.astype(BF16)
    pair_ref[PAD:, :] = value_total.astype(BF16)


def lead_backward(count, q, up, shares, deltas, lead_weights, prefix_keys, prefix_values, biases):
    tokens, width = q.shape
    groups = width // LANES
    small = pl.BlockSpec((PAD, LANES), lambda g: (0, g))
    stats = pl.BlockSpec((1, 2 * GROUP, tokens), lambda g: (g, 0, 0))
    return pl.pallas_call(
        functools.partial(lead_back_kernel, count),
        grid=(groups,),
        in_specs=[
            pl.BlockSpec((tokens, LANES), lambda g: (0, g)),
            pl.BlockSpec((LANES, tokens), lambda g: (g, 0)),
            stats,
            stats,
            pl.BlockSpec((1, GROUP * PAD, tokens), lambda g: (g, 0, 0)),
            small,
            small,
            pl.BlockSpec((8, LANES), lambda g: (0, g)),
        ],
        out_specs=[
            pl.BlockSpec((2 * PAD, LANES), lambda g: (0, g)),
            pl.BlockSpec((LANES, tokens), lambda g: (g, 0)),
        ],
        out_shape=[
            jax.ShapeDtypeStruct((2 * PAD, width), BF16),
            shape_of((width, tokens), BF16),
        ],
        compiler_params=params(14 * MIB),
        cost_estimate=cost(groups * 4 * GROUP * PAD * tokens * LANES, 10 * MIB),
    )(*all_far((q, up, shares, deltas, lead_weights)), prefix_keys, prefix_values, biases)


def attend_back_kernel(
    half,
    last_keys,
    last_queries,
    has_earlier,
    q_ref,
    k_ref,
    v_ref,
    up_ref,
    rst_ref,
    del_ref,
    pt_ref,
    dqt_in_ref,
    *refs,
):
    dq_ref, dk_ref, dv_ref = refs[-5:-2]
    weight_grads = refs[-2:]
    queries = q_ref.shape[0]
    lane = lax.broadcasted_iota(jnp.int32, (queries, 128), 1) // HEAD_DIM
    masks = [(lane == head).astype(F32).astype(BF16) for head in range(2)]
    zeros = jnp.zeros((HEAD_DIM, queries), BF16)
    turned = k_ref[...].T
    ups = {}
    grads = {}
    query_grads = []
    key_grads = []
    value_grads = []

    def pair_of(head):
        return slice((head // 2) * 128, (head // 2 + 1) * 128)

    def rows_of(head):
        return slice(head * HEAD_DIM, (head + 1) * HEAD_DIM)

    def share_of(head):
        return rst_ref[0, half * GROUP + head : half * GROUP + head + 1, :]

    def weight_grad(head):
        up = (up_ref[rows_of(head), :].astype(F32) * share_of(head)).astype(BF16)
        ups[head] = jnp.concatenate([up, zeros] if head % 2 == 0 else [zeros, up], axis=0)
        weight_grads[head % 2][...] = dot_nn(v_ref[:, pair_of(head)], ups[head])

    def score_grad(head):
        delta = del_ref[0, head : head + 1, :] * share_of(head)
        return (pt_ref[head].astype(F32) * (weight_grads[head % 2][...] - delta)).astype(BF16)

    def value_term(head):
        return dot_nt(pt_ref[head], ups[head])

    def key_term(head):
        return dot_nn(grads[head], q_ref[:, pair_of(head)] * masks[head % 2])

    def query_term(head):
        return dqt_in_ref[rows_of(head), :].astype(F32) + dot_nn(turned[rows_of(head)], grads[head])

    weight_grad(0)
    for head in range(GROUP):
        if head + 1 < GROUP:
            weight_grad(head + 1)
        grads[head] = score_grad(head)
        value = value_term(head)
        query_grads.append(query_term(head))
        key = key_term(head)
        if head % 2:
            key_grads[-1] = key_grads[-1] + key
            value_grads[-1] = value_grads[-1] + value
        else:
            key_grads.append(key)
            value_grads.append(value)
    query_grad = jnp.concatenate(query_grads, axis=0)
    key_grad = jnp.concatenate(key_grads, axis=1)
    value_grad = jnp.concatenate(value_grads, axis=1)
    if not last_keys:
        dq_ref[...] = query_grad.astype(BF16)
    else:
        dq_ref[...] = (query_grad * (1.0 / math.sqrt(HEAD_DIM))).astype(BF16).T
    if has_earlier:
        key_grad = key_grad + refs[0][...].astype(F32)
        value_grad = value_grad + refs[1][...].astype(F32)
    if last_queries:
        key_grad = key_grad * (1.0 / LOG2E)
    dk_ref[...] = key_grad.astype(BF16)
    dv_ref[...] = value_grad.astype(BF16)


def attend_back(
    key_half, query_half, last_keys, last_queries, q, k, v, up, shares, deltas, weights, dqt, earlier
):
    tokens, width = q.shape
    rows = tokens // 2
    groups = width // LANES
    query_columns = pl.BlockSpec((LANES, rows), lambda g: (g, query_half))
    stats = pl.BlockSpec((1, 2 * GROUP, rows), lambda g: (g, 0, query_half))
    finished = pl.BlockSpec((rows, LANES), lambda g: (0, g))
    out_columns = pl.BlockSpec((LANES, rows), lambda g: (g, 0))
    sofar = query_columns if dqt.shape[1] == tokens else out_columns
    macs = groups * GROUP * rows * rows * 256 * 4
    return pl.pallas_call(
        functools.partial(
            attend_back_kernel, key_half, last_keys, last_queries, len(earlier) > 0
        ),
        grid=(groups,),
        in_specs=[
            pl.BlockSpec((rows, LANES), lambda g: (query_half, g)),
            pl.BlockSpec((rows, LANES), lambda g: (key_half, g)),
            pl.BlockSpec((rows, LANES), lambda g: (key_half, g)),
            query_columns,
            stats,
            stats,
            pl.BlockSpec((None, GROUP, rows, rows), lambda g: (key_half, g, 0, query_half)),
            sofar,
        ]
        + [finished] * len(earlier),
        out_specs=[finished if last_keys else out_columns, finished, finished],
        out_shape=[
            shape_of((rows, width) if last_keys else (width, rows), BF16),
            shape_of((rows, width), BF16),
            shape_of((rows, width), BF16),
        ],
        scratch_shapes=[pltpu.VMEM((rows, rows), F32)] * 2,
        compiler_params=params(18 * MIB),
        cost_estimate=cost(macs, 12 * MIB),
    )(*all_far((q, k, v, up, shares, deltas, weights, dqt, *earlier)))


def gelu_pair(values):
    scaled = values * 0.7071067811865476
    below = 0.5 * lax.erf(scaled) + 0.5
    decay = jnp.exp2(scaled * scaled * (-LOG2E))
    return values * below, below + values * 0.3989422804014327 * decay


def row_mean(values):
    return jnp.mean(values, axis=-1, keepdims=True)


def front_kernel(
    tiles,
    place_ref,
    lengths_ref,
    x_own_ref,
    x_other_ref,
    ot_own_ref,
    ot_other_ref,
    st_own_ref,
    st_other_ref,
    og_own_ref,
    og_other_ref,
    gain_one_ref,
    gain_two_ref,
    down_bias_ref,
    up_bias_ref,
    wo_ref,
    fin_ref,
    fout_ref,
    down_ref,
    up_ref,
    out_own_ref,
    out_other_ref,
    rst_ref,
    mix_ref,
    slope_ref,
    grad_low_ref,
    norm_grad_ref,
    normed_ref,
    inv_ref,
    kept_ref,
    sent_ref,
    bias_grad_ref,
    act_ref,
    squeeze_ref,
    low_ref,
):
    step = pl.program_id(0)
    tile = x_own_ref.shape[0]
    width = x_own_ref.shape[1]
    hidden = fin_ref.shape[1]
    chunk = 512
    chunks = [slice(first, first + chunk) for first in range(0, hidden, chunk)]
    own = step < tiles // 2
    x = jnp.where(own, x_own_ref[...], x_other_ref[...]).astype(F32)
    top_own, top_other = st_own_ref[:, :GROUP, :], st_other_ref[:, :GROUP, :]
    top = jnp.maximum(top_own, top_other)
    share_own, share_other = jnp.exp2(top_own - top), jnp.exp2(top_other - top)
    inverse = 1.0 / (
        st_own_ref[:, GROUP:, :] * share_own + st_other_ref[:, GROUP:, :] * share_other
    )
    rst_ref[:, :GROUP, :] = share_own * inverse
    rst_ref[:, GROUP:, :] = share_other * inverse
    mixes = []
    for head in range(width // HEAD_DIM):
        rows = slice(head * HEAD_DIM, (head + 1) * HEAD_DIM)
        group, place = head // GROUP, head % GROUP
        mixes.append(
            (
                ot_own_ref[rows, :].astype(F32) * rst_ref[group, place : place + 1, :]
                + ot_other_ref[rows, :].astype(F32) * rst_ref[group, GROUP + place : GROUP + place + 1, :]
            ).astype(BF16)
        )
    mix = jnp.concatenate(mixes, axis=0)
    mix_ref[...] = mix
    resid_one = x + dot_tn(mix, wo_ref[...])
    centred = resid_one - row_mean(resid_one)
    inv_one = lax.rsqrt(row_mean(centred * centred) + 1e-05)
    normed = centred * inv_one
    normed_ref[...] = normed.astype(BF16)
    inv_ref[...] = inv_one
    norm_one = normed * gain_one_ref[...]
    norm_low = norm_one.astype(BF16)

    squeeze = dot_nn(norm_low, down_ref[...]) + down_bias_ref[...]
    inner = dot_nn(norm_low, fin_ref[:, chunks[0]])
    squeeze_act, squeeze_slope = gelu_pair(squeeze)
    squeeze_act = squeeze_act.astype(BF16)
    resid_two = norm_one + 4.0 * (dot_nn(squeeze_act, up_ref[...]) + up_bias_ref[...])
    for place, columns in enumerate(chunks):
        more = place + 1 < len(chunks)
        coming = dot_nn(norm_low, fin_ref[:, chunks[place + 1]]) if more else None
        act, slope = gelu_pair(inner)
        slope_ref[:, columns] = slope.astype(BF16)
        resid_two = resid_two + dot_nn(act.astype(BF16), fout_ref[columns, :])
        inner = coming

    centred = resid_two - row_mean(resid_two)
    inv_two = lax.rsqrt(row_mean(centred * centred) + 1e-05)
    normed_two = centred * inv_two
    base = place_of(step // (tiles // 2), place_ref, (tiles // 2) * tile) + step % (tiles // 2) * tile
    place = base + lax.broadcasted_iota(jnp.int32, (tile, 1), 0)
    valid = (place < length_of(place_ref, lengths_ref)).astype(F32)
    gain_two = gain_two_ref[...]
    out = (normed_two * gain_two * valid).astype(BF16)
    upstream = jnp.where(own, og_own_ref[...], og_other_ref[...]).astype(F32) * valid * gain_two
    grad_two = inv_two * (
        upstream - row_mean(upstream) - normed_two * row_mean(upstream * normed_two)
    )
    grad_low = grad_two.astype(BF16)
    grad_adapt = 4.0 * grad_low
    grad_squeeze = (dot_nt(grad_adapt, up_ref[...]) * squeeze_slope).astype(BF16)
    norm_grad_ref[...] = (grad_two + dot_nt(grad_squeeze, down_ref[...])).astype(BF16)
    here = pl.ds(pl.multiple_of(step * tile, tile), tile)
    grad_low_ref[here, :] = grad_low
    act_ref[here, :] = squeeze_act
    squeeze_ref[here, :] = grad_squeeze
    low_ref[here, :] = norm_low
    up_bias_grad = jnp.sum(grad_adapt.astype(F32), axis=0, keepdims=True)
    down_bias_grad = jnp.sum(grad_squeeze.astype(F32), axis=0, keepdims=True)
    adapt = down_bias_grad.shape[1]

    @pl.when(own)
    def _():
        out_own_ref[...] = out

    @pl.when(jnp.logical_not(own))
    def _():
        out_other_ref[...] = out

    @pl.when(step == 0)
    def _():
        bias_grad_ref[...] = jnp.zeros_like(bias_grad_ref)
        bias_grad_ref[0:1, :] = up_bias_grad
        bias_grad_ref[1:2, :adapt] = down_bias_grad

    @pl.when(step > 0)
    def _():
        bias_grad_ref[0:1, :] += up_bias_grad
        bias_grad_ref[1:2, :adapt] += down_bias_grad

    @pl.when(step == tiles - 1)
    def _():
        first = place_ref[1] == 0
        up_total = (4.0 * dot_tn(act_ref[...], grad_low_ref[...])).astype(BF16)
        down_total = dot_tn(squeeze_ref[...], low_ref[...]).astype(BF16)
        kept_ref[...] = jnp.where(first, up_total, down_total)
        sent_ref[...] = jnp.where(first, down_total, up_total)


def front(
    place, lengths, x_own, x_other, mix_parts, tops_sums, og_own, og_other, w_output, attn_gain,
    ffn_in, ffn_out, ffn_gain, down, down_bias, up, up_bias,
):
    rows, width = x_own.shape
    tokens = 2 * rows
    hidden = ffn_in.shape[1]
    adapt = down.shape[1]
    groups = width // LANES
    tile = 256
    tiles = tokens // tile
    near = pl.BlockSpec((tile, width), lambda i: (jnp.minimum(i, tiles // 2 - 1), 0))
    far = pl.BlockSpec((tile, width), lambda i: (jnp.maximum(i - tiles // 2, 0), 0))
    row_block = pl.BlockSpec((tile, width), lambda i: (i, 0))
    column_block = pl.BlockSpec((width, tile), lambda i: (0, i))
    stats = pl.BlockSpec((groups, 2 * GROUP, tile), lambda i: (0, 0, i))
    mixes = [pl.BlockSpec((None, width, tile), lambda i, half=half: (half, 0, i)) for half in range(2)]
    tops = [
        pl.BlockSpec((None, groups, 2 * GROUP, tile), lambda i, half=half: (half, 0, 0, i))
        for half in range(2)
    ]
    return pl.pallas_call(
        functools.partial(front_kernel, tiles),
        grid=(tiles,),
        in_specs=[
            SMEM_SPEC, SMEM_SPEC, near, far, *mixes, *tops, near, far,
            whole((1, width)), whole((1, width)), whole((1, adapt)), whole((1, width)),
        ] + [CORE_SPEC] * 5,
        out_specs=[
            near, far, stats, column_block, pl.BlockSpec((tile, hidden), lambda i: (i, 0)),
            kept((tokens, width)), row_block, row_block, pl.BlockSpec((tile, 1), lambda i: (i, 0)),
            kept((adapt, width)), kept((adapt, width)), whole((8, width)),
        ],
        out_shape=[
            shape_of((rows, width), BF16),
            shape_of((rows, width), BF16),
            shape_of((groups, 2 * GROUP, tokens), F32),
            shape_of((width, tokens), BF16),
            shape_of((tokens, hidden), BF16),
            shape_of((tokens, width), BF16),
            shape_of((tokens, width), BF16),
            shape_of((tokens, width), BF16),
            shape_of((tokens, 1), F32),
            shape_of((adapt, width), BF16),
            shape_of((adapt, width), BF16),
            shape_of((8, width), F32),
        ],
        scratch_shapes=[
            pltpu.VMEM((tokens, adapt), BF16),
            pltpu.VMEM((tokens, adapt), BF16),
            pltpu.VMEM((tokens, width), BF16),
        ],
        compiler_params=params(32 * MIB),
        cost_estimate=cost(tokens * width * (width + 2 * hidden + 6 * adapt), 60 * MIB),
    )(
        place,
        lengths,
        *all_far((x_own, x_other, mix_parts, mix_parts, tops_sums, tops_sums, og_own, og_other)),
        attn_gain[None], ffn_gain[None], down_bias[None], up_bias[None],
        *[bring(item) for item in (w_output, ffn_in, ffn_out, down, up)],
    )


def rear_kernel(
    grad_low_ref, norm_grad_ref, slope_ref, normed_ref, inv_ref, mix_ref, gain_ref, wo_ref, fin_ref,
    fout_ref, grad_one_ref, up_ref, del_ref,
):
    hidden = fin_ref.shape[1]
    chunk = 1024
    chunks = [slice(first, first + chunk) for first in range(0, hidden, chunk)]
    grad_low = grad_low_ref[...]
    grad_norm = norm_grad_ref[...].astype(F32)
    inner = dot_nt(grad_low, fout_ref[chunks[0], :])
    for place, columns in enumerate(chunks):
        more = place + 1 < len(chunks)
        coming = dot_nt(grad_low, fout_ref[chunks[place + 1], :]) if more else None
        low = (inner * slope_ref[:, columns].astype(F32)).astype(BF16)
        grad_norm = grad_norm + dot_nt(low, fin_ref[:, columns])
        inner = coming
    grad = grad_norm * gain_ref[...]
    normed = normed_ref[...].astype(F32)
    grad_one = inv_ref[...] * (grad - row_mean(grad) - normed * row_mean(grad * normed))
    grad_low_one = grad_one.astype(BF16)
    grad_one_ref[...] = grad_low_one
    up = dot_nt(wo_ref[...], grad_low_one).astype(BF16)
    up_ref[...] = up
    product = up.astype(F32) * mix_ref[...].astype(F32)
    for head in range(product.shape[0] // HEAD_DIM):
        rows = slice(head * HEAD_DIM, (head + 1) * HEAD_DIM)
        group, place = head // GROUP, head % GROUP
        del_ref[group, place : place + 1, :] = jnp.sum(product[rows], axis=0, keepdims=True)
    del_ref[:, GROUP:, :] = jnp.zeros_like(del_ref[:, GROUP:, :])


def rear(grad_low, norm_grad, slope, normed, inv, mix, w_output, attn_gain, ffn_in, ffn_out):
    tokens, width = grad_low.shape
    hidden = ffn_in.shape[1]
    groups = width // LANES
    tile = 256
    row_block = pl.BlockSpec((tile, width), lambda i: (i, 0))
    column_block = pl.BlockSpec((width, tile), lambda i: (0, i))
    return pl.pallas_call(
        rear_kernel,
        grid=(tokens // tile,),
        in_specs=[
            row_block, row_block, pl.BlockSpec((tile, hidden), lambda i: (i, 0)), row_block,
            pl.BlockSpec((tile, 1), lambda i: (i, 0)), column_block, whole((1, width)),
        ] + [CORE_SPEC] * 3,
        out_specs=[
            row_block, column_block, pl.BlockSpec((groups, 2 * GROUP, tile), lambda i: (0, 0, i)),
        ],
        out_shape=[
            shape_of((tokens, width), BF16),
            shape_of((width, tokens), BF16),
            shape_of((groups, 2 * GROUP, tokens), F32),
        ],
        compiler_params=params(22 * MIB),
        cost_estimate=cost(tokens * width * (width + 2 * hidden), 50 * MIB),
    )(*all_far((grad_low, norm_grad, slope, normed, inv, mix)), attn_gain[None], bring(w_output), bring(ffn_in), bring(ffn_out))


def input_grad_kernel(last, place_ref, grad_ref, dq_ref, dk_ref, dv_ref, wq_ref, wk_ref, wv_ref, *refs):
    total = grad_ref[...].astype(F32) + dot_nt(dq_ref[...], wq_ref[...])
    total = total + dot_nt(dk_ref[...], wk_ref[...])
    total = total + dot_nt(dv_ref[...], wv_ref[...])
    total = total.astype(BF16)
    if not last:
        refs[0][...] = total
        return
    arrived_ref, half_ref, far_ref, both_ref, up_ref, down_ref = refs
    merge_kernel(place_ref, total, arrived_ref, both_ref)
    first = place_ref[1] == 0
    half, other = half_ref[...].astype(F32), far_ref[...].astype(F32)
    up_ref[...] = jnp.where(first, half, other)
    down_ref[...] = jnp.where(first, other, half).T


def input_grad(place, half, grad_one, dq, dk, dv, weights, last):
    rows, width = dk.shape
    step = rows // 2
    block = pl.BlockSpec((step, width), lambda i: (i, 0))
    out_specs, out_shape = block, shape_of((rows, width), BF16)
    if last:
        out_specs = [
            pl.BlockSpec((step, 2, width), lambda i: (i, 0, 0)),
            block,
            pl.BlockSpec((width, step), lambda i: (0, i)),
        ]
        out_shape = [
            shape_of((rows, 2, width), BF16),
            shape_of((rows, width), F32),
            shape_of((width, rows), F32),
        ]
    return pl.pallas_call(
        functools.partial(input_grad_kernel, bool(last)),
        grid=(2,),
        in_specs=[SMEM_SPEC, pl.BlockSpec((step, width), lambda i: (2 * half + i, 0))]
        + [block] * 3
        + [CORE_SPEC] * 3
        + [block] * len(last),
        out_specs=out_specs,
        out_shape=out_shape,
        compiler_params=params(26 * MIB),
        cost_estimate=cost(3 * rows * width * width, 14 * MIB),
    )(place, *all_far((grad_one, dq, dk, dv)), *[bring(item) for item in weights], *last)


def swap(value, seq_bit, dp_bits):
    width = lax.axis_size("dp")
    count = lax.axis_size("seq") * width
    pairs = [
        (device, ((device // width) ^ seq_bit) * width + ((device % width) ^ dp_bits))
        for device in range(count)
    ]
    return lax.ppermute(value, ("seq", "dp"), pairs)


def gather_line(value):
    width = lax.axis_size("dp")
    groups = [[4 * line + place for line in range(width // 4)] for place in range(4)]
    return lax.all_gather(value, "dp", axis_index_groups=groups)


def total(values):
    return jnp.sum(values.astype(F32), axis=0)


def square_place():
    return 2 * ((lax.axis_index("dp") // 2) % 2) + lax.axis_index("seq")


def square_swaps(values):
    return [swap(values[offset - 1], offset % 2, 2 * (offset // 2)) for offset in range(1, 4)]


def sum_square(value):
    place = square_place()
    quarters = value.reshape(4, value.shape[0] // 4, value.shape[1])
    pick = [
        lax.dynamic_index_in_dim(quarters, place ^ offset, 0, keepdims=False) for offset in range(4)
    ]
    return pick[:1] + square_swaps(pick[1:])


def add(terms):
    value = terms[0].astype(F32)
    for term in terms[1:]:
        value = value + term.astype(F32)
    return value.astype(BF16)


def tie(*values):
    return lax.optimization_barrier(values)


def on_pair(
    hidden_in,
    lengths,
    w_query,
    w_key,
    w_value,
    w_output,
    attn_gain,
    ffn_in,
    ffn_out,
    ffn_gain,
    adapter_down,
    adapter_down_bias,
    adapter_up,
    adapter_up_bias,
    prefix_embed,
    prefix_hidden_w,
    prefix_hidden_b,
    prefix_out_w,
    prefix_out_b,
    out_grad,
):
    rows, _, width = hidden_in.shape
    count = prefix_embed.shape[0]
    position = lax.axis_index("seq")
    core = lax.axis_index("dp") % 2
    place = jnp.stack([position, core]).astype(jnp.int32)

    x_own, x_send = split(place, hidden_in)
    x_other = shifted(x_send, "seq", 1)

    embed = jnp.pad(prefix_embed, ((0, PAD - count), (0, 0)))
    prefix_act, prefix_keys, prefix_values = prefix_forward(
        embed, prefix_hidden_w, prefix_hidden_b, prefix_out_w, prefix_out_b
    )
    x_own, prefix_keys = tie(x_own, prefix_keys)
    lead = (prefix_keys, prefix_values)
    *triple, og_own, og_send = project(0, x_own, w_query, w_key, w_value, (), place, out_grad)
    og_other = shifted(og_send, "seq", 1)
    begun = attend(count, place, lengths, 0, 1, *triple, lead, ())
    q, k, v = project(1, x_other, w_query, w_key, w_value, triple)
    weights, mix_parts, tops_sums, lead_weights = attend(
        count, place, lengths, 1, 3, q, k, v, lead, begun
    )

    (
        out_own, out_send, shares, mix, slope, grad_low, norm_grad, normed, inv_one,
        adapt_kept, adapt_sent, bias_grads,
    ) = front(
        place, lengths, x_own, x_other, mix_parts, tops_sums, og_own, og_other,
        w_output, attn_gain, ffn_in, ffn_out, ffn_gain, adapter_down, adapter_down_bias,
        adapter_up, adapter_up_bias,
    )
    out_other = shifted(out_send, "seq", 1)
    core_terms = [adapt_kept, swap(adapt_sent, 0, 1)]
    grad_one, upstream, deltas = rear(
        grad_low, norm_grad, slope, normed, inv_one, mix, w_output, attn_gain, ffn_in, ffn_out
    )
    upstream, out_other, adapt_sum = tie(upstream, out_other, add(core_terms))
    square_terms = sum_square(adapt_sum)
    pair, dqt = lead_backward(
        count, q, upstream, shares, deltas, lead_weights, prefix_keys, prefix_values, bias_grads
    )
    pair_core = swap(pair, 0, 1)

    back = (q, k, v)
    part_own, dk_other, dv_other = attend_back(
        1, 0, False, False, *back, upstream, shares, deltas, weights, dqt, ()
    )
    dk_other, pair, adapt_sum = tie(dk_other, add([pair, pair_core]), add(square_terms))
    adapt_line = gather_line(adapt_sum)
    pair_square = square_swaps([pair] * 3)
    part_other, dk_other, dv_other = attend_back(
        1, 1, False, True, *back, upstream, shares, deltas, weights, dqt, (dk_other, dv_other)
    )
    pair_sum = pair.astype(F32) + sum(item.astype(F32) for item in pair_square)
    part_other, pair_sum = tie(part_other, pair_sum)
    dq_other, dk_own, dv_own = attend_back(
        0, 1, True, False, *back, upstream, shares, deltas, weights, part_other, ()
    )
    adapt_sum = jnp.sum(adapt_line.astype(F32), axis=0).astype(BF16)
    dq_other, adapt_sum, pair_sum = tie(dq_other, adapt_sum, pair_sum)
    pair_line = gather_line(pair_sum)
    adapt_x, adapt_y = swap(adapt_sum, 1, 0), swap(adapt_sum, 0, 2)
    triple_weights = (w_query, w_key, w_value)
    grad_other = input_grad(place, 1, grad_one, dq_other, dk_other, dv_other, triple_weights, ())
    grad_other, dk_own, adapt_x = tie(grad_other, dk_own, adapt_x)
    grad_back = shifted(grad_other, "seq", 1)
    adapt_xy = swap(adapt_x, 0, 2)
    dq_own, dk_own, dv_own = attend_back(
        0, 0, True, True, *back, upstream, shares, deltas, weights, part_own, (dk_own, dv_own)
    )
    dq_own, pair_line, out_other, adapt_y, adapt_xy = tie(
        dq_own, pair_line, out_other, adapt_y, adapt_xy
    )
    adapt_half = jnp.stack([adapt_sum, adapt_x, adapt_y, adapt_xy])
    place_here = square_place()
    adapt_half = jnp.concatenate(
        [lax.dynamic_slice_in_dim(adapt_half, spot ^ place_here, 1, 0) for spot in range(4)]
    ).reshape(adapt_kept.shape)
    adapt_far = swap(adapt_half, 0, 1)
    layer_out, *prefix_grads = prefix_backward(
        count,
        adapter_down_bias.shape[0],
        pair_line,
        prefix_act,
        embed,
        prefix_hidden_w,
        prefix_out_w,
        place,
        out_own,
        out_other,
    )
    layer_out, grad_back, dq_own = tie(layer_out, grad_back, dq_own)
    out_w_grad = prefix_grads[3]
    input_total, up_total, down_total = input_grad(
        place, 0, grad_one, dq_own, dk_own, dv_own, triple_weights, (grad_back, adapt_half, adapt_far)
    )
    return (
        layer_out,
        input_total,
        down_total,
        prefix_grads[6][0],
        up_total,
        prefix_grads[5][0],
        prefix_grads[0],
        prefix_grads[1],
        prefix_grads[2][0],
        out_w_grad,
        prefix_grads[4][0],
    )


def solution(mesh):
    in_specs = (
        P("seq", "dp", None),
        P("dp"),
        P(),
        P(),
        P(),
        P(),
        P(),
        P(),
        P(),
        P(),
        P(),
        P(),
        P(),
        P(),
        P(),
        P(),
        P(),
        P(),
        P(),
        P("seq", "dp", None),
    )
    out_specs = (
        P("seq", "dp", None),
        P("seq", "dp", None),
        P(),
        P(),
        P(),
        P(),
        P(),
        P(),
        P(),
        P(),
        P(),
    )
    pairs = mesh.shape["seq"] == 2 and mesh.shape["dp"] % 8 == 0

    def on_one(*arrays):
        step = on_pair if pairs and arrays[0].shape[1] == 2 else on_device
        return step(*arrays)

    return jax.shard_map(
        on_one, mesh=mesh, in_specs=in_specs, out_specs=out_specs, check_vma=False
    )
```

```python
import functools
import math

import jax
import jax.numpy as jnp
from jax import lax
from jax.experimental import pallas as pl
from jax.experimental.pallas import tpu as pltpu
from jax.sharding import PartitionSpec as P

HEADS = 16


HIGHEST_PRECISION = lax.Precision.HIGHEST


def shifted(value, axis, steps):
    count = lax.axis_size(axis)
    pairs = [(source, (source + steps) % count) for source in range(count)]
    return lax.ppermute(value, axis, pairs)


def mixed(left, right):
    return jnp.dot(left, right, preferred_element_type=jnp.float32)


def mixed_left(left, right):
    return lax.dot_general(
        left, right, (((0,), (0,)), ((), ())), preferred_element_type=jnp.float32
    )


def mixed_right(left, right):
    return lax.dot_general(
        left, right, (((1,), (1,)), ((), ())), preferred_element_type=jnp.float32
    )


def precise(left, right):
    return jnp.dot(left, right, precision=HIGHEST_PRECISION, preferred_element_type=jnp.float32)


def precise_left(left, right):
    return lax.dot_general(
        left,
        right,
        (((0,), (0,)), ((), ())),
        precision=HIGHEST_PRECISION,
        preferred_element_type=jnp.float32,
    )


def precise_right(left, right):
    return lax.dot_general(
        left,
        right,
        (((1,), (1,)), ((), ())),
        precision=HIGHEST_PRECISION,
        preferred_element_type=jnp.float32,
    )


def gelu_value(inputs):
    return 0.5 * inputs * (1.0 + lax.erf(inputs * 0.7071067811865476))


def gelu_slope(inputs):
    return (
        0.5 * (1.0 + lax.erf(inputs * 0.7071067811865476))
        + inputs * jnp.exp(-0.5 * inputs * inputs) * 0.3989422804014327
    )


def normalize(values):
    row_mean = jnp.mean(values, axis=-1, keepdims=True)
    centred = values - row_mean
    spread = jnp.mean(centred * centred, axis=-1, keepdims=True)
    inv_std = lax.rsqrt(spread + 1e-05)
    return (centred * inv_std, inv_std)


def norm_back(upstream, normed, inv_std):
    mean_grad = jnp.mean(upstream, axis=-1, keepdims=True)
    mean_proj = jnp.mean(upstream * normed, axis=-1, keepdims=True)
    return inv_std * (upstream - mean_grad - normed * mean_proj)


def key_allowed(offset, key_count, seq_lengths):
    places = offset + lax.iota(jnp.int32, key_count)
    return places[None, :] < seq_lengths[:, None]


def lead_state(queries4, prefix_keys4, prefix_values4):
    inv_root = 1.0 / math.sqrt(queries4.shape[3])
    scores = (
        jnp.einsum("rshd,phd->rshp", queries4, prefix_keys4, preferred_element_type=jnp.float32)
        * inv_root
    )
    running_max = jnp.max(scores, axis=3)
    weights = jnp.exp(scores - running_max[..., None])
    running_sum = jnp.sum(weights, axis=3)
    running_mix = jnp.einsum(
        "rshp,phd->rshd",
        weights.astype(jnp.bfloat16),
        prefix_values4,
        preferred_element_type=jnp.float32,
    )
    return (running_max, running_sum, running_mix)


def fold_block(carried, key_block, value_block, offset, queries4, seq_lengths):
    key_count, seqs_here = (key_block.shape[0], key_block.shape[1])
    head_count, head_dim = (queries4.shape[2], queries4.shape[3])
    inv_root = 1.0 / math.sqrt(head_dim)
    keys4 = key_block.reshape(key_count, seqs_here, head_count, head_dim)
    values4 = value_block.reshape(key_count, seqs_here, head_count, head_dim)
    running_max, running_sum, running_mix = carried
    scores = (
        jnp.einsum("rshd,tshd->rsht", queries4, keys4, preferred_element_type=jnp.float32)
        * inv_root
    )
    allowed = key_allowed(offset, key_count, seq_lengths)[None, :, None, :]
    scores = jnp.where(allowed, scores, -jnp.inf)
    new_max = jnp.maximum(running_max, jnp.max(scores, axis=3))
    weights = jnp.exp(scores - new_max[..., None])
    rescale = jnp.exp(running_max - new_max)
    running_sum = running_sum * rescale + jnp.sum(weights, axis=3)
    running_mix = running_mix * rescale[..., None] + jnp.einsum(
        "rsht,tshd->rshd", weights.astype(jnp.bfloat16), values4, preferred_element_type=jnp.float32
    )
    return (new_max, running_sum, running_mix)


def lead_back(queries4, upstream4, log_total, row_delta, prefix_keys4, prefix_values4):
    inv_root = 1.0 / math.sqrt(queries4.shape[3])
    scores = (
        jnp.einsum("rshd,phd->rshp", queries4, prefix_keys4, preferred_element_type=jnp.float32)
        * inv_root
    )
    weights = jnp.exp(scores - log_total[..., None])
    weight_grads = jnp.einsum(
        "rshd,phd->rshp", upstream4, prefix_values4, preferred_element_type=jnp.float32
    )
    score_grads = (weights * (weight_grads - row_delta[..., None])).astype(jnp.bfloat16)
    query_term = (
        jnp.einsum("rshp,phd->rshd", score_grads, prefix_keys4, preferred_element_type=jnp.float32)
        * inv_root
    )
    key_term = (
        jnp.einsum("rshp,rshd->phd", score_grads, queries4, preferred_element_type=jnp.float32)
        * inv_root
    )
    value_term = jnp.einsum(
        "rshp,rshd->phd",
        weights.astype(jnp.bfloat16),
        upstream4,
        preferred_element_type=jnp.float32,
    )
    return (query_term, key_term, value_term)


def block_back(
    queries4, upstream4, log_total, row_delta, key_block, value_block, offset, seq_lengths
):
    key_count, seqs_here, model_width = key_block.shape
    head_count, head_dim = (queries4.shape[2], queries4.shape[3])
    inv_root = 1.0 / math.sqrt(head_dim)
    keys4 = key_block.reshape(key_count, seqs_here, head_count, head_dim)
    values4 = value_block.reshape(key_count, seqs_here, head_count, head_dim)
    scores = (
        jnp.einsum("rshd,tshd->rsht", queries4, keys4, preferred_element_type=jnp.float32)
        * inv_root
    )
    allowed = key_allowed(offset, key_count, seq_lengths)[None, :, None, :]
    scores = jnp.where(allowed, scores, -jnp.inf)
    weights = jnp.exp(scores - log_total[..., None])
    weight_grads = jnp.einsum(
        "rshd,tshd->rsht", upstream4, values4, preferred_element_type=jnp.float32
    )
    score_grads = (weights * (weight_grads - row_delta[..., None])).astype(jnp.bfloat16)
    query_term = (
        jnp.einsum("rsht,tshd->rshd", score_grads, keys4, preferred_element_type=jnp.float32)
        * inv_root
    )
    key_term = (
        jnp.einsum("rsht,rshd->tshd", score_grads, queries4, preferred_element_type=jnp.float32)
        * inv_root
    )
    value_term = jnp.einsum(
        "rsht,rshd->tshd",
        weights.astype(jnp.bfloat16),
        upstream4,
        preferred_element_type=jnp.float32,
    )
    pair_term = jnp.stack(
        [
            key_term.reshape(key_count, seqs_here, model_width),
            value_term.reshape(key_count, seqs_here, model_width),
        ]
    )
    return (query_term, pair_term)


def prefix_back(pair_grad, prefix_act, prefix_embed, hidden_weight, out_weight):
    out_w_grad = precise_left(prefix_act, pair_grad)
    out_b_grad = jnp.sum(pair_grad, axis=0)
    act_grad = precise_right(pair_grad, out_weight) * (1.0 - prefix_act * prefix_act)
    hidden_w_grad = precise_left(prefix_embed, act_grad)
    hidden_b_grad = jnp.sum(act_grad, axis=0)
    embed_grad = precise_right(act_grad, hidden_weight)
    return (embed_grad, hidden_w_grad, hidden_b_grad, out_w_grad, out_b_grad)


def on_device(
    hidden_in,
    lengths,
    w_query,
    w_key,
    w_value,
    w_output,
    attn_gain,
    ffn_in,
    ffn_out,
    ffn_gain,
    adapter_down,
    adapter_down_bias,
    adapter_up,
    adapter_up_bias,
    prefix_embed,
    prefix_hidden_w,
    prefix_hidden_b,
    prefix_out_w,
    prefix_out_b,
    out_grad,
):
    rows_here, seqs_here, model_width = hidden_in.shape
    token_count = rows_here * seqs_here
    head_count = HEADS
    head_dim = model_width // head_count
    axis_count = lax.axis_size("seq")
    position = lax.axis_index("seq")
    tokens = hidden_in.reshape(token_count, model_width)
    projected = jnp.stack([mixed(tokens, w_query), mixed(tokens, w_key), mixed(tokens, w_value)])
    triple = projected.astype(jnp.bfloat16).reshape(3, rows_here, seqs_here, model_width)
    hidden_weight = prefix_hidden_w.astype(jnp.float32)
    out_weight = prefix_out_w.astype(jnp.float32)
    prefix_act = jnp.tanh(precise(prefix_embed, hidden_weight) + prefix_hidden_b)
    prefix_pair = precise(prefix_act, out_weight) + prefix_out_b
    prefix_keys4 = (
        prefix_pair[:, :model_width].astype(jnp.bfloat16).reshape(-1, head_count, head_dim)
    )
    prefix_values4 = (
        prefix_pair[:, model_width:].astype(jnp.bfloat16).reshape(-1, head_count, head_dim)
    )
    row_places = position * rows_here + lax.iota(jnp.int32, rows_here)
    valid = (row_places[:, None] < lengths[None, :]).astype(jnp.float32).reshape(token_count, 1)
    queries4 = triple[0].reshape(rows_here, seqs_here, head_count, head_dim)
    key_value = triple[1:]
    pieces = lax.all_gather(key_value, "seq", axis=1, tiled=True)
    carried = fold_block(
        lead_state(queries4, prefix_keys4, prefix_values4),
        pieces[0],
        pieces[1],
        jnp.int32(0),
        queries4,
        lengths,
    )
    mix_full = carried[2] / carried[1][..., None]
    log_total = carried[0] + jnp.log(carried[1])
    mix_low = mix_full.astype(jnp.bfloat16).reshape(token_count, model_width)
    attn_proj = mixed(mix_low, w_output)
    normed_one, inv_one = normalize(tokens.astype(jnp.float32) + attn_proj)
    norm_one = normed_one * attn_gain
    norm_low = norm_one.astype(jnp.bfloat16)
    inner_pre = mixed(norm_low, ffn_in)
    inner_act = gelu_value(inner_pre).astype(jnp.bfloat16)
    squeeze = mixed(norm_low, adapter_down) + adapter_down_bias
    squeeze_act = gelu_value(squeeze).astype(jnp.bfloat16)
    ffn_sum = mixed(inner_act, ffn_out)
    adapter_sum = mixed(squeeze_act, adapter_up) + adapter_up_bias
    normed_two, inv_two = normalize(norm_one + ffn_sum + 4.0 * adapter_sum)
    layer_out = (
        (normed_two * ffn_gain * valid)
        .astype(jnp.bfloat16)
        .reshape(rows_here, seqs_here, model_width)
    )
    upstream_top = out_grad.reshape(token_count, model_width).astype(jnp.float32) * valid
    grad_two = norm_back(upstream_top * ffn_gain, normed_two, inv_two)
    grad_ffn_low = grad_two.astype(jnp.bfloat16)
    grad_adapt_low = (4.0 * grad_two).astype(jnp.bfloat16)
    up_grad = mixed_left(squeeze_act, grad_adapt_low)
    up_bias_grad = jnp.sum(grad_adapt_low.astype(jnp.float32), axis=0)
    grad_squeeze_low = (mixed_right(grad_adapt_low, adapter_up) * gelu_slope(squeeze)).astype(
        jnp.bfloat16
    )
    down_grad = mixed_left(norm_low, grad_squeeze_low)
    down_bias_grad = jnp.sum(grad_squeeze_low.astype(jnp.float32), axis=0)
    grad_inner_low = (mixed_right(grad_ffn_low, ffn_out) * gelu_slope(inner_pre)).astype(
        jnp.bfloat16
    )
    grad_norm = (
        grad_two + mixed_right(grad_squeeze_low, adapter_down) + mixed_right(grad_inner_low, ffn_in)
    )
    grad_one = norm_back(grad_norm * attn_gain, normed_one, inv_one)
    grad_attn_low = grad_one.astype(jnp.bfloat16)
    grad_mix_low = mixed_right(grad_attn_low, w_output).astype(jnp.bfloat16)
    upstream4 = grad_mix_low.reshape(rows_here, seqs_here, head_count, head_dim)
    row_delta = jnp.sum(upstream4.astype(jnp.float32) * mix_full, axis=3)
    query_grad, prefix_key_grad, prefix_value_grad = lead_back(
        queries4, upstream4, log_total, row_delta, prefix_keys4, prefix_values4
    )

    def visit(step_index, carried):
        moving, grads_moving, query_total = carried
        source = (position - step_index) % axis_count
        query_term, pair_term = block_back(
            queries4,
            upstream4,
            log_total,
            row_delta,
            moving[0],
            moving[1],
            source * rows_here,
            lengths,
        )
        return (moving, grads_moving + pair_term, query_total + query_term)

    def travel(step_index, carried):
        moving, grads_moving, query_total = visit(step_index, carried)
        moving = shifted(moving, "seq", 1)
        grads_moving = shifted(grads_moving.astype(jnp.bfloat16), "seq", 1).astype(
            grads_moving.dtype
        )
        return (moving, grads_moving, query_total)

    initial = (
        key_value,
        jnp.zeros((2, rows_here, seqs_here, model_width), jnp.float32),
        query_grad,
    )
    carried = lax.fori_loop(0, axis_count - 1, travel, initial)
    carried = visit(axis_count - 1, carried)
    pair_grads = shifted(carried[1].astype(jnp.bfloat16), "seq", 1).astype(jnp.float32)
    triple_grad = jnp.concatenate(
        [carried[2].reshape(1, rows_here, seqs_here, model_width), pair_grads]
    ).astype(jnp.bfloat16)
    hidden_grad = grad_one + mixed_right(triple_grad[0].reshape(token_count, model_width), w_query)
    hidden_grad = hidden_grad + mixed_right(triple_grad[1].reshape(token_count, model_width), w_key)
    hidden_grad = hidden_grad + mixed_right(
        triple_grad[2].reshape(token_count, model_width), w_value
    )
    hidden_grad = hidden_grad.astype(jnp.bfloat16).reshape(rows_here, seqs_here, model_width)
    pair_grad = jnp.concatenate(
        [prefix_key_grad.reshape(-1, model_width), prefix_value_grad.reshape(-1, model_width)],
        axis=1,
    )
    prefix_grads = prefix_back(pair_grad, prefix_act, prefix_embed, hidden_weight, out_weight)
    summed = lax.psum(
        (
            down_grad,
            down_bias_grad,
            up_grad,
            up_bias_grad,
            prefix_grads[0],
            prefix_grads[1],
            prefix_grads[2],
            prefix_grads[3],
            prefix_grads[4],
        ),
        ("seq", "dp"),
    )
    adapter_totals = summed[:4]
    prefix_totals = summed[4:]
    return (
        layer_out,
        hidden_grad,
        adapter_totals[0],
        adapter_totals[1],
        adapter_totals[2],
        adapter_totals[3],
        prefix_totals[0],
        prefix_totals[1],
        prefix_totals[2],
        prefix_totals[3],
        prefix_totals[4],
    )


BF16 = jnp.bfloat16
F32 = jnp.float32
MIB = 1024 * 1024
GROUP = 4
HEAD_DIM = 64
LANES = GROUP * HEAD_DIM
PAD = 32
MASKED = -1e30
LOG2E = 1.4426950408889634
VMEM_LIMIT = 60 * MIB


def dot_nn(left, right):
    return lax.dot_general(left, right, (((1,), (0,)), ((), ())), preferred_element_type=F32)


def dot_nt(left, right):
    return lax.dot_general(left, right, (((1,), (1,)), ((), ())), preferred_element_type=F32)


def dot_tn(left, right):
    return lax.dot_general(left, right, (((0,), (0,)), ((), ())), preferred_element_type=F32)


def shape_of(shape, dtype):
    return pltpu.HBM(shape, dtype)


def far(value):
    return pltpu.with_memory_space_constraint(value, pltpu.HBM)


def bring(value):
    return pltpu.with_memory_space_constraint(value, pltpu.VMEM)


def all_far(values):
    return [far(value) for value in values]


def params(limit=VMEM_LIMIT):
    return pltpu.CompilerParams(vmem_limit_bytes=limit)


def cost(macs, moved):
    return pl.CostEstimate(flops=int(2 * macs), bytes_accessed=int(moved), transcendentals=0)


SMEM_SPEC = pl.BlockSpec(memory_space=pltpu.SMEM)
ANY_SPEC = pl.BlockSpec(memory_space=pl.ANY)
CORE_SPEC = pl.BlockSpec(memory_space=pltpu.VMEM)


def whole(shape):
    return pl.BlockSpec(shape, lambda *_: (0,) * len(shape))


def kept(shape):
    return pl.BlockSpec(shape, lambda *_: (0,) * len(shape), pipeline_mode=pl.Buffered(1))


def split_kernel(place_ref, both_ref, own_ref, other_ref):
    apart = jnp.swapaxes(both_ref[...], 0, 1)
    first = place_ref[0] == 0
    own_ref[...] = jnp.where(first, apart[0], apart[1])
    other_ref[...] = jnp.where(first, apart[1], apart[0])


def split(place, both):
    rows, _, width = both.shape
    step = rows // 2
    half = pl.BlockSpec((step, width), lambda i: (i, 0))
    return pl.pallas_call(
        split_kernel,
        grid=(2,),
        in_specs=[SMEM_SPEC, pl.BlockSpec((step, 2, width), lambda i: (i, 0, 0))],
        out_specs=[half, half],
        out_shape=[shape_of((rows, width), both.dtype)] * 2,
        compiler_params=params(16 * MIB),
        cost_estimate=cost(0, 4 * rows * width * 2),
    )(place, far(both))


def merge_kernel(place_ref, own_ref, other_ref, both_ref):
    first = place_ref[0] == 0
    own, other = own_ref[...], other_ref[...]
    apart = jnp.stack([jnp.where(first, own, other), jnp.where(first, other, own)])
    both_ref[...] = jnp.swapaxes(apart, 0, 1)


def place_of(half, place_ref, rows):
    return jnp.where(half == 0, place_ref[0], 1 - place_ref[0]) * rows


def length_of(place_ref, lengths_ref):
    return jnp.where(place_ref[0] == 0, lengths_ref[0], lengths_ref[1])


def parts_of(values, count):
    parts = []
    for _ in range(count):
        part = values.astype(BF16)
        parts.append(part)
        values = values - part.astype(F32)
    return parts


def exact_dot(values, weight, dot):
    rows = values.shape[0]
    product = dot(jnp.concatenate(parts_of(values, 3), axis=0), weight)
    return product[:rows] + product[rows : 2 * rows] + product[2 * rows :]


def prefix_kernel(embed_ref, hw_ref, hb_ref, ow_ref, ob_ref, act_ref, key_ref, value_ref):
    width = key_ref.shape[1]
    act = jnp.tanh(exact_dot(embed_ref[...], hw_ref[...], dot_nn) + hb_ref[...])
    act_ref[...] = act
    pair = exact_dot(act, ow_ref[...], dot_nn) + ob_ref[...]
    key_ref[...] = pair[:, :width].astype(BF16)
    value_ref[...] = pair[:, width:].astype(BF16)


def prefix_forward(embed, hidden_w, hidden_b, out_w, out_b):
    width, hidden = hidden_w.shape
    return pl.pallas_call(
        prefix_kernel,
        out_shape=[
            shape_of((PAD, hidden), F32),
            shape_of((PAD, width), BF16),
            shape_of((PAD, width), BF16),
        ],
        compiler_params=params(16 * MIB),
        cost_estimate=cost(3 * PAD * hidden * 3 * width * 4, 6 * hidden * width),
    )(embed, far(hidden_w), hidden_b[None], far(out_w), out_b[None])


def prefix_back_kernel(
    count, pairs_ref, act_ref, embed_ref, hw_ref, ow_ref, place_ref, own_ref, other_ref,
    both_ref, eg_ref, hwg_ref, hbg_ref, owg_ref, obg_ref, ubg_ref, dbg_ref,
):
    merge_kernel(place_ref, own_ref[...], other_ref, both_ref)
    total = pairs_ref[0]
    for line in range(1, pairs_ref.shape[0]):
        total = total + pairs_ref[line]
    ubg_ref[...] = total[count : count + 1]
    dbg_ref[...] = total[count + 1 : count + 2, : dbg_ref.shape[1]]
    pair = jnp.concatenate([total[:PAD], total[PAD:]], axis=1)
    rows = lax.broadcasted_iota(jnp.int32, pair.shape, 0)
    pair = jnp.where(rows < count, pair, 0.0)
    act = act_ref[...]
    obg_ref[...] = jnp.sum(pair, axis=0, keepdims=True)
    high, low = parts_of(pair, 2)
    back = dot_nt(jnp.concatenate([high, low], axis=0), ow_ref[...])
    act_grad = (back[:PAD] + back[PAD:]) * (1.0 - act * act)
    act_high, act_low = parts_of(act, 2)
    owg_ref[...] = dot_tn(
        jnp.concatenate([act_high, act_low, act_high], axis=0),
        jnp.concatenate([high, high, low], axis=0),
    )
    hbg_ref[...] = jnp.sum(act_grad, axis=0, keepdims=True)
    high, low = parts_of(act_grad, 2)
    embed_high, embed_low = parts_of(embed_ref[...], 2)
    hwg_ref[...] = dot_tn(
        jnp.concatenate([embed_high, embed_low, embed_high], axis=0),
        jnp.concatenate([high, high, low], axis=0),
    )
    back = dot_nt(jnp.concatenate([high, low], axis=0), hw_ref[...])
    eg_ref[...] = (back[:PAD] + back[PAD:])[:count]


def prefix_backward(count, adapt, pairs, act, embed, hidden_w, out_w, place, own, other):
    width, hidden = hidden_w.shape
    core = [CORE_SPEC] * 5
    return pl.pallas_call(
        functools.partial(prefix_back_kernel, count),
        in_specs=core + [SMEM_SPEC, CORE_SPEC, CORE_SPEC],
        out_shape=[
            shape_of((own.shape[0], 2, width), BF16),
            shape_of((count, width), F32),
            shape_of((width, hidden), F32),
            shape_of((1, hidden), F32),
            shape_of((hidden, 2 * width), F32),
            shape_of((1, 2 * width), F32),
            shape_of((1, width), F32),
            shape_of((1, adapt), F32),
        ],
        compiler_params=params(24 * MIB),
        cost_estimate=cost(96 * hidden * width * 6, 20 * hidden * width),
    )(far(pairs), act, embed, far(hidden_w), far(out_w), place, far(own), far(other))


def project_kernel(apart, x_ref, wq_ref, wk_ref, wv_ref, *refs):
    x = x_ref[...]
    if apart:
        place_ref, both_ref, q_ref, k_ref, v_ref, own_ref, other_ref = refs
        split_kernel(place_ref, both_ref, own_ref, other_ref)
    else:
        q_ref, k_ref, v_ref = refs[-3:]
    scale = LOG2E / math.sqrt(HEAD_DIM)
    q_ref[...] = (dot_nn(x, wq_ref[...]) * scale).astype(BF16)
    k_ref[...] = dot_nn(x, wk_ref[...]).astype(BF16)
    v_ref[...] = dot_nn(x, wv_ref[...]).astype(BF16)


def project(half, x, w_query, w_key, w_value, earlier, place=None, both=None):
    rows, width = x.shape
    step = rows // 2
    apart = both is not None
    block = pl.BlockSpec((step, width), lambda i: (i, 0))
    out_specs = [pl.BlockSpec((step, width), lambda i: (2 * half + i, 0))] * 3
    out_shape = [shape_of((2 * rows, width), BF16)] * 3
    more_specs, more = [ANY_SPEC] * len(earlier), all_far(earlier)
    if apart:
        more_specs = [SMEM_SPEC, pl.BlockSpec((step, 2, width), lambda i: (i, 0, 0))]
        more = [place, far(both)]
        out_specs = out_specs + [block] * 2
        out_shape = out_shape + [shape_of((rows, width), BF16)] * 2
    return pl.pallas_call(
        functools.partial(project_kernel, apart),
        grid=(2,),
        in_specs=[block] + [CORE_SPEC] * 3 + more_specs,
        out_specs=out_specs,
        out_shape=out_shape,
        input_output_aliases={4 + i: i for i in range(len(earlier))},
        compiler_params=params(20 * MIB),
        cost_estimate=cost(3 * rows * width * width, 2 * (4 * rows * width + 3 * width * width)),
    )(far(x) if apart else x, bring(w_query), bring(w_key), bring(w_value), *more)


def head_lanes(head, rows, lanes):
    place = lax.broadcasted_iota(jnp.int32, (rows, lanes), 1)
    return (place // HEAD_DIM == head).astype(F32).astype(BF16)


def first_lane(values):
    lane = lax.broadcasted_iota(jnp.int32, (values.shape[0], 128), 1)
    return jnp.where(lane == 0, values, 0.0).astype(BF16)


def block_diagonal(rows):
    return jnp.concatenate(
        [rows * head_lanes(head, rows.shape[0], LANES) for head in range(GROUP)], axis=0
    )


def attend_kernel(
    prefixed, first, place_ref, lengths_ref, q_ref, k_ref, v_ref, pk_ref, pv_ref, *refs
):
    pt_ref, ot_ref, st_ref, pp_ref, *scores = refs[-6:]
    keys = k_ref.shape[0]
    queries = q_ref.shape[0]
    half = (pl.program_id(0) + first) // 2

    def quadrant(count):
        place = place_of(half, place_ref, keys) + lax.broadcasted_iota(jnp.int32, (keys, 128), 0)
        bias = first_lane(jnp.where(place < length_of(place_ref, lengths_ref), 0.0, MASKED))
        ones = first_lane(jnp.ones((queries, 128), F32))
        tail = jnp.ones((16, keys), BF16)
        masks = [head_lanes(head, queries, 128) for head in range(2)]

        def score(head):
            pair = slice((head // 2) * 128, (head // 2 + 1) * 128)
            k_aug = jnp.concatenate([k_ref[:, pair], bias], axis=1)
            q_aug = jnp.concatenate([q_ref[:, pair] * masks[head % 2], ones], axis=1)
            scores[head % 2][...] = dot_nt(k_aug, q_aug)

        def weigh(head):
            own = scores[head % 2]
            top = jnp.max(own[...], axis=0, keepdims=True)
            if count:
                lead_scores = lead[head * PAD : (head + 1) * PAD]
                top = jnp.maximum(top, jnp.max(lead_scores, axis=0, keepdims=True))
            pt_ref[head] = jnp.exp2(own[...] - top).astype(BF16)
            st_ref[0, head : head + 1, :] = top
            if not count:
                return 0.0
            lead_weights = jnp.exp2(lead_scores - top).astype(BF16)
            pp_ref[0, head * PAD : (head + 1) * PAD, :] = lead_weights
            return jnp.sum(lead_weights.astype(F32), axis=0, keepdims=True)

        def mix(head, lead_total):
            rows = slice(head * HEAD_DIM, (head + 1) * HEAD_DIM)
            mixed_rows = dot_nn(jnp.concatenate([turned[rows], tail], axis=0), pt_ref[head])
            mixed = mixed_rows[:HEAD_DIM]
            if count:
                lead_weights = pp_ref[0, head * PAD : (head + 1) * PAD, :]
                mixed = mixed + dot_nn(lead_turned[rows], lead_weights)
            ot_ref[rows, :] = mixed.astype(BF16)
            total_row = mixed_rows[HEAD_DIM : HEAD_DIM + 1] + lead_total
            st_ref[0, GROUP + head : GROUP + head + 1, :] = total_row

        score(0)
        turned = v_ref[...].T
        if count:
            lead_turned = pv_ref[...].T
            lead = dot_nt(block_diagonal(pk_ref[...]), q_ref[...])
            row = lax.broadcasted_iota(jnp.int32, lead.shape, 0)
            lead = jnp.where(row % PAD < count, lead, MASKED)
        lead_totals = []
        for head in range(GROUP):
            if head + 1 < GROUP:
                score(head + 1)
            lead_totals.append(weigh(head))
            if head:
                mix(head - 1, lead_totals[head - 1])
        mix(GROUP - 1, lead_totals[GROUP - 1])

    @pl.when(half == 0)
    def _():
        quadrant(prefixed)

    @pl.when(half == 1)
    def _():
        quadrant(0)


def attend(count, place, lengths, first, quadrants, q, k, v, lead, earlier):
    tokens, width = q.shape
    rows = tokens // 2
    groups = width // LANES
    last = groups - 1

    def lead_place(i, g):
        quadrant = i + first
        return (jnp.where(quadrant < 2, g, last), 0, jnp.minimum(quadrant, 1))

    keys = pl.BlockSpec((rows, LANES), lambda i, g: ((i + first) // 2, g))
    in_specs = [
        SMEM_SPEC,
        SMEM_SPEC,
        pl.BlockSpec((rows, LANES), lambda i, g: ((i + first) % 2, g)),
        keys,
        keys,
    ]
    in_specs += [pl.BlockSpec((PAD, LANES), lambda i, g: (0, g))] * 2
    out_specs = [
        pl.BlockSpec(
            (None, GROUP, rows, rows), lambda i, g: ((i + first) // 2, g, 0, (i + first) % 2)
        ),
        pl.BlockSpec((None, LANES, rows), lambda i, g: ((i + first) // 2, g, (i + first) % 2)),
        pl.BlockSpec(
            (None, 1, 2 * GROUP, rows), lambda i, g: ((i + first) // 2, g, 0, (i + first) % 2)
        ),
        pl.BlockSpec((1, GROUP * PAD, rows), lead_place),
    ]
    out_shape = [
        shape_of((2, groups * GROUP, rows, tokens), BF16),
        shape_of((2, width, tokens), BF16),
        shape_of((2, groups, 2 * GROUP, tokens), F32),
        shape_of((groups, GROUP * PAD, tokens), BF16),
    ]
    macs = quadrants * groups * GROUP * rows * rows * 256 * 2
    return pl.pallas_call(
        functools.partial(attend_kernel, count, first),
        grid=(quadrants, groups),
        in_specs=in_specs + [ANY_SPEC] * len(earlier),
        out_specs=out_specs,
        out_shape=out_shape,
        input_output_aliases={7 + i: i for i in range(len(earlier))},
        scratch_shapes=[pltpu.VMEM((rows, rows), F32)] * 2,
        compiler_params=params(16 * MIB),
        cost_estimate=cost(macs, quadrants * 14 * MIB),
    )(place, lengths, *all_far((q, k, v, *lead, *earlier)))


def lead_back_kernel(
    count, q_ref, up_ref, rst_ref, del_ref, pp_ref, pk_ref, pv_ref, bias_ref, pair_ref, dqt_ref
):
    queries = q_ref.shape[0]
    ups = []
    deltas = []
    for head in range(GROUP):
        rows = slice(head * HEAD_DIM, (head + 1) * HEAD_DIM)
        share = rst_ref[0, head : head + 1, :]
        ups.append((up_ref[rows, :].astype(F32) * share).astype(BF16))
        delta = del_ref[0, head : head + 1, :] * share
        deltas.append(jnp.broadcast_to(delta, (PAD, queries)))
    up = jnp.concatenate(ups, axis=0)
    delta = jnp.concatenate(deltas, axis=0)
    weights = pp_ref[0]
    key_diagonal = block_diagonal(pk_ref[...])
    value_diagonal = block_diagonal(pv_ref[...])
    weight_grads = dot_nn(value_diagonal, up)
    score_grads = (weights.astype(F32) * (weight_grads - delta)).astype(BF16)
    dqt_ref[...] = dot_tn(key_diagonal, score_grads).astype(BF16)
    key_grads = dot_nn(score_grads, q_ref[...]) * (1.0 / LOG2E)
    value_grads = dot_nt(weights, up)
    lane = lax.broadcasted_iota(jnp.int32, (PAD, LANES), 1) // HEAD_DIM
    key_total = jnp.zeros((PAD, LANES), F32)
    value_total = jnp.zeros((PAD, LANES), F32)
    for head in range(GROUP):
        rows = slice(head * PAD, (head + 1) * PAD)
        key_total = jnp.where(lane == head, key_grads[rows], key_total)
        value_total = jnp.where(lane == head, value_grads[rows], value_total)
    row = lax.broadcasted_iota(jnp.int32, (PAD, LANES), 0)
    key_total = jnp.where(row == count, bias_ref[0:1, :], key_total)
    key_total = jnp.where(row == count + 1, bias_ref[1:2, :], key_total)
    pair_ref[:PAD, :] = key_total.astype(BF16)
    pair_ref[PAD:, :] = value_total.astype(BF16)


def lead_backward(count, q, up, shares, deltas, lead_weights, prefix_keys, prefix_values, biases):
    tokens, width = q.shape
    groups = width // LANES
    small = pl.BlockSpec((PAD, LANES), lambda g: (0, g))
    stats = pl.BlockSpec((1, 2 * GROUP, tokens), lambda g: (g, 0, 0))
    return pl.pallas_call(
        functools.partial(lead_back_kernel, count),
        grid=(groups,),
        in_specs=[
            pl.BlockSpec((tokens, LANES), lambda g: (0, g)),
            pl.BlockSpec((LANES, tokens), lambda g: (g, 0)),
            stats,
            stats,
            pl.BlockSpec((1, GROUP * PAD, tokens), lambda g: (g, 0, 0)),
            small,
            small,
            pl.BlockSpec((8, LANES), lambda g: (0, g)),
        ],
        out_specs=[
            pl.BlockSpec((2 * PAD, LANES), lambda g: (0, g)),
            pl.BlockSpec((LANES, tokens), lambda g: (g, 0)),
        ],
        out_shape=[
            jax.ShapeDtypeStruct((2 * PAD, width), BF16),
            shape_of((width, tokens), BF16),
        ],
        compiler_params=params(14 * MIB),
        cost_estimate=cost(groups * 4 * GROUP * PAD * tokens * LANES, 10 * MIB),
    )(*all_far((q, up, shares, deltas, lead_weights)), prefix_keys, prefix_values, biases)


def attend_back_kernel(
    half,
    last_keys,
    last_queries,
    has_earlier,
    q_ref,
    k_ref,
    v_ref,
    up_ref,
    rst_ref,
    del_ref,
    pt_ref,
    dqt_in_ref,
    *refs,
):
    dq_ref, dk_ref, dv_ref = refs[-5:-2]
    weight_grads = refs[-2:]
    queries = q_ref.shape[0]
    lane = lax.broadcasted_iota(jnp.int32, (queries, 128), 1) // HEAD_DIM
    masks = [(lane == head).astype(F32).astype(BF16) for head in range(2)]
    zeros = jnp.zeros((HEAD_DIM, queries), BF16)
    turned = k_ref[...].T
    ups = {}
    grads = {}
    query_grads = []
    key_grads = []
    value_grads = []

    def pair_of(head):
        return slice((head // 2) * 128, (head // 2 + 1) * 128)

    def rows_of(head):
        return slice(head * HEAD_DIM, (head + 1) * HEAD_DIM)

    def share_of(head):
        return rst_ref[0, half * GROUP + head : half * GROUP + head + 1, :]

    def weight_grad(head):
        up = (up_ref[rows_of(head), :].astype(F32) * share_of(head)).astype(BF16)
        ups[head] = jnp.concatenate([up, zeros] if head % 2 == 0 else [zeros, up], axis=0)
        weight_grads[head % 2][...] = dot_nn(v_ref[:, pair_of(head)], ups[head])

    def score_grad(head):
        delta = del_ref[0, head : head + 1, :] * share_of(head)
        return (pt_ref[head].astype(F32) * (weight_grads[head % 2][...] - delta)).astype(BF16)

    def value_term(head):
        return dot_nt(pt_ref[head], ups[head])

    def key_term(head):
        return dot_nn(grads[head], q_ref[:, pair_of(head)] * masks[head % 2])

    def query_term(head):
        return dqt_in_ref[rows_of(head), :].astype(F32) + dot_nn(turned[rows_of(head)], grads[head])

    weight_grad(0)
    for head in range(GROUP):
        if head + 1 < GROUP:
            weight_grad(head + 1)
        grads[head] = score_grad(head)
        value = value_term(head)
        query_grads.append(query_term(head))
        key = key_term(head)
        if head % 2:
            key_grads[-1] = key_grads[-1] + key
            value_grads[-1] = value_grads[-1] + value
        else:
            key_grads.append(key)
            value_grads.append(value)
    query_grad = jnp.concatenate(query_grads, axis=0)
    key_grad = jnp.concatenate(key_grads, axis=1)
    value_grad = jnp.concatenate(value_grads, axis=1)
    if not last_keys:
        dq_ref[...] = query_grad.astype(BF16)
    else:
        dq_ref[...] = (query_grad * (1.0 / math.sqrt(HEAD_DIM))).astype(BF16).T
    if has_earlier:
        key_grad = key_grad + refs[0][...].astype(F32)
        value_grad = value_grad + refs[1][...].astype(F32)
    if last_queries:
        key_grad = key_grad * (1.0 / LOG2E)
    dk_ref[...] = key_grad.astype(BF16)
    dv_ref[...] = value_grad.astype(BF16)


def attend_back(
    key_half, query_half, last_keys, last_queries, q, k, v, up, shares, deltas, weights, dqt, earlier
):
    tokens, width = q.shape
    rows = tokens // 2
    groups = width // LANES
    query_columns = pl.BlockSpec((LANES, rows), lambda g: (g, query_half))
    stats = pl.BlockSpec((1, 2 * GROUP, rows), lambda g: (g, 0, query_half))
    finished = pl.BlockSpec((rows, LANES), lambda g: (0, g))
    out_columns = pl.BlockSpec((LANES, rows), lambda g: (g, 0))
    sofar = query_columns if dqt.shape[1] == tokens else out_columns
    macs = groups * GROUP * rows * rows * 256 * 4
    return pl.pallas_call(
        functools.partial(
            attend_back_kernel, key_half, last_keys, last_queries, len(earlier) > 0
        ),
        grid=(groups,),
        in_specs=[
            pl.BlockSpec((rows, LANES), lambda g: (query_half, g)),
            pl.BlockSpec((rows, LANES), lambda g: (key_half, g)),
            pl.BlockSpec((rows, LANES), lambda g: (key_half, g)),
            query_columns,
            stats,
            stats,
            pl.BlockSpec((None, GROUP, rows, rows), lambda g: (key_half, g, 0, query_half)),
            sofar,
        ]
        + [finished] * len(earlier),
        out_specs=[finished if last_keys else out_columns, finished, finished],
        out_shape=[
            shape_of((rows, width) if last_keys else (width, rows), BF16),
            shape_of((rows, width), BF16),
            shape_of((rows, width), BF16),
        ],
        scratch_shapes=[pltpu.VMEM((rows, rows), F32)] * 2,
        compiler_params=params(18 * MIB),
        cost_estimate=cost(macs, 12 * MIB),
    )(*all_far((q, k, v, up, shares, deltas, weights, dqt, *earlier)))


def gelu_pair(values):
    scaled = values * 0.7071067811865476
    below = 0.5 * lax.erf(scaled) + 0.5
    decay = jnp.exp2(scaled * scaled * (-LOG2E))
    return values * below, below + values * 0.3989422804014327 * decay


def row_mean(values):
    return jnp.mean(values, axis=-1, keepdims=True)


def front_kernel(
    tiles,
    place_ref,
    lengths_ref,
    x_own_ref,
    x_other_ref,
    ot_own_ref,
    ot_other_ref,
    st_own_ref,
    st_other_ref,
    og_own_ref,
    og_other_ref,
    gain_one_ref,
    gain_two_ref,
    down_bias_ref,
    up_bias_ref,
    wo_ref,
    fin_ref,
    fout_ref,
    down_ref,
    up_ref,
    out_own_ref,
    out_other_ref,
    rst_ref,
    mix_ref,
    slope_ref,
    grad_low_ref,
    norm_grad_ref,
    normed_ref,
    inv_ref,
    kept_ref,
    sent_ref,
    bias_grad_ref,
    act_ref,
    squeeze_ref,
    low_ref,
):
    step = pl.program_id(0)
    tile = x_own_ref.shape[0]
    width = x_own_ref.shape[1]
    hidden = fin_ref.shape[1]
    chunk = 512
    chunks = [slice(first, first + chunk) for first in range(0, hidden, chunk)]
    own = step < tiles // 2
    x = jnp.where(own, x_own_ref[...], x_other_ref[...]).astype(F32)
    top_own, top_other = st_own_ref[:, :GROUP, :], st_other_ref[:, :GROUP, :]
    top = jnp.maximum(top_own, top_other)
    share_own, share_other = jnp.exp2(top_own - top), jnp.exp2(top_other - top)
    inverse = 1.0 / (
        st_own_ref[:, GROUP:, :] * share_own + st_other_ref[:, GROUP:, :] * share_other
    )
    rst_ref[:, :GROUP, :] = share_own * inverse
    rst_ref[:, GROUP:, :] = share_other * inverse
    mixes = []
    for head in range(width // HEAD_DIM):
        rows = slice(head * HEAD_DIM, (head + 1) * HEAD_DIM)
        group, place = head // GROUP, head % GROUP
        mixes.append(
            (
                ot_own_ref[rows, :].astype(F32) * rst_ref[group, place : place + 1, :]
                + ot_other_ref[rows, :].astype(F32) * rst_ref[group, GROUP + place : GROUP + place + 1, :]
            ).astype(BF16)
        )
    mix = jnp.concatenate(mixes, axis=0)
    mix_ref[...] = mix
    resid_one = x + dot_tn(mix, wo_ref[...])
    centred = resid_one - row_mean(resid_one)
    inv_one = lax.rsqrt(row_mean(centred * centred) + 1e-05)
    normed = centred * inv_one
    normed_ref[...] = normed.astype(BF16)
    inv_ref[...] = inv_one
    norm_one = normed * gain_one_ref[...]
    norm_low = norm_one.astype(BF16)

    squeeze = dot_nn(norm_low, down_ref[...]) + down_bias_ref[...]
    inner = dot_nn(norm_low, fin_ref[:, chunks[0]])
    squeeze_act, squeeze_slope = gelu_pair(squeeze)
    squeeze_act = squeeze_act.astype(BF16)
    resid_two = norm_one + 4.0 * (dot_nn(squeeze_act, up_ref[...]) + up_bias_ref[...])
    for place, columns in enumerate(chunks):
        more = place + 1 < len(chunks)
        coming = dot_nn(norm_low, fin_ref[:, chunks[place + 1]]) if more else None
        act, slope = gelu_pair(inner)
        slope_ref[:, columns] = slope.astype(BF16)
        resid_two = resid_two + dot_nn(act.astype(BF16), fout_ref[columns, :])
        inner = coming

    centred = resid_two - row_mean(resid_two)
    inv_two = lax.rsqrt(row_mean(centred * centred) + 1e-05)
    normed_two = centred * inv_two
    base = place_of(step // (tiles // 2), place_ref, (tiles // 2) * tile) + step % (tiles // 2) * tile
    place = base + lax.broadcasted_iota(jnp.int32, (tile, 1), 0)
    valid = (place < length_of(place_ref, lengths_ref)).astype(F32)
    gain_two = gain_two_ref[...]
    out = (normed_two * gain_two * valid).astype(BF16)
    upstream = jnp.where(own, og_own_ref[...], og_other_ref[...]).astype(F32) * valid * gain_two
    grad_two = inv_two * (
        upstream - row_mean(upstream) - normed_two * row_mean(upstream * normed_two)
    )
    grad_low = grad_two.astype(BF16)
    grad_adapt = 4.0 * grad_low
    grad_squeeze = (dot_nt(grad_adapt, up_ref[...]) * squeeze_slope).astype(BF16)
    norm_grad_ref[...] = (grad_two + dot_nt(grad_squeeze, down_ref[...])).astype(BF16)
    here = pl.ds(pl.multiple_of(step * tile, tile), tile)
    grad_low_ref[here, :] = grad_low
    act_ref[here, :] = squeeze_act
    squeeze_ref[here, :] = grad_squeeze
    low_ref[here, :] = norm_low
    up_bias_grad = jnp.sum(grad_adapt.astype(F32), axis=0, keepdims=True)
    down_bias_grad = jnp.sum(grad_squeeze.astype(F32), axis=0, keepdims=True)
    adapt = down_bias_grad.shape[1]

    @pl.when(own)
    def _():
        out_own_ref[...] = out

    @pl.when(jnp.logical_not(own))
    def _():
        out_other_ref[...] = out

    @pl.when(step == 0)
    def _():
        bias_grad_ref[...] = jnp.zeros_like(bias_grad_ref)
        bias_grad_ref[0:1, :] = up_bias_grad
        bias_grad_ref[1:2, :adapt] = down_bias_grad

    @pl.when(step > 0)
    def _():
        bias_grad_ref[0:1, :] += up_bias_grad
        bias_grad_ref[1:2, :adapt] += down_bias_grad

    @pl.when(step == tiles - 1)
    def _():
        first = place_ref[1] == 0
        up_total = (4.0 * dot_tn(act_ref[...], grad_low_ref[...])).astype(BF16)
        down_total = dot_tn(squeeze_ref[...], low_ref[...]).astype(BF16)
        kept_ref[...] = jnp.where(first, up_total, down_total)
        sent_ref[...] = jnp.where(first, down_total, up_total)


def front(
    place, lengths, x_own, x_other, mix_parts, tops_sums, og_own, og_other, w_output, attn_gain,
    ffn_in, ffn_out, ffn_gain, down, down_bias, up, up_bias,
):
    rows, width = x_own.shape
    tokens = 2 * rows
    hidden = ffn_in.shape[1]
    adapt = down.shape[1]
    groups = width // LANES
    tile = 256
    tiles = tokens // tile
    near = pl.BlockSpec((tile, width), lambda i: (jnp.minimum(i, tiles // 2 - 1), 0))
    far = pl.BlockSpec((tile, width), lambda i: (jnp.maximum(i - tiles // 2, 0), 0))
    row_block = pl.BlockSpec((tile, width), lambda i: (i, 0))
    column_block = pl.BlockSpec((width, tile), lambda i: (0, i))
    stats = pl.BlockSpec((groups, 2 * GROUP, tile), lambda i: (0, 0, i))
    mixes = [pl.BlockSpec((None, width, tile), lambda i, half=half: (half, 0, i)) for half in range(2)]
    tops = [
        pl.BlockSpec((None, groups, 2 * GROUP, tile), lambda i, half=half: (half, 0, 0, i))
        for half in range(2)
    ]
    return pl.pallas_call(
        functools.partial(front_kernel, tiles),
        grid=(tiles,),
        in_specs=[
            SMEM_SPEC, SMEM_SPEC, near, far, *mixes, *tops, near, far,
            whole((1, width)), whole((1, width)), whole((1, adapt)), whole((1, width)),
        ] + [CORE_SPEC] * 5,
        out_specs=[
            near, far, stats, column_block, pl.BlockSpec((tile, hidden), lambda i: (i, 0)),
            kept((tokens, width)), row_block, row_block, pl.BlockSpec((tile, 1), lambda i: (i, 0)),
            kept((adapt, width)), kept((adapt, width)), whole((8, width)),
        ],
        out_shape=[
            shape_of((rows, width), BF16),
            shape_of((rows, width), BF16),
            shape_of((groups, 2 * GROUP, tokens), F32),
            shape_of((width, tokens), BF16),
            shape_of((tokens, hidden), BF16),
            shape_of((tokens, width), BF16),
            shape_of((tokens, width), BF16),
            shape_of((tokens, width), BF16),
            shape_of((tokens, 1), F32),
            shape_of((adapt, width), BF16),
            shape_of((adapt, width), BF16),
            shape_of((8, width), F32),
        ],
        scratch_shapes=[
            pltpu.VMEM((tokens, adapt), BF16),
            pltpu.VMEM((tokens, adapt), BF16),
            pltpu.VMEM((tokens, width), BF16),
        ],
        compiler_params=params(32 * MIB),
        cost_estimate=cost(tokens * width * (width + 2 * hidden + 6 * adapt), 60 * MIB),
    )(
        place,
        lengths,
        *all_far((x_own, x_other, mix_parts, mix_parts, tops_sums, tops_sums, og_own, og_other)),
        attn_gain[None], ffn_gain[None], down_bias[None], up_bias[None],
        *[bring(item) for item in (w_output, ffn_in, ffn_out, down, up)],
    )


def rear_kernel(
    grad_low_ref, norm_grad_ref, slope_ref, normed_ref, inv_ref, mix_ref, gain_ref, wo_ref, fin_ref,
    fout_ref, grad_one_ref, up_ref, del_ref,
):
    hidden = fin_ref.shape[1]
    chunk = 1024
    chunks = [slice(first, first + chunk) for first in range(0, hidden, chunk)]
    grad_low = grad_low_ref[...]
    grad_norm = norm_grad_ref[...].astype(F32)
    inner = dot_nt(grad_low, fout_ref[chunks[0], :])
    for place, columns in enumerate(chunks):
        more = place + 1 < len(chunks)
        coming = dot_nt(grad_low, fout_ref[chunks[place + 1], :]) if more else None
        low = (inner * slope_ref[:, columns].astype(F32)).astype(BF16)
        grad_norm = grad_norm + dot_nt(low, fin_ref[:, columns])
        inner = coming
    grad = grad_norm * gain_ref[...]
    normed = normed_ref[...].astype(F32)
    grad_one = inv_ref[...] * (grad - row_mean(grad) - normed * row_mean(grad * normed))
    grad_low_one = grad_one.astype(BF16)
    grad_one_ref[...] = grad_low_one
    up = dot_nt(wo_ref[...], grad_low_one).astype(BF16)
    up_ref[...] = up
    product = up.astype(F32) * mix_ref[...].astype(F32)
    for head in range(product.shape[0] // HEAD_DIM):
        rows = slice(head * HEAD_DIM, (head + 1) * HEAD_DIM)
        group, place = head // GROUP, head % GROUP
        del_ref[group, place : place + 1, :] = jnp.sum(product[rows], axis=0, keepdims=True)
    del_ref[:, GROUP:, :] = jnp.zeros_like(del_ref[:, GROUP:, :])


def rear(grad_low, norm_grad, slope, normed, inv, mix, w_output, attn_gain, ffn_in, ffn_out):
    tokens, width = grad_low.shape
    hidden = ffn_in.shape[1]
    groups = width // LANES
    tile = 256
    row_block = pl.BlockSpec((tile, width), lambda i: (i, 0))
    column_block = pl.BlockSpec((width, tile), lambda i: (0, i))
    return pl.pallas_call(
        rear_kernel,
        grid=(tokens // tile,),
        in_specs=[
            row_block, row_block, pl.BlockSpec((tile, hidden), lambda i: (i, 0)), row_block,
            pl.BlockSpec((tile, 1), lambda i: (i, 0)), column_block, whole((1, width)),
        ] + [CORE_SPEC] * 3,
        out_specs=[
            row_block, column_block, pl.BlockSpec((groups, 2 * GROUP, tile), lambda i: (0, 0, i)),
        ],
        out_shape=[
            shape_of((tokens, width), BF16),
            shape_of((width, tokens), BF16),
            shape_of((groups, 2 * GROUP, tokens), F32),
        ],
        compiler_params=params(22 * MIB),
        cost_estimate=cost(tokens * width * (width + 2 * hidden), 50 * MIB),
    )(*all_far((grad_low, norm_grad, slope, normed, inv, mix)), attn_gain[None], bring(w_output), bring(ffn_in), bring(ffn_out))


def input_grad_kernel(last, place_ref, grad_ref, dq_ref, dk_ref, dv_ref, wq_ref, wk_ref, wv_ref, *refs):
    total = grad_ref[...].astype(F32) + dot_nt(dq_ref[...], wq_ref[...])
    total = total + dot_nt(dk_ref[...], wk_ref[...])
    total = total + dot_nt(dv_ref[...], wv_ref[...])
    total = total.astype(BF16)
    if not last:
        refs[0][...] = total
        return
    arrived_ref, half_ref, far_ref, both_ref, up_ref, down_ref = refs
    merge_kernel(place_ref, total, arrived_ref, both_ref)
    first = place_ref[1] == 0
    half, other = half_ref[...].astype(F32), far_ref[...].astype(F32)
    up_ref[...] = jnp.where(first, half, other)
    down_ref[...] = jnp.where(first, other, half).T


def input_grad(place, half, grad_one, dq, dk, dv, weights, last):
    rows, width = dk.shape
    step = rows // 2
    block = pl.BlockSpec((step, width), lambda i: (i, 0))
    out_specs, out_shape = block, shape_of((rows, width), BF16)
    if last:
        out_specs = [
            pl.BlockSpec((step, 2, width), lambda i: (i, 0, 0)),
            block,
            pl.BlockSpec((width, step), lambda i: (0, i)),
        ]
        out_shape = [
            shape_of((rows, 2, width), BF16),
            shape_of((rows, width), F32),
            shape_of((width, rows), F32),
        ]
    return pl.pallas_call(
        functools.partial(input_grad_kernel, bool(last)),
        grid=(2,),
        in_specs=[SMEM_SPEC, pl.BlockSpec((step, width), lambda i: (2 * half + i, 0))]
        + [block] * 3
        + [CORE_SPEC if last else kept((width, width))] * 3
        + [block] * len(last),
        out_specs=out_specs,
        out_shape=out_shape,
        compiler_params=params(26 * MIB),
        cost_estimate=cost(3 * rows * width * width, 14 * MIB),
    )(place, *all_far((grad_one, dq, dk, dv)), *[(bring if last else far)(item) for item in weights], *last)


def swap(value, seq_bit, dp_bits):
    width = lax.axis_size("dp")
    count = lax.axis_size("seq") * width
    pairs = [
        (device, ((device // width) ^ seq_bit) * width + ((device % width) ^ dp_bits))
        for device in range(count)
    ]
    return lax.ppermute(value, ("seq", "dp"), pairs)


def gather_line(value):
    width = lax.axis_size("dp")
    groups = [[4 * line + place for line in range(width // 4)] for place in range(4)]
    return lax.all_gather(value, "dp", axis_index_groups=groups)


def total(values):
    return jnp.sum(values.astype(F32), axis=0)


def square_place():
    return 2 * ((lax.axis_index("dp") // 2) % 2) + lax.axis_index("seq")


def square_swaps(values):
    return [swap(values[offset - 1], offset % 2, 2 * (offset // 2)) for offset in range(1, 4)]


def sum_square(value):
    place = square_place()
    quarters = value.reshape(4, value.shape[0] // 4, value.shape[1])
    pick = [
        lax.dynamic_index_in_dim(quarters, place ^ offset, 0, keepdims=False) for offset in range(4)
    ]
    return pick[:1] + square_swaps(pick[1:])


def add(terms):
    value = terms[0].astype(F32)
    for term in terms[1:]:
        value = value + term.astype(F32)
    return value.astype(BF16)


def tie(*values):
    return lax.optimization_barrier(values)


def on_pair(
    hidden_in,
    lengths,
    w_query,
    w_key,
    w_value,
    w_output,
    attn_gain,
    ffn_in,
    ffn_out,
    ffn_gain,
    adapter_down,
    adapter_down_bias,
    adapter_up,
    adapter_up_bias,
    prefix_embed,
    prefix_hidden_w,
    prefix_hidden_b,
    prefix_out_w,
    prefix_out_b,
    out_grad,
):
    rows, _, width = hidden_in.shape
    count = prefix_embed.shape[0]
    position = lax.axis_index("seq")
    core = lax.axis_index("dp") % 2
    place = jnp.stack([position, core]).astype(jnp.int32)

    x_own, x_send = split(place, hidden_in)
    x_other = shifted(x_send, "seq", 1)

    embed = jnp.pad(prefix_embed, ((0, PAD - count), (0, 0)))
    prefix_act, prefix_keys, prefix_values = prefix_forward(
        embed, prefix_hidden_w, prefix_hidden_b, prefix_out_w, prefix_out_b
    )
    x_own, prefix_keys = tie(x_own, prefix_keys)
    lead = (prefix_keys, prefix_values)
    *triple, og_own, og_send = project(0, x_own, w_query, w_key, w_value, (), place, out_grad)
    og_other = shifted(og_send, "seq", 1)
    begun = attend(count, place, lengths, 0, 1, *triple, lead, ())
    q, k, v = project(1, x_other, w_query, w_key, w_value, triple)
    weights, mix_parts, tops_sums, lead_weights = attend(
        count, place, lengths, 1, 3, q, k, v, lead, begun
    )

    (
        out_own, out_send, shares, mix, slope, grad_low, norm_grad, normed, inv_one,
        adapt_kept, adapt_sent, bias_grads,
    ) = front(
        place, lengths, x_own, x_other, mix_parts, tops_sums, og_own, og_other,
        w_output, attn_gain, ffn_in, ffn_out, ffn_gain, adapter_down, adapter_down_bias,
        adapter_up, adapter_up_bias,
    )
    out_other = shifted(out_send, "seq", 1)
    core_terms = [adapt_kept, swap(adapt_sent, 0, 1)]
    grad_one, upstream, deltas = rear(
        grad_low, norm_grad, slope, normed, inv_one, mix, w_output, attn_gain, ffn_in, ffn_out
    )
    upstream, out_other, adapt_sum = tie(upstream, out_other, add(core_terms))
    square_terms = sum_square(adapt_sum)
    pair, dqt = lead_backward(
        count, q, upstream, shares, deltas, lead_weights, prefix_keys, prefix_values, bias_grads
    )
    pair_core = swap(pair, 0, 1)

    back = (q, k, v)
    part_own, dk_other, dv_other = attend_back(
        1, 0, False, False, *back, upstream, shares, deltas, weights, dqt, ()
    )
    dk_other, pair, adapt_sum = tie(dk_other, add([pair, pair_core]), add(square_terms))
    adapt_line = gather_line(adapt_sum)
    pair_square = square_swaps([pair] * 3)
    part_other, dk_other, dv_other = attend_back(
        1, 1, False, True, *back, upstream, shares, deltas, weights, dqt, (dk_other, dv_other)
    )
    pair_sum = pair.astype(F32) + sum(item.astype(F32) for item in pair_square)
    part_other, pair_sum = tie(part_other, pair_sum)
    pair_line = gather_line(pair_sum)
    dq_other, dk_own, dv_own = attend_back(
        0, 1, True, False, *back, upstream, shares, deltas, weights, part_other, ()
    )
    adapt_sum = jnp.sum(adapt_line.astype(F32), axis=0).astype(BF16)
    dq_other, adapt_sum = tie(dq_other, adapt_sum)
    adapt_x, adapt_y = swap(adapt_sum, 1, 0), swap(adapt_sum, 0, 2)
    triple_weights = (w_query, w_key, w_value)
    grad_other = input_grad(place, 1, grad_one, dq_other, dk_other, dv_other, triple_weights, ())
    grad_other, dk_own, adapt_x = tie(grad_other, dk_own, adapt_x)
    grad_back = shifted(grad_other, "seq", 1)
    adapt_xy = swap(adapt_x, 0, 2)
    dq_own, dk_own, dv_own = attend_back(
        0, 0, True, True, *back, upstream, shares, deltas, weights, part_own, (dk_own, dv_own)
    )
    dq_own, pair_line, out_other, adapt_y, adapt_xy = tie(
        dq_own, pair_line, out_other, adapt_y, adapt_xy
    )
    adapt_half = jnp.stack([adapt_sum, adapt_x, adapt_y, adapt_xy])
    place_here = square_place()
    adapt_half = jnp.concatenate(
        [lax.dynamic_slice_in_dim(adapt_half, spot ^ place_here, 1, 0) for spot in range(4)]
    ).reshape(adapt_kept.shape)
    adapt_far = swap(adapt_half, 0, 1)
    layer_out, *prefix_grads = prefix_backward(
        count,
        adapter_down_bias.shape[0],
        pair_line,
        prefix_act,
        embed,
        prefix_hidden_w,
        prefix_out_w,
        place,
        out_own,
        out_other,
    )
    layer_out, grad_back, dq_own = tie(layer_out, grad_back, dq_own)
    out_w_grad = prefix_grads[3]
    input_total, up_total, down_total = input_grad(
        place, 0, grad_one, dq_own, dk_own, dv_own, triple_weights, (grad_back, adapt_half, adapt_far)
    )
    return (
        layer_out,
        input_total,
        down_total,
        prefix_grads[6][0],
        up_total,
        prefix_grads[5][0],
        prefix_grads[0],
        prefix_grads[1],
        prefix_grads[2][0],
        out_w_grad,
        prefix_grads[4][0],
    )


def solution(mesh):
    in_specs = (
        P("seq", "dp", None),
        P("dp"),
        P(),
        P(),
        P(),
        P(),
        P(),
        P(),
        P(),
        P(),
        P(),
        P(),
        P(),
        P(),
        P(),
        P(),
        P(),
        P(),
        P(),
        P("seq", "dp", None),
    )
    out_specs = (
        P("seq", "dp", None),
        P("seq", "dp", None),
        P(),
        P(),
        P(),
        P(),
        P(),
        P(),
        P(),
        P(),
        P(),
    )
    pairs = mesh.shape["seq"] == 2 and mesh.shape["dp"] % 8 == 0

    def on_one(*arrays):
        step = on_pair if pairs and arrays[0].shape[1] == 2 else on_device
        return step(*arrays)

    return jax.shard_map(
        on_one, mesh=mesh, in_specs=in_specs, out_specs=out_specs, check_vma=False
    )
```

```python
import functools
import math

import jax
import jax.numpy as jnp
from jax import lax
from jax.experimental import pallas as pl
from jax.experimental.pallas import tpu as pltpu
from jax.sharding import PartitionSpec as P

HEADS = 16


HIGHEST_PRECISION = lax.Precision.HIGHEST


def shifted(value, axis, steps):
    count = lax.axis_size(axis)
    pairs = [(source, (source + steps) % count) for source in range(count)]
    return lax.ppermute(value, axis, pairs)


def mixed(left, right):
    return jnp.dot(left, right, preferred_element_type=jnp.float32)


def mixed_left(left, right):
    return lax.dot_general(
        left, right, (((0,), (0,)), ((), ())), preferred_element_type=jnp.float32
    )


def mixed_right(left, right):
    return lax.dot_general(
        left, right, (((1,), (1,)), ((), ())), preferred_element_type=jnp.float32
    )


def precise(left, right):
    return jnp.dot(left, right, precision=HIGHEST_PRECISION, preferred_element_type=jnp.float32)


def precise_left(left, right):
    return lax.dot_general(
        left,
        right,
        (((0,), (0,)), ((), ())),
        precision=HIGHEST_PRECISION,
        preferred_element_type=jnp.float32,
    )


def precise_right(left, right):
    return lax.dot_general(
        left,
        right,
        (((1,), (1,)), ((), ())),
        precision=HIGHEST_PRECISION,
        preferred_element_type=jnp.float32,
    )


def gelu_value(inputs):
    return 0.5 * inputs * (1.0 + lax.erf(inputs * 0.7071067811865476))


def gelu_slope(inputs):
    return (
        0.5 * (1.0 + lax.erf(inputs * 0.7071067811865476))
        + inputs * jnp.exp(-0.5 * inputs * inputs) * 0.3989422804014327
    )


def normalize(values):
    row_mean = jnp.mean(values, axis=-1, keepdims=True)
    centred = values - row_mean
    spread = jnp.mean(centred * centred, axis=-1, keepdims=True)
    inv_std = lax.rsqrt(spread + 1e-05)
    return (centred * inv_std, inv_std)


def norm_back(upstream, normed, inv_std):
    mean_grad = jnp.mean(upstream, axis=-1, keepdims=True)
    mean_proj = jnp.mean(upstream * normed, axis=-1, keepdims=True)
    return inv_std * (upstream - mean_grad - normed * mean_proj)


def key_allowed(offset, key_count, seq_lengths):
    places = offset + lax.iota(jnp.int32, key_count)
    return places[None, :] < seq_lengths[:, None]


def lead_state(queries4, prefix_keys4, prefix_values4):
    inv_root = 1.0 / math.sqrt(queries4.shape[3])
    scores = (
        jnp.einsum("rshd,phd->rshp", queries4, prefix_keys4, preferred_element_type=jnp.float32)
        * inv_root
    )
    running_max = jnp.max(scores, axis=3)
    weights = jnp.exp(scores - running_max[..., None])
    running_sum = jnp.sum(weights, axis=3)
    running_mix = jnp.einsum(
        "rshp,phd->rshd",
        weights.astype(jnp.bfloat16),
        prefix_values4,
        preferred_element_type=jnp.float32,
    )
    return (running_max, running_sum, running_mix)


def fold_block(carried, key_block, value_block, offset, queries4, seq_lengths):
    key_count, seqs_here = (key_block.shape[0], key_block.shape[1])
    head_count, head_dim = (queries4.shape[2], queries4.shape[3])
    inv_root = 1.0 / math.sqrt(head_dim)
    keys4 = key_block.reshape(key_count, seqs_here, head_count, head_dim)
    values4 = value_block.reshape(key_count, seqs_here, head_count, head_dim)
    running_max, running_sum, running_mix = carried
    scores = (
        jnp.einsum("rshd,tshd->rsht", queries4, keys4, preferred_element_type=jnp.float32)
        * inv_root
    )
    allowed = key_allowed(offset, key_count, seq_lengths)[None, :, None, :]
    scores = jnp.where(allowed, scores, -jnp.inf)
    new_max = jnp.maximum(running_max, jnp.max(scores, axis=3))
    weights = jnp.exp(scores - new_max[..., None])
    rescale = jnp.exp(running_max - new_max)
    running_sum = running_sum * rescale + jnp.sum(weights, axis=3)
    running_mix = running_mix * rescale[..., None] + jnp.einsum(
        "rsht,tshd->rshd", weights.astype(jnp.bfloat16), values4, preferred_element_type=jnp.float32
    )
    return (new_max, running_sum, running_mix)


def lead_back(queries4, upstream4, log_total, row_delta, prefix_keys4, prefix_values4):
    inv_root = 1.0 / math.sqrt(queries4.shape[3])
    scores = (
        jnp.einsum("rshd,phd->rshp", queries4, prefix_keys4, preferred_element_type=jnp.float32)
        * inv_root
    )
    weights = jnp.exp(scores - log_total[..., None])
    weight_grads = jnp.einsum(
        "rshd,phd->rshp", upstream4, prefix_values4, preferred_element_type=jnp.float32
    )
    score_grads = (weights * (weight_grads - row_delta[..., None])).astype(jnp.bfloat16)
    query_term = (
        jnp.einsum("rshp,phd->rshd", score_grads, prefix_keys4, preferred_element_type=jnp.float32)
        * inv_root
    )
    key_term = (
        jnp.einsum("rshp,rshd->phd", score_grads, queries4, preferred_element_type=jnp.float32)
        * inv_root
    )
    value_term = jnp.einsum(
        "rshp,rshd->phd",
        weights.astype(jnp.bfloat16),
        upstream4,
        preferred_element_type=jnp.float32,
    )
    return (query_term, key_term, value_term)


def block_back(
    queries4, upstream4, log_total, row_delta, key_block, value_block, offset, seq_lengths
):
    key_count, seqs_here, model_width = key_block.shape
    head_count, head_dim = (queries4.shape[2], queries4.shape[3])
    inv_root = 1.0 / math.sqrt(head_dim)
    keys4 = key_block.reshape(key_count, seqs_here, head_count, head_dim)
    values4 = value_block.reshape(key_count, seqs_here, head_count, head_dim)
    scores = (
        jnp.einsum("rshd,tshd->rsht", queries4, keys4, preferred_element_type=jnp.float32)
        * inv_root
    )
    allowed = key_allowed(offset, key_count, seq_lengths)[None, :, None, :]
    scores = jnp.where(allowed, scores, -jnp.inf)
    weights = jnp.exp(scores - log_total[..., None])
    weight_grads = jnp.einsum(
        "rshd,tshd->rsht", upstream4, values4, preferred_element_type=jnp.float32
    )
    score_grads = (weights * (weight_grads - row_delta[..., None])).astype(jnp.bfloat16)
    query_term = (
        jnp.einsum("rsht,tshd->rshd", score_grads, keys4, preferred_element_type=jnp.float32)
        * inv_root
    )
    key_term = (
        jnp.einsum("rsht,rshd->tshd", score_grads, queries4, preferred_element_type=jnp.float32)
        * inv_root
    )
    value_term = jnp.einsum(
        "rsht,rshd->tshd",
        weights.astype(jnp.bfloat16),
        upstream4,
        preferred_element_type=jnp.float32,
    )
    pair_term = jnp.stack(
        [
            key_term.reshape(key_count, seqs_here, model_width),
            value_term.reshape(key_count, seqs_here, model_width),
        ]
    )
    return (query_term, pair_term)


def prefix_back(pair_grad, prefix_act, prefix_embed, hidden_weight, out_weight):
    out_w_grad = precise_left(prefix_act, pair_grad)
    out_b_grad = jnp.sum(pair_grad, axis=0)
    act_grad = precise_right(pair_grad, out_weight) * (1.0 - prefix_act * prefix_act)
    hidden_w_grad = precise_left(prefix_embed, act_grad)
    hidden_b_grad = jnp.sum(act_grad, axis=0)
    embed_grad = precise_right(act_grad, hidden_weight)
    return (embed_grad, hidden_w_grad, hidden_b_grad, out_w_grad, out_b_grad)


def on_device(
    hidden_in,
    lengths,
    w_query,
    w_key,
    w_value,
    w_output,
    attn_gain,
    ffn_in,
    ffn_out,
    ffn_gain,
    adapter_down,
    adapter_down_bias,
    adapter_up,
    adapter_up_bias,
    prefix_embed,
    prefix_hidden_w,
    prefix_hidden_b,
    prefix_out_w,
    prefix_out_b,
    out_grad,
):
    rows_here, seqs_here, model_width = hidden_in.shape
    token_count = rows_here * seqs_here
    head_count = HEADS
    head_dim = model_width // head_count
    axis_count = lax.axis_size("seq")
    position = lax.axis_index("seq")
    tokens = hidden_in.reshape(token_count, model_width)
    projected = jnp.stack([mixed(tokens, w_query), mixed(tokens, w_key), mixed(tokens, w_value)])
    triple = projected.astype(jnp.bfloat16).reshape(3, rows_here, seqs_here, model_width)
    hidden_weight = prefix_hidden_w.astype(jnp.float32)
    out_weight = prefix_out_w.astype(jnp.float32)
    prefix_act = jnp.tanh(precise(prefix_embed, hidden_weight) + prefix_hidden_b)
    prefix_pair = precise(prefix_act, out_weight) + prefix_out_b
    prefix_keys4 = (
        prefix_pair[:, :model_width].astype(jnp.bfloat16).reshape(-1, head_count, head_dim)
    )
    prefix_values4 = (
        prefix_pair[:, model_width:].astype(jnp.bfloat16).reshape(-1, head_count, head_dim)
    )
    row_places = position * rows_here + lax.iota(jnp.int32, rows_here)
    valid = (row_places[:, None] < lengths[None, :]).astype(jnp.float32).reshape(token_count, 1)
    queries4 = triple[0].reshape(rows_here, seqs_here, head_count, head_dim)
    key_value = triple[1:]
    pieces = lax.all_gather(key_value, "seq", axis=1, tiled=True)
    carried = fold_block(
        lead_state(queries4, prefix_keys4, prefix_values4),
        pieces[0],
        pieces[1],
        jnp.int32(0),
        queries4,
        lengths,
    )
    mix_full = carried[2] / carried[1][..., None]
    log_total = carried[0] + jnp.log(carried[1])
    mix_low = mix_full.astype(jnp.bfloat16).reshape(token_count, model_width)
    attn_proj = mixed(mix_low, w_output)
    normed_one, inv_one = normalize(tokens.astype(jnp.float32) + attn_proj)
    norm_one = normed_one * attn_gain
    norm_low = norm_one.astype(jnp.bfloat16)
    inner_pre = mixed(norm_low, ffn_in)
    inner_act = gelu_value(inner_pre).astype(jnp.bfloat16)
    squeeze = mixed(norm_low, adapter_down) + adapter_down_bias
    squeeze_act = gelu_value(squeeze).astype(jnp.bfloat16)
    ffn_sum = mixed(inner_act, ffn_out)
    adapter_sum = mixed(squeeze_act, adapter_up) + adapter_up_bias
    normed_two, inv_two = normalize(norm_one + ffn_sum + 4.0 * adapter_sum)
    layer_out = (
        (normed_two * ffn_gain * valid)
        .astype(jnp.bfloat16)
        .reshape(rows_here, seqs_here, model_width)
    )
    upstream_top = out_grad.reshape(token_count, model_width).astype(jnp.float32) * valid
    grad_two = norm_back(upstream_top * ffn_gain, normed_two, inv_two)
    grad_ffn_low = grad_two.astype(jnp.bfloat16)
    grad_adapt_low = (4.0 * grad_two).astype(jnp.bfloat16)
    up_grad = mixed_left(squeeze_act, grad_adapt_low)
    up_bias_grad = jnp.sum(grad_adapt_low.astype(jnp.float32), axis=0)
    grad_squeeze_low = (mixed_right(grad_adapt_low, adapter_up) * gelu_slope(squeeze)).astype(
        jnp.bfloat16
    )
    down_grad = mixed_left(norm_low, grad_squeeze_low)
    down_bias_grad = jnp.sum(grad_squeeze_low.astype(jnp.float32), axis=0)
    grad_inner_low = (mixed_right(grad_ffn_low, ffn_out) * gelu_slope(inner_pre)).astype(
        jnp.bfloat16
    )
    grad_norm = (
        grad_two + mixed_right(grad_squeeze_low, adapter_down) + mixed_right(grad_inner_low, ffn_in)
    )
    grad_one = norm_back(grad_norm * attn_gain, normed_one, inv_one)
    grad_attn_low = grad_one.astype(jnp.bfloat16)
    grad_mix_low = mixed_right(grad_attn_low, w_output).astype(jnp.bfloat16)
    upstream4 = grad_mix_low.reshape(rows_here, seqs_here, head_count, head_dim)
    row_delta = jnp.sum(upstream4.astype(jnp.float32) * mix_full, axis=3)
    query_grad, prefix_key_grad, prefix_value_grad = lead_back(
        queries4, upstream4, log_total, row_delta, prefix_keys4, prefix_values4
    )

    def visit(step_index, carried):
        moving, grads_moving, query_total = carried
        source = (position - step_index) % axis_count
        query_term, pair_term = block_back(
            queries4,
            upstream4,
            log_total,
            row_delta,
            moving[0],
            moving[1],
            source * rows_here,
            lengths,
        )
        return (moving, grads_moving + pair_term, query_total + query_term)

    def travel(step_index, carried):
        moving, grads_moving, query_total = visit(step_index, carried)
        moving = shifted(moving, "seq", 1)
        grads_moving = shifted(grads_moving.astype(jnp.bfloat16), "seq", 1).astype(
            grads_moving.dtype
        )
        return (moving, grads_moving, query_total)

    initial = (
        key_value,
        jnp.zeros((2, rows_here, seqs_here, model_width), jnp.float32),
        query_grad,
    )
    carried = lax.fori_loop(0, axis_count - 1, travel, initial)
    carried = visit(axis_count - 1, carried)
    pair_grads = shifted(carried[1].astype(jnp.bfloat16), "seq", 1).astype(jnp.float32)
    triple_grad = jnp.concatenate(
        [carried[2].reshape(1, rows_here, seqs_here, model_width), pair_grads]
    ).astype(jnp.bfloat16)
    hidden_grad = grad_one + mixed_right(triple_grad[0].reshape(token_count, model_width), w_query)
    hidden_grad = hidden_grad + mixed_right(triple_grad[1].reshape(token_count, model_width), w_key)
    hidden_grad = hidden_grad + mixed_right(
        triple_grad[2].reshape(token_count, model_width), w_value
    )
    hidden_grad = hidden_grad.astype(jnp.bfloat16).reshape(rows_here, seqs_here, model_width)
    pair_grad = jnp.concatenate(
        [prefix_key_grad.reshape(-1, model_width), prefix_value_grad.reshape(-1, model_width)],
        axis=1,
    )
    prefix_grads = prefix_back(pair_grad, prefix_act, prefix_embed, hidden_weight, out_weight)
    summed = lax.psum(
        (
            down_grad,
            down_bias_grad,
            up_grad,
            up_bias_grad,
            prefix_grads[0],
            prefix_grads[1],
            prefix_grads[2],
            prefix_grads[3],
            prefix_grads[4],
        ),
        ("seq", "dp"),
    )
    adapter_totals = summed[:4]
    prefix_totals = summed[4:]
    return (
        layer_out,
        hidden_grad,
        adapter_totals[0],
        adapter_totals[1],
        adapter_totals[2],
        adapter_totals[3],
        prefix_totals[0],
        prefix_totals[1],
        prefix_totals[2],
        prefix_totals[3],
        prefix_totals[4],
    )


BF16 = jnp.bfloat16
F32 = jnp.float32
MIB = 1024 * 1024
GROUP = 4
HEAD_DIM = 64
LANES = GROUP * HEAD_DIM
PAD = 32
MASKED = -1e30
LOG2E = 1.4426950408889634
VMEM_LIMIT = 60 * MIB


def dot_nn(left, right):
    return lax.dot_general(left, right, (((1,), (0,)), ((), ())), preferred_element_type=F32)


def dot_nt(left, right):
    return lax.dot_general(left, right, (((1,), (1,)), ((), ())), preferred_element_type=F32)


def dot_tn(left, right):
    return lax.dot_general(left, right, (((0,), (0,)), ((), ())), preferred_element_type=F32)


def shape_of(shape, dtype):
    return pltpu.HBM(shape, dtype)


def far(value):
    return pltpu.with_memory_space_constraint(value, pltpu.HBM)


def bring(value):
    return pltpu.with_memory_space_constraint(value, pltpu.VMEM)


def all_far(values):
    return [far(value) for value in values]


def params(limit=VMEM_LIMIT):
    return pltpu.CompilerParams(vmem_limit_bytes=limit)


def cost(macs, moved):
    return pl.CostEstimate(flops=int(2 * macs), bytes_accessed=int(moved), transcendentals=0)


SMEM_SPEC = pl.BlockSpec(memory_space=pltpu.SMEM)
ANY_SPEC = pl.BlockSpec(memory_space=pl.ANY)
CORE_SPEC = pl.BlockSpec(memory_space=pltpu.VMEM)


def whole(shape):
    return pl.BlockSpec(shape, lambda *_: (0,) * len(shape))


def kept(shape):
    return pl.BlockSpec(shape, lambda *_: (0,) * len(shape), pipeline_mode=pl.Buffered(1))


def split_kernel(place_ref, both_ref, own_ref, other_ref):
    apart = jnp.swapaxes(both_ref[...], 0, 1)
    first = place_ref[0] == 0
    own_ref[...] = jnp.where(first, apart[0], apart[1])
    other_ref[...] = jnp.where(first, apart[1], apart[0])


def split(place, both):
    rows, _, width = both.shape
    step = rows // 2
    half = pl.BlockSpec((step, width), lambda i: (i, 0))
    return pl.pallas_call(
        split_kernel,
        grid=(2,),
        in_specs=[SMEM_SPEC, pl.BlockSpec((step, 2, width), lambda i: (i, 0, 0))],
        out_specs=[half, half],
        out_shape=[shape_of((rows, width), both.dtype)] * 2,
        compiler_params=params(16 * MIB),
        cost_estimate=cost(0, 4 * rows * width * 2),
    )(place, far(both))


def merge_kernel(place_ref, own_ref, other_ref, both_ref):
    first = place_ref[0] == 0
    own, other = own_ref[...], other_ref[...]
    apart = jnp.stack([jnp.where(first, own, other), jnp.where(first, other, own)])
    both_ref[...] = jnp.swapaxes(apart, 0, 1)


def place_of(half, place_ref, rows):
    return jnp.where(half == 0, place_ref[0], 1 - place_ref[0]) * rows


def length_of(place_ref, lengths_ref):
    return jnp.where(place_ref[0] == 0, lengths_ref[0], lengths_ref[1])


def parts_of(values, count):
    parts = []
    for _ in range(count):
        part = values.astype(BF16)
        parts.append(part)
        values = values - part.astype(F32)
    return parts


def exact_dot(values, weight, dot):
    rows = values.shape[0]
    product = dot(jnp.concatenate(parts_of(values, 3), axis=0), weight)
    return product[:rows] + product[rows : 2 * rows] + product[2 * rows :]


def prefix_kernel(embed_ref, hw_ref, hb_ref, ow_ref, ob_ref, act_ref, key_ref, value_ref):
    width = key_ref.shape[1]
    act = jnp.tanh(exact_dot(embed_ref[...], hw_ref[...], dot_nn) + hb_ref[...])
    act_ref[...] = act
    pair = exact_dot(act, ow_ref[...], dot_nn) + ob_ref[...]
    key_ref[...] = pair[:, :width].astype(BF16)
    value_ref[...] = pair[:, width:].astype(BF16)


def prefix_forward(embed, hidden_w, hidden_b, out_w, out_b):
    width, hidden = hidden_w.shape
    return pl.pallas_call(
        prefix_kernel,
        out_shape=[
            shape_of((PAD, hidden), F32),
            shape_of((PAD, width), BF16),
            shape_of((PAD, width), BF16),
        ],
        compiler_params=params(16 * MIB),
        cost_estimate=cost(3 * PAD * hidden * 3 * width * 4, 6 * hidden * width),
    )(embed, far(hidden_w), hidden_b[None], far(out_w), out_b[None])


def prefix_back_kernel(
    count, pairs_ref, act_ref, embed_ref, hw_ref, ow_ref, place_ref, own_ref, other_ref,
    both_ref, eg_ref, hwg_ref, hbg_ref, owg_ref, obg_ref, ubg_ref, dbg_ref,
):
    merge_kernel(place_ref, own_ref[...], other_ref, both_ref)
    total = pairs_ref[0]
    for line in range(1, pairs_ref.shape[0]):
        total = total + pairs_ref[line]
    ubg_ref[...] = total[count : count + 1]
    dbg_ref[...] = total[count + 1 : count + 2, : dbg_ref.shape[1]]
    pair = jnp.concatenate([total[:PAD], total[PAD:]], axis=1)
    rows = lax.broadcasted_iota(jnp.int32, pair.shape, 0)
    pair = jnp.where(rows < count, pair, 0.0)
    act = act_ref[...]
    obg_ref[...] = jnp.sum(pair, axis=0, keepdims=True)
    high, low = parts_of(pair, 2)
    back = dot_nt(jnp.concatenate([high, low], axis=0), ow_ref[...])
    act_grad = (back[:PAD] + back[PAD:]) * (1.0 - act * act)
    act_high, act_low = parts_of(act, 2)
    owg_ref[...] = dot_tn(
        jnp.concatenate([act_high, act_low, act_high], axis=0),
        jnp.concatenate([high, high, low], axis=0),
    )
    hbg_ref[...] = jnp.sum(act_grad, axis=0, keepdims=True)
    high, low = parts_of(act_grad, 2)
    embed_high, embed_low = parts_of(embed_ref[...], 2)
    hwg_ref[...] = dot_tn(
        jnp.concatenate([embed_high, embed_low, embed_high], axis=0),
        jnp.concatenate([high, high, low], axis=0),
    )
    back = dot_nt(jnp.concatenate([high, low], axis=0), hw_ref[...])
    eg_ref[...] = (back[:PAD] + back[PAD:])[:count]


def prefix_backward(count, adapt, pairs, act, embed, hidden_w, out_w, place, own, other):
    width, hidden = hidden_w.shape
    core = [CORE_SPEC] * 5
    return pl.pallas_call(
        functools.partial(prefix_back_kernel, count),
        in_specs=core + [SMEM_SPEC, CORE_SPEC, CORE_SPEC],
        out_shape=[
            shape_of((own.shape[0], 2, width), BF16),
            shape_of((count, width), F32),
            shape_of((width, hidden), F32),
            shape_of((1, hidden), F32),
            shape_of((hidden, 2 * width), F32),
            shape_of((1, 2 * width), F32),
            shape_of((1, width), F32),
            shape_of((1, adapt), F32),
        ],
        compiler_params=params(24 * MIB),
        cost_estimate=cost(96 * hidden * width * 6, 20 * hidden * width),
    )(far(pairs), act, embed, far(hidden_w), far(out_w), place, far(own), far(other))


def project_kernel(apart, x_ref, wq_ref, wk_ref, wv_ref, *refs):
    x = x_ref[...]
    if apart:
        place_ref, both_ref, q_ref, k_ref, v_ref, own_ref, other_ref = refs
        split_kernel(place_ref, both_ref, own_ref, other_ref)
    else:
        q_ref, k_ref, v_ref = refs[-3:]
    scale = LOG2E / math.sqrt(HEAD_DIM)
    q_ref[...] = (dot_nn(x, wq_ref[...]) * scale).astype(BF16)
    k_ref[...] = dot_nn(x, wk_ref[...]).astype(BF16)
    v_ref[...] = dot_nn(x, wv_ref[...]).astype(BF16)


def project(half, x, w_query, w_key, w_value, earlier, place=None, both=None):
    rows, width = x.shape
    step = rows // 2
    apart = both is not None
    block = pl.BlockSpec((step, width), lambda i: (i, 0))
    out_specs = [pl.BlockSpec((step, width), lambda i: (2 * half + i, 0))] * 3
    out_shape = [shape_of((2 * rows, width), BF16)] * 3
    more_specs, more = [ANY_SPEC] * len(earlier), all_far(earlier)
    if apart:
        more_specs = [SMEM_SPEC, pl.BlockSpec((step, 2, width), lambda i: (i, 0, 0))]
        more = [place, far(both)]
        out_specs = out_specs + [block] * 2
        out_shape = out_shape + [shape_of((rows, width), BF16)] * 2
    return pl.pallas_call(
        functools.partial(project_kernel, apart),
        grid=(2,),
        in_specs=[block] + [CORE_SPEC] * 3 + more_specs,
        out_specs=out_specs,
        out_shape=out_shape,
        input_output_aliases={4 + i: i for i in range(len(earlier))},
        compiler_params=params(20 * MIB),
        cost_estimate=cost(3 * rows * width * width, 2 * (4 * rows * width + 3 * width * width)),
    )(far(x) if apart else x, bring(w_query), bring(w_key), bring(w_value), *more)


def head_lanes(head, rows, lanes):
    place = lax.broadcasted_iota(jnp.int32, (rows, lanes), 1)
    return (place // HEAD_DIM == head).astype(F32).astype(BF16)


def first_lane(values):
    lane = lax.broadcasted_iota(jnp.int32, (values.shape[0], 128), 1)
    return jnp.where(lane == 0, values, 0.0).astype(BF16)


def block_diagonal(rows):
    return jnp.concatenate(
        [rows * head_lanes(head, rows.shape[0], LANES) for head in range(GROUP)], axis=0
    )


def attend_kernel(
    prefixed, first, place_ref, lengths_ref, q_ref, k_ref, v_ref, pk_ref, pv_ref, *refs
):
    pt_ref, ot_ref, st_ref, pp_ref, *scores = refs[-6:]
    keys = k_ref.shape[0]
    queries = q_ref.shape[0]
    half = (pl.program_id(0) + first) // 2

    def quadrant(count):
        place = place_of(half, place_ref, keys) + lax.broadcasted_iota(jnp.int32, (keys, 128), 0)
        bias = first_lane(jnp.where(place < length_of(place_ref, lengths_ref), 0.0, MASKED))
        ones = first_lane(jnp.ones((queries, 128), F32))
        tail = jnp.ones((16, keys), BF16)
        masks = [head_lanes(head, queries, 128) for head in range(2)]

        def score(head):
            pair = slice((head // 2) * 128, (head // 2 + 1) * 128)
            k_aug = jnp.concatenate([k_ref[:, pair], bias], axis=1)
            q_aug = jnp.concatenate([q_ref[:, pair] * masks[head % 2], ones], axis=1)
            scores[head % 2][...] = dot_nt(k_aug, q_aug)

        def weigh(head):
            own = scores[head % 2]
            top = jnp.max(own[...], axis=0, keepdims=True)
            if count:
                lead_scores = lead[head * PAD : (head + 1) * PAD]
                top = jnp.maximum(top, jnp.max(lead_scores, axis=0, keepdims=True))
            pt_ref[head] = jnp.exp2(own[...] - top).astype(BF16)
            st_ref[0, head : head + 1, :] = top
            if not count:
                return 0.0
            lead_weights = jnp.exp2(lead_scores - top).astype(BF16)
            pp_ref[0, head * PAD : (head + 1) * PAD, :] = lead_weights
            return jnp.sum(lead_weights.astype(F32), axis=0, keepdims=True)

        def mix(head, lead_total):
            rows = slice(head * HEAD_DIM, (head + 1) * HEAD_DIM)
            mixed_rows = dot_nn(jnp.concatenate([turned[rows], tail], axis=0), pt_ref[head])
            mixed = mixed_rows[:HEAD_DIM]
            if count:
                lead_weights = pp_ref[0, head * PAD : (head + 1) * PAD, :]
                mixed = mixed + dot_nn(lead_turned[rows], lead_weights)
            ot_ref[rows, :] = mixed.astype(BF16)
            total_row = mixed_rows[HEAD_DIM : HEAD_DIM + 1] + lead_total
            st_ref[0, GROUP + head : GROUP + head + 1, :] = total_row

        score(0)
        turned = v_ref[...].T
        if count:
            lead_turned = pv_ref[...].T
            lead = dot_nt(block_diagonal(pk_ref[...]), q_ref[...])
            row = lax.broadcasted_iota(jnp.int32, lead.shape, 0)
            lead = jnp.where(row % PAD < count, lead, MASKED)
        lead_totals = []
        for head in range(GROUP):
            if head + 1 < GROUP:
                score(head + 1)
            lead_totals.append(weigh(head))
            if head:
                mix(head - 1, lead_totals[head - 1])
        mix(GROUP - 1, lead_totals[GROUP - 1])

    @pl.when(half == 0)
    def _():
        quadrant(prefixed)

    @pl.when(half == 1)
    def _():
        quadrant(0)


def attend(count, place, lengths, first, quadrants, q, k, v, lead, earlier):
    tokens, width = q.shape
    rows = tokens // 2
    groups = width // LANES
    last = groups - 1

    def lead_place(i, g):
        quadrant = i + first
        return (jnp.where(quadrant < 2, g, last), 0, jnp.minimum(quadrant, 1))

    keys = pl.BlockSpec((rows, LANES), lambda i, g: ((i + first) // 2, g))
    in_specs = [
        SMEM_SPEC,
        SMEM_SPEC,
        pl.BlockSpec((rows, LANES), lambda i, g: ((i + first) % 2, g)),
        keys,
        keys,
    ]
    in_specs += [pl.BlockSpec((PAD, LANES), lambda i, g: (0, g))] * 2
    out_specs = [
        pl.BlockSpec(
            (None, GROUP, rows, rows), lambda i, g: ((i + first) // 2, g, 0, (i + first) % 2)
        ),
        pl.BlockSpec((None, LANES, rows), lambda i, g: ((i + first) // 2, g, (i + first) % 2)),
        pl.BlockSpec(
            (None, 1, 2 * GROUP, rows), lambda i, g: ((i + first) // 2, g, 0, (i + first) % 2)
        ),
        pl.BlockSpec((1, GROUP * PAD, rows), lead_place),
    ]
    out_shape = [
        shape_of((2, groups * GROUP, rows, tokens), BF16),
        shape_of((2, width, tokens), BF16),
        shape_of((2, groups, 2 * GROUP, tokens), F32),
        shape_of((groups, GROUP * PAD, tokens), BF16),
    ]
    macs = quadrants * groups * GROUP * rows * rows * 256 * 2
    return pl.pallas_call(
        functools.partial(attend_kernel, count, first),
        grid=(quadrants, groups),
        in_specs=in_specs + [ANY_SPEC] * len(earlier),
        out_specs=out_specs,
        out_shape=out_shape,
        input_output_aliases={7 + i: i for i in range(len(earlier))},
        scratch_shapes=[pltpu.VMEM((rows, rows), F32)] * 2,
        compiler_params=params(16 * MIB),
        cost_estimate=cost(macs, quadrants * 14 * MIB),
    )(place, lengths, *all_far((q, k, v, *lead, *earlier)))


def lead_back_kernel(
    count, q_ref, up_ref, rst_ref, del_ref, pp_ref, pk_ref, pv_ref, bias_ref, pair_ref, dqt_ref
):
    queries = q_ref.shape[0]
    for part in range(rst_ref.shape[0]):
        lanes = slice(part * LANES, (part + 1) * LANES)
        ups = []
        deltas = []
        for head in range(GROUP):
            rows = slice(part * LANES + head * HEAD_DIM, part * LANES + (head + 1) * HEAD_DIM)
            share = rst_ref[part, head : head + 1, :]
            ups.append((up_ref[rows, :].astype(F32) * share).astype(BF16))
            delta = del_ref[part, head : head + 1, :] * share
            deltas.append(jnp.broadcast_to(delta, (PAD, queries)))
        up = jnp.concatenate(ups, axis=0)
        delta = jnp.concatenate(deltas, axis=0)
        weights = pp_ref[part]
        weight_grads = dot_nn(block_diagonal(pv_ref[:, lanes]), up)
        score_grads = (weights.astype(F32) * (weight_grads - delta)).astype(BF16)
        dqt_ref[lanes, :] = dot_tn(block_diagonal(pk_ref[:, lanes]), score_grads).astype(BF16)
        key_grads = dot_nn(score_grads, q_ref[:, lanes]) * (1.0 / LOG2E)
        value_grads = dot_nt(weights, up)
        lane = lax.broadcasted_iota(jnp.int32, (PAD, LANES), 1) // HEAD_DIM
        key_total = jnp.zeros((PAD, LANES), F32)
        value_total = jnp.zeros((PAD, LANES), F32)
        for head in range(GROUP):
            rows = slice(head * PAD, (head + 1) * PAD)
            key_total = jnp.where(lane == head, key_grads[rows], key_total)
            value_total = jnp.where(lane == head, value_grads[rows], value_total)
        row = lax.broadcasted_iota(jnp.int32, (PAD, LANES), 0)
        key_total = jnp.where(row == count, bias_ref[0:1, lanes], key_total)
        key_total = jnp.where(row == count + 1, bias_ref[1:2, lanes], key_total)
        pair_ref[:PAD, lanes] = key_total.astype(BF16)
        pair_ref[PAD:, lanes] = value_total.astype(BF16)


def lead_backward(count, q, up, shares, deltas, lead_weights, prefix_keys, prefix_values, biases):
    tokens, width = q.shape
    groups = width // LANES
    each = 2 if groups % 2 == 0 else 1
    span = each * LANES
    small = pl.BlockSpec((PAD, span), lambda g: (0, g))
    stats = pl.BlockSpec((each, 2 * GROUP, tokens), lambda g: (g, 0, 0))
    return pl.pallas_call(
        functools.partial(lead_back_kernel, count),
        grid=(groups // each,),
        in_specs=[
            pl.BlockSpec((tokens, span), lambda g: (0, g)),
            pl.BlockSpec((span, tokens), lambda g: (g, 0)),
            stats,
            stats,
            pl.BlockSpec((each, GROUP * PAD, tokens), lambda g: (g, 0, 0)),
            small,
            small,
            pl.BlockSpec((8, span), lambda g: (0, g)),
        ],
        out_specs=[
            pl.BlockSpec((2 * PAD, span), lambda g: (0, g)),
            pl.BlockSpec((span, tokens), lambda g: (g, 0)),
        ],
        out_shape=[
            jax.ShapeDtypeStruct((2 * PAD, width), BF16),
            shape_of((width, tokens), BF16),
        ],
        compiler_params=params(18 * MIB),
        cost_estimate=cost(groups * 4 * GROUP * PAD * tokens * LANES, 10 * MIB),
    )(*all_far((q, up, shares, deltas, lead_weights)), prefix_keys, prefix_values, biases)


def attend_back_kernel(
    half,
    last_keys,
    last_queries,
    has_earlier,
    q_ref,
    k_ref,
    v_ref,
    up_ref,
    rst_ref,
    del_ref,
    pt_ref,
    dqt_in_ref,
    *refs,
):
    dq_ref, dk_ref, dv_ref = refs[-5:-2]
    weight_grads = refs[-2:]
    queries = q_ref.shape[0]
    lane = lax.broadcasted_iota(jnp.int32, (queries, 128), 1) // HEAD_DIM
    masks = [(lane == head).astype(F32).astype(BF16) for head in range(2)]
    zeros = jnp.zeros((HEAD_DIM, queries), BF16)
    turned = k_ref[...].T
    ups = {}
    grads = {}
    query_grads = []
    key_grads = []
    value_grads = []

    def pair_of(head):
        return slice((head // 2) * 128, (head // 2 + 1) * 128)

    def rows_of(head):
        return slice(head * HEAD_DIM, (head + 1) * HEAD_DIM)

    def share_of(head):
        return rst_ref[0, half * GROUP + head : half * GROUP + head + 1, :]

    def weight_grad(head):
        up = (up_ref[rows_of(head), :].astype(F32) * share_of(head)).astype(BF16)
        ups[head] = jnp.concatenate([up, zeros] if head % 2 == 0 else [zeros, up], axis=0)
        weight_grads[head % 2][...] = dot_nn(v_ref[:, pair_of(head)], ups[head])

    def score_grad(head):
        delta = del_ref[0, head : head + 1, :] * share_of(head)
        return (pt_ref[head].astype(F32) * (weight_grads[head % 2][...] - delta)).astype(BF16)

    def value_term(head):
        return dot_nt(pt_ref[head], ups[head])

    def key_term(head):
        return dot_nn(grads[head], q_ref[:, pair_of(head)] * masks[head % 2])

    def query_term(head):
        return dqt_in_ref[rows_of(head), :].astype(F32) + dot_nn(turned[rows_of(head)], grads[head])

    weight_grad(0)
    for head in range(GROUP):
        if head + 1 < GROUP:
            weight_grad(head + 1)
        grads[head] = score_grad(head)
        value = value_term(head)
        query_grads.append(query_term(head))
        key = key_term(head)
        if head % 2:
            key_grads[-1] = key_grads[-1] + key
            value_grads[-1] = value_grads[-1] + value
        else:
            key_grads.append(key)
            value_grads.append(value)
    query_grad = jnp.concatenate(query_grads, axis=0)
    key_grad = jnp.concatenate(key_grads, axis=1)
    value_grad = jnp.concatenate(value_grads, axis=1)
    if not last_keys:
        dq_ref[...] = query_grad.astype(BF16)
    else:
        dq_ref[...] = (query_grad * (1.0 / math.sqrt(HEAD_DIM))).astype(BF16).T
    if has_earlier:
        key_grad = key_grad + refs[0][...].astype(F32)
        value_grad = value_grad + refs[1][...].astype(F32)
    if last_queries:
        key_grad = key_grad * (1.0 / LOG2E)
    dk_ref[...] = key_grad.astype(BF16)
    dv_ref[...] = value_grad.astype(BF16)


def attend_back(
    key_half, query_half, last_keys, last_queries, q, k, v, up, shares, deltas, weights, dqt, earlier
):
    tokens, width = q.shape
    rows = tokens // 2
    groups = width // LANES
    query_columns = pl.BlockSpec((LANES, rows), lambda g: (g, query_half))
    stats = pl.BlockSpec((1, 2 * GROUP, rows), lambda g: (g, 0, query_half))
    finished = pl.BlockSpec((rows, LANES), lambda g: (0, g))
    out_columns = pl.BlockSpec((LANES, rows), lambda g: (g, 0))
    sofar = query_columns if dqt.shape[1] == tokens else out_columns
    macs = groups * GROUP * rows * rows * 256 * 4
    return pl.pallas_call(
        functools.partial(
            attend_back_kernel, key_half, last_keys, last_queries, len(earlier) > 0
        ),
        grid=(groups,),
        in_specs=[
            pl.BlockSpec((rows, LANES), lambda g: (query_half, g)),
            pl.BlockSpec((rows, LANES), lambda g: (key_half, g)),
            pl.BlockSpec((rows, LANES), lambda g: (key_half, g)),
            query_columns,
            stats,
            stats,
            pl.BlockSpec((None, GROUP, rows, rows), lambda g: (key_half, g, 0, query_half)),
            sofar,
        ]
        + [finished] * len(earlier),
        out_specs=[finished if last_keys else out_columns, finished, finished],
        out_shape=[
            shape_of((rows, width) if last_keys else (width, rows), BF16),
            shape_of((rows, width), BF16),
            shape_of((rows, width), BF16),
        ],
        scratch_shapes=[pltpu.VMEM((rows, rows), F32)] * 2,
        compiler_params=params(18 * MIB),
        cost_estimate=cost(macs, 12 * MIB),
    )(*all_far((q, k, v, up, shares, deltas, weights, dqt, *earlier)))


def gelu_pair(values):
    scaled = values * 0.7071067811865476
    below = 0.5 * lax.erf(scaled) + 0.5
    decay = jnp.exp2(scaled * scaled * (-LOG2E))
    return values * below, below + values * 0.3989422804014327 * decay


def row_mean(values):
    return jnp.mean(values, axis=-1, keepdims=True)


def front_kernel(
    tiles,
    place_ref,
    lengths_ref,
    x_own_ref,
    x_other_ref,
    ot_own_ref,
    ot_other_ref,
    st_own_ref,
    st_other_ref,
    og_own_ref,
    og_other_ref,
    gain_one_ref,
    gain_two_ref,
    down_bias_ref,
    up_bias_ref,
    wo_ref,
    fin_ref,
    fout_ref,
    down_ref,
    up_ref,
    out_own_ref,
    out_other_ref,
    rst_ref,
    mix_ref,
    slope_ref,
    grad_low_ref,
    norm_grad_ref,
    normed_ref,
    inv_ref,
    kept_ref,
    sent_ref,
    bias_grad_ref,
    act_ref,
    squeeze_ref,
    low_ref,
):
    step = pl.program_id(0)
    tile = x_own_ref.shape[0]
    width = x_own_ref.shape[1]
    hidden = fin_ref.shape[1]
    chunk = 512
    chunks = [slice(first, first + chunk) for first in range(0, hidden, chunk)]
    own = step < tiles // 2
    x = jnp.where(own, x_own_ref[...], x_other_ref[...]).astype(F32)
    top_own, top_other = st_own_ref[:, :GROUP, :], st_other_ref[:, :GROUP, :]
    top = jnp.maximum(top_own, top_other)
    share_own, share_other = jnp.exp2(top_own - top), jnp.exp2(top_other - top)
    inverse = 1.0 / (
        st_own_ref[:, GROUP:, :] * share_own + st_other_ref[:, GROUP:, :] * share_other
    )
    rst_ref[:, :GROUP, :] = share_own * inverse
    rst_ref[:, GROUP:, :] = share_other * inverse
    mixes = []
    for head in range(width // HEAD_DIM):
        rows = slice(head * HEAD_DIM, (head + 1) * HEAD_DIM)
        group, place = head // GROUP, head % GROUP
        mixes.append(
            (
                ot_own_ref[rows, :].astype(F32) * rst_ref[group, place : place + 1, :]
                + ot_other_ref[rows, :].astype(F32) * rst_ref[group, GROUP + place : GROUP + place + 1, :]
            ).astype(BF16)
        )
    mix = jnp.concatenate(mixes, axis=0)
    mix_ref[...] = mix
    resid_one = x + dot_tn(mix, wo_ref[...])
    centred = resid_one - row_mean(resid_one)
    inv_one = lax.rsqrt(row_mean(centred * centred) + 1e-05)
    normed = centred * inv_one
    normed_ref[...] = normed.astype(BF16)
    inv_ref[...] = inv_one
    norm_one = normed * gain_one_ref[...]
    norm_low = norm_one.astype(BF16)

    squeeze = dot_nn(norm_low, down_ref[...]) + down_bias_ref[...]
    inner = dot_nn(norm_low, fin_ref[:, chunks[0]])
    squeeze_act, squeeze_slope = gelu_pair(squeeze)
    squeeze_act = squeeze_act.astype(BF16)
    resid_two = norm_one + 4.0 * (dot_nn(squeeze_act, up_ref[...]) + up_bias_ref[...])
    for place, columns in enumerate(chunks):
        more = place + 1 < len(chunks)
        coming = dot_nn(norm_low, fin_ref[:, chunks[place + 1]]) if more else None
        act, slope = gelu_pair(inner)
        slope_ref[:, columns] = slope.astype(BF16)
        resid_two = resid_two + dot_nn(act.astype(BF16), fout_ref[columns, :])
        inner = coming

    centred = resid_two - row_mean(resid_two)
    inv_two = lax.rsqrt(row_mean(centred * centred) + 1e-05)
    normed_two = centred * inv_two
    base = place_of(step // (tiles // 2), place_ref, (tiles // 2) * tile) + step % (tiles // 2) * tile
    place = base + lax.broadcasted_iota(jnp.int32, (tile, 1), 0)
    valid = (place < length_of(place_ref, lengths_ref)).astype(F32)
    gain_two = gain_two_ref[...]
    out = (normed_two * gain_two * valid).astype(BF16)
    upstream = jnp.where(own, og_own_ref[...], og_other_ref[...]).astype(F32) * valid * gain_two
    grad_two = inv_two * (
        upstream - row_mean(upstream) - normed_two * row_mean(upstream * normed_two)
    )
    grad_low = grad_two.astype(BF16)
    grad_adapt = 4.0 * grad_low
    grad_squeeze = (dot_nt(grad_adapt, up_ref[...]) * squeeze_slope).astype(BF16)
    norm_grad_ref[...] = (grad_two + dot_nt(grad_squeeze, down_ref[...])).astype(BF16)
    here = pl.ds(pl.multiple_of(step * tile, tile), tile)
    grad_low_ref[here, :] = grad_low
    act_ref[here, :] = squeeze_act
    squeeze_ref[here, :] = grad_squeeze
    low_ref[here, :] = norm_low
    up_bias_grad = jnp.sum(grad_adapt.astype(F32), axis=0, keepdims=True)
    down_bias_grad = jnp.sum(grad_squeeze.astype(F32), axis=0, keepdims=True)
    adapt = down_bias_grad.shape[1]

    @pl.when(own)
    def _():
        out_own_ref[...] = out

    @pl.when(jnp.logical_not(own))
    def _():
        out_other_ref[...] = out

    @pl.when(step == 0)
    def _():
        bias_grad_ref[...] = jnp.zeros_like(bias_grad_ref)
        bias_grad_ref[0:1, :] = up_bias_grad
        bias_grad_ref[1:2, :adapt] = down_bias_grad

    @pl.when(step > 0)
    def _():
        bias_grad_ref[0:1, :] += up_bias_grad
        bias_grad_ref[1:2, :adapt] += down_bias_grad

    @pl.when(step == tiles - 1)
    def _():
        first = place_ref[1] == 0
        up_total = (4.0 * dot_tn(act_ref[...], grad_low_ref[...])).astype(BF16)
        down_total = dot_tn(squeeze_ref[...], low_ref[...]).astype(BF16)
        kept_ref[...] = jnp.where(first, up_total, down_total)
        sent_ref[...] = jnp.where(first, down_total, up_total)


def front(
    place, lengths, x_own, x_other, mix_parts, tops_sums, og_own, og_other, w_output, attn_gain,
    ffn_in, ffn_out, ffn_gain, down, down_bias, up, up_bias,
):
    rows, width = x_own.shape
    tokens = 2 * rows
    hidden = ffn_in.shape[1]
    adapt = down.shape[1]
    groups = width // LANES
    tile = 256
    tiles = tokens // tile
    near = pl.BlockSpec((tile, width), lambda i: (jnp.minimum(i, tiles // 2 - 1), 0))
    far = pl.BlockSpec((tile, width), lambda i: (jnp.maximum(i - tiles // 2, 0), 0))
    row_block = pl.BlockSpec((tile, width), lambda i: (i, 0))
    column_block = pl.BlockSpec((width, tile), lambda i: (0, i))
    stats = pl.BlockSpec((groups, 2 * GROUP, tile), lambda i: (0, 0, i))
    mixes = [pl.BlockSpec((None, width, tile), lambda i, half=half: (half, 0, i)) for half in range(2)]
    tops = [
        pl.BlockSpec((None, groups, 2 * GROUP, tile), lambda i, half=half: (half, 0, 0, i))
        for half in range(2)
    ]
    return pl.pallas_call(
        functools.partial(front_kernel, tiles),
        grid=(tiles,),
        in_specs=[
            SMEM_SPEC, SMEM_SPEC, near, far, *mixes, *tops, near, far,
            whole((1, width)), whole((1, width)), whole((1, adapt)), whole((1, width)),
        ] + [CORE_SPEC] * 5,
        out_specs=[
            near, far, stats, column_block, pl.BlockSpec((tile, hidden), lambda i: (i, 0)),
            kept((tokens, width)), row_block, row_block, pl.BlockSpec((tile, 1), lambda i: (i, 0)),
            kept((adapt, width)), kept((adapt, width)), whole((8, width)),
        ],
        out_shape=[
            shape_of((rows, width), BF16),
            shape_of((rows, width), BF16),
            shape_of((groups, 2 * GROUP, tokens), F32),
            shape_of((width, tokens), BF16),
            shape_of((tokens, hidden), BF16),
            shape_of((tokens, width), BF16),
            shape_of((tokens, width), BF16),
            shape_of((tokens, width), BF16),
            shape_of((tokens, 1), F32),
            shape_of((adapt, width), BF16),
            shape_of((adapt, width), BF16),
            shape_of((8, width), F32),
        ],
        scratch_shapes=[
            pltpu.VMEM((tokens, adapt), BF16),
            pltpu.VMEM((tokens, adapt), BF16),
            pltpu.VMEM((tokens, width), BF16),
        ],
        compiler_params=params(32 * MIB),
        cost_estimate=cost(tokens * width * (width + 2 * hidden + 6 * adapt), 60 * MIB),
    )(
        place,
        lengths,
        *all_far((x_own, x_other, mix_parts, mix_parts, tops_sums, tops_sums, og_own, og_other)),
        attn_gain[None], ffn_gain[None], down_bias[None], up_bias[None],
        *[bring(item) for item in (w_output, ffn_in, ffn_out, down, up)],
    )


def rear_kernel(
    grad_low_ref, norm_grad_ref, slope_ref, normed_ref, inv_ref, mix_ref, gain_ref, wo_ref, fin_ref,
    fout_ref, grad_one_ref, up_ref, del_ref,
):
    hidden = fin_ref.shape[1]
    chunk = 1024
    chunks = [slice(first, first + chunk) for first in range(0, hidden, chunk)]
    grad_low = grad_low_ref[...]
    grad_norm = norm_grad_ref[...].astype(F32)
    inner = dot_nt(grad_low, fout_ref[chunks[0], :])
    for place, columns in enumerate(chunks):
        more = place + 1 < len(chunks)
        coming = dot_nt(grad_low, fout_ref[chunks[place + 1], :]) if more else None
        low = (inner * slope_ref[:, columns].astype(F32)).astype(BF16)
        grad_norm = grad_norm + dot_nt(low, fin_ref[:, columns])
        inner = coming
    grad = grad_norm * gain_ref[...]
    normed = normed_ref[...].astype(F32)
    grad_one = inv_ref[...] * (grad - row_mean(grad) - normed * row_mean(grad * normed))
    grad_low_one = grad_one.astype(BF16)
    grad_one_ref[...] = grad_low_one
    up = dot_nt(wo_ref[...], grad_low_one).astype(BF16)
    up_ref[...] = up
    product = up.astype(F32) * mix_ref[...].astype(F32)
    for head in range(product.shape[0] // HEAD_DIM):
        rows = slice(head * HEAD_DIM, (head + 1) * HEAD_DIM)
        group, place = head // GROUP, head % GROUP
        del_ref[group, place : place + 1, :] = jnp.sum(product[rows], axis=0, keepdims=True)
    del_ref[:, GROUP:, :] = jnp.zeros_like(del_ref[:, GROUP:, :])


def rear(grad_low, norm_grad, slope, normed, inv, mix, w_output, attn_gain, ffn_in, ffn_out):
    tokens, width = grad_low.shape
    hidden = ffn_in.shape[1]
    groups = width // LANES
    tile = 256
    row_block = pl.BlockSpec((tile, width), lambda i: (i, 0))
    column_block = pl.BlockSpec((width, tile), lambda i: (0, i))
    return pl.pallas_call(
        rear_kernel,
        grid=(tokens // tile,),
        in_specs=[
            row_block, row_block, pl.BlockSpec((tile, hidden), lambda i: (i, 0)), row_block,
            pl.BlockSpec((tile, 1), lambda i: (i, 0)), column_block, whole((1, width)),
        ] + [CORE_SPEC] * 3,
        out_specs=[
            row_block, column_block, pl.BlockSpec((groups, 2 * GROUP, tile), lambda i: (0, 0, i)),
        ],
        out_shape=[
            shape_of((tokens, width), BF16),
            shape_of((width, tokens), BF16),
            shape_of((groups, 2 * GROUP, tokens), F32),
        ],
        compiler_params=params(22 * MIB),
        cost_estimate=cost(tokens * width * (width + 2 * hidden), 50 * MIB),
    )(*all_far((grad_low, norm_grad, slope, normed, inv, mix)), attn_gain[None], bring(w_output), bring(ffn_in), bring(ffn_out))


def input_grad_kernel(last, place_ref, grad_ref, dq_ref, dk_ref, dv_ref, wq_ref, wk_ref, wv_ref, *refs):
    total = grad_ref[...].astype(F32) + dot_nt(dq_ref[...], wq_ref[...])
    total = total + dot_nt(dk_ref[...], wk_ref[...])
    total = total + dot_nt(dv_ref[...], wv_ref[...])
    total = total.astype(BF16)
    if not last:
        refs[0][...] = total
        return
    arrived_ref, half_ref, far_ref, both_ref, up_ref, down_ref = refs
    merge_kernel(place_ref, total, arrived_ref, both_ref)
    first = place_ref[1] == 0
    half, other = half_ref[...].astype(F32), far_ref[...].astype(F32)
    up_ref[...] = jnp.where(first, half, other)
    down_ref[...] = jnp.where(first, other, half).T


def input_grad(place, half, grad_one, dq, dk, dv, weights, last):
    rows, width = dk.shape
    step = rows // 2
    block = pl.BlockSpec((step, width), lambda i: (i, 0))
    columns = width // 2
    out_specs = pl.BlockSpec((rows, columns), lambda j: (0, j))
    out_shape = shape_of((rows, width), BF16)
    grad_spec = pl.BlockSpec((rows, columns), lambda j: (half, j))
    operand_spec = kept((rows, width))
    weight_spec = pl.BlockSpec((columns, width), lambda j: (j, 0))
    if last:
        grad_spec = pl.BlockSpec((step, width), lambda i: (2 * half + i, 0))
        operand_spec, weight_spec = block, CORE_SPEC
        out_specs = [
            pl.BlockSpec((step, 2, width), lambda i: (i, 0, 0)),
            block,
            pl.BlockSpec((width, step), lambda i: (0, i)),
        ]
        out_shape = [
            shape_of((rows, 2, width), BF16),
            shape_of((rows, width), F32),
            shape_of((width, rows), F32),
        ]
    return pl.pallas_call(
        functools.partial(input_grad_kernel, bool(last)),
        grid=(2,),
        in_specs=[SMEM_SPEC, grad_spec]
        + [operand_spec] * 3
        + [weight_spec] * 3
        + [block] * len(last),
        out_specs=out_specs,
        out_shape=out_shape,
        compiler_params=params(26 * MIB),
        cost_estimate=cost(3 * rows * width * width, 14 * MIB),
    )(place, *all_far((grad_one, dq, dk, dv)), *[(bring if last else far)(item) for item in weights], *last)


def swap(value, seq_bit, dp_bits):
    width = lax.axis_size("dp")
    count = lax.axis_size("seq") * width
    pairs = [
        (device, ((device // width) ^ seq_bit) * width + ((device % width) ^ dp_bits))
        for device in range(count)
    ]
    return lax.ppermute(value, ("seq", "dp"), pairs)


def gather_line(value):
    width = lax.axis_size("dp")
    groups = [[4 * line + place for line in range(width // 4)] for place in range(4)]
    return lax.all_gather(value, "dp", axis_index_groups=groups)


def total(values):
    return jnp.sum(values.astype(F32), axis=0)


def square_place():
    return 2 * ((lax.axis_index("dp") // 2) % 2) + lax.axis_index("seq")


def square_swaps(values):
    return [swap(values[offset - 1], offset % 2, 2 * (offset // 2)) for offset in range(1, 4)]


def sum_square(value):
    place = square_place()
    quarters = value.reshape(4, value.shape[0] // 4, value.shape[1])
    pick = [
        lax.dynamic_index_in_dim(quarters, place ^ offset, 0, keepdims=False) for offset in range(4)
    ]
    return pick[:1] + square_swaps(pick[1:])


def add(terms):
    value = terms[0].astype(F32)
    for term in terms[1:]:
        value = value + term.astype(F32)
    return value.astype(BF16)


def tie(*values):
    return lax.optimization_barrier(values)


def on_pair(
    hidden_in,
    lengths,
    w_query,
    w_key,
    w_value,
    w_output,
    attn_gain,
    ffn_in,
    ffn_out,
    ffn_gain,
    adapter_down,
    adapter_down_bias,
    adapter_up,
    adapter_up_bias,
    prefix_embed,
    prefix_hidden_w,
    prefix_hidden_b,
    prefix_out_w,
    prefix_out_b,
    out_grad,
):
    rows, _, width = hidden_in.shape
    count = prefix_embed.shape[0]
    position = lax.axis_index("seq")
    core = lax.axis_index("dp") % 2
    place = jnp.stack([position, core]).astype(jnp.int32)

    x_own, x_send = split(place, hidden_in)
    x_other = shifted(x_send, "seq", 1)

    embed = jnp.pad(prefix_embed, ((0, PAD - count), (0, 0)))
    prefix_act, prefix_keys, prefix_values = prefix_forward(
        embed, prefix_hidden_w, prefix_hidden_b, prefix_out_w, prefix_out_b
    )
    x_own, prefix_keys = tie(x_own, prefix_keys)
    lead = (prefix_keys, prefix_values)
    *triple, og_own, og_send = project(0, x_own, w_query, w_key, w_value, (), place, out_grad)
    og_other = shifted(og_send, "seq", 1)
    begun = attend(count, place, lengths, 0, 1, *triple, lead, ())
    q, k, v = project(1, x_other, w_query, w_key, w_value, triple)
    weights, mix_parts, tops_sums, lead_weights = attend(
        count, place, lengths, 1, 3, q, k, v, lead, begun
    )

    (
        out_own, out_send, shares, mix, slope, grad_low, norm_grad, normed, inv_one,
        adapt_kept, adapt_sent, bias_grads,
    ) = front(
        place, lengths, x_own, x_other, mix_parts, tops_sums, og_own, og_other,
        w_output, attn_gain, ffn_in, ffn_out, ffn_gain, adapter_down, adapter_down_bias,
        adapter_up, adapter_up_bias,
    )
    out_other = shifted(out_send, "seq", 1)
    core_terms = [adapt_kept, swap(adapt_sent, 0, 1)]
    grad_one, upstream, deltas = rear(
        grad_low, norm_grad, slope, normed, inv_one, mix, w_output, attn_gain, ffn_in, ffn_out
    )
    upstream, out_other, adapt_sum = tie(upstream, out_other, add(core_terms))
    square_terms = sum_square(adapt_sum)
    pair, dqt = lead_backward(
        count, q, upstream, shares, deltas, lead_weights, prefix_keys, prefix_values, bias_grads
    )
    pair_core = swap(pair, 0, 1)

    back = (q, k, v)
    part_own, dk_other, dv_other = attend_back(
        1, 0, False, False, *back, upstream, shares, deltas, weights, dqt, ()
    )
    dk_other, pair, adapt_sum = tie(dk_other, add([pair, pair_core]), add(square_terms))
    adapt_line = gather_line(adapt_sum)
    pair_square = square_swaps([pair] * 3)
    part_other, dk_other, dv_other = attend_back(
        1, 1, False, True, *back, upstream, shares, deltas, weights, dqt, (dk_other, dv_other)
    )
    pair_sum = pair.astype(F32) + sum(item.astype(F32) for item in pair_square)
    part_other, pair_sum = tie(part_other, pair_sum)
    pair_line = gather_line(pair_sum)
    dq_other, dk_own, dv_own = attend_back(
        0, 1, True, False, *back, upstream, shares, deltas, weights, part_other, ()
    )
    adapt_sum = jnp.sum(adapt_line.astype(F32), axis=0).astype(BF16)
    dq_other, adapt_sum = tie(dq_other, adapt_sum)
    adapt_x, adapt_y = swap(adapt_sum, 1, 0), swap(adapt_sum, 0, 2)
    triple_weights = (w_query, w_key, w_value)
    grad_other = input_grad(place, 1, grad_one, dq_other, dk_other, dv_other, triple_weights, ())
    grad_other, dk_own, adapt_x = tie(grad_other, dk_own, adapt_x)
    grad_back = shifted(grad_other, "seq", 1)
    adapt_xy = swap(adapt_x, 0, 2)
    dq_own, dk_own, dv_own = attend_back(
        0, 0, True, True, *back, upstream, shares, deltas, weights, part_own, (dk_own, dv_own)
    )
    dq_own, pair_line, out_other, adapt_y, adapt_xy = tie(
        dq_own, pair_line, out_other, adapt_y, adapt_xy
    )
    adapt_half = jnp.stack([adapt_sum, adapt_x, adapt_y, adapt_xy])
    place_here = square_place()
    adapt_half = jnp.concatenate(
        [lax.dynamic_slice_in_dim(adapt_half, spot ^ place_here, 1, 0) for spot in range(4)]
    ).reshape(adapt_kept.shape)
    adapt_far = swap(adapt_half, 0, 1)
    layer_out, *prefix_grads = prefix_backward(
        count,
        adapter_down_bias.shape[0],
        pair_line,
        prefix_act,
        embed,
        prefix_hidden_w,
        prefix_out_w,
        place,
        out_own,
        out_other,
    )
    layer_out, grad_back, dq_own = tie(layer_out, grad_back, dq_own)
    out_w_grad = prefix_grads[3]
    input_total, up_total, down_total = input_grad(
        place, 0, grad_one, dq_own, dk_own, dv_own, triple_weights, (grad_back, adapt_half, adapt_far)
    )
    return (
        layer_out,
        input_total,
        down_total,
        prefix_grads[6][0],
        up_total,
        prefix_grads[5][0],
        prefix_grads[0],
        prefix_grads[1],
        prefix_grads[2][0],
        out_w_grad,
        prefix_grads[4][0],
    )


def solution(mesh):
    in_specs = (
        P("seq", "dp", None),
        P("dp"),
        P(),
        P(),
        P(),
        P(),
        P(),
        P(),
        P(),
        P(),
        P(),
        P(),
        P(),
        P(),
        P(),
        P(),
        P(),
        P(),
        P(),
        P("seq", "dp", None),
    )
    out_specs = (
        P("seq", "dp", None),
        P("seq", "dp", None),
        P(),
        P(),
        P(),
        P(),
        P(),
        P(),
        P(),
        P(),
        P(),
    )
    pairs = mesh.shape["seq"] == 2 and mesh.shape["dp"] % 8 == 0

    def on_one(*arrays):
        step = on_pair if pairs and arrays[0].shape[1] == 2 else on_device
        return step(*arrays)

    return jax.shard_map(
        on_one, mesh=mesh, in_specs=in_specs, out_specs=out_specs, check_vma=False
    )
```

```python
import functools
import math

import jax
import jax.numpy as jnp
from jax import lax
from jax.experimental import pallas as pl
from jax.experimental.pallas import tpu as pltpu
from jax.sharding import PartitionSpec as P

HEADS = 16


HIGHEST_PRECISION = lax.Precision.HIGHEST


def shifted(value, axis, steps):
    count = lax.axis_size(axis)
    pairs = [(source, (source + steps) % count) for source in range(count)]
    return lax.ppermute(value, axis, pairs)


def mixed(left, right):
    return jnp.dot(left, right, preferred_element_type=jnp.float32)


def mixed_left(left, right):
    return lax.dot_general(
        left, right, (((0,), (0,)), ((), ())), preferred_element_type=jnp.float32
    )


def mixed_right(left, right):
    return lax.dot_general(
        left, right, (((1,), (1,)), ((), ())), preferred_element_type=jnp.float32
    )


def precise(left, right):
    return jnp.dot(left, right, precision=HIGHEST_PRECISION, preferred_element_type=jnp.float32)


def precise_left(left, right):
    return lax.dot_general(
        left,
        right,
        (((0,), (0,)), ((), ())),
        precision=HIGHEST_PRECISION,
        preferred_element_type=jnp.float32,
    )


def precise_right(left, right):
    return lax.dot_general(
        left,
        right,
        (((1,), (1,)), ((), ())),
        precision=HIGHEST_PRECISION,
        preferred_element_type=jnp.float32,
    )


def gelu_value(inputs):
    return 0.5 * inputs * (1.0 + lax.erf(inputs * 0.7071067811865476))


def gelu_slope(inputs):
    return (
        0.5 * (1.0 + lax.erf(inputs * 0.7071067811865476))
        + inputs * jnp.exp(-0.5 * inputs * inputs) * 0.3989422804014327
    )


def normalize(values):
    row_mean = jnp.mean(values, axis=-1, keepdims=True)
    centred = values - row_mean
    spread = jnp.mean(centred * centred, axis=-1, keepdims=True)
    inv_std = lax.rsqrt(spread + 1e-05)
    return (centred * inv_std, inv_std)


def norm_back(upstream, normed, inv_std):
    mean_grad = jnp.mean(upstream, axis=-1, keepdims=True)
    mean_proj = jnp.mean(upstream * normed, axis=-1, keepdims=True)
    return inv_std * (upstream - mean_grad - normed * mean_proj)


def key_allowed(offset, key_count, seq_lengths):
    places = offset + lax.iota(jnp.int32, key_count)
    return places[None, :] < seq_lengths[:, None]


def lead_state(queries4, prefix_keys4, prefix_values4):
    inv_root = 1.0 / math.sqrt(queries4.shape[3])
    scores = (
        jnp.einsum("rshd,phd->rshp", queries4, prefix_keys4, preferred_element_type=jnp.float32)
        * inv_root
    )
    running_max = jnp.max(scores, axis=3)
    weights = jnp.exp(scores - running_max[..., None])
    running_sum = jnp.sum(weights, axis=3)
    running_mix = jnp.einsum(
        "rshp,phd->rshd",
        weights.astype(jnp.bfloat16),
        prefix_values4,
        preferred_element_type=jnp.float32,
    )
    return (running_max, running_sum, running_mix)


def fold_block(carried, key_block, value_block, offset, queries4, seq_lengths):
    key_count, seqs_here = (key_block.shape[0], key_block.shape[1])
    head_count, head_dim = (queries4.shape[2], queries4.shape[3])
    inv_root = 1.0 / math.sqrt(head_dim)
    keys4 = key_block.reshape(key_count, seqs_here, head_count, head_dim)
    values4 = value_block.reshape(key_count, seqs_here, head_count, head_dim)
    running_max, running_sum, running_mix = carried
    scores = (
        jnp.einsum("rshd,tshd->rsht", queries4, keys4, preferred_element_type=jnp.float32)
        * inv_root
    )
    allowed = key_allowed(offset, key_count, seq_lengths)[None, :, None, :]
    scores = jnp.where(allowed, scores, -jnp.inf)
    new_max = jnp.maximum(running_max, jnp.max(scores, axis=3))
    weights = jnp.exp(scores - new_max[..., None])
    rescale = jnp.exp(running_max - new_max)
    running_sum = running_sum * rescale + jnp.sum(weights, axis=3)
    running_mix = running_mix * rescale[..., None] + jnp.einsum(
        "rsht,tshd->rshd", weights.astype(jnp.bfloat16), values4, preferred_element_type=jnp.float32
    )
    return (new_max, running_sum, running_mix)


def lead_back(queries4, upstream4, log_total, row_delta, prefix_keys4, prefix_values4):
    inv_root = 1.0 / math.sqrt(queries4.shape[3])
    scores = (
        jnp.einsum("rshd,phd->rshp", queries4, prefix_keys4, preferred_element_type=jnp.float32)
        * inv_root
    )
    weights = jnp.exp(scores - log_total[..., None])
    weight_grads = jnp.einsum(
        "rshd,phd->rshp", upstream4, prefix_values4, preferred_element_type=jnp.float32
    )
    score_grads = (weights * (weight_grads - row_delta[..., None])).astype(jnp.bfloat16)
    query_term = (
        jnp.einsum("rshp,phd->rshd", score_grads, prefix_keys4, preferred_element_type=jnp.float32)
        * inv_root
    )
    key_term = (
        jnp.einsum("rshp,rshd->phd", score_grads, queries4, preferred_element_type=jnp.float32)
        * inv_root
    )
    value_term = jnp.einsum(
        "rshp,rshd->phd",
        weights.astype(jnp.bfloat16),
        upstream4,
        preferred_element_type=jnp.float32,
    )
    return (query_term, key_term, value_term)


def block_back(
    queries4, upstream4, log_total, row_delta, key_block, value_block, offset, seq_lengths
):
    key_count, seqs_here, model_width = key_block.shape
    head_count, head_dim = (queries4.shape[2], queries4.shape[3])
    inv_root = 1.0 / math.sqrt(head_dim)
    keys4 = key_block.reshape(key_count, seqs_here, head_count, head_dim)
    values4 = value_block.reshape(key_count, seqs_here, head_count, head_dim)
    scores = (
        jnp.einsum("rshd,tshd->rsht", queries4, keys4, preferred_element_type=jnp.float32)
        * inv_root
    )
    allowed = key_allowed(offset, key_count, seq_lengths)[None, :, None, :]
    scores = jnp.where(allowed, scores, -jnp.inf)
    weights = jnp.exp(scores - log_total[..., None])
    weight_grads = jnp.einsum(
        "rshd,tshd->rsht", upstream4, values4, preferred_element_type=jnp.float32
    )
    score_grads = (weights * (weight_grads - row_delta[..., None])).astype(jnp.bfloat16)
    query_term = (
        jnp.einsum("rsht,tshd->rshd", score_grads, keys4, preferred_element_type=jnp.float32)
        * inv_root
    )
    key_term = (
        jnp.einsum("rsht,rshd->tshd", score_grads, queries4, preferred_element_type=jnp.float32)
        * inv_root
    )
    value_term = jnp.einsum(
        "rsht,rshd->tshd",
        weights.astype(jnp.bfloat16),
        upstream4,
        preferred_element_type=jnp.float32,
    )
    pair_term = jnp.stack(
        [
            key_term.reshape(key_count, seqs_here, model_width),
            value_term.reshape(key_count, seqs_here, model_width),
        ]
    )
    return (query_term, pair_term)


def prefix_back(pair_grad, prefix_act, prefix_embed, hidden_weight, out_weight):
    out_w_grad = precise_left(prefix_act, pair_grad)
    out_b_grad = jnp.sum(pair_grad, axis=0)
    act_grad = precise_right(pair_grad, out_weight) * (1.0 - prefix_act * prefix_act)
    hidden_w_grad = precise_left(prefix_embed, act_grad)
    hidden_b_grad = jnp.sum(act_grad, axis=0)
    embed_grad = precise_right(act_grad, hidden_weight)
    return (embed_grad, hidden_w_grad, hidden_b_grad, out_w_grad, out_b_grad)


def on_device(
    hidden_in,
    lengths,
    w_query,
    w_key,
    w_value,
    w_output,
    attn_gain,
    ffn_in,
    ffn_out,
    ffn_gain,
    adapter_down,
    adapter_down_bias,
    adapter_up,
    adapter_up_bias,
    prefix_embed,
    prefix_hidden_w,
    prefix_hidden_b,
    prefix_out_w,
    prefix_out_b,
    out_grad,
):
    rows_here, seqs_here, model_width = hidden_in.shape
    token_count = rows_here * seqs_here
    head_count = HEADS
    head_dim = model_width // head_count
    axis_count = lax.axis_size("seq")
    position = lax.axis_index("seq")
    tokens = hidden_in.reshape(token_count, model_width)
    projected = jnp.stack([mixed(tokens, w_query), mixed(tokens, w_key), mixed(tokens, w_value)])
    triple = projected.astype(jnp.bfloat16).reshape(3, rows_here, seqs_here, model_width)
    hidden_weight = prefix_hidden_w.astype(jnp.float32)
    out_weight = prefix_out_w.astype(jnp.float32)
    prefix_act = jnp.tanh(precise(prefix_embed, hidden_weight) + prefix_hidden_b)
    prefix_pair = precise(prefix_act, out_weight) + prefix_out_b
    prefix_keys4 = (
        prefix_pair[:, :model_width].astype(jnp.bfloat16).reshape(-1, head_count, head_dim)
    )
    prefix_values4 = (
        prefix_pair[:, model_width:].astype(jnp.bfloat16).reshape(-1, head_count, head_dim)
    )
    row_places = position * rows_here + lax.iota(jnp.int32, rows_here)
    valid = (row_places[:, None] < lengths[None, :]).astype(jnp.float32).reshape(token_count, 1)
    queries4 = triple[0].reshape(rows_here, seqs_here, head_count, head_dim)
    key_value = triple[1:]
    pieces = lax.all_gather(key_value, "seq", axis=1, tiled=True)
    carried = fold_block(
        lead_state(queries4, prefix_keys4, prefix_values4),
        pieces[0],
        pieces[1],
        jnp.int32(0),
        queries4,
        lengths,
    )
    mix_full = carried[2] / carried[1][..., None]
    log_total = carried[0] + jnp.log(carried[1])
    mix_low = mix_full.astype(jnp.bfloat16).reshape(token_count, model_width)
    attn_proj = mixed(mix_low, w_output)
    normed_one, inv_one = normalize(tokens.astype(jnp.float32) + attn_proj)
    norm_one = normed_one * attn_gain
    norm_low = norm_one.astype(jnp.bfloat16)
    inner_pre = mixed(norm_low, ffn_in)
    inner_act = gelu_value(inner_pre).astype(jnp.bfloat16)
    squeeze = mixed(norm_low, adapter_down) + adapter_down_bias
    squeeze_act = gelu_value(squeeze).astype(jnp.bfloat16)
    ffn_sum = mixed(inner_act, ffn_out)
    adapter_sum = mixed(squeeze_act, adapter_up) + adapter_up_bias
    normed_two, inv_two = normalize(norm_one + ffn_sum + 4.0 * adapter_sum)
    layer_out = (
        (normed_two * ffn_gain * valid)
        .astype(jnp.bfloat16)
        .reshape(rows_here, seqs_here, model_width)
    )
    upstream_top = out_grad.reshape(token_count, model_width).astype(jnp.float32) * valid
    grad_two = norm_back(upstream_top * ffn_gain, normed_two, inv_two)
    grad_ffn_low = grad_two.astype(jnp.bfloat16)
    grad_adapt_low = (4.0 * grad_two).astype(jnp.bfloat16)
    up_grad = mixed_left(squeeze_act, grad_adapt_low)
    up_bias_grad = jnp.sum(grad_adapt_low.astype(jnp.float32), axis=0)
    grad_squeeze_low = (mixed_right(grad_adapt_low, adapter_up) * gelu_slope(squeeze)).astype(
        jnp.bfloat16
    )
    down_grad = mixed_left(norm_low, grad_squeeze_low)
    down_bias_grad = jnp.sum(grad_squeeze_low.astype(jnp.float32), axis=0)
    grad_inner_low = (mixed_right(grad_ffn_low, ffn_out) * gelu_slope(inner_pre)).astype(
        jnp.bfloat16
    )
    grad_norm = (
        grad_two + mixed_right(grad_squeeze_low, adapter_down) + mixed_right(grad_inner_low, ffn_in)
    )
    grad_one = norm_back(grad_norm * attn_gain, normed_one, inv_one)
    grad_attn_low = grad_one.astype(jnp.bfloat16)
    grad_mix_low = mixed_right(grad_attn_low, w_output).astype(jnp.bfloat16)
    upstream4 = grad_mix_low.reshape(rows_here, seqs_here, head_count, head_dim)
    row_delta = jnp.sum(upstream4.astype(jnp.float32) * mix_full, axis=3)
    query_grad, prefix_key_grad, prefix_value_grad = lead_back(
        queries4, upstream4, log_total, row_delta, prefix_keys4, prefix_values4
    )

    def visit(step_index, carried):
        moving, grads_moving, query_total = carried
        source = (position - step_index) % axis_count
        query_term, pair_term = block_back(
            queries4,
            upstream4,
            log_total,
            row_delta,
            moving[0],
            moving[1],
            source * rows_here,
            lengths,
        )
        return (moving, grads_moving + pair_term, query_total + query_term)

    def travel(step_index, carried):
        moving, grads_moving, query_total = visit(step_index, carried)
        moving = shifted(moving, "seq", 1)
        grads_moving = shifted(grads_moving.astype(jnp.bfloat16), "seq", 1).astype(
            grads_moving.dtype
        )
        return (moving, grads_moving, query_total)

    initial = (
        key_value,
        jnp.zeros((2, rows_here, seqs_here, model_width), jnp.float32),
        query_grad,
    )
    carried = lax.fori_loop(0, axis_count - 1, travel, initial)
    carried = visit(axis_count - 1, carried)
    pair_grads = shifted(carried[1].astype(jnp.bfloat16), "seq", 1).astype(jnp.float32)
    triple_grad = jnp.concatenate(
        [carried[2].reshape(1, rows_here, seqs_here, model_width), pair_grads]
    ).astype(jnp.bfloat16)
    hidden_grad = grad_one + mixed_right(triple_grad[0].reshape(token_count, model_width), w_query)
    hidden_grad = hidden_grad + mixed_right(triple_grad[1].reshape(token_count, model_width), w_key)
    hidden_grad = hidden_grad + mixed_right(
        triple_grad[2].reshape(token_count, model_width), w_value
    )
    hidden_grad = hidden_grad.astype(jnp.bfloat16).reshape(rows_here, seqs_here, model_width)
    pair_grad = jnp.concatenate(
        [prefix_key_grad.reshape(-1, model_width), prefix_value_grad.reshape(-1, model_width)],
        axis=1,
    )
    prefix_grads = prefix_back(pair_grad, prefix_act, prefix_embed, hidden_weight, out_weight)
    summed = lax.psum(
        (
            down_grad,
            down_bias_grad,
            up_grad,
            up_bias_grad,
            prefix_grads[0],
            prefix_grads[1],
            prefix_grads[2],
            prefix_grads[3],
            prefix_grads[4],
        ),
        ("seq", "dp"),
    )
    adapter_totals = summed[:4]
    prefix_totals = summed[4:]
    return (
        layer_out,
        hidden_grad,
        adapter_totals[0],
        adapter_totals[1],
        adapter_totals[2],
        adapter_totals[3],
        prefix_totals[0],
        prefix_totals[1],
        prefix_totals[2],
        prefix_totals[3],
        prefix_totals[4],
    )


BF16 = jnp.bfloat16
F32 = jnp.float32
MIB = 1024 * 1024
GROUP = 4
HEAD_DIM = 64
LANES = GROUP * HEAD_DIM
PAD = 32
MASKED = -1e30
LOG2E = 1.4426950408889634
VMEM_LIMIT = 60 * MIB


def dot_nn(left, right):
    return lax.dot_general(left, right, (((1,), (0,)), ((), ())), preferred_element_type=F32)


def dot_nt(left, right):
    return lax.dot_general(left, right, (((1,), (1,)), ((), ())), preferred_element_type=F32)


def dot_tn(left, right):
    return lax.dot_general(left, right, (((0,), (0,)), ((), ())), preferred_element_type=F32)


def shape_of(shape, dtype):
    return pltpu.HBM(shape, dtype)


def far(value):
    return pltpu.with_memory_space_constraint(value, pltpu.HBM)


def bring(value):
    return pltpu.with_memory_space_constraint(value, pltpu.VMEM)


def all_far(values):
    return [far(value) for value in values]


def params(limit=VMEM_LIMIT):
    return pltpu.CompilerParams(vmem_limit_bytes=limit)


def cost(macs, moved):
    return pl.CostEstimate(flops=int(2 * macs), bytes_accessed=int(moved), transcendentals=0)


SMEM_SPEC = pl.BlockSpec(memory_space=pltpu.SMEM)
ANY_SPEC = pl.BlockSpec(memory_space=pl.ANY)
CORE_SPEC = pl.BlockSpec(memory_space=pltpu.VMEM)


def whole(shape):
    return pl.BlockSpec(shape, lambda *_: (0,) * len(shape))


def kept(shape):
    return pl.BlockSpec(shape, lambda *_: (0,) * len(shape), pipeline_mode=pl.Buffered(1))


def split_kernel(place_ref, both_ref, own_ref, other_ref):
    apart = jnp.swapaxes(both_ref[...], 0, 1)
    first = place_ref[0] == 0
    own_ref[...] = jnp.where(first, apart[0], apart[1])
    other_ref[...] = jnp.where(first, apart[1], apart[0])


def other_kernel(place_ref, both_ref, other_ref):
    apart = jnp.swapaxes(both_ref[...], 0, 1)
    other_ref[...] = jnp.where(place_ref[0] == 0, apart[1], apart[0])


def other_of(place, both):
    rows, _, width = both.shape
    step = rows // 2
    return pl.pallas_call(
        other_kernel,
        grid=(2,),
        in_specs=[SMEM_SPEC, pl.BlockSpec((step, 2, width), lambda i: (i, 0, 0))],
        out_specs=pl.BlockSpec((step, width), lambda i: (i, 0)),
        out_shape=shape_of((rows, width), both.dtype),
        compiler_params=params(16 * MIB),
        cost_estimate=cost(0, 3 * rows * width * 2),
    )(place, far(both))


def merge_kernel(place_ref, own_ref, other_ref, both_ref):
    first = place_ref[0] == 0
    own, other = own_ref[...], other_ref[...]
    apart = jnp.stack([jnp.where(first, own, other), jnp.where(first, other, own)])
    both_ref[...] = jnp.swapaxes(apart, 0, 1)


def place_of(half, place_ref, rows):
    return jnp.where(half == 0, place_ref[0], 1 - place_ref[0]) * rows


def length_of(place_ref, lengths_ref):
    return jnp.where(place_ref[0] == 0, lengths_ref[0], lengths_ref[1])


def parts_of(values, count):
    parts = []
    for _ in range(count):
        part = values.astype(BF16)
        parts.append(part)
        values = values - part.astype(F32)
    return parts


def exact_dot(values, weight, dot):
    rows = values.shape[0]
    product = dot(jnp.concatenate(parts_of(values, 3), axis=0), weight)
    return product[:rows] + product[rows : 2 * rows] + product[2 * rows :]


def prefix_kernel(embed_ref, hw_ref, hb_ref, ow_ref, ob_ref, act_ref, key_ref, value_ref):
    width = key_ref.shape[1]
    act = jnp.tanh(exact_dot(embed_ref[...], hw_ref[...], dot_nn) + hb_ref[...])
    act_ref[...] = act
    pair = exact_dot(act, ow_ref[...], dot_nn) + ob_ref[...]
    key_ref[...] = pair[:, :width].astype(BF16)
    value_ref[...] = pair[:, width:].astype(BF16)


def prefix_forward(embed, hidden_w, hidden_b, out_w, out_b):
    width, hidden = hidden_w.shape
    return pl.pallas_call(
        prefix_kernel,
        out_shape=[
            shape_of((PAD, hidden), F32),
            shape_of((PAD, width), BF16),
            shape_of((PAD, width), BF16),
        ],
        compiler_params=params(16 * MIB),
        cost_estimate=cost(3 * PAD * hidden * 3 * width * 4, 6 * hidden * width),
    )(embed, far(hidden_w), hidden_b[None], far(out_w), out_b[None])


def prefix_back_kernel(
    count, pairs_ref, act_ref, embed_ref, hw_ref, ow_ref, place_ref, own_ref, other_ref,
    both_ref, eg_ref, hwg_ref, hbg_ref, owg_ref, obg_ref, ubg_ref, dbg_ref,
):
    merge_kernel(place_ref, own_ref[...], other_ref, both_ref)
    total = pairs_ref[0]
    for line in range(1, pairs_ref.shape[0]):
        total = total + pairs_ref[line]
    ubg_ref[...] = total[count : count + 1]
    dbg_ref[...] = total[count + 1 : count + 2, : dbg_ref.shape[1]]
    pair = jnp.concatenate([total[:PAD], total[PAD:]], axis=1)
    rows = lax.broadcasted_iota(jnp.int32, pair.shape, 0)
    pair = jnp.where(rows < count, pair, 0.0)
    act = act_ref[...]
    obg_ref[...] = jnp.sum(pair, axis=0, keepdims=True)
    high, low = parts_of(pair, 2)
    back = dot_nt(jnp.concatenate([high, low], axis=0), ow_ref[...])
    act_grad = (back[:PAD] + back[PAD:]) * (1.0 - act * act)
    act_high, act_low = parts_of(act, 2)
    owg_ref[...] = dot_tn(
        jnp.concatenate([act_high, act_low, act_high], axis=0),
        jnp.concatenate([high, high, low], axis=0),
    )
    hbg_ref[...] = jnp.sum(act_grad, axis=0, keepdims=True)
    high, low = parts_of(act_grad, 2)
    embed_high, embed_low = parts_of(embed_ref[...], 2)
    hwg_ref[...] = dot_tn(
        jnp.concatenate([embed_high, embed_low, embed_high], axis=0),
        jnp.concatenate([high, high, low], axis=0),
    )
    back = dot_nt(jnp.concatenate([high, low], axis=0), hw_ref[...])
    eg_ref[...] = (back[:PAD] + back[PAD:])[:count]


def prefix_backward(count, adapt, pairs, act, embed, hidden_w, out_w, place, own, other):
    width, hidden = hidden_w.shape
    core = [CORE_SPEC] * 5
    return pl.pallas_call(
        functools.partial(prefix_back_kernel, count),
        in_specs=core + [SMEM_SPEC, CORE_SPEC, CORE_SPEC],
        out_shape=[
            shape_of((own.shape[0], 2, width), BF16),
            shape_of((count, width), F32),
            shape_of((width, hidden), F32),
            shape_of((1, hidden), F32),
            shape_of((hidden, 2 * width), F32),
            shape_of((1, 2 * width), F32),
            shape_of((1, width), F32),
            shape_of((1, adapt), F32),
        ],
        compiler_params=params(24 * MIB),
        cost_estimate=cost(96 * hidden * width * 6, 20 * hidden * width),
    )(far(pairs), act, embed, far(hidden_w), far(out_w), place, far(own), far(other))


def project_kernel(apart, x_ref, wq_ref, wk_ref, wv_ref, *refs):
    if apart:
        place_ref, both_ref, q_ref, k_ref, v_ref, own_ref, other_ref, x_own_ref = refs
        split_kernel(place_ref, both_ref, own_ref, other_ref)
        rows = jnp.swapaxes(x_ref[...], 0, 1)
        x = jnp.where(place_ref[0] == 0, rows[0], rows[1])
        x_own_ref[...] = x
    else:
        q_ref, k_ref, v_ref = refs[-3:]
        x = x_ref[...]
    scale = LOG2E / math.sqrt(HEAD_DIM)
    q_ref[...] = (dot_nn(x, wq_ref[...]) * scale).astype(BF16)
    k_ref[...] = dot_nn(x, wk_ref[...]).astype(BF16)
    v_ref[...] = dot_nn(x, wv_ref[...]).astype(BF16)


def project(half, x, w_query, w_key, w_value, earlier, place=None, both=None):
    rows, width = x.shape[0], x.shape[-1]
    step = rows // 2
    apart = both is not None
    block = pl.BlockSpec((step, width), lambda i: (i, 0))
    out_specs = [pl.BlockSpec((step, width), lambda i: (2 * half + i, 0))] * 3
    out_shape = [shape_of((2 * rows, width), BF16)] * 3
    more_specs, more = [ANY_SPEC] * len(earlier), all_far(earlier)
    if apart:
        more_specs = [SMEM_SPEC, pl.BlockSpec((step, 2, width), lambda i: (i, 0, 0))]
        more = [place, far(both)]
        out_specs = out_specs + [block] * 3
        out_shape = out_shape + [shape_of((rows, width), BF16)] * 3
    return pl.pallas_call(
        functools.partial(project_kernel, apart),
        grid=(2,),
        in_specs=[more_specs[1] if apart else block] + [CORE_SPEC] * 3 + more_specs,
        out_specs=out_specs,
        out_shape=out_shape,
        input_output_aliases={4 + i: i for i in range(len(earlier))},
        compiler_params=params(20 * MIB),
        cost_estimate=cost(3 * rows * width * width, 2 * (4 * rows * width + 3 * width * width)),
    )(far(x) if apart else x, bring(w_query), bring(w_key), bring(w_value), *more)


def head_lanes(head, rows, lanes):
    place = lax.broadcasted_iota(jnp.int32, (rows, lanes), 1)
    return (place // HEAD_DIM == head).astype(F32).astype(BF16)


def first_lane(values):
    lane = lax.broadcasted_iota(jnp.int32, (values.shape[0], 128), 1)
    return jnp.where(lane == 0, values, 0.0).astype(BF16)


def block_diagonal(rows):
    return jnp.concatenate(
        [rows * head_lanes(head, rows.shape[0], LANES) for head in range(GROUP)], axis=0
    )


def attend_kernel(
    prefixed, first, place_ref, lengths_ref, q_ref, k_ref, v_ref, pk_ref, pv_ref, *refs
):
    pt_ref, ot_ref, st_ref, pp_ref, *scores = refs[-6:]
    keys = k_ref.shape[0]
    queries = q_ref.shape[0]
    half = (pl.program_id(0) + first) // 2

    def quadrant(count):
        place = place_of(half, place_ref, keys) + lax.broadcasted_iota(jnp.int32, (keys, 128), 0)
        bias = first_lane(jnp.where(place < length_of(place_ref, lengths_ref), 0.0, MASKED))
        ones = first_lane(jnp.ones((queries, 128), F32))
        tail = jnp.ones((16, keys), BF16)
        masks = [head_lanes(head, queries, 128) for head in range(2)]

        def score(head):
            pair = slice((head // 2) * 128, (head // 2 + 1) * 128)
            k_aug = jnp.concatenate([k_ref[:, pair], bias], axis=1)
            q_aug = jnp.concatenate([q_ref[:, pair] * masks[head % 2], ones], axis=1)
            scores[head % 2][...] = dot_nt(k_aug, q_aug)

        def weigh(head):
            own = scores[head % 2]
            top = jnp.max(own[...], axis=0, keepdims=True)
            if count:
                lead_scores = lead[head * PAD : (head + 1) * PAD]
                top = jnp.maximum(top, jnp.max(lead_scores, axis=0, keepdims=True))
            pt_ref[head] = jnp.exp2(own[...] - top).astype(BF16)
            st_ref[0, head : head + 1, :] = top
            if not count:
                return 0.0
            lead_weights = jnp.exp2(lead_scores - top).astype(BF16)
            pp_ref[0, head * PAD : (head + 1) * PAD, :] = lead_weights
            return jnp.sum(lead_weights.astype(F32), axis=0, keepdims=True)

        def mix(head, lead_total):
            rows = slice(head * HEAD_DIM, (head + 1) * HEAD_DIM)
            mixed_rows = dot_nn(jnp.concatenate([turned[rows], tail], axis=0), pt_ref[head])
            mixed = mixed_rows[:HEAD_DIM]
            if count:
                lead_weights = pp_ref[0, head * PAD : (head + 1) * PAD, :]
                mixed = mixed + dot_nn(lead_turned[rows], lead_weights)
            ot_ref[rows, :] = mixed.astype(BF16)
            total_row = mixed_rows[HEAD_DIM : HEAD_DIM + 1] + lead_total
            st_ref[0, GROUP + head : GROUP + head + 1, :] = total_row

        score(0)
        turned = v_ref[...].T
        if count:
            lead_turned = pv_ref[...].T
            lead = dot_nt(block_diagonal(pk_ref[...]), q_ref[...])
            row = lax.broadcasted_iota(jnp.int32, lead.shape, 0)
            lead = jnp.where(row % PAD < count, lead, MASKED)
        lead_totals = []
        for head in range(GROUP):
            if head + 1 < GROUP:
                score(head + 1)
            lead_totals.append(weigh(head))
            if head:
                mix(head - 1, lead_totals[head - 1])
        mix(GROUP - 1, lead_totals[GROUP - 1])

    @pl.when(half == 0)
    def _():
        quadrant(prefixed)

    @pl.when(half == 1)
    def _():
        quadrant(0)


def attend(count, place, lengths, first, quadrants, q, k, v, lead, earlier):
    tokens, width = q.shape
    rows = tokens // 2
    groups = width // LANES
    last = groups - 1

    def lead_place(i, g):
        quadrant = i + first
        return (jnp.where(quadrant < 2, g, last), 0, jnp.minimum(quadrant, 1))

    keys = pl.BlockSpec((rows, LANES), lambda i, g: ((i + first) // 2, g))
    in_specs = [
        SMEM_SPEC,
        SMEM_SPEC,
        pl.BlockSpec((rows, LANES), lambda i, g: ((i + first) % 2, g)),
        keys,
        keys,
    ]
    in_specs += [pl.BlockSpec((PAD, LANES), lambda i, g: (0, g))] * 2
    out_specs = [
        pl.BlockSpec(
            (None, GROUP, rows, rows), lambda i, g: ((i + first) // 2, g, 0, (i + first) % 2)
        ),
        pl.BlockSpec((None, LANES, rows), lambda i, g: ((i + first) // 2, g, (i + first) % 2)),
        pl.BlockSpec(
            (None, 1, 2 * GROUP, rows), lambda i, g: ((i + first) // 2, g, 0, (i + first) % 2)
        ),
        pl.BlockSpec((1, GROUP * PAD, rows), lead_place),
    ]
    out_shape = [
        shape_of((2, groups * GROUP, rows, tokens), BF16),
        shape_of((2, width, tokens), BF16),
        shape_of((2, groups, 2 * GROUP, tokens), F32),
        shape_of((groups, GROUP * PAD, tokens), BF16),
    ]
    macs = quadrants * groups * GROUP * rows * rows * 256 * 2
    return pl.pallas_call(
        functools.partial(attend_kernel, count, first),
        grid=(quadrants, groups),
        in_specs=in_specs + [ANY_SPEC] * len(earlier),
        out_specs=out_specs,
        out_shape=out_shape,
        input_output_aliases={7 + i: i for i in range(len(earlier))},
        scratch_shapes=[pltpu.VMEM((rows, rows), F32)] * 2,
        compiler_params=params(16 * MIB),
        cost_estimate=cost(macs, quadrants * 14 * MIB),
    )(place, lengths, *all_far((q, k, v, *lead, *earlier)))


def lead_back_kernel(
    count, q_ref, up_ref, rst_ref, del_ref, pp_ref, pk_ref, pv_ref, bias_ref, pair_ref, dqt_ref
):
    queries = q_ref.shape[0]
    for part in range(rst_ref.shape[0]):
        lanes = slice(part * LANES, (part + 1) * LANES)
        ups = []
        deltas = []
        for head in range(GROUP):
            rows = slice(part * LANES + head * HEAD_DIM, part * LANES + (head + 1) * HEAD_DIM)
            share = rst_ref[part, head : head + 1, :]
            ups.append((up_ref[rows, :].astype(F32) * share).astype(BF16))
            delta = del_ref[part, head : head + 1, :] * share
            deltas.append(jnp.broadcast_to(delta, (PAD, queries)))
        up = jnp.concatenate(ups, axis=0)
        delta = jnp.concatenate(deltas, axis=0)
        weights = pp_ref[part]
        weight_grads = dot_nn(block_diagonal(pv_ref[:, lanes]), up)
        score_grads = (weights.astype(F32) * (weight_grads - delta)).astype(BF16)
        dqt_ref[lanes, :] = dot_tn(block_diagonal(pk_ref[:, lanes]), score_grads).astype(BF16)
        key_grads = dot_nn(score_grads, q_ref[:, lanes]) * (1.0 / LOG2E)
        value_grads = dot_nt(weights, up)
        lane = lax.broadcasted_iota(jnp.int32, (PAD, LANES), 1) // HEAD_DIM
        key_total = jnp.zeros((PAD, LANES), F32)
        value_total = jnp.zeros((PAD, LANES), F32)
        for head in range(GROUP):
            rows = slice(head * PAD, (head + 1) * PAD)
            key_total = jnp.where(lane == head, key_grads[rows], key_total)
            value_total = jnp.where(lane == head, value_grads[rows], value_total)
        row = lax.broadcasted_iota(jnp.int32, (PAD, LANES), 0)
        key_total = jnp.where(row == count, bias_ref[0:1, lanes], key_total)
        key_total = jnp.where(row == count + 1, bias_ref[1:2, lanes], key_total)
        pair_ref[:PAD, lanes] = key_total.astype(BF16)
        pair_ref[PAD:, lanes] = value_total.astype(BF16)


def lead_backward(count, q, up, shares, deltas, lead_weights, prefix_keys, prefix_values, biases):
    tokens, width = q.shape
    groups = width // LANES
    each = 2 if groups % 2 == 0 else 1
    span = each * LANES
    small = pl.BlockSpec((PAD, span), lambda g: (0, g))
    stats = pl.BlockSpec((each, 2 * GROUP, tokens), lambda g: (g, 0, 0))
    return pl.pallas_call(
        functools.partial(lead_back_kernel, count),
        grid=(groups // each,),
        in_specs=[
            pl.BlockSpec((tokens, span), lambda g: (0, g)),
            pl.BlockSpec((span, tokens), lambda g: (g, 0)),
            stats,
            stats,
            pl.BlockSpec((each, GROUP * PAD, tokens), lambda g: (g, 0, 0)),
            small,
            small,
            pl.BlockSpec((8, span), lambda g: (0, g)),
        ],
        out_specs=[
            pl.BlockSpec((2 * PAD, span), lambda g: (0, g)),
            pl.BlockSpec((span, tokens), lambda g: (g, 0)),
        ],
        out_shape=[
            jax.ShapeDtypeStruct((2 * PAD, width), BF16),
            shape_of((width, tokens), BF16),
        ],
        compiler_params=params(18 * MIB),
        cost_estimate=cost(groups * 4 * GROUP * PAD * tokens * LANES, 10 * MIB),
    )(*all_far((q, up, shares, deltas, lead_weights)), prefix_keys, prefix_values, biases)


def attend_back_kernel(
    half,
    last_keys,
    last_queries,
    has_earlier,
    q_ref,
    k_ref,
    v_ref,
    up_ref,
    rst_ref,
    del_ref,
    pt_ref,
    dqt_in_ref,
    *refs,
):
    dq_ref, dk_ref, dv_ref = refs[-5:-2]
    weight_grads = refs[-2:]
    queries = q_ref.shape[0]
    lane = lax.broadcasted_iota(jnp.int32, (queries, 128), 1) // HEAD_DIM
    masks = [(lane == head).astype(F32).astype(BF16) for head in range(2)]
    zeros = jnp.zeros((HEAD_DIM, queries), BF16)
    turned = k_ref[...].T
    ups = {}
    grads = {}
    query_grads = []
    key_grads = []
    value_grads = []

    def pair_of(head):
        return slice((head // 2) * 128, (head // 2 + 1) * 128)

    def rows_of(head):
        return slice(head * HEAD_DIM, (head + 1) * HEAD_DIM)

    def share_of(head):
        return rst_ref[0, half * GROUP + head : half * GROUP + head + 1, :]

    def weight_grad(head):
        up = (up_ref[rows_of(head), :].astype(F32) * share_of(head)).astype(BF16)
        ups[head] = jnp.concatenate([up, zeros] if head % 2 == 0 else [zeros, up], axis=0)
        weight_grads[head % 2][...] = dot_nn(v_ref[:, pair_of(head)], ups[head])

    def score_grad(head):
        delta = del_ref[0, head : head + 1, :] * share_of(head)
        return (pt_ref[head].astype(F32) * (weight_grads[head % 2][...] - delta)).astype(BF16)

    def value_term(head):
        return dot_nt(pt_ref[head], ups[head])

    def key_term(head):
        return dot_nn(grads[head], q_ref[:, pair_of(head)] * masks[head % 2])

    def query_term(head):
        return dqt_in_ref[rows_of(head), :].astype(F32) + dot_nn(turned[rows_of(head)], grads[head])

    weight_grad(0)
    for head in range(GROUP):
        if head + 1 < GROUP:
            weight_grad(head + 1)
        grads[head] = score_grad(head)
        value = value_term(head)
        query_grads.append(query_term(head))
        key = key_term(head)
        if head % 2:
            key_grads[-1] = key_grads[-1] + key
            value_grads[-1] = value_grads[-1] + value
        else:
            key_grads.append(key)
            value_grads.append(value)
    query_grad = jnp.concatenate(query_grads, axis=0)
    key_grad = jnp.concatenate(key_grads, axis=1)
    value_grad = jnp.concatenate(value_grads, axis=1)
    if not last_keys:
        dq_ref[...] = query_grad.astype(BF16)
    else:
        dq_ref[...] = (query_grad * (1.0 / math.sqrt(HEAD_DIM))).astype(BF16).T
    if has_earlier:
        key_grad = key_grad + refs[0][...].astype(F32)
        value_grad = value_grad + refs[1][...].astype(F32)
    if last_queries:
        key_grad = key_grad * (1.0 / LOG2E)
    dk_ref[...] = key_grad.astype(BF16)
    dv_ref[...] = value_grad.astype(BF16)


def attend_back(
    key_half, query_half, last_keys, last_queries, q, k, v, up, shares, deltas, weights, dqt, earlier
):
    tokens, width = q.shape
    rows = tokens // 2
    groups = width // LANES
    query_columns = pl.BlockSpec((LANES, rows), lambda g: (g, query_half))
    stats = pl.BlockSpec((1, 2 * GROUP, rows), lambda g: (g, 0, query_half))
    finished = pl.BlockSpec((rows, LANES), lambda g: (0, g))
    out_columns = pl.BlockSpec((LANES, rows), lambda g: (g, 0))
    sofar = query_columns if dqt.shape[1] == tokens else out_columns
    macs = groups * GROUP * rows * rows * 256 * 4
    return pl.pallas_call(
        functools.partial(
            attend_back_kernel, key_half, last_keys, last_queries, len(earlier) > 0
        ),
        grid=(groups,),
        in_specs=[
            pl.BlockSpec((rows, LANES), lambda g: (query_half, g)),
            pl.BlockSpec((rows, LANES), lambda g: (key_half, g)),
            pl.BlockSpec((rows, LANES), lambda g: (key_half, g)),
            query_columns,
            stats,
            stats,
            pl.BlockSpec((None, GROUP, rows, rows), lambda g: (key_half, g, 0, query_half)),
            sofar,
        ]
        + [finished] * len(earlier),
        out_specs=[finished if last_keys else out_columns, finished, finished],
        out_shape=[
            shape_of((rows, width) if last_keys else (width, rows), BF16),
            shape_of((rows, width), BF16),
            shape_of((rows, width), BF16),
        ],
        scratch_shapes=[pltpu.VMEM((rows, rows), F32)] * 2,
        compiler_params=params(18 * MIB),
        cost_estimate=cost(macs, 12 * MIB),
    )(*all_far((q, k, v, up, shares, deltas, weights, dqt, *earlier)))


def gelu_pair(values):
    scaled = values * 0.7071067811865476
    below = 0.5 * lax.erf(scaled) + 0.5
    decay = jnp.exp2(scaled * scaled * (-LOG2E))
    return values * below, below + values * 0.3989422804014327 * decay


def row_mean(values):
    return jnp.mean(values, axis=-1, keepdims=True)


def front_kernel(
    tiles,
    place_ref,
    lengths_ref,
    x_own_ref,
    x_other_ref,
    ot_own_ref,
    ot_other_ref,
    st_own_ref,
    st_other_ref,
    og_own_ref,
    og_other_ref,
    gain_one_ref,
    gain_two_ref,
    down_bias_ref,
    up_bias_ref,
    wo_ref,
    fin_ref,
    fout_ref,
    down_ref,
    up_ref,
    out_own_ref,
    out_other_ref,
    rst_ref,
    mix_ref,
    slope_ref,
    grad_low_ref,
    norm_grad_ref,
    normed_ref,
    inv_ref,
    kept_ref,
    sent_ref,
    bias_grad_ref,
    act_ref,
    squeeze_ref,
    low_ref,
):
    step = pl.program_id(0)
    tile = x_own_ref.shape[0]
    width = x_own_ref.shape[1]
    hidden = fin_ref.shape[1]
    chunk = 512
    chunks = [slice(first, first + chunk) for first in range(0, hidden, chunk)]
    own = step < tiles // 2
    x = jnp.where(own, x_own_ref[...], x_other_ref[...]).astype(F32)
    top_own, top_other = st_own_ref[:, :GROUP, :], st_other_ref[:, :GROUP, :]
    top = jnp.maximum(top_own, top_other)
    share_own, share_other = jnp.exp2(top_own - top), jnp.exp2(top_other - top)
    inverse = 1.0 / (
        st_own_ref[:, GROUP:, :] * share_own + st_other_ref[:, GROUP:, :] * share_other
    )
    rst_ref[:, :GROUP, :] = share_own * inverse
    rst_ref[:, GROUP:, :] = share_other * inverse
    mixes = []
    for head in range(width // HEAD_DIM):
        rows = slice(head * HEAD_DIM, (head + 1) * HEAD_DIM)
        group, place = head // GROUP, head % GROUP
        mixes.append(
            (
                ot_own_ref[rows, :].astype(F32) * rst_ref[group, place : place + 1, :]
                + ot_other_ref[rows, :].astype(F32) * rst_ref[group, GROUP + place : GROUP + place + 1, :]
            ).astype(BF16)
        )
    mix = jnp.concatenate(mixes, axis=0)
    mix_ref[...] = mix
    resid_one = x + dot_tn(mix, wo_ref[...])
    centred = resid_one - row_mean(resid_one)
    inv_one = lax.rsqrt(row_mean(centred * centred) + 1e-05)
    normed = centred * inv_one
    normed_ref[...] = normed.astype(BF16)
    inv_ref[...] = inv_one
    norm_one = normed * gain_one_ref[...]
    norm_low = norm_one.astype(BF16)

    squeeze = dot_nn(norm_low, down_ref[...]) + down_bias_ref[...]
    inner = dot_nn(norm_low, fin_ref[:, chunks[0]])
    squeeze_act, squeeze_slope = gelu_pair(squeeze)
    squeeze_act = squeeze_act.astype(BF16)
    resid_two = norm_one + 4.0 * (dot_nn(squeeze_act, up_ref[...]) + up_bias_ref[...])
    for place, columns in enumerate(chunks):
        more = place + 1 < len(chunks)
        coming = dot_nn(norm_low, fin_ref[:, chunks[place + 1]]) if more else None
        act, slope = gelu_pair(inner)
        slope_ref[:, columns] = slope.astype(BF16)
        resid_two = resid_two + dot_nn(act.astype(BF16), fout_ref[columns, :])
        inner = coming

    centred = resid_two - row_mean(resid_two)
    inv_two = lax.rsqrt(row_mean(centred * centred) + 1e-05)
    normed_two = centred * inv_two
    base = place_of(step // (tiles // 2), place_ref, (tiles // 2) * tile) + step % (tiles // 2) * tile
    place = base + lax.broadcasted_iota(jnp.int32, (tile, 1), 0)
    valid = (place < length_of(place_ref, lengths_ref)).astype(F32)
    gain_two = gain_two_ref[...]
    out = (normed_two * gain_two * valid).astype(BF16)
    upstream = jnp.where(own, og_own_ref[...], og_other_ref[...]).astype(F32) * valid * gain_two
    grad_two = inv_two * (
        upstream - row_mean(upstream) - normed_two * row_mean(upstream * normed_two)
    )
    grad_low = grad_two.astype(BF16)
    grad_adapt = 4.0 * grad_low
    grad_squeeze = (dot_nt(grad_adapt, up_ref[...]) * squeeze_slope).astype(BF16)
    norm_grad_ref[...] = (grad_two + dot_nt(grad_squeeze, down_ref[...])).astype(BF16)
    here = pl.ds(pl.multiple_of(step * tile, tile), tile)
    grad_low_ref[here, :] = grad_low
    act_ref[here, :] = squeeze_act
    squeeze_ref[here, :] = grad_squeeze
    low_ref[here, :] = norm_low
    up_bias_grad = jnp.sum(grad_adapt.astype(F32), axis=0, keepdims=True)
    down_bias_grad = jnp.sum(grad_squeeze.astype(F32), axis=0, keepdims=True)
    adapt = down_bias_grad.shape[1]

    @pl.when(own)
    def _():
        out_own_ref[...] = out

    @pl.when(jnp.logical_not(own))
    def _():
        out_other_ref[...] = out

    @pl.when(step == 0)
    def _():
        bias_grad_ref[...] = jnp.zeros_like(bias_grad_ref)
        bias_grad_ref[0:1, :] = up_bias_grad
        bias_grad_ref[1:2, :adapt] = down_bias_grad

    @pl.when(step > 0)
    def _():
        bias_grad_ref[0:1, :] += up_bias_grad
        bias_grad_ref[1:2, :adapt] += down_bias_grad

    @pl.when(step == tiles - 1)
    def _():
        first = place_ref[1] == 0
        up_total = (4.0 * dot_tn(act_ref[...], grad_low_ref[...])).astype(BF16)
        down_total = dot_tn(squeeze_ref[...], low_ref[...]).astype(BF16)
        kept_ref[...] = jnp.where(first, up_total, down_total)
        sent_ref[...] = jnp.where(first, down_total, up_total)


def front(
    place, lengths, x_own, x_other, mix_parts, tops_sums, og_own, og_other, w_output, attn_gain,
    ffn_in, ffn_out, ffn_gain, down, down_bias, up, up_bias,
):
    rows, width = x_own.shape
    tokens = 2 * rows
    hidden = ffn_in.shape[1]
    adapt = down.shape[1]
    groups = width // LANES
    tile = 256
    tiles = tokens // tile
    near = pl.BlockSpec((tile, width), lambda i: (jnp.minimum(i, tiles // 2 - 1), 0))
    far = pl.BlockSpec((tile, width), lambda i: (jnp.maximum(i - tiles // 2, 0), 0))
    row_block = pl.BlockSpec((tile, width), lambda i: (i, 0))
    column_block = pl.BlockSpec((width, tile), lambda i: (0, i))
    stats = pl.BlockSpec((groups, 2 * GROUP, tile), lambda i: (0, 0, i))
    mixes = [pl.BlockSpec((None, width, tile), lambda i, half=half: (half, 0, i)) for half in range(2)]
    tops = [
        pl.BlockSpec((None, groups, 2 * GROUP, tile), lambda i, half=half: (half, 0, 0, i))
        for half in range(2)
    ]
    return pl.pallas_call(
        functools.partial(front_kernel, tiles),
        grid=(tiles,),
        in_specs=[
            SMEM_SPEC, SMEM_SPEC, near, far, *mixes, *tops, near, far,
            whole((1, width)), whole((1, width)), whole((1, adapt)), whole((1, width)),
        ] + [CORE_SPEC] * 5,
        out_specs=[
            near, far, stats, column_block, pl.BlockSpec((tile, hidden), lambda i: (i, 0)),
            kept((tokens, width)), row_block, row_block, pl.BlockSpec((tile, 1), lambda i: (i, 0)),
            kept((adapt, width)), kept((adapt, width)), whole((8, width)),
        ],
        out_shape=[
            shape_of((rows, width), BF16),
            shape_of((rows, width), BF16),
            shape_of((groups, 2 * GROUP, tokens), F32),
            shape_of((width, tokens), BF16),
            shape_of((tokens, hidden), BF16),
            shape_of((tokens, width), BF16),
            shape_of((tokens, width), BF16),
            shape_of((tokens, width), BF16),
            shape_of((tokens, 1), F32),
            shape_of((adapt, width), BF16),
            shape_of((adapt, width), BF16),
            shape_of((8, width), F32),
        ],
        scratch_shapes=[
            pltpu.VMEM((tokens, adapt), BF16),
            pltpu.VMEM((tokens, adapt), BF16),
            pltpu.VMEM((tokens, width), BF16),
        ],
        compiler_params=params(32 * MIB),
        cost_estimate=cost(tokens * width * (width + 2 * hidden + 6 * adapt), 60 * MIB),
    )(
        place,
        lengths,
        *all_far((x_own, x_other, mix_parts, mix_parts, tops_sums, tops_sums, og_own, og_other)),
        attn_gain[None], ffn_gain[None], down_bias[None], up_bias[None],
        *[bring(item) for item in (w_output, ffn_in, ffn_out, down, up)],
    )


def rear_kernel(
    grad_low_ref, norm_grad_ref, slope_ref, normed_ref, inv_ref, mix_ref, gain_ref, wo_ref, fin_ref,
    fout_ref, grad_one_ref, up_ref, del_ref,
):
    hidden = fin_ref.shape[1]
    chunk = 1024
    chunks = [slice(first, first + chunk) for first in range(0, hidden, chunk)]
    grad_low = grad_low_ref[...]
    grad_norm = norm_grad_ref[...].astype(F32)
    inner = dot_nt(grad_low, fout_ref[chunks[0], :])
    for place, columns in enumerate(chunks):
        more = place + 1 < len(chunks)
        coming = dot_nt(grad_low, fout_ref[chunks[place + 1], :]) if more else None
        low = (inner * slope_ref[:, columns].astype(F32)).astype(BF16)
        grad_norm = grad_norm + dot_nt(low, fin_ref[:, columns])
        inner = coming
    grad = grad_norm * gain_ref[...]
    normed = normed_ref[...].astype(F32)
    grad_one = inv_ref[...] * (grad - row_mean(grad) - normed * row_mean(grad * normed))
    grad_low_one = grad_one.astype(BF16)
    grad_one_ref[...] = grad_low_one
    up = dot_nt(wo_ref[...], grad_low_one).astype(BF16)
    up_ref[...] = up
    product = up.astype(F32) * mix_ref[...].astype(F32)
    for head in range(product.shape[0] // HEAD_DIM):
        rows = slice(head * HEAD_DIM, (head + 1) * HEAD_DIM)
        group, place = head // GROUP, head % GROUP
        del_ref[group, place : place + 1, :] = jnp.sum(product[rows], axis=0, keepdims=True)
    del_ref[:, GROUP:, :] = jnp.zeros_like(del_ref[:, GROUP:, :])


def rear(grad_low, norm_grad, slope, normed, inv, mix, w_output, attn_gain, ffn_in, ffn_out):
    tokens, width = grad_low.shape
    hidden = ffn_in.shape[1]
    groups = width // LANES
    tile = 256
    row_block = pl.BlockSpec((tile, width), lambda i: (i, 0))
    column_block = pl.BlockSpec((width, tile), lambda i: (0, i))
    return pl.pallas_call(
        rear_kernel,
        grid=(tokens // tile,),
        in_specs=[
            row_block, row_block, pl.BlockSpec((tile, hidden), lambda i: (i, 0)), row_block,
            pl.BlockSpec((tile, 1), lambda i: (i, 0)), column_block, whole((1, width)),
        ] + [CORE_SPEC] * 3,
        out_specs=[
            row_block, column_block, pl.BlockSpec((groups, 2 * GROUP, tile), lambda i: (0, 0, i)),
        ],
        out_shape=[
            shape_of((tokens, width), BF16),
            shape_of((width, tokens), BF16),
            shape_of((groups, 2 * GROUP, tokens), F32),
        ],
        compiler_params=params(22 * MIB),
        cost_estimate=cost(tokens * width * (width + 2 * hidden), 50 * MIB),
    )(*all_far((grad_low, norm_grad, slope, normed, inv, mix)), attn_gain[None], bring(w_output), bring(ffn_in), bring(ffn_out))


def input_grad_kernel(last, place_ref, grad_ref, dq_ref, dk_ref, dv_ref, wq_ref, wk_ref, wv_ref, *refs):
    total = grad_ref[...].astype(F32) + dot_nt(dq_ref[...], wq_ref[...])
    total = total + dot_nt(dk_ref[...], wk_ref[...])
    total = total + dot_nt(dv_ref[...], wv_ref[...])
    total = total.astype(BF16)
    if not last:
        refs[0][...] = total
        return
    arrived_ref, half_ref, far_ref, both_ref, up_ref, down_ref = refs
    merge_kernel(place_ref, total, arrived_ref, both_ref)
    first = place_ref[1] == 0
    half, other = half_ref[...].astype(F32), far_ref[...].astype(F32)
    up_ref[...] = jnp.where(first, half, other)
    down_ref[...] = jnp.where(first, other, half).T


def input_grad(place, half, grad_one, dq, dk, dv, weights, last):
    rows, width = dk.shape
    step = rows // 2
    block = pl.BlockSpec((step, width), lambda i: (i, 0))
    columns = width // 2
    out_specs = pl.BlockSpec((rows, columns), lambda j: (0, j))
    out_shape = shape_of((rows, width), BF16)
    grad_spec = pl.BlockSpec((rows, columns), lambda j: (half, j))
    operand_spec = kept((rows, width))
    weight_spec = pl.BlockSpec((columns, width), lambda j: (j, 0))
    if last:
        grad_spec = pl.BlockSpec((step, width), lambda i: (2 * half + i, 0))
        operand_spec, weight_spec = block, CORE_SPEC
        out_specs = [
            pl.BlockSpec((step, 2, width), lambda i: (i, 0, 0)),
            block,
            pl.BlockSpec((width, step), lambda i: (0, i)),
        ]
        out_shape = [
            shape_of((rows, 2, width), BF16),
            shape_of((rows, width), F32),
            shape_of((width, rows), F32),
        ]
    return pl.pallas_call(
        functools.partial(input_grad_kernel, bool(last)),
        grid=(2,),
        in_specs=[SMEM_SPEC, grad_spec]
        + [operand_spec] * 3
        + [weight_spec] * 3
        + [block] * len(last),
        out_specs=out_specs,
        out_shape=out_shape,
        compiler_params=params(26 * MIB),
        cost_estimate=cost(3 * rows * width * width, 14 * MIB),
    )(place, *all_far((grad_one, dq, dk, dv)), *[(bring if last else far)(item) for item in weights], *last)


def swap(value, seq_bit, dp_bits):
    width = lax.axis_size("dp")
    count = lax.axis_size("seq") * width
    pairs = [
        (device, ((device // width) ^ seq_bit) * width + ((device % width) ^ dp_bits))
        for device in range(count)
    ]
    return lax.ppermute(value, ("seq", "dp"), pairs)


def gather_line(value):
    width = lax.axis_size("dp")
    groups = [[4 * line + place for line in range(width // 4)] for place in range(4)]
    return lax.all_gather(value, "dp", axis_index_groups=groups)


def total(values):
    return jnp.sum(values.astype(F32), axis=0)


def square_place():
    return 2 * ((lax.axis_index("dp") // 2) % 2) + lax.axis_index("seq")


def square_swaps(values):
    return [swap(values[offset - 1], offset % 2, 2 * (offset // 2)) for offset in range(1, 4)]


def sum_square(value):
    place = square_place()
    quarters = value.reshape(4, value.shape[0] // 4, value.shape[1])
    pick = [
        lax.dynamic_index_in_dim(quarters, place ^ offset, 0, keepdims=False) for offset in range(4)
    ]
    return pick[:1] + square_swaps(pick[1:])


def add(terms):
    value = terms[0].astype(F32)
    for term in terms[1:]:
        value = value + term.astype(F32)
    return value.astype(BF16)


def tie(*values):
    return lax.optimization_barrier(values)


def on_pair(
    hidden_in,
    lengths,
    w_query,
    w_key,
    w_value,
    w_output,
    attn_gain,
    ffn_in,
    ffn_out,
    ffn_gain,
    adapter_down,
    adapter_down_bias,
    adapter_up,
    adapter_up_bias,
    prefix_embed,
    prefix_hidden_w,
    prefix_hidden_b,
    prefix_out_w,
    prefix_out_b,
    out_grad,
):
    rows, _, width = hidden_in.shape
    count = prefix_embed.shape[0]
    position = lax.axis_index("seq")
    core = lax.axis_index("dp") % 2
    place = jnp.stack([position, core]).astype(jnp.int32)

    x_other = shifted(other_of(place, hidden_in), "seq", 1)

    embed = jnp.pad(prefix_embed, ((0, PAD - count), (0, 0)))
    prefix_act, prefix_keys, prefix_values = prefix_forward(
        embed, prefix_hidden_w, prefix_hidden_b, prefix_out_w, prefix_out_b
    )
    out_grad, prefix_keys = tie(out_grad, prefix_keys)
    lead = (prefix_keys, prefix_values)
    *triple, og_own, og_send, x_own = project(
        0, hidden_in, w_query, w_key, w_value, (), place, out_grad
    )
    og_other = shifted(og_send, "seq", 1)
    begun = attend(count, place, lengths, 0, 1, *triple, lead, ())
    q, k, v = project(1, x_other, w_query, w_key, w_value, triple)
    weights, mix_parts, tops_sums, lead_weights = attend(
        count, place, lengths, 1, 3, q, k, v, lead, begun
    )

    (
        out_own, out_send, shares, mix, slope, grad_low, norm_grad, normed, inv_one,
        adapt_kept, adapt_sent, bias_grads,
    ) = front(
        place, lengths, x_own, x_other, mix_parts, tops_sums, og_own, og_other,
        w_output, attn_gain, ffn_in, ffn_out, ffn_gain, adapter_down, adapter_down_bias,
        adapter_up, adapter_up_bias,
    )
    out_other = shifted(out_send, "seq", 1)
    core_terms = [adapt_kept, swap(adapt_sent, 0, 1)]
    grad_one, upstream, deltas = rear(
        grad_low, norm_grad, slope, normed, inv_one, mix, w_output, attn_gain, ffn_in, ffn_out
    )
    upstream, out_other, adapt_sum = tie(upstream, out_other, add(core_terms))
    square_terms = sum_square(adapt_sum)
    pair, dqt = lead_backward(
        count, q, upstream, shares, deltas, lead_weights, prefix_keys, prefix_values, bias_grads
    )
    pair_core = swap(pair, 0, 1)

    back = (q, k, v)
    part_own, dk_other, dv_other = attend_back(
        1, 0, False, False, *back, upstream, shares, deltas, weights, dqt, ()
    )
    dk_other, pair, adapt_sum = tie(dk_other, add([pair, pair_core]), add(square_terms))
    adapt_line = gather_line(adapt_sum)
    pair_square = square_swaps([pair] * 3)
    part_other, dk_other, dv_other = attend_back(
        1, 1, False, True, *back, upstream, shares, deltas, weights, dqt, (dk_other, dv_other)
    )
    pair_sum = pair.astype(F32) + sum(item.astype(F32) for item in pair_square)
    part_other, pair_sum = tie(part_other, pair_sum)
    pair_line = gather_line(pair_sum)
    dq_other, dk_own, dv_own = attend_back(
        0, 1, True, False, *back, upstream, shares, deltas, weights, part_other, ()
    )
    adapt_sum = jnp.sum(adapt_line.astype(F32), axis=0).astype(BF16)
    dq_other, adapt_sum = tie(dq_other, adapt_sum)
    adapt_x, adapt_y = swap(adapt_sum, 1, 0), swap(adapt_sum, 0, 2)
    triple_weights = (w_query, w_key, w_value)
    grad_other = input_grad(place, 1, grad_one, dq_other, dk_other, dv_other, triple_weights, ())
    grad_other, dk_own, adapt_x = tie(grad_other, dk_own, adapt_x)
    grad_back = shifted(grad_other, "seq", 1)
    adapt_xy = swap(adapt_x, 0, 2)
    dq_own, dk_own, dv_own = attend_back(
        0, 0, True, True, *back, upstream, shares, deltas, weights, part_own, (dk_own, dv_own)
    )
    dq_own, pair_line, out_other, adapt_y, adapt_xy = tie(
        dq_own, pair_line, out_other, adapt_y, adapt_xy
    )
    adapt_half = jnp.stack([adapt_sum, adapt_x, adapt_y, adapt_xy])
    place_here = square_place()
    adapt_half = jnp.concatenate(
        [lax.dynamic_slice_in_dim(adapt_half, spot ^ place_here, 1, 0) for spot in range(4)]
    ).reshape(adapt_kept.shape)
    adapt_far = swap(adapt_half, 0, 1)
    layer_out, *prefix_grads = prefix_backward(
        count,
        adapter_down_bias.shape[0],
        pair_line,
        prefix_act,
        embed,
        prefix_hidden_w,
        prefix_out_w,
        place,
        out_own,
        out_other,
    )
    layer_out, grad_back, dq_own = tie(layer_out, grad_back, dq_own)
    out_w_grad = prefix_grads[3]
    input_total, up_total, down_total = input_grad(
        place, 0, grad_one, dq_own, dk_own, dv_own, triple_weights, (grad_back, adapt_half, adapt_far)
    )
    return (
        layer_out,
        input_total,
        down_total,
        prefix_grads[6][0],
        up_total,
        prefix_grads[5][0],
        prefix_grads[0],
        prefix_grads[1],
        prefix_grads[2][0],
        out_w_grad,
        prefix_grads[4][0],
    )


def solution(mesh):
    in_specs = (
        P("seq", "dp", None),
        P("dp"),
        P(),
        P(),
        P(),
        P(),
        P(),
        P(),
        P(),
        P(),
        P(),
        P(),
        P(),
        P(),
        P(),
        P(),
        P(),
        P(),
        P(),
        P("seq", "dp", None),
    )
    out_specs = (
        P("seq", "dp", None),
        P("seq", "dp", None),
        P(),
        P(),
        P(),
        P(),
        P(),
        P(),
        P(),
        P(),
        P(),
    )
    pairs = mesh.shape["seq"] == 2 and mesh.shape["dp"] % 8 == 0

    def on_one(*arrays):
        step = on_pair if pairs and arrays[0].shape[1] == 2 else on_device
        return step(*arrays)

    return jax.shard_map(
        on_one, mesh=mesh, in_specs=in_specs, out_specs=out_specs, check_vma=False
    )
```
